32 devices in a mesh: seq: 8 (over y, x, core), fsdp: 4 (over z).
Axes of the slice: x: 2, y: 2, z: 4, core: 2. Of those that a mesh axis runs over, the one named last changes fastest.
Arguments:
- tokens: bfloat16 [4, 1024, 2048], P('fsdp', 'seq'), may hold values from -6 to 6
- starts: int32 [4, 1024], P('fsdp', 'seq'), may hold values from 0 to 1, as said below
- first_gain: float32 [2048], P(('seq', 'fsdp')), may hold values from 0.1 to 1.9
- query_weight: float32 [2048, 2048], P(('seq', 'fsdp')), may hold values from -0.0625 to 0.0625
- key_weight: float32 [2048, 2048], P(('seq', 'fsdp')), may hold values from -0.0625 to 0.0625
- value_weight: float32 [2048, 2048], P(('seq', 'fsdp')), may hold values from -0.125 to 0.125
- output_weight: float32 [2048, 2048], P(('seq', 'fsdp')), may hold values from -0.375 to 0.375
- bias_table: float32 [1024], P(('seq', 'fsdp')), may hold values from -5 to 5
- second_gain: float32 [2048], P(('seq', 'fsdp')), may hold values from 0.1 to 1.9
- gate_weight: float32 [5120, 2048], P(('seq', 'fsdp')), may hold values from -0.125 to 0.125
- up_weight: float32 [5120, 2048], P(('seq', 'fsdp')), may hold values from -0.125 to 0.125
- down_weight: float32 [5120, 2048], P(('seq', 'fsdp')), may hold values from -0.078125 to 0.078125
- cotangent: bfloat16 [4, 1024, 2048], P('fsdp', 'seq'), may hold values from -6 to 6
Outputs:
- layer_out: bfloat16 [4, 1024, 2048], P('fsdp', 'seq')
- grad_tokens: bfloat16 [4, 1024, 2048], P('fsdp', 'seq')
- grad_first_gain: float32 [2048], P(('seq', 'fsdp'))
- grad_query_weight: float32 [2048, 2048], P(('seq', 'fsdp'))
- grad_key_weight: float32 [2048, 2048], P(('seq', 'fsdp'))
- grad_value_weight: float32 [2048, 2048], P(('seq', 'fsdp'))
- grad_output_weight: float32 [2048, 2048], P(('seq', 'fsdp'))
- grad_bias_table: float32 [1024], P(('seq', 'fsdp'))
- grad_second_gain: float32 [2048], P(('seq', 'fsdp'))
- grad_gate_weight: float32 [5120, 2048], P(('seq', 'fsdp'))
- grad_up_weight: float32 [5120, 2048], P(('seq', 'fsdp'))
- grad_down_weight: float32 [5120, 2048], P(('seq', 'fsdp'))
The draws below stay inside these ranges and needn't reach their ends.
Inputs may be any that keep to these rules, and one draw needn't show every extreme that they name: `starts`: in every stream position 0 is 1; one document begins within the first 128 positions and the next start lies within the last 128 positions.
All inputs are finite; a program needn't handle non-finite values.
Results may differ from the reference program's by a relative error of at most 0.024.
Values may be sent and summed in bfloat16 or wider, within the bound.
No kernel may reach another device: no remote copies, remote signals or barrier semaphores. Data moves between devices by JAX's collectives and lax.ppermute only.
A program may use at most 192 MiB of HBM per device.

```python
import jax
import jax.numpy as jnp
from jax import lax

D = 2048
H = 32
DK = 64
FF = 5120
BUCKETS = 32
TOK_DEV = 128
SEQLEN = 1024
STREAMS = 4


def draw_starts(key, part):
    key = jax.random.fold_in(key, 11)

    def one_stream(stream_key):
        key_first, key_last, key_coin = jax.random.split(stream_key, 3)
        first_pos = jax.random.randint(key_first, (), 1, TOK_DEV)
        last_pos = jax.random.randint(key_last, (), SEQLEN - TOK_DEV + 1, SEQLEN)
        position = jnp.arange(SEQLEN, dtype=jnp.int32)
        coin = jax.random.randint(key_coin, (SEQLEN,), 0, 6) == 0
        inside = (position > first_pos) & (position < last_pos)
        flag = jnp.where(inside, False, coin) | (position == 0) | (position == first_pos) | (position == last_pos)
        return flag.astype(jnp.int32)
    return jax.vmap(one_stream)(jax.random.split(key, STREAMS))


def steps_of(own_key, extent, cuts, least, high):
    factor_of, own = 1.0, jax.random.fold_in(own_key, 6)
    for dim, parts in cuts:
        steps = jnp.exp(jax.random.uniform(jax.random.fold_in(own, dim), (parts,), jnp.float32, least / len(cuts), high / len(cuts)))
        factor_of = factor_of * jnp.repeat(steps, extent[dim] // parts).reshape([-1 if axis == dim else 1 for axis in range(len(extent))])
    return factor_of


def noise(key, extent, deviation, reach, cuts=(), kind=jnp.bfloat16):
    level = steps_of(key, extent, cuts, -0.22, 0.18) if cuts else 1.0
    values = jax.random.normal(key, extent, jnp.float32) * deviation * level
    return jnp.minimum(jnp.maximum(values, -reach), reach).astype(kind)


def setup_inputs(seed: int = 0) -> dict:
    splits = jax.random.split(jax.random.key(seed), 14)
    return {
        "tokens": noise(splits[0], (STREAMS, SEQLEN, D), 1.0, 6.0, ((0, 4), (1, 8))),
        "starts": draw_starts(jax.random.fold_in(splits[13], 71), 0),
        "first_gain": jnp.clip(1.0 + 0.18 * jax.random.normal(splits[2], (D,), jnp.float32), 0.1, 1.9),
        "query_weight": noise(splits[3], (D, D), (4 * D) ** -0.5, 0.0625, ((0, 32),), jnp.float32),
        "key_weight": noise(splits[4], (D, D), (4 * D) ** -0.5, 0.0625, ((0, 32),), jnp.float32),
        "value_weight": noise(splits[5], (D, D), D ** -0.5, 0.125, ((0, 32),), jnp.float32),
        "output_weight": noise(splits[6], (D, D), (D // 8) ** -0.5, 0.375, ((0, 32),), jnp.float32),
        "bias_table": noise(splits[7], (H * BUCKETS,), 1.0, 5.0, ((0, 32),), jnp.float32),
        "second_gain": jnp.clip(1.0 + 0.18 * jax.random.normal(splits[8], (D,), jnp.float32), 0.1, 1.9),
        "gate_weight": noise(splits[9], (FF, D), D ** -0.5, 0.125, ((0, 32),), jnp.float32),
        "up_weight": noise(splits[10], (FF, D), D ** -0.5, 0.125, ((0, 32),), jnp.float32),
        "down_weight": noise(splits[11], (FF, D), FF ** -0.5, 0.078125, ((0, 32),), jnp.float32),
        "cotangent": noise(splits[12], (STREAMS, SEQLEN, D), 1.0, 6.0, ((0, 4), (1, 8))),
    }


EPSILON = 1e-06
NEGATIVE = -1000000000.0
BUCKET_EDGES = (12, 16, 23, 32, 46, 64, 91)
PRECISE = lax.Precision.HIGHEST

@jax.custom_vjp
def low(v):
    return lax.optimization_barrier(v.astype(jnp.bfloat16)).astype(jnp.float32)

@jax.custom_vjp
def low_back(v):
    return v

def low_keep(v):
    return (low(v), None)

def low_pass(kept, grad):
    return (grad,)

def back_keep(v):
    return (v, None)

def back_low(kept, grad):
    return (low(grad),)
low.defvjp(low_keep, low_pass)
low_back.defvjp(back_keep, back_low)

def bucket_index(offset):
    distance = jnp.abs(offset)
    coarse = 8 + sum(((distance >= edge).astype(jnp.int32) for edge in BUCKET_EDGES))
    return jnp.where(distance < 8, distance, coarse) + 16 * (offset > 0).astype(jnp.int32)

def rms_norm(values, gain):
    return values * lax.rsqrt(lax.optimization_barrier(jnp.mean(values * values, axis=-1, keepdims=True)) + EPSILON) * gain

def gated_gelu(gate, up_part):
    return jax.nn.gelu(gate, approximate=True) * up_part

def matmul(left, right):
    return jnp.dot(left, right, precision=PRECISE)

def attention(query_head, key_head, value_head, segment, bias_rows):
    seq_len = query_head.shape[0]
    row_count = min(512, seq_len)

    def one_block(first_row):
        query_blk = lax.dynamic_slice_in_dim(query_head, first_row, row_count, 0)
        seg_rows = lax.dynamic_slice_in_dim(segment, first_row, row_count, 0)
        logits = jnp.einsum('rhd,khd->hrk', query_blk, key_head, precision=PRECISE)
        offsets = jnp.arange(seq_len, dtype=jnp.int32)[None, :] - (first_row + jnp.arange(row_count, dtype=jnp.int32))[:, None]
        bias_block = jnp.take(bias_rows, bucket_index(offsets), axis=1)
        scores = low_back(logits + bias_block)
        scores = jnp.where((seg_rows[:, None] == segment[None, :])[None], scores, NEGATIVE)
        row_max = lax.optimization_barrier(jnp.max(scores, axis=-1, keepdims=True))
        exp_scores = jnp.exp(scores - row_max)
        attn_prob = low(exp_scores / lax.optimization_barrier(jnp.sum(exp_scores, axis=-1, keepdims=True)))
        return jnp.einsum('hrk,khd->rhd', attn_prob, value_head, precision=PRECISE)
    block_starts = jnp.arange(seq_len // row_count, dtype=jnp.int32) * row_count
    mixed = lax.map(jax.checkpoint(one_block), block_starts)
    return mixed.reshape(seq_len, -1)

def encoder_layer(inputs, segment, params):
    first_gain, query_weight, key_weight, value_weight, output_weight, bias_table, second_gain, gate_weight, up_weight, down_weight = params
    seq_len = inputs.shape[0]
    hidden_one = low(rms_norm(inputs, low(first_gain)))
    query_all = low_back(low(matmul(hidden_one, low(query_weight).T)))
    key_all = low_back(low(matmul(hidden_one, low(key_weight).T)))
    value_all = low_back(low(matmul(hidden_one, low(value_weight).T)))
    bias_rows = low(bias_table).reshape(H, BUCKETS)
    mixed = attention(query_all.reshape(seq_len, H, DK), key_all.reshape(seq_len, H, DK), value_all.reshape(seq_len, H, DK), segment, bias_rows)
    attn_out = low_back(low(mixed))
    resid_one = inputs + low_back(matmul(attn_out, low(output_weight)))
    hidden_two = low(rms_norm(resid_one, low(second_gain)))
    gate = low_back(matmul(hidden_two, low(gate_weight).T))
    up_part = low_back(matmul(hidden_two, low(up_weight).T))
    inner = low(gated_gelu(gate, up_part))
    return resid_one + matmul(inner, low(down_weight))

def reference(tokens, starts, first_gain, query_weight, key_weight, value_weight, output_weight, bias_table, second_gain, gate_weight, up_weight, down_weight, cotangent):
    params_all = (first_gain, query_weight, key_weight, value_weight, output_weight, bias_table, second_gain, gate_weight, up_weight, down_weight)

    def one_stream(totals, items):
        stream_tokens, stream_starts, stream_cot = items
        segment = jnp.cumsum(stream_starts, dtype=jnp.int32)

        def forward(inputs, params):
            return encoder_layer(inputs, segment, params)
        result, backward = jax.vjp(forward, stream_tokens.astype(jnp.float32), params_all)
        grad_inputs, grad_params = backward(stream_cot.astype(jnp.float32))
        totals = tuple((total_one + grad_one for total_one, grad_one in zip(totals, grad_params)))
        return (totals, (result.astype(jnp.bfloat16), grad_inputs.astype(jnp.bfloat16)))
    initial = tuple((jnp.zeros_like(param) for param in params_all))
    totals, (layer_out, grad_tokens) = lax.scan(one_stream, initial, (tokens, starts, cotangent))
    return (layer_out, grad_tokens, totals[0], totals[1], totals[2], totals[3], totals[4], totals[5], totals[6], totals[7], totals[8], totals[9])
```

```python
import functools

import jax
import jax.numpy as jnp
from jax import lax
from jax.experimental import pallas as pl
from jax.experimental.pallas import tpu as pltpu
from jax.sharding import PartitionSpec as P

H = 32
DK = 64
BUCKETS = 32


EPSILON = 1e-06
NEGATIVE = -1000000000.0
BUCKET_EDGES = (12, 16, 23, 32, 46, 64, 91)
PRECISE = lax.Precision.HIGHEST


def bucket_index(offset):
    distance = jnp.abs(offset)
    coarse = 8 + sum(((distance >= edge).astype(jnp.int32) for edge in BUCKET_EDGES))
    return jnp.where(distance < 8, distance, coarse) + 16 * (offset > 0).astype(jnp.int32)


def rms_norm(values, gain):
    return values * lax.rsqrt(jnp.mean(values * values, axis=-1, keepdims=True) + EPSILON) * gain


def gated_gelu(gate, up_part):
    return jax.nn.gelu(gate, approximate=True) * up_part


def matmul(left, right):
    return jnp.dot(left, right, preferred_element_type=jnp.float32)


def contract_rows(left, right):
    return lax.dot_general(
        left, right, (((0,), (0,)), ((), ())), preferred_element_type=jnp.float32
    )


def contract_cols(left, right):
    return lax.dot_general(
        left, right, (((1,), (1,)), ((), ())), preferred_element_type=jnp.float32
    )


BLK = 256
PAIR = 128
VMEM_BYTES = 56 * 1024 * 1024


def nt(left, right):
    return lax.dot_general(
        left, right, (((1,), (1,)), ((), ())), preferred_element_type=jnp.float32
    )


def nn(left, right):
    return jnp.dot(left, right, preferred_element_type=jnp.float32)


def tn(left, right):
    return lax.dot_general(
        left, right, (((0,), (0,)), ((), ())), preferred_element_type=jnp.float32
    )


def head_mask(values, head):
    lane = lax.broadcasted_iota(jnp.int32, values.shape, 1)
    keep = (lane < DK) if head == 0 else (lane >= DK)
    return jnp.where(keep, values, jnp.zeros_like(values))


def fill_strip(strip_ref, head, band_row, tiles):
    wide = jnp.broadcast_to(band_row, (BLK, band_row.shape[1]))
    rolled = pltpu.roll(wide, 0, 1, stride=1, stride_axis=0)
    span = (2 * tiles - 1) * BLK
    near = (tiles - 2) * BLK
    if near > 0:
        strip_ref[head, :, 0:near] = jnp.broadcast_to(band_row[:, 0:1], (BLK, near))
        strip_ref[head, :, near + 3 * BLK : span] = jnp.broadcast_to(
            band_row[:, 4 * BLK - 1 : 4 * BLK], (BLK, span - near - 3 * BLK)
        )
    strip_ref[head, :, near : near + 3 * BLK] = rolled[:, BLK:]


def forward_kernel(tiles, seg_row_ref, seg_col_ref, band_ref, q_ref, k_ref, v_ref, o_ref, lse_ref, strip_ref):
    blk = pl.program_id(1)

    @pl.when(blk == 0)
    def _():
        for head in range(2):
            fill_strip(strip_ref, head, band_ref[0, head : head + 1, :], tiles)

    keys = tiles * BLK
    start = pl.multiple_of((tiles - 1 - blk) * BLK, BLK)
    same = seg_col_ref[...] == seg_row_ref[...]
    total = jnp.zeros((BLK, PAIR), jnp.float32)
    rows = []
    for head in range(2):
        scores = nt(head_mask(q_ref[...], head), k_ref[...]) + strip_ref[head, :, pl.ds(start, keys)]
        scores = jnp.where(same, scores, NEGATIVE)
        top = jnp.max(scores, axis=1, keepdims=True)
        weight = jnp.exp(scores - top)
        norm = jnp.sum(weight, axis=1, keepdims=True)
        prob = (weight * (1.0 / norm)).astype(jnp.bfloat16)
        total = total + nn(prob, head_mask(v_ref[...], head))
        rows.append(jnp.transpose(jnp.broadcast_to(top + jnp.log(norm), (BLK, PAIR)))[0:1, :])
    o_ref[...] = total.astype(jnp.bfloat16)
    lse_ref[0] = jnp.concatenate(rows, axis=0)


def attention_forward(q, k, v, segment, band):
    seq_len, width = q.shape
    tiles = seq_len // BLK
    pairs = width // PAIR
    wide = 4 * BLK
    return pl.pallas_call(
        functools.partial(forward_kernel, tiles),
        grid=(pairs, tiles),
        in_specs=[
            pl.BlockSpec((1, seq_len), lambda p, b: (0, 0)),
            pl.BlockSpec((BLK, 1), lambda p, b: (b, 0)),
            pl.BlockSpec((1, 2, wide), lambda p, b: (p, 0, 0)),
            pl.BlockSpec((BLK, PAIR), lambda p, b: (b, p)),
            pl.BlockSpec((seq_len, PAIR), lambda p, b: (0, p)),
            pl.BlockSpec((seq_len, PAIR), lambda p, b: (0, p)),
        ],
        out_specs=[
            pl.BlockSpec((BLK, PAIR), lambda p, b: (b, p)),
            pl.BlockSpec((1, 2, BLK), lambda p, b: (p, 0, b)),
        ],
        out_shape=[
            jax.ShapeDtypeStruct((seq_len, width), jnp.bfloat16),
            jax.ShapeDtypeStruct((pairs, 2, seq_len), jnp.float32),
        ],
        scratch_shapes=[pltpu.VMEM((2, BLK, (2 * tiles - 1) * BLK), jnp.float32)],
        compiler_params=pltpu.CompilerParams(vmem_limit_bytes=VMEM_BYTES),
        cost_estimate=pl.CostEstimate(
            flops=8 * seq_len * seq_len * PAIR * pairs, bytes_accessed=8 * seq_len * width, transcendentals=2 * pairs * seq_len * seq_len
        ),
        name="attention_forward",
    )(segment[None, :], segment[:, None], band, q, k, v)


def diagonal_sums(tile):
    wide = jnp.concatenate([tile, jnp.zeros_like(tile)], axis=1)
    width = 2 * BLK
    row = lax.broadcasted_iota(jnp.int32, wide.shape, 0)
    shift = 1
    while shift < BLK:
        wide = jnp.where((row & shift) != 0, pltpu.roll(wide, width - shift, 1), wide)
        shift *= 2
    return jnp.sum(wide, axis=0, keepdims=True)


def backward_kernel(tiles, seg_row_ref, seg_col_ref, band_ref, q_ref, k_ref, v_ref, do_ref, lse_ref,
                    dq_ref, dk_ref, dv_ref, diag_ref, strip_ref, dk_acc, dv_acc, bias_acc, p_ref, dp_ref):
    blk = pl.program_id(1)

    @pl.when(blk == 0)
    def _():
        for head in range(2):
            fill_strip(strip_ref, head, band_ref[0, head : head + 1, :], tiles)
        dk_acc[...] = jnp.zeros_like(dk_acc)
        dv_acc[...] = jnp.zeros_like(dv_acc)
        bias_acc[...] = jnp.zeros_like(bias_acc)

    seg_row = seg_row_ref[...]
    grad_q = jnp.zeros((BLK, PAIR), jnp.float32)
    for head in range(2):
        q_h = head_mask(q_ref[...], head)
        do_h = head_mask(do_ref[...], head)
        lse = lse_ref[0, head : head + 1, :]
        delta = jnp.zeros((1, BLK), jnp.float32)
        for tile in range(tiles):
            at = slice(tile * BLK, (tile + 1) * BLK)
            column = pl.multiple_of((blk - tile + tiles - 1) * BLK, BLK)
            scores = nt(k_ref[at, :], q_h) + strip_ref[head, :, pl.ds(column, BLK)]
            scores = jnp.where(seg_col_ref[at, :] == seg_row, scores, NEGATIVE)
            prob = jnp.exp(scores - lse)
            grad_p = nt(v_ref[at, :], do_h)
            delta = delta + jnp.sum(prob * grad_p, axis=0, keepdims=True)
            dv_acc[at, :] += nn(prob.astype(jnp.bfloat16), do_h)
            p_ref[at, :] = prob
            dp_ref[at, :] = grad_p
        for tile in range(tiles):
            at = slice(tile * BLK, (tile + 1) * BLK)
            grad_s = (p_ref[at, :] * (dp_ref[at, :] - delta)).astype(jnp.bfloat16)
            dk_acc[at, :] += nn(grad_s, q_h)
            grad_q = grad_q + tn(grad_s, head_mask(k_ref[at, :], head))
            away = jnp.clip(blk - tile, -2, 2) + 2
            bias_acc[head, away] += grad_s.astype(jnp.float32)
    dq_ref[...] = grad_q.astype(jnp.bfloat16)

    @pl.when(blk == tiles - 1)
    def _():
        dk_ref[...] = dk_acc[...].astype(jnp.bfloat16)
        dv_ref[...] = dv_acc[...].astype(jnp.bfloat16)
        for head in range(2):
            for away in range(5):
                diag_ref[0, head, away : away + 1, :] = diagonal_sums(bias_acc[head, away])


def attention_backward(q, k, v, grad_o, lse, segment, band_back):
    seq_len, width = q.shape
    tiles = seq_len // BLK
    pairs = width // PAIR
    wide = 4 * BLK
    whole = pl.BlockSpec((seq_len, PAIR), lambda p, b: (0, p))
    rows = pl.BlockSpec((BLK, PAIR), lambda p, b: (b, p))
    return pl.pallas_call(
        functools.partial(backward_kernel, tiles),
        grid=(pairs, tiles),
        in_specs=[
            pl.BlockSpec((1, BLK), lambda p, b: (0, b)),
            pl.BlockSpec((seq_len, 1), lambda p, b: (0, 0)),
            pl.BlockSpec((1, 2, wide), lambda p, b: (p, 0, 0)),
            rows, whole, whole, rows,
            pl.BlockSpec((1, 2, BLK), lambda p, b: (p, 0, b)),
        ],
        out_specs=[rows, whole, whole, pl.BlockSpec((1, 2, 5, 2 * BLK), lambda p, b: (p, 0, 0, 0))],
        out_shape=[
            jax.ShapeDtypeStruct((seq_len, width), jnp.bfloat16),
            jax.ShapeDtypeStruct((seq_len, width), jnp.bfloat16),
            jax.ShapeDtypeStruct((seq_len, width), jnp.bfloat16),
            jax.ShapeDtypeStruct((pairs, 2, 5, 2 * BLK), jnp.float32),
        ],
        scratch_shapes=[
            pltpu.VMEM((2, BLK, (2 * tiles - 1) * BLK), jnp.float32),
            pltpu.VMEM((seq_len, PAIR), jnp.float32),
            pltpu.VMEM((seq_len, PAIR), jnp.float32),
            pltpu.VMEM((2, 5, BLK, BLK), jnp.float32),
            pltpu.VMEM((seq_len, BLK), jnp.float32),
            pltpu.VMEM((seq_len, BLK), jnp.float32),
        ],
        compiler_params=pltpu.CompilerParams(vmem_limit_bytes=VMEM_BYTES),
        cost_estimate=pl.CostEstimate(
            flops=20 * seq_len * seq_len * PAIR * pairs, bytes_accessed=16 * seq_len * width, transcendentals=2 * pairs * seq_len * seq_len
        ),
        name="attention_backward",
    )(segment[None, :], segment[:, None], band_back, q, k, v, grad_o, lse)


def one_hot_buckets(offset):
    return (bucket_index(offset)[..., None] == jnp.arange(BUCKETS, dtype=jnp.int32)).astype(
        jnp.float32
    )


def bias_bands(bias_rows):
    offset = jnp.arange(4 * BLK, dtype=jnp.int32) - 2 * BLK
    contract = (((1,), (1,)), ((), ()))
    ahead = lax.dot_general(bias_rows, one_hot_buckets(offset), contract, precision=PRECISE)
    behind = lax.dot_general(bias_rows, one_hot_buckets(-offset), contract, precision=PRECISE)
    shape = (bias_rows.shape[0] // 2, 2, 4 * BLK)
    return ahead.reshape(shape), behind.reshape(shape)


def bucket_sums(diagonals):
    heads = diagonals.shape[0] * 2
    lane = jnp.arange(2 * BLK, dtype=jnp.int32)
    within = jnp.where(lane < BLK, lane, lane - 2 * BLK)
    away = (jnp.arange(5, dtype=jnp.int32) - 2) * BLK
    onehot = one_hot_buckets(-within[None, :] - away[:, None])
    return jnp.dot(
        diagonals.reshape(heads, -1), onehot.reshape(-1, BUCKETS), precision=PRECISE
    )


def gather_rows(values):
    return lax.all_gather(values, "seq", axis=0, tiled=True)


def scatter_rows(values):
    return lax.psum_scatter(
        values.astype(jnp.bfloat16), "seq", scatter_dimension=0, tiled=True
    ).astype(jnp.float32)


def per_device(
    tokens,
    starts,
    first_gain,
    query_weight,
    key_weight,
    value_weight,
    output_weight,
    bias_table,
    second_gain,
    gate_weight,
    up_weight,
    down_weight,
    cotangent,
):
    segment = jnp.cumsum(lax.all_gather(starts, "seq", axis=1, tiled=True)[0], dtype=jnp.int32)
    inputs = tokens[0].astype(jnp.float32)
    grad_out = cotangent[0]
    head_count = H // lax.axis_size("seq")
    head_first = lax.axis_index("seq") * head_count
    query_low = query_weight.astype(jnp.bfloat16)
    key_low = key_weight.astype(jnp.bfloat16)
    value_low = value_weight.astype(jnp.bfloat16)
    output_low = output_weight.astype(jnp.bfloat16)
    gate_low = gate_weight.astype(jnp.bfloat16)
    up_low = up_weight.astype(jnp.bfloat16)
    down_low = down_weight.astype(jnp.bfloat16)
    first_low = first_gain.astype(jnp.bfloat16)
    second_low = second_gain.astype(jnp.bfloat16)
    table_low = bias_table.astype(jnp.bfloat16)
    query_part, key_part, value_part, output_part, gate_part, up_rows, down_part = (
        lax.all_gather(query_low, "fsdp", axis=0, tiled=True),
        lax.all_gather(key_low, "fsdp", axis=0, tiled=True),
        lax.all_gather(value_low, "fsdp", axis=0, tiled=True),
        lax.all_gather(output_low, "fsdp", axis=0, tiled=True),
        lax.all_gather(gate_low, "fsdp", axis=0, tiled=True),
        lax.all_gather(up_low, "fsdp", axis=0, tiled=True),
        lax.all_gather(down_low, "fsdp", axis=0, tiled=True),
    )
    gain_one, gain_two, table_full = (
        lax.all_gather(first_low, ("seq", "fsdp"), axis=0, tiled=True),
        lax.all_gather(second_low, ("seq", "fsdp"), axis=0, tiled=True),
        lax.all_gather(table_low, ("seq", "fsdp"), axis=0, tiled=True),
    )
    gain_first = gain_one.astype(jnp.float32)
    gain_second = gain_two.astype(jnp.float32)
    bias_rows = lax.dynamic_slice_in_dim(
        table_full.astype(jnp.float32).reshape(H, BUCKETS), head_first, head_count, 0
    )
    hidden_one = rms_norm(inputs, gain_first).astype(jnp.bfloat16)
    hidden_all = gather_rows(hidden_one)
    query_head = (
        contract_cols(hidden_all, query_part).astype(jnp.bfloat16)
    )
    key_head = (
        contract_cols(hidden_all, key_part).astype(jnp.bfloat16)
    )
    value_head = (
        contract_cols(hidden_all, value_part).astype(jnp.bfloat16)
    )
    band_ahead, band_behind = bias_bands(bias_rows)
    mixed, row_lse = attention_forward(query_head, key_head, value_head, segment, band_ahead)
    resid_one = inputs + scatter_rows(matmul(mixed, output_part))
    hidden_two = rms_norm(resid_one, gain_second).astype(jnp.bfloat16)
    hidden_two_all = gather_rows(hidden_two)
    gate = contract_cols(hidden_two_all, gate_part)
    up_part = contract_cols(hidden_two_all, up_rows)
    inner = gated_gelu(gate, up_part).astype(jnp.bfloat16)
    layer_out = (resid_one + scatter_rows(matmul(inner, down_part))).astype(jnp.bfloat16)
    grad_out_all = gather_rows(grad_out)
    grad_inner = contract_cols(grad_out_all, down_part)
    grad_down = contract_rows(inner, grad_out_all)
    grad_gate, grad_up = jax.vjp(gated_gelu, gate, up_part)[1](grad_inner)
    grad_gate = grad_gate.astype(jnp.bfloat16)
    grad_up = grad_up.astype(jnp.bfloat16)
    grad_gate_w = contract_rows(grad_gate, hidden_two_all)
    grad_up_w = contract_rows(grad_up, hidden_two_all)
    grad_hidden_two = scatter_rows(matmul(grad_gate, gate_part) + matmul(grad_up, up_rows))
    grad_norm_two, grad_gain_two = jax.vjp(rms_norm, resid_one, gain_second)[1](grad_hidden_two)
    grad_resid = grad_out.astype(jnp.float32) + grad_norm_two
    grad_branch = grad_resid.astype(jnp.bfloat16)
    branch_all = gather_rows(grad_branch)
    grad_output_w = contract_rows(mixed, branch_all)
    grad_heads = (
        contract_cols(branch_all, output_part).astype(jnp.bfloat16)
    )
    grad_query_seq, grad_key_seq, grad_value_seq, diagonals = attention_backward(
        query_head, key_head, value_head, grad_heads, row_lse, segment, band_behind
    )
    grad_bias = bucket_sums(diagonals)
    grad_query_w = contract_rows(grad_query_seq, hidden_all)
    grad_key_w = contract_rows(grad_key_seq, hidden_all)
    grad_value_w = contract_rows(grad_value_seq, hidden_all)
    grad_hidden_one = scatter_rows(
        matmul(grad_query_seq, query_part)
        + matmul(grad_key_seq, key_part)
        + matmul(grad_value_seq, value_part)
    )
    grad_norm_one, grad_gain_one = jax.vjp(rms_norm, inputs, gain_first)[1](grad_hidden_one)
    grad_tokens = (grad_resid + grad_norm_one).astype(jnp.bfloat16)
    grad_table = lax.dynamic_update_slice_in_dim(
        jnp.zeros((H, BUCKETS), jnp.float32), grad_bias, head_first, 0
    ).reshape(-1)
    weight_grads = (
        lax.psum_scatter(
            grad_query_w.astype(jnp.bfloat16), "fsdp", scatter_dimension=0, tiled=True
        ).astype(jnp.float32),
        lax.psum_scatter(
            grad_key_w.astype(jnp.bfloat16), "fsdp", scatter_dimension=0, tiled=True
        ).astype(jnp.float32),
        lax.psum_scatter(
            grad_value_w.astype(jnp.bfloat16), "fsdp", scatter_dimension=0, tiled=True
        ).astype(jnp.float32),
        lax.psum_scatter(
            grad_output_w.astype(jnp.bfloat16), "fsdp", scatter_dimension=0, tiled=True
        ).astype(jnp.float32),
        lax.psum_scatter(
            grad_gate_w.astype(jnp.bfloat16), "fsdp", scatter_dimension=0, tiled=True
        ).astype(jnp.float32),
        lax.psum_scatter(
            grad_up_w.astype(jnp.bfloat16), "fsdp", scatter_dimension=0, tiled=True
        ).astype(jnp.float32),
        lax.psum_scatter(
            grad_down.astype(jnp.bfloat16), "fsdp", scatter_dimension=0, tiled=True
        ).astype(jnp.float32),
    )
    small_grads = (
        lax.psum_scatter(grad_gain_one, ("seq", "fsdp"), scatter_dimension=0, tiled=True),
        lax.psum_scatter(grad_gain_two, ("seq", "fsdp"), scatter_dimension=0, tiled=True),
        lax.psum_scatter(grad_table, ("seq", "fsdp"), scatter_dimension=0, tiled=True),
    )
    return (
        layer_out[None],
        grad_tokens[None],
        small_grads[0],
        weight_grads[0],
        weight_grads[1],
        weight_grads[2],
        weight_grads[3],
        small_grads[2],
        small_grads[1],
        weight_grads[4],
        weight_grads[5],
        weight_grads[6],
    )


def solution(mesh):
    in_specs = (
        P("fsdp", "seq", None),
        P("fsdp", "seq"),
        P(("seq", "fsdp")),
        P(("seq", "fsdp"), None),
        P(("seq", "fsdp"), None),
        P(("seq", "fsdp"), None),
        P(("seq", "fsdp"), None),
        P(("seq", "fsdp")),
        P(("seq", "fsdp")),
        P(("seq", "fsdp"), None),
        P(("seq", "fsdp"), None),
        P(("seq", "fsdp"), None),
        P("fsdp", "seq", None),
    )
    out_specs = (
        P("fsdp", "seq", None),
        P("fsdp", "seq", None),
        P(("seq", "fsdp")),
        P(("seq", "fsdp"), None),
        P(("seq", "fsdp"), None),
        P(("seq", "fsdp"), None),
        P(("seq", "fsdp"), None),
        P(("seq", "fsdp")),
        P(("seq", "fsdp")),
        P(("seq", "fsdp"), None),
        P(("seq", "fsdp"), None),
        P(("seq", "fsdp"), None),
    )
    return jax.shard_map(
        per_device, mesh=mesh, in_specs=in_specs, out_specs=out_specs, check_vma=False
    )
```

```python
import functools

import jax
import jax.numpy as jnp
from jax import lax
from jax.experimental import pallas as pl
from jax.experimental.pallas import tpu as pltpu
from jax.sharding import PartitionSpec as P

H = 32
DK = 64
BUCKETS = 32


EPSILON = 1e-06
NEGATIVE = -1000000000.0
BUCKET_EDGES = (12, 16, 23, 32, 46, 64, 91)
PRECISE = lax.Precision.HIGHEST
BLK = 256
PAIR = 128
VMEM_BYTES = 56 * 1024 * 1024
GELU_SCALE = 0.7978845608028654
GELU_CUBE = 0.044715


def bucket_index(offset):
    distance = jnp.abs(offset)
    coarse = 8 + sum(((distance >= edge).astype(jnp.int32) for edge in BUCKET_EDGES))
    return jnp.where(distance < 8, distance, coarse) + 16 * (offset > 0).astype(jnp.int32)


def nt(left, right):
    return lax.dot_general(
        left, right, (((1,), (1,)), ((), ())), preferred_element_type=jnp.float32
    )


def nn(left, right):
    return jnp.dot(left, right, preferred_element_type=jnp.float32)


def tn(left, right):
    return lax.dot_general(
        left, right, (((0,), (0,)), ((), ())), preferred_element_type=jnp.float32
    )


def params():
    return pltpu.CompilerParams(vmem_limit_bytes=VMEM_BYTES)


def cost(flops, bytes_accessed, transcendentals=0):
    return pl.CostEstimate(
        flops=flops, bytes_accessed=bytes_accessed, transcendentals=transcendentals
    )


def head_mask(values, head):
    lane = lax.broadcasted_iota(jnp.int32, values.shape, 1)
    keep = (lane < DK) if head == 0 else (lane >= DK)
    return jnp.where(keep, values, jnp.zeros_like(values))


def fill_strip(strip_ref, head, band_row, tiles):
    wide = jnp.broadcast_to(band_row, (BLK, band_row.shape[1]))
    rolled = pltpu.roll(wide, 0, 1, stride=1, stride_axis=0)
    span = (2 * tiles - 1) * BLK
    near = (tiles - 2) * BLK
    if near > 0:
        strip_ref[head, :, 0:near] = jnp.broadcast_to(band_row[:, 0:1], (BLK, near))
        strip_ref[head, :, near + 3 * BLK : span] = jnp.broadcast_to(
            band_row[:, 4 * BLK - 1 : 4 * BLK], (BLK, span - near - 3 * BLK)
        )
    strip_ref[head, :, near : near + 3 * BLK] = rolled[:, BLK:]


def forward_kernel(tiles, seg_row_ref, seg_col_ref, band_ref, q_ref, k_ref, v_ref, o_ref, lse_ref, strip_ref):
    blk = pl.program_id(0)

    @pl.when(blk == 0)
    def _():
        for head in range(2):
            fill_strip(strip_ref, head, band_ref[head : head + 1, :], tiles)

    keys = tiles * BLK
    start = pl.multiple_of((tiles - 1 - blk) * BLK, BLK)
    same = seg_col_ref[...] == seg_row_ref[...]
    total = jnp.zeros((BLK, PAIR), jnp.float32)
    rows = []
    for head in range(2):
        scores = nt(head_mask(q_ref[...], head), k_ref[...]) + strip_ref[head, :, pl.ds(start, keys)]
        scores = jnp.where(same, scores, NEGATIVE)
        top = jnp.max(scores, axis=1, keepdims=True)
        weight = jnp.exp(scores - top)
        norm = jnp.sum(weight, axis=1, keepdims=True)
        prob = (weight * (1.0 / norm)).astype(jnp.bfloat16)
        total = total + nn(prob, head_mask(v_ref[...], head))
        rows.append(jnp.transpose(jnp.broadcast_to(top + jnp.log(norm), (BLK, PAIR)))[0:1, :])
    o_ref[...] = total.astype(jnp.bfloat16)
    lse_ref[...] = jnp.concatenate(rows, axis=0)


def attention_forward(qkv, segment, band):
    seq_len = qkv.shape[0]
    tiles = seq_len // BLK
    return pl.pallas_call(
        functools.partial(forward_kernel, tiles),
        grid=(tiles,),
        in_specs=[
            pl.BlockSpec((1, seq_len), lambda b: (0, 0)),
            pl.BlockSpec((BLK, 1), lambda b: (b, 0)),
            pl.BlockSpec((2, 4 * BLK), lambda b: (0, 0)),
            pl.BlockSpec((BLK, PAIR), lambda b: (b, 0)),
            pl.BlockSpec((seq_len, PAIR), lambda b: (0, 1)),
            pl.BlockSpec((seq_len, PAIR), lambda b: (0, 2)),
        ],
        out_specs=[
            pl.BlockSpec((BLK, PAIR), lambda b: (b, 0)),
            pl.BlockSpec((2, BLK), lambda b: (0, b)),
        ],
        out_shape=[
            jax.ShapeDtypeStruct((seq_len, PAIR), jnp.bfloat16),
            jax.ShapeDtypeStruct((2, seq_len), jnp.float32),
        ],
        scratch_shapes=[pltpu.VMEM((2, BLK, (2 * tiles - 1) * BLK), jnp.float32)],
        compiler_params=params(),
        cost_estimate=cost(
            8 * seq_len * seq_len * PAIR, 8 * seq_len * PAIR, 2 * seq_len * seq_len
        ),
        name="attention_forward",
    )(segment[None, :], segment[:, None], band, qkv, qkv, qkv)


def diagonal_sums(tile):
    wide = jnp.concatenate([tile, jnp.zeros_like(tile)], axis=1)
    width = 2 * BLK
    row = lax.broadcasted_iota(jnp.int32, wide.shape, 0)
    shift = 1
    while shift < BLK:
        wide = jnp.where((row & shift) != 0, pltpu.roll(wide, width - shift, 1), wide)
        shift *= 2
    return jnp.sum(wide, axis=0, keepdims=True)


def backward_kernel(tiles, seg_row_ref, seg_col_ref, band_ref, q_ref, k_ref, v_ref, do_ref, lse_ref,
                    dq_ref, dk_ref, dv_ref, diag_ref, strip_ref, dk_acc, dv_acc, bias_acc, p_ref, dp_ref):
    blk = pl.program_id(0)

    @pl.when(blk == 0)
    def _():
        for head in range(2):
            fill_strip(strip_ref, head, band_ref[head : head + 1, :], tiles)
        dk_acc[...] = jnp.zeros_like(dk_acc)
        dv_acc[...] = jnp.zeros_like(dv_acc)
        bias_acc[...] = jnp.zeros_like(bias_acc)

    seg_row = seg_row_ref[...]
    grad_q = jnp.zeros((BLK, PAIR), jnp.float32)
    for head in range(2):
        q_h = head_mask(q_ref[...], head)
        do_h = head_mask(do_ref[...], head)
        lse = lse_ref[head : head + 1, :]
        delta = jnp.zeros((1, BLK), jnp.float32)
        for tile in range(tiles):
            at = slice(tile * BLK, (tile + 1) * BLK)
            column = pl.multiple_of((blk - tile + tiles - 1) * BLK, BLK)
            scores = nt(k_ref[at, :], q_h) + strip_ref[head, :, pl.ds(column, BLK)]
            scores = jnp.where(seg_col_ref[at, :] == seg_row, scores, NEGATIVE)
            prob = jnp.exp(scores - lse)
            grad_p = nt(v_ref[at, :], do_h)
            delta = delta + jnp.sum(prob * grad_p, axis=0, keepdims=True)
            dv_acc[at, :] += nn(prob.astype(jnp.bfloat16), do_h)
            p_ref[at, :] = prob
            dp_ref[at, :] = grad_p
        for tile in range(tiles):
            at = slice(tile * BLK, (tile + 1) * BLK)
            grad_s = (p_ref[at, :] * (dp_ref[at, :] - delta)).astype(jnp.bfloat16)
            dk_acc[at, :] += nn(grad_s, q_h)
            grad_q = grad_q + tn(grad_s, head_mask(k_ref[at, :], head))
            away = jnp.clip(blk - tile, -2, 2) + 2
            bias_acc[head, away] += grad_s.astype(jnp.float32)
    dq_ref[...] = grad_q.astype(jnp.bfloat16)

    @pl.when(blk == tiles - 1)
    def _():
        dk_ref[...] = dk_acc[...].astype(jnp.bfloat16)
        dv_ref[...] = dv_acc[...].astype(jnp.bfloat16)
        for head in range(2):
            for away in range(5):
                diag_ref[head, away : away + 1, :] = diagonal_sums(bias_acc[head, away])


def attention_backward(qkv, grad_o, lse, segment, band_back):
    seq_len = qkv.shape[0]
    tiles = seq_len // BLK
    rows = pl.BlockSpec((BLK, PAIR), lambda b: (b, 0))
    whole = pl.BlockSpec((seq_len, PAIR), lambda b: (0, 0))
    result = jax.ShapeDtypeStruct((seq_len, PAIR), jnp.bfloat16)
    return pl.pallas_call(
        functools.partial(backward_kernel, tiles),
        grid=(tiles,),
        in_specs=[
            pl.BlockSpec((1, BLK), lambda b: (0, b)),
            pl.BlockSpec((seq_len, 1), lambda b: (0, 0)),
            pl.BlockSpec((2, 4 * BLK), lambda b: (0, 0)),
            rows,
            pl.BlockSpec((seq_len, PAIR), lambda b: (0, 1)),
            pl.BlockSpec((seq_len, PAIR), lambda b: (0, 2)),
            rows,
            pl.BlockSpec((2, BLK), lambda b: (0, b)),
        ],
        out_specs=[rows, whole, whole, pl.BlockSpec((2, 5, 2 * BLK), lambda b: (0, 0, 0))],
        out_shape=[
            result,
            result,
            result,
            jax.ShapeDtypeStruct((2, 5, 2 * BLK), jnp.float32),
        ],
        scratch_shapes=[
            pltpu.VMEM((2, BLK, (2 * tiles - 1) * BLK), jnp.float32),
            pltpu.VMEM((seq_len, PAIR), jnp.float32),
            pltpu.VMEM((seq_len, PAIR), jnp.float32),
            pltpu.VMEM((2, 5, BLK, BLK), jnp.float32),
            pltpu.VMEM((seq_len, BLK), jnp.float32),
            pltpu.VMEM((seq_len, BLK), jnp.float32),
        ],
        compiler_params=params(),
        cost_estimate=cost(
            20 * seq_len * seq_len * PAIR, 16 * seq_len * PAIR, 2 * seq_len * seq_len
        ),
        name="attention_backward",
    )(segment[None, :], segment[:, None], band_back, qkv, qkv, qkv, grad_o, lse)


def one_hot_buckets(offset):
    return (bucket_index(offset)[..., None] == jnp.arange(BUCKETS, dtype=jnp.int32)).astype(
        jnp.float32
    )


def bias_bands(bias_rows):
    offset = jnp.arange(4 * BLK, dtype=jnp.int32) - 2 * BLK
    contract = (((1,), (1,)), ((), ()))
    ahead = lax.dot_general(bias_rows, one_hot_buckets(offset), contract, precision=PRECISE)
    behind = lax.dot_general(bias_rows, one_hot_buckets(-offset), contract, precision=PRECISE)
    return ahead, behind


def bucket_sums(diagonals):
    lane = jnp.arange(2 * BLK, dtype=jnp.int32)
    within = jnp.where(lane < BLK, lane, lane - 2 * BLK)
    away = (jnp.arange(5, dtype=jnp.int32) - 2) * BLK
    onehot = one_hot_buckets(-within[None, :] - away[:, None])
    return jnp.dot(diagonals.reshape(2, -1), onehot.reshape(-1, BUCKETS), precision=PRECISE)


def piece_rows(own_ref, piece, rows):
    return pl.ds(pl.multiple_of((own_ref[0] ^ piece) * rows, rows), rows)


def norm_project_kernel(count, own_ref, gain_ref, weight_ref, *refs):
    pieces, hidden_ref, out_ref = refs[:count], refs[count], refs[count + 1]
    rows = pieces[0].shape[0]
    for piece in range(count):
        values = pieces[piece][...].astype(jnp.float32)
        scale = lax.rsqrt(jnp.mean(values * values, axis=-1, keepdims=True) + EPSILON)
        hidden_ref[piece_rows(own_ref, piece, rows), :] = (
            values * scale * gain_ref[...]
        ).astype(jnp.bfloat16)
    for chunk in range(count * rows // BLK):
        at = slice(chunk * BLK, (chunk + 1) * BLK)
        out_ref[at, :] = nt(hidden_ref[at, :], weight_ref[...]).astype(jnp.bfloat16)


def norm_project(own, gain, weight, pieces):
    count = len(pieces)
    rows, width = pieces[0].shape
    total, features = count * rows, weight.shape[0]
    vmem = pl.BlockSpec(memory_space=pltpu.VMEM)
    return pl.pallas_call(
        functools.partial(norm_project_kernel, count),
        in_specs=[pl.BlockSpec(memory_space=pltpu.SMEM)] + [vmem] * (2 + count),
        out_specs=[vmem, vmem],
        out_shape=[
            jax.ShapeDtypeStruct((total, width), jnp.bfloat16),
            jax.ShapeDtypeStruct((total, features), jnp.bfloat16),
        ],
        compiler_params=params(),
        cost_estimate=cost(
            2 * total * width * features, 2 * (2 * total * width + features * (width + total))
        ),
        name="norm_project",
    )(own, gain[None, :], weight, *pieces)


def project_kernel(hidden_ref, weight_ref, out_ref):
    out_ref[...] = nt(hidden_ref[...], weight_ref[...]).astype(jnp.bfloat16)


def project(hidden, weight):
    total, width = hidden.shape
    features = weight.shape[0]
    return pl.pallas_call(
        project_kernel,
        grid=(total // BLK,),
        in_specs=[
            pl.BlockSpec((BLK, width), lambda b: (b, 0)),
            pl.BlockSpec((features, width), lambda b: (0, 0)),
        ],
        out_specs=pl.BlockSpec((BLK, features), lambda b: (b, 0)),
        out_shape=jax.ShapeDtypeStruct((total, features), jnp.bfloat16),
        compiler_params=params(),
        cost_estimate=cost(
            2 * total * width * features, 2 * (total * width + features * (width + total))
        ),
        name="project",
    )(hidden, weight)


def spread_kernel(count, terms, own_ref, *refs):
    lefts, rights, outs = refs[:terms], refs[terms : 2 * terms], refs[2 * terms :]
    rows = outs[0].shape[0]
    for piece in range(count):
        at = piece_rows(own_ref, piece, rows)
        total = nn(lefts[0][at, :], rights[0][...])
        for term in range(1, terms):
            total = total + nn(lefts[term][at, :], rights[term][...])
        outs[piece][...] = total.astype(jnp.bfloat16)


def spread(own, count, lefts, rights):
    total, width = lefts[0].shape[0], rights[0].shape[1]
    depth = sum(right.shape[0] for right in rights)
    vmem = pl.BlockSpec(memory_space=pltpu.VMEM)
    return pl.pallas_call(
        functools.partial(spread_kernel, count, len(lefts)),
        in_specs=[pl.BlockSpec(memory_space=pltpu.SMEM)] + [vmem] * (2 * len(lefts)),
        out_specs=[vmem] * count,
        out_shape=[jax.ShapeDtypeStruct((total // count, width), jnp.bfloat16)] * count,
        compiler_params=params(),
        cost_estimate=cost(
            2 * total * width * depth, 2 * (total * width + depth * (width + total))
        ),
        name="spread",
    )(own, *lefts, *rights)


def heads_back_kernel(count, pairs, own_ref, *refs):
    weights, refs = refs[:pairs], refs[pairs:]
    mixed, refs = refs[:pairs], refs[pairs:]
    pieces, refs = refs[:count], refs[count:]
    heads, grads, whole = refs[:pairs], refs[pairs : 2 * pairs], refs[2 * pairs]
    rows = pieces[0].shape[0]
    for piece in range(count):
        whole[piece_rows(own_ref, piece, rows), :] = pieces[piece][...]
    for chunk in range(count * rows // BLK):
        at = slice(chunk * BLK, (chunk + 1) * BLK)
        for pair in range(pairs):
            heads[pair][at, :] = nt(whole[at, :], weights[pair][...]).astype(jnp.bfloat16)
    for pair in range(pairs):
        grads[pair][...] = tn(mixed[pair][...], whole[...]).astype(jnp.bfloat16)


def heads_back(own, weights, mixed, pieces):
    count, pairs = len(pieces), len(weights)
    rows, width = pieces[0].shape
    total = count * rows
    vmem = pl.BlockSpec(memory_space=pltpu.VMEM)
    outs = pl.pallas_call(
        functools.partial(heads_back_kernel, count, pairs),
        in_specs=[pl.BlockSpec(memory_space=pltpu.SMEM)] + [vmem] * (2 * pairs + count),
        out_specs=[vmem] * (2 * pairs),
        out_shape=[jax.ShapeDtypeStruct((total, PAIR), jnp.bfloat16)] * pairs
        + [jax.ShapeDtypeStruct((PAIR, width), jnp.bfloat16)] * pairs,
        scratch_shapes=[pltpu.VMEM((total, width), jnp.bfloat16)],
        compiler_params=params(),
        cost_estimate=cost(4 * total * width * PAIR * pairs, 2 * total * width),
        name="heads_back",
    )(own, *weights, *mixed, *pieces)
    return outs[:pairs], outs[pairs:]


def qkv_grad_kernel(gain_ref, hidden_ref, dq_ref, dk_ref, dv_ref, weight_ref, out_ref, sum_ref):
    total = None
    for part, ref in enumerate((dq_ref, dk_ref, dv_ref)):
        at = slice(part * PAIR, (part + 1) * PAIR)
        grad = tn(ref[...], hidden_ref[...])
        out_ref[at, :] = grad.astype(jnp.bfloat16)
        term = jnp.sum(grad * weight_ref[at, :].astype(jnp.float32), axis=0, keepdims=True)
        total = term if total is None else total + term
    sum_ref[...] = total / gain_ref[...]


def qkv_grad(gain, hidden, dq, dk, dv, weight):
    total, width = hidden.shape
    cols = 512
    col = pl.BlockSpec((1, cols), lambda c: (0, c))
    back = pl.BlockSpec((total, PAIR), lambda c: (0, 0))
    rows = pl.BlockSpec((3 * PAIR, cols), lambda c: (0, c))
    return pl.pallas_call(
        qkv_grad_kernel,
        grid=(width // cols,),
        in_specs=[col, pl.BlockSpec((total, cols), lambda c: (0, c)), back, back, back, rows],
        out_specs=[rows, col],
        out_shape=[
            jax.ShapeDtypeStruct((3 * PAIR, width), jnp.bfloat16),
            jax.ShapeDtypeStruct((1, width), jnp.float32),
        ],
        compiler_params=params(),
        cost_estimate=cost(6 * total * width * PAIR, 2 * total * width + 12 * PAIR * width),
        name="qkv_grad",
    )(gain[None, :], hidden, dq, dk, dv, weight)


def feed_kernel(count, gate_w, up_w, down_w, *refs):
    hidden, refs = refs[:count], refs[count:]
    cot, refs = refs[:count], refs[count:]
    inner_ref, dgate_ref, dup_ref = refs[:3]
    outs = refs[3:]
    rows = hidden[0].shape[0]
    for piece in range(0, count, 2):
        values = jnp.concatenate([hidden[piece][...], hidden[piece + 1][...]], axis=0)
        grads = jnp.concatenate([cot[piece][...], cot[piece + 1][...]], axis=0)
        at = slice(piece * rows, (piece + 2) * rows)
        gate = nt(values, gate_w[...])
        up = nt(values, up_w[...])
        grad_m = nt(grads, down_w[...])
        square = gate * gate
        bend = jnp.tanh(GELU_SCALE * gate * (1.0 + GELU_CUBE * square))
        half = 0.5 * (1.0 + bend)
        act = gate * half
        slope = half + 0.5 * gate * (1.0 - bend * bend) * (
            GELU_SCALE * (1.0 + 3.0 * GELU_CUBE * square)
        )
        inner_ref[at, :] = (act * up).astype(jnp.bfloat16)
        dgate = (grad_m * up * slope).astype(jnp.bfloat16)
        dup = (grad_m * act).astype(jnp.bfloat16)
        dgate_ref[at, :] = dgate
        dup_ref[at, :] = dup
        grad_h = nn(dgate, gate_w[...]) + nn(dup, up_w[...])
        outs[piece][...] = grad_h[:rows].astype(jnp.bfloat16)
        outs[piece + 1][...] = grad_h[rows:].astype(jnp.bfloat16)


def feed(gate_w, up_w, down_w, hidden, cot):
    count = len(hidden)
    rows, width = hidden[0].shape
    total, units = count * rows, gate_w.shape[0]
    vmem = pl.BlockSpec(memory_space=pltpu.VMEM)
    outs = pl.pallas_call(
        functools.partial(feed_kernel, count),
        in_specs=[vmem] * (3 + 2 * count),
        out_specs=[vmem] * (3 + count),
        out_shape=[jax.ShapeDtypeStruct((total, units), jnp.bfloat16)] * 3
        + [jax.ShapeDtypeStruct((rows, width), jnp.bfloat16)] * count,
        compiler_params=params(),
        cost_estimate=cost(10 * total * width * units, 2 * 3 * (total + units) * width),
        name="feed",
    )(gate_w, up_w, down_w, *hidden, *cot)
    return outs[:3], outs[3:]


def wide(values):
    return values.astype(jnp.float32)


def low(values):
    return values.astype(jnp.bfloat16)


def after(values, others):
    return lax.optimization_barrier((values, others))[0]


class Links:
    def __init__(self, seq, fsdp):
        self.seq = seq
        self.fsdp = fsdp
        self.cores = max(1, 8 // fsdp)
        self.square = seq == 4 * self.cores

    def swap(self, values, bits):
        return lax.ppermute(values, "seq", [(i, i ^ bits) for i in range(self.seq)])

    def quad(self, own):
        near_x = self.swap(own, self.cores)
        near_y = self.swap(own, 2 * self.cores)
        half = own.shape[0] // 2
        first = self.swap(near_y[:half], self.cores)
        second = self.swap(near_x[half:], 2 * self.cores)
        return [own, near_x, near_y, jnp.concatenate([first, second], axis=0)]

    def chip_gather(self, own):
        if self.square:
            return self.quad(own)
        return [own] + [self.swap(own, r * self.cores) for r in range(1, self.seq // self.cores)]

    def chip_scatter(self, pieces):
        if not self.square:
            total = wide(pieces[0])
            for index in range(1, len(pieces)):
                total = total + wide(self.swap(low(pieces[index]), index * self.cores))
            return total
        x_bit, y_bit = self.cores, 2 * self.cores
        half = pieces[0].shape[0] // 2
        own, x_to, y_to, d_to = pieces
        sent = self.swap(low(jnp.stack([x_to[:half], d_to[:half]])), x_bit)
        own_a = wide(own[:half]) + wide(sent[0])
        y_a = wide(y_to[:half]) + wide(sent[1])
        back = self.swap(low(jnp.stack([y_to[half:], d_to[half:]])), y_bit)
        own_b = wide(own[half:]) + wide(back[0])
        x_b = wide(x_to[half:]) + wide(back[1])
        own_a = own_a + wide(self.swap(low(y_a), y_bit))
        own_b = own_b + wide(self.swap(low(x_b), x_bit))
        return jnp.concatenate([own_a, own_b], axis=0)

    def with_cores(self, pieces):
        if self.cores == 1:
            return list(pieces)
        out = []
        for piece in pieces:
            out += [piece, self.swap(piece, 1)]
        return out

    def join_cores(self, pieces):
        if self.cores == 1:
            return list(pieces)
        return [
            wide(pieces[i]) + wide(self.swap(low(pieces[i + 1]), 1))
            for i in range(0, len(pieces), 2)
        ]

    def stream_gather(self, own):
        return self.with_cores(self.chip_gather(own))

    def stream_scatter(self, pieces):
        return self.chip_scatter(self.join_cores(pieces))

    def line_gather(self, own):
        n = self.fsdp
        ups, downs = [own], [own]
        for k in range(1, n):
            ups.append(lax.ppermute(ups[-1], "fsdp", [(i, i + 1) for i in range(k - 1, n - 1)]))
            downs.append(lax.ppermute(downs[-1], "fsdp", [(i, i - 1) for i in range(1, n - k + 1)]))
        below = lax.axis_index("fsdp")
        return [own] + [jnp.where(below >= k, ups[k], downs[n - k]) for k in range(1, n)]

    def line_scatter(self, slots):
        n = self.fsdp
        up = down = None
        for k in range(n - 1, 0, -1):
            send = slots[n - k] if up is None else wide(slots[n - k]) + wide(up)
            up = lax.ppermute(low(send), "fsdp", [(i, i + 1) for i in range(n - k)])
            send = slots[k] if down is None else wide(slots[k]) + wide(down)
            down = lax.ppermute(low(send), "fsdp", [(i, i - 1) for i in range(k, n)])
        return wide(slots[0]) + wide(up) + wide(down)

    def column_gather(self, own):
        return self.with_cores(self.line_gather(own))

    def column_scatter(self, pieces):
        return self.line_scatter(self.join_cores(pieces))

    def line_small(self, own):
        n = self.fsdp
        return [own] + [
            lax.ppermute(own, "fsdp", [(i, (i + k) % n) for i in range(n)]) for k in range(1, n)
        ]

    def line_order(self, slots):
        n = self.fsdp
        order = (lax.axis_index("fsdp") - jnp.arange(n, dtype=jnp.int32)) % n
        return jnp.stack(slots)[order]

    def seq_small(self, own):
        values = own[None]
        bit = 1
        while bit < self.seq:
            other = self.swap(values, bit)
            high = (lax.axis_index("seq") & bit) != 0
            values = jnp.concatenate(
                [jnp.where(high, other, values), jnp.where(high, values, other)], axis=0
            )
            bit *= 2
        return values

    def all_small(self, own):
        return self.seq_small(self.line_order(self.line_small(own)))

    def sum_small(self, values):
        n = self.fsdp
        bit = self.seq // 2
        while bit:
            high = (lax.axis_index("seq") & bit) != 0
            lower, upper = values[:bit], values[bit:]
            values = jnp.where(high, upper, lower) + self.swap(jnp.where(high, lower, upper), bit)
            bit //= 2
        return self.line_sum(self.line_order(list(values[0])))

    def line_sum(self, slots):
        n = self.fsdp
        total = slots[0]
        for k in range(1, n):
            total = total + lax.ppermute(slots[k], "fsdp", [(i, (i - k) % n) for i in range(n)])
        return total


def per_device(
    seq,
    fsdp,
    tokens,
    starts,
    first_gain,
    query_weight,
    key_weight,
    value_weight,
    output_weight,
    bias_table,
    second_gain,
    gate_weight,
    up_weight,
    down_weight,
    cotangent,
):
    links = Links(seq, fsdp)
    own = lax.axis_index("seq")[None]
    width = tokens.shape[2]
    heads = H // seq
    pairs = heads // 2
    by_slot = heads == fsdp
    rows = query_weight.shape[0]
    hidden_rows = gate_weight.shape[0]
    grad_out = cotangent[0]

    def pair_rows(slots):
        if by_slot:
            return [jnp.concatenate([slots[p], slots[p + 2]], axis=0) for p in range(pairs)]
        ordered = links.line_order(slots)
        ordered = ordered.reshape((-1,) + ordered.shape[2:])
        size = ordered.shape[0] // pairs
        return [ordered[p * size : (p + 1) * size] for p in range(pairs)]

    def slot_rows(values):
        if by_slot:
            size = values[0].shape[0] // 2
            return [values[k % 2][k // 2 * size : (k // 2 + 1) * size] for k in range(fsdp)]
        joined = jnp.concatenate(values, axis=0)
        ordered = joined.reshape((fsdp, -1) + joined.shape[1:])
        return list(links.line_order(list(ordered)))

    segment = jnp.cumsum(links.seq_small(starts[0]).reshape(-1), dtype=jnp.int32)
    gains = links.all_small(low(jnp.stack([first_gain, second_gain])))
    gains = wide(jnp.moveaxis(gains, 2, 0).reshape(2, -1))
    gain_first, gain_second = gains[0], gains[1]
    tables = [wide(table) for table in pair_rows(links.line_small(low(bias_table)))]
    bands = [bias_bands(table.reshape(2, BUCKETS)) for table in tables]

    token_pieces = links.stream_gather(tokens[0])
    qkv_slots = links.line_gather(
        low(jnp.stack([query_weight, key_weight, value_weight], axis=1)).reshape(rows, -1)
        if not by_slot
        else low(jnp.concatenate([query_weight, key_weight, value_weight], axis=0))
    )
    if by_slot:
        qkv_pairs = [
            jnp.concatenate(
                [
                    qkv_slots[p + 2 * t][part * rows : (part + 1) * rows]
                    for part in range(3)
                    for t in range(2)
                ],
                axis=0,
            )
            for p in range(pairs)
        ]
    else:
        qkv_pairs = [
            jnp.moveaxis(value.reshape(-1, 3, width), 1, 0).reshape(-1, width)
            for value in pair_rows(qkv_slots)
        ]
    output_slots = links.line_gather(after(low(output_weight), qkv_slots[1:]))
    output_pairs = pair_rows(output_slots)
    cot_pieces = links.column_gather(after(grad_out, output_slots[1:]))
    feed_own = low(jnp.concatenate([gate_weight, up_weight, down_weight], axis=0))
    feed_pieces = links.chip_gather(after(feed_own, token_pieces[1:]))
    gate_part, up_part, down_part = (
        jnp.concatenate(
            [piece[part * hidden_rows : (part + 1) * hidden_rows] for piece in feed_pieces], axis=0
        )
        for part in range(3)
    )

    hidden_one, qkv_first = norm_project(own, gain_first, qkv_pairs[0], token_pieces)
    qkv = [qkv_first] + [project(hidden_one, weight) for weight in qkv_pairs[1:]]
    mixed, row_lse = [], []
    for p in range(pairs):
        out, lse = attention_forward(qkv[p], segment, bands[p][0])
        mixed.append(out)
        row_lse.append(lse)
    partial = spread(own, seq, mixed, output_pairs)
    inputs = wide(tokens[0])
    resid_one = inputs + links.stream_scatter(partial)

    scale_two = lax.rsqrt(jnp.mean(resid_one * resid_one, axis=-1, keepdims=True) + EPSILON)
    normed_two = resid_one * scale_two
    hidden_two = low(normed_two * gain_second)
    hidden_pieces = links.column_gather(hidden_two)
    (inner, grad_gate, grad_up), grad_pieces = feed(
        gate_part, up_part, down_part, hidden_pieces, cot_pieces
    )
    grad_hidden_two = links.column_scatter(grad_pieces)
    hidden_all = jnp.concatenate(hidden_pieces, axis=0)
    cot_all = jnp.concatenate(cot_pieces, axis=0)

    shared = grad_hidden_two * gain_second
    grad_resid = wide(grad_out) + scale_two * (
        shared - normed_two * jnp.mean(shared * normed_two, axis=-1, keepdims=True)
    )
    branch_pieces = links.stream_gather(low(grad_resid))
    gain_two_rows = jnp.sum(grad_hidden_two * normed_two, axis=0)

    out_partial = low(nn(after(inner, grad_hidden_two), down_part))
    out_pieces = list(out_partial.reshape(len(hidden_pieces), -1, width))
    layer_out = low(resid_one + links.column_scatter(out_pieces))

    def feed_grad(left, right):
        return low(tn(left, right)).reshape(len(feed_pieces), hidden_rows, width)

    def feed_sum(grads):
        return links.chip_scatter(list(grads))

    grad_down_w = feed_sum(feed_grad(inner, cot_all))
    grad_gate_w, grad_up_w = (
        feed_sum(after(feed_grad(value, hidden_all), branch_pieces[1:]))
        for value in (grad_gate, grad_up)
    )

    grad_heads, grad_output_pairs = heads_back(own, output_pairs, mixed, branch_pieces)
    grad_output_w = links.line_scatter(slot_rows(grad_output_pairs))
    backs, tables_grad, qkv_grads, gain_sums = [None] * pairs, [None] * pairs, [None] * pairs, []
    for p in reversed(range(pairs)):
        dq, dk, dv, diagonals = attention_backward(
            qkv[p], grad_heads[p], row_lse[p], segment, bands[p][1]
        )
        backs[p] = (dq, dk, dv)
        tables_grad[p] = bucket_sums(diagonals).reshape(-1)
        qkv_grads[p], sums = qkv_grad(gain_first, hidden_one, dq, dk, dv, qkv_pairs[p])
        gain_sums.append(sums[0])
    lefts = [value for back in backs for value in back]
    rights = [
        weight[part * PAIR : (part + 1) * PAIR] for weight in qkv_pairs for part in range(3)
    ]
    grad_hidden_one = links.stream_scatter(spread(own, seq, lefts, rights))
    if by_slot:
        grad_slots = [
            jnp.concatenate(
                [
                    qkv_grads[k % 2][part * PAIR + k // 2 * rows :][:rows] for part in range(3)
                ],
                axis=0,
            )
            for k in range(fsdp)
        ]
        grad_qkv = links.line_scatter(grad_slots)
        grad_qkv = [grad_qkv[part * rows : (part + 1) * rows] for part in range(3)]
    else:
        grad_qkv = [
            links.line_scatter(
                slot_rows([value[part * PAIR : (part + 1) * PAIR] for value in qkv_grads])
            )
            for part in range(3)
        ]
    scale_one = lax.rsqrt(jnp.mean(inputs * inputs, axis=-1, keepdims=True) + EPSILON)
    normed_one = inputs * scale_one
    shared = grad_hidden_one * gain_first
    grad_tokens = low(
        grad_resid
        + scale_one * (shared - normed_one * jnp.mean(shared * normed_one, axis=-1, keepdims=True))
    )

    grad_table = links.line_sum(slot_rows(tables_grad))
    grad_gain_two = links.sum_small(gain_two_rows.reshape(seq, fsdp, -1))
    grad_gain_one = links.sum_small(sum(gain_sums).reshape(seq, fsdp, -1))
    return (
        layer_out[None],
        grad_tokens[None],
        grad_gain_one,
        grad_qkv[0],
        grad_qkv[1],
        grad_qkv[2],
        grad_output_w,
        grad_table,
        grad_gain_two,
        grad_gate_w,
        grad_up_w,
        grad_down_w,
    )


def solution(mesh):
    rows = P(("seq", "fsdp"), None)
    row = P(("seq", "fsdp"))
    activations = P("fsdp", "seq", None)
    in_specs = (
        activations,
        P("fsdp", "seq"),
        row,
        rows,
        rows,
        rows,
        rows,
        row,
        row,
        rows,
        rows,
        rows,
        activations,
    )
    out_specs = (
        activations,
        activations,
        row,
        rows,
        rows,
        rows,
        rows,
        row,
        row,
        rows,
        rows,
        rows,
    )
    return jax.shard_map(
        functools.partial(per_device, mesh.shape["seq"], mesh.shape["fsdp"]),
        mesh=mesh,
        in_specs=in_specs,
        out_specs=out_specs,
        check_vma=False,
    )
```

```python
import functools

import jax
import jax.numpy as jnp
from jax import lax
from jax.experimental import pallas as pl
from jax.experimental.pallas import tpu as pltpu
from jax.sharding import PartitionSpec as P

H = 32
DK = 64
BUCKETS = 32


EPSILON = 1e-06
NEGATIVE = -1000000000.0
BUCKET_EDGES = (12, 16, 23, 32, 46, 64, 91)
PRECISE = lax.Precision.HIGHEST
BLK = 256
PAIR = 128
VMEM_BYTES = 56 * 1024 * 1024
GELU_SCALE = 0.7978845608028654
GELU_CUBE = 0.044715


def bucket_index(offset):
    distance = jnp.abs(offset)
    coarse = 8 + sum(((distance >= edge).astype(jnp.int32) for edge in BUCKET_EDGES))
    return jnp.where(distance < 8, distance, coarse) + 16 * (offset > 0).astype(jnp.int32)


def nt(left, right):
    return lax.dot_general(
        left, right, (((1,), (1,)), ((), ())), preferred_element_type=jnp.float32
    )


def nn(left, right):
    return jnp.dot(left, right, preferred_element_type=jnp.float32)


def tn(left, right):
    return lax.dot_general(
        left, right, (((0,), (0,)), ((), ())), preferred_element_type=jnp.float32
    )


def params():
    return pltpu.CompilerParams(vmem_limit_bytes=VMEM_BYTES)


def cost(flops, bytes_accessed, transcendentals=0):
    return pl.CostEstimate(
        flops=flops, bytes_accessed=bytes_accessed, transcendentals=transcendentals
    )


def head_mask(values, head):
    lane = lax.broadcasted_iota(jnp.int32, values.shape, 1)
    keep = (lane < DK) if head == 0 else (lane >= DK)
    return jnp.where(keep, values, jnp.zeros_like(values))


def fill_strip(strip_ref, head, band_row, tiles):
    wide = jnp.broadcast_to(band_row, (BLK, band_row.shape[1]))
    rolled = pltpu.roll(wide, 0, 1, stride=1, stride_axis=0)
    span = (2 * tiles - 1) * BLK
    near = (tiles - 2) * BLK
    if near > 0:
        strip_ref[head, :, 0:near] = jnp.broadcast_to(band_row[:, 0:1], (BLK, near))
        strip_ref[head, :, near + 3 * BLK : span] = jnp.broadcast_to(
            band_row[:, 4 * BLK - 1 : 4 * BLK], (BLK, span - near - 3 * BLK)
        )
    strip_ref[head, :, near : near + 3 * BLK] = rolled[:, BLK:]


def forward_kernel(tiles, seg_row_ref, seg_col_ref, band_ref, q_ref, k_ref, v_ref, o_ref, lse_ref, strip_ref):
    blk = pl.program_id(0)

    @pl.when(blk == 0)
    def _():
        for head in range(2):
            fill_strip(strip_ref, head, band_ref[head : head + 1, :], tiles)

    keys = tiles * BLK
    start = pl.multiple_of((tiles - 1 - blk) * BLK, BLK)
    same = seg_col_ref[...] == seg_row_ref[...]
    total = jnp.zeros((BLK, PAIR), jnp.float32)
    rows = []
    for head in range(2):
        scores = nt(head_mask(q_ref[...], head), k_ref[...]) + strip_ref[head, :, pl.ds(start, keys)]
        scores = jnp.where(same, scores, NEGATIVE)
        top = jnp.max(scores, axis=1, keepdims=True)
        weight = jnp.exp(scores - top)
        norm = jnp.sum(weight, axis=1, keepdims=True)
        prob = (weight * (1.0 / norm)).astype(jnp.bfloat16)
        total = total + nn(prob, head_mask(v_ref[...], head))
        rows.append(jnp.transpose(jnp.broadcast_to(top + jnp.log(norm), (BLK, PAIR)))[0:1, :])
    o_ref[...] = total.astype(jnp.bfloat16)
    lse_ref[...] = jnp.concatenate(rows, axis=0)


def attention_forward(qkv, segment, band):
    seq_len = qkv.shape[0]
    tiles = seq_len // BLK
    return pl.pallas_call(
        functools.partial(forward_kernel, tiles),
        grid=(tiles,),
        in_specs=[
            pl.BlockSpec((1, seq_len), lambda b: (0, 0)),
            pl.BlockSpec((BLK, 1), lambda b: (b, 0)),
            pl.BlockSpec((2, 4 * BLK), lambda b: (0, 0)),
            pl.BlockSpec((BLK, PAIR), lambda b: (b, 0)),
            pl.BlockSpec((seq_len, PAIR), lambda b: (0, 1)),
            pl.BlockSpec((seq_len, PAIR), lambda b: (0, 2)),
        ],
        out_specs=[
            pl.BlockSpec((BLK, PAIR), lambda b: (b, 0)),
            pl.BlockSpec((2, BLK), lambda b: (0, b)),
        ],
        out_shape=[
            jax.ShapeDtypeStruct((seq_len, PAIR), jnp.bfloat16),
            jax.ShapeDtypeStruct((2, seq_len), jnp.float32),
        ],
        scratch_shapes=[pltpu.VMEM((2, BLK, (2 * tiles - 1) * BLK), jnp.float32)],
        compiler_params=params(),
        cost_estimate=cost(
            8 * seq_len * seq_len * PAIR, 8 * seq_len * PAIR, 2 * seq_len * seq_len
        ),
        name="attention_forward",
    )(segment[None, :], segment[:, None], band, qkv, qkv, qkv)


def diagonal_sums(tile):
    wide = jnp.concatenate([tile, jnp.zeros_like(tile)], axis=1)
    width = 2 * BLK
    row = lax.broadcasted_iota(jnp.int32, wide.shape, 0)
    shift = 1
    while shift < BLK:
        wide = jnp.where((row & shift) != 0, pltpu.roll(wide, width - shift, 1), wide)
        shift *= 2
    return jnp.sum(wide, axis=0, keepdims=True)


def backward_kernel(tiles, seg_row_ref, seg_col_ref, band_ref, q_ref, k_ref, v_ref, do_ref, lse_ref,
                    dq_ref, dk_ref, dv_ref, diag_ref, strip_ref, dk_acc, dv_acc, bias_acc, p_ref, dp_ref):
    blk = pl.program_id(0)

    @pl.when(blk == 0)
    def _():
        for head in range(2):
            fill_strip(strip_ref, head, band_ref[head : head + 1, :], tiles)
        dk_acc[...] = jnp.zeros_like(dk_acc)
        dv_acc[...] = jnp.zeros_like(dv_acc)
        bias_acc[...] = jnp.zeros_like(bias_acc)

    seg_row = seg_row_ref[...]
    grad_q = jnp.zeros((BLK, PAIR), jnp.float32)
    for head in range(2):
        q_h = head_mask(q_ref[...], head)
        do_h = head_mask(do_ref[...], head)
        lse = lse_ref[head : head + 1, :]
        delta = jnp.zeros((1, BLK), jnp.float32)
        for tile in range(tiles):
            at = slice(tile * BLK, (tile + 1) * BLK)
            column = pl.multiple_of((blk - tile + tiles - 1) * BLK, BLK)
            scores = nt(k_ref[at, :], q_h) + strip_ref[head, :, pl.ds(column, BLK)]
            scores = jnp.where(seg_col_ref[at, :] == seg_row, scores, NEGATIVE)
            prob = jnp.exp(scores - lse)
            grad_p = nt(v_ref[at, :], do_h)
            delta = delta + jnp.sum(prob * grad_p, axis=0, keepdims=True)
            dv_acc[at, :] += nn(prob.astype(jnp.bfloat16), do_h)
            p_ref[at, :] = prob
            dp_ref[at, :] = grad_p
        for tile in range(tiles):
            at = slice(tile * BLK, (tile + 1) * BLK)
            grad_s = (p_ref[at, :] * (dp_ref[at, :] - delta)).astype(jnp.bfloat16)
            dk_acc[at, :] += nn(grad_s, q_h)
            grad_q = grad_q + tn(grad_s, head_mask(k_ref[at, :], head))
            away = jnp.clip(blk - tile, -2, 2) + 2
            bias_acc[head, away] += grad_s.astype(jnp.float32)
    dq_ref[...] = grad_q.astype(jnp.bfloat16)

    @pl.when(blk == tiles - 1)
    def _():
        dk_ref[...] = dk_acc[...].astype(jnp.bfloat16)
        dv_ref[...] = dv_acc[...].astype(jnp.bfloat16)
        for head in range(2):
            for away in range(5):
                diag_ref[head, away : away + 1, :] = diagonal_sums(bias_acc[head, away])


def attention_backward(qkv, grad_o, lse, segment, band_back):
    seq_len = qkv.shape[0]
    tiles = seq_len // BLK
    rows = pl.BlockSpec((BLK, PAIR), lambda b: (b, 0))
    whole = pl.BlockSpec((seq_len, PAIR), lambda b: (0, 0))
    result = jax.ShapeDtypeStruct((seq_len, PAIR), jnp.bfloat16)
    return pl.pallas_call(
        functools.partial(backward_kernel, tiles),
        grid=(tiles,),
        in_specs=[
            pl.BlockSpec((1, BLK), lambda b: (0, b)),
            pl.BlockSpec((seq_len, 1), lambda b: (0, 0)),
            pl.BlockSpec((2, 4 * BLK), lambda b: (0, 0)),
            rows,
            pl.BlockSpec((seq_len, PAIR), lambda b: (0, 1)),
            pl.BlockSpec((seq_len, PAIR), lambda b: (0, 2)),
            rows,
            pl.BlockSpec((2, BLK), lambda b: (0, b)),
        ],
        out_specs=[rows, whole, whole, pl.BlockSpec((2, 5, 2 * BLK), lambda b: (0, 0, 0))],
        out_shape=[
            result,
            result,
            result,
            jax.ShapeDtypeStruct((2, 5, 2 * BLK), jnp.float32),
        ],
        scratch_shapes=[
            pltpu.VMEM((2, BLK, (2 * tiles - 1) * BLK), jnp.float32),
            pltpu.VMEM((seq_len, PAIR), jnp.float32),
            pltpu.VMEM((seq_len, PAIR), jnp.float32),
            pltpu.VMEM((2, 5, BLK, BLK), jnp.float32),
            pltpu.VMEM((seq_len, BLK), jnp.float32),
            pltpu.VMEM((seq_len, BLK), jnp.float32),
        ],
        compiler_params=params(),
        cost_estimate=cost(
            20 * seq_len * seq_len * PAIR, 16 * seq_len * PAIR, 2 * seq_len * seq_len
        ),
        name="attention_backward",
    )(segment[None, :], segment[:, None], band_back, qkv, qkv, qkv, grad_o, lse)


def one_hot_buckets(offset):
    return (bucket_index(offset)[..., None] == jnp.arange(BUCKETS, dtype=jnp.int32)).astype(
        jnp.float32
    )


def bias_bands(bias_rows):
    offset = jnp.arange(4 * BLK, dtype=jnp.int32) - 2 * BLK
    contract = (((1,), (1,)), ((), ()))
    ahead = lax.dot_general(bias_rows, one_hot_buckets(offset), contract, precision=PRECISE)
    behind = lax.dot_general(bias_rows, one_hot_buckets(-offset), contract, precision=PRECISE)
    return ahead, behind


def bucket_sums(diagonals):
    lane = jnp.arange(2 * BLK, dtype=jnp.int32)
    within = jnp.where(lane < BLK, lane, lane - 2 * BLK)
    away = (jnp.arange(5, dtype=jnp.int32) - 2) * BLK
    onehot = one_hot_buckets(-within[None, :] - away[:, None])
    return jnp.dot(diagonals.reshape(2, -1), onehot.reshape(-1, BUCKETS), precision=PRECISE)


CHIPS = 4
CORE, ACROSS, ALONG = 1, 2, 4
PLACES = ((6, 7), (0, 4), (5, 3), (1, 2))


def wide(values):
    return values.astype(jnp.float32)


def low(values):
    return values.astype(jnp.bfloat16)


def piece_rows(own_ref, piece, start, rows, total):
    base = (own_ref[0] ^ piece) * total + start
    return pl.ds(pl.multiple_of(base, rows), rows)


def gathered(refs):
    out = []
    for core in range(2):
        own, near_x, near_y, first, second = refs[5 * core : 5 * core + 5]
        out += [(core, 0, own), (2 + core, 0, near_x), (4 + core, 0, near_y)]
        out += [(6 + core, 0, first), (6 + core, first.shape[0], second)]
    return out


def join_slots(weight_ref, slots):
    for part in range(3):
        for index, slot in enumerate(slots):
            weight_ref[part * PAIR + index * DK : part * PAIR + (index + 1) * DK, :] = slot[
                part * DK : (part + 1) * DK, :
            ]


def norm_project_kernel(own_ref, gain_ref, slot_a, slot_b, *refs):
    hidden_ref, out_ref, weight_ref = refs[10:]
    total = refs[0].shape[0]
    for piece, start, ref in gathered(refs[:10]):
        values = wide(ref[...])
        scale = lax.rsqrt(jnp.mean(values * values, axis=-1, keepdims=True) + EPSILON)
        at = piece_rows(own_ref, piece, start, ref.shape[0], total)
        hidden_ref[at, :] = low(values * scale * gain_ref[...])
    join_slots(weight_ref, (slot_a, slot_b))
    for chunk in range(8 * total // BLK):
        at = slice(chunk * BLK, (chunk + 1) * BLK)
        out_ref[at, :] = low(nt(hidden_ref[at, :], weight_ref[...]))


VMEM = pl.BlockSpec(memory_space=pltpu.VMEM)
SMEM = pl.BlockSpec(memory_space=pltpu.SMEM)


def norm_project(own, gain, slots, pieces):
    rows, width = pieces[0].shape
    total, features = 8 * rows, 3 * PAIR
    return pl.pallas_call(
        norm_project_kernel,
        in_specs=[SMEM] + [VMEM] * 13,
        out_specs=[VMEM] * 3,
        out_shape=[
            jax.ShapeDtypeStruct((total, width), jnp.bfloat16),
            jax.ShapeDtypeStruct((total, features), jnp.bfloat16),
            jax.ShapeDtypeStruct((features, width), jnp.bfloat16),
        ],
        compiler_params=params(),
        cost_estimate=cost(
            2 * total * width * features, 2 * (2 * total * width + features * (width + total))
        ),
        name="norm_project",
    )(own, gain[None, :], *slots, *pieces)


def project_kernel(hidden_ref, slot_a, slot_b, out_ref, weight_ref):
    @pl.when(pl.program_id(0) == 0)
    def _():
        join_slots(weight_ref, (slot_a, slot_b))

    out_ref[...] = low(nt(hidden_ref[...], weight_ref[...]))


def project(hidden, slots):
    total, width = hidden.shape
    features = 3 * PAIR
    slot = pl.BlockSpec((3 * DK, width), lambda b: (0, 0))
    return pl.pallas_call(
        project_kernel,
        grid=(total // BLK,),
        in_specs=[pl.BlockSpec((BLK, width), lambda b: (b, 0)), slot, slot],
        out_specs=[
            pl.BlockSpec((BLK, features), lambda b: (b, 0)),
            pl.BlockSpec((features, width), lambda b: (0, 0)),
        ],
        out_shape=[
            jax.ShapeDtypeStruct((total, features), jnp.bfloat16),
            jax.ShapeDtypeStruct((features, width), jnp.bfloat16),
        ],
        compiler_params=params(),
        cost_estimate=cost(
            2 * total * width * features, 2 * (total * width + features * (width + total))
        ),
        name="project",
    )(hidden, *slots)


def spread_kernel(counts, own_ref, *refs):
    lefts, rights = refs[: counts[0]], refs[counts[0] : counts[0] + counts[1]]
    outs, weight = refs[-3:-1], refs[-1]
    start = 0
    for right in rights:
        weight[start : start + right.shape[0], :] = right[...]
        start += right.shape[0]
    total = lefts[0].shape[0] // 8
    half = total // 2
    for piece in range(8):
        at = piece_rows(own_ref, piece, 0, total, total)
        values = None
        for index, left in enumerate(lefts):
            term = nn(left[at, :], weight[index * PAIR : (index + 1) * PAIR, :])
            values = term if values is None else values + term
        out = outs[piece % 2]
        for index, place in enumerate(PLACES[piece // 2]):
            out[place * half : (place + 1) * half, :] = low(
                values[index * half : (index + 1) * half, :]
            )


def spread(own, lefts, rights):
    total, width = lefts[0].shape[0], rights[0].shape[1]
    depth = sum(left.shape[1] for left in lefts)
    return pl.pallas_call(
        functools.partial(spread_kernel, (len(lefts), len(rights))),
        in_specs=[SMEM] + [VMEM] * (len(lefts) + len(rights)),
        out_specs=[VMEM] * 2,
        out_shape=[jax.ShapeDtypeStruct((total // 2, width), jnp.bfloat16)] * 2,
        scratch_shapes=[pltpu.VMEM((depth, width), jnp.bfloat16)],
        compiler_params=params(),
        cost_estimate=cost(
            2 * total * width * depth, 2 * (total * width + depth * (width + total))
        ),
        name="spread",
    )(own, *lefts, *rights)


def heads_back_kernel(own_ref, weight_a0, weight_a1, weight_b0, weight_b1, mixed_a, mixed_b, *refs):
    heads_a, heads_b, grad_a, grad_b, whole, weight = refs[10:]
    total = refs[0].shape[0]
    for piece, start, ref in gathered(refs[:10]):
        whole[piece_rows(own_ref, piece, start, ref.shape[0], total), :] = ref[...]
    for index, ref in enumerate((weight_a0, weight_a1, weight_b0, weight_b1)):
        weight[index * DK : (index + 1) * DK, :] = ref[...]
    for chunk in range(8 * total // BLK):
        at = slice(chunk * BLK, (chunk + 1) * BLK)
        heads = low(nt(whole[at, :], weight[...]))
        heads_a[at, :] = heads[:, :PAIR]
        heads_b[at, :] = heads[:, PAIR:]
    grad_a[...] = low(tn(mixed_a[...], whole[...]))
    grad_b[...] = low(tn(mixed_b[...], whole[...]))


def heads_back(own, weights, mixed, pieces):
    rows, width = pieces[0].shape
    total = 8 * rows
    outs = pl.pallas_call(
        heads_back_kernel,
        in_specs=[SMEM] + [VMEM] * 16,
        out_specs=[VMEM] * 4,
        out_shape=[jax.ShapeDtypeStruct((total, PAIR), jnp.bfloat16)] * 2
        + [jax.ShapeDtypeStruct((PAIR, width), jnp.bfloat16)] * 2,
        scratch_shapes=[
            pltpu.VMEM((total, width), jnp.bfloat16),
            pltpu.VMEM((2 * PAIR, width), jnp.bfloat16),
        ],
        compiler_params=params(),
        cost_estimate=cost(8 * total * width * PAIR, 2 * total * width),
        name="heads_back",
    )(own, *weights, *mixed, *pieces)
    return outs[:2], outs[2:]


def qkv_grad_kernel(gain_ref, hidden_ref, dq_ref, dk_ref, dv_ref, weight_ref, slot_a, slot_b, sum_ref):
    total = None
    for part, ref in enumerate((dq_ref, dk_ref, dv_ref)):
        grad = tn(ref[...], hidden_ref[...])
        slot_a[part * DK : (part + 1) * DK, :] = low(grad[:DK])
        slot_b[part * DK : (part + 1) * DK, :] = low(grad[DK:])
        at = slice(part * PAIR, (part + 1) * PAIR)
        term = jnp.sum(grad * wide(weight_ref[at, :]), axis=0, keepdims=True)
        total = term if total is None else total + term
    sum_ref[...] = total / gain_ref[...]


def qkv_grad(gain, hidden, dq, dk, dv, weight):
    total, width = hidden.shape
    cols = 512
    col = pl.BlockSpec((1, cols), lambda c: (0, c))
    back = pl.BlockSpec((total, PAIR), lambda c: (0, 0))
    slot = pl.BlockSpec((3 * DK, cols), lambda c: (0, c))
    return pl.pallas_call(
        qkv_grad_kernel,
        grid=(width // cols,),
        in_specs=[
            col,
            pl.BlockSpec((total, cols), lambda c: (0, c)),
            back,
            back,
            back,
            pl.BlockSpec((3 * PAIR, cols), lambda c: (0, c)),
        ],
        out_specs=[slot, slot, col],
        out_shape=[
            jax.ShapeDtypeStruct((3 * DK, width), jnp.bfloat16),
            jax.ShapeDtypeStruct((3 * DK, width), jnp.bfloat16),
            jax.ShapeDtypeStruct((1, width), jnp.float32),
        ],
        compiler_params=params(),
        cost_estimate=cost(6 * total * width * PAIR, 2 * total * width + 12 * PAIR * width),
        name="qkv_grad",
    )(gain[None, :], hidden, dq, dk, dv, weight)


def feed_kernel(*refs):
    own, near_x, near_y, first, second = refs[:5]
    hidden, cot = refs[5:13], refs[13:21]
    inner_ref, dgate_ref, dup_ref, down_w, out_own, out_other, gate_w, up_w = refs[21:]
    units = own.shape[0] // 3
    half = units // 2
    for part, weight in enumerate((gate_w, up_w, down_w)):
        base = part * units
        for chip, ref in ((0, own), (1, near_x), (2, near_y)):
            for index, place in enumerate(PLACES[chip]):
                weight[place * half : (place + 1) * half, :] = ref[
                    base + index * half : base + (index + 1) * half, :
                ]
        for index, place in enumerate(PLACES[3]):
            start = base + index * half
            ref, start = (first, start) if start < 3 * half else (second, start - 3 * half)
            weight[place * half : (place + 1) * half, :] = ref[start : start + half, :]
    rows = hidden[0].shape[0]
    for piece in range(0, 8, 2):
        values = jnp.concatenate([hidden[piece][...], hidden[piece + 1][...]], axis=0)
        grads = jnp.concatenate([cot[piece][...], cot[piece + 1][...]], axis=0)
        at = slice(piece * rows, (piece + 2) * rows)
        gate = nt(values, gate_w[...])
        up = nt(values, up_w[...])
        grad_m = nt(grads, down_w[...])
        square = gate * gate
        bend = jnp.tanh(GELU_SCALE * gate * (1.0 + GELU_CUBE * square))
        part = 0.5 * (1.0 + bend)
        act = gate * part
        slope = part + 0.5 * gate * (1.0 - bend * bend) * (
            GELU_SCALE * (1.0 + 3.0 * GELU_CUBE * square)
        )
        inner_ref[at, :] = low(act * up)
        dgate = low(grad_m * up * slope)
        dup = low(grad_m * act)
        dgate_ref[at, :] = dgate
        dup_ref[at, :] = dup
        grad_h = low(nn(dgate, gate_w[...]) + nn(dup, up_w[...]))
        out = out_own if piece < 4 else out_other
        out[(piece % 4) * rows : (piece % 4 + 2) * rows, :] = grad_h


def feed(weights, hidden, cot):
    rows, width = hidden[0].shape
    total, units = 8 * rows, CHIPS * weights[0].shape[0] // 3
    outs = pl.pallas_call(
        feed_kernel,
        in_specs=[VMEM] * 21,
        out_specs=[VMEM] * 6,
        out_shape=[jax.ShapeDtypeStruct((total, units), jnp.bfloat16)] * 3
        + [jax.ShapeDtypeStruct((units, width), jnp.bfloat16)]
        + [jax.ShapeDtypeStruct((total // 2, width), jnp.bfloat16)] * 2,
        scratch_shapes=[pltpu.VMEM((units, width), jnp.bfloat16)] * 2,
        compiler_params=params(),
        cost_estimate=cost(10 * total * width * units, 2 * 3 * (total + units) * width),
        name="feed",
    )(*weights, *hidden, *cot)
    return outs


def fence(*values):
    return lax.optimization_barrier(values)


def swap(values, bits):
    return lax.ppermute(values, "seq", [(i, i ^ bits) for i in range(2 * CHIPS)])


def ring(values, step):
    n = lax.axis_size("fsdp")
    return lax.ppermute(values, "fsdp", [(i, (i + step) % n) for i in range(n)])


def line_order(slots):
    n = len(slots)
    order = (lax.axis_index("fsdp") - jnp.arange(n, dtype=jnp.int32)) % n
    return jnp.stack(slots)[order]


def both(values, other, bits):
    high = (lax.axis_index("seq") & bits) != 0
    return jnp.concatenate(
        [jnp.where(high, other, values), jnp.where(high, values, other)], axis=0
    )


def halves(values, bits):
    high = (lax.axis_index("seq") & bits) != 0
    size = values.shape[0] // 2
    lower, upper = values[:size], values[size:]
    return jnp.where(high, upper, lower), jnp.where(high, lower, upper)


def plane_sends(own, other=None):
    size = own.shape[0] // 4
    total = own if other is None else wide(own) + wide(other)
    return low(total[:size]), low(total[size : 2 * size]), total[2 * size :]


def plane_second(keep, from_x, from_y):
    size = keep.shape[0] // 4
    to_x = low(wide(keep[:size]) + wide(from_y[:size]))
    to_y = low(wide(keep[size : 2 * size]) + wide(from_x[size:]))
    return to_x, to_y


def plane_total(keep, from_x, from_y, second_x, second_y):
    size = keep.shape[0] // 4
    first = wide(keep[2 * size : 3 * size]) + wide(from_x[:size]) + wide(second_y)
    second = wide(keep[3 * size :]) + wide(from_y[size:]) + wide(second_x)
    return jnp.concatenate([first, second], axis=0)


def slot_sum(own, other, slot):
    rows = own.shape[0] // 4
    at = slice(slot * rows, (slot + 1) * rows)
    return wide(own[at]) + wide(other[at])


def per_device(
    tokens,
    starts,
    first_gain,
    query_weight,
    key_weight,
    value_weight,
    output_weight,
    bias_table,
    second_gain,
    gate_weight,
    up_weight,
    down_weight,
    cotangent,
):
    index = lax.axis_index("seq")[None]
    width = tokens.shape[2]
    own = tokens[0]
    half = own.shape[0] // 2
    grad_out = cotangent[0]
    units = gate_weight.shape[0]
    qkv0 = low(jnp.concatenate([query_weight, key_weight, value_weight], axis=0))
    out0 = low(output_weight)
    feed0 = low(jnp.concatenate([gate_weight, up_weight, down_weight], axis=0))
    feed_half = feed0.shape[0] // 2
    small = low(jnp.concatenate([first_gain, second_gain, bias_table]))

    tok_x, tok_y, tok_c = swap(own, ACROSS), swap(own, ALONG), swap(own, CORE)
    qkv1 = ring(qkv0, 1)
    small_slots = [small] + [ring(small, k) for k in range(1, 4)]
    tok_x, tok_y, small_slots = fence(tok_x, tok_y, small_slots)

    gain_part = line_order([value[: -bias_table.shape[0]] for value in small_slots]).reshape(-1)
    packed = jnp.concatenate([gain_part, low(starts[0])])[None]
    tok_d1, tok_d2 = swap(tok_y[:half], ACROSS), swap(tok_x[half:], ALONG)
    tok_cx, tok_cy = swap(tok_x, CORE), swap(tok_y, CORE)
    packed = both(packed, swap(packed, CORE), CORE)
    tok_d1, tok_d2, packed, feed0 = fence(tok_d1, tok_d2, packed, feed0)

    tok_c1, tok_c2 = swap(tok_d1, CORE), swap(tok_d2, CORE)
    packed = both(packed, swap(packed, ACROSS), ACROSS)
    feed_x, feed_y = swap(feed0, ACROSS), swap(feed0, ALONG)
    packed, qkv1, out0, tok_c1, tok_c2 = fence(packed, qkv1, out0, tok_c1, tok_c2)

    qkv2 = ring(qkv1, 1)
    out1 = ring(out0, 1)
    packed = both(packed, swap(packed, ALONG), ALONG)
    gain_count = gain_part.shape[0]
    gains = wide(packed[:, :gain_count]).reshape(-1, 4, 2, first_gain.shape[0])
    gain_first = gains[:, :, 0].reshape(-1)
    gain_second = gains[:, :, 1].reshape(-1)
    segment = jnp.cumsum(packed[:, gain_count:].reshape(-1).astype(jnp.int32), dtype=jnp.int32)
    tables = [wide(value[-bias_table.shape[0] :]) for value in small_slots]
    bands = [bias_bands(jnp.stack(tables[2 * p : 2 * p + 2])) for p in range(2)]
    segment, gain_first, gain_second, bands, qkv1 = fence(
        segment, gain_first, gain_second, bands, qkv1
    )

    tok_pieces = (own, tok_x, tok_y, tok_d1, tok_d2, tok_c, tok_cx, tok_cy, tok_c1, tok_c2)
    hidden_one, qkv_a, weight_a = norm_project(index, gain_first, (qkv0, qkv1), tok_pieces)
    hidden_one, qkv_a, weight_a, qkv2, out1 = fence(hidden_one, qkv_a, weight_a, qkv2, out1)

    qkv3 = ring(qkv2, 1)
    out2 = ring(out1, 1)
    mixed_a, lse_a = attention_forward(qkv_a, segment, bands[0][0])
    mixed_a, lse_a, hidden_one, qkv3, out2, feed_x, feed_y, grad_out = fence(
        mixed_a, lse_a, hidden_one, qkv3, out2, feed_x, feed_y, grad_out
    )

    out3 = ring(out2, 1)
    cot1 = ring(grad_out, 1)
    cot_c0 = swap(grad_out, CORE)
    feed_d1, feed_d2 = swap(feed_y[:feed_half], ACROSS), swap(feed_x[feed_half:], ALONG)
    qkv_b, weight_b = project(hidden_one, (qkv2, qkv3))
    mixed_b, lse_b = attention_forward(qkv_b, segment, bands[1][0])
    mixed_b, lse_b, out3, cot1 = fence(mixed_b, lse_b, out3, cot1)

    cot2 = ring(cot1, 1)
    cot_c1 = swap(cot1, CORE)
    out_slots = (out0, out1, out2, out3)
    part_own, part_other = spread(index, (mixed_a, mixed_b), out_slots)
    part_other = swap(part_other, CORE)
    send_x, send_y, keep = plane_sends(part_own, part_other)
    send_x, send_y, keep, cot2 = fence(send_x, send_y, keep, cot2)

    from_x, from_y = swap(send_x, ACROSS), swap(send_y, ALONG)
    cot3 = ring(cot2, 1)
    cot_c2 = swap(cot2, CORE)
    send_x, send_y = plane_second(keep, from_x, from_y)
    second_x, second_y = swap(send_x, ACROSS), swap(send_y, ALONG)
    inputs = wide(own)
    resid_one = inputs + plane_total(keep, from_x, from_y, second_x, second_y)

    scale_two = lax.rsqrt(jnp.mean(resid_one * resid_one, axis=-1, keepdims=True) + EPSILON)
    normed_two = resid_one * scale_two
    hid0 = low(normed_two * gain_second)
    hid0, cot3, cot_c2, resid_one, scale_two = fence(hid0, cot3, cot_c2, resid_one, scale_two)
    hid1, hid_c0, cot_c3 = ring(hid0, 1), swap(hid0, CORE), swap(cot3, CORE)
    hid1, hid_c0, cot_c3 = fence(hid1, hid_c0, cot_c3)
    hid2, hid_c1 = ring(hid1, 1), swap(hid1, CORE)
    hid2, hid_c1 = fence(hid2, hid_c1)
    hid3, hid_c2 = ring(hid2, 1), swap(hid2, CORE)
    hid3, hid_c2 = fence(hid3, hid_c2)
    hid_c3 = swap(hid3, CORE)
    hid_pieces = (hid0, hid1, hid2, hid3, hid_c0, hid_c1, hid_c2, hid_c3)
    cot_pieces = (grad_out, cot1, cot2, cot3, cot_c0, cot_c1, cot_c2, cot_c3)
    inner, grad_gate, grad_up, down_all, dh_own, dh_other = feed(
        (feed0, feed_x, feed_y, feed_d1, feed_d2), hid_pieces, cot_pieces
    )
    inner, grad_gate, grad_up, down_all, dh_own, dh_other, hid_pieces, cot_pieces = fence(
        inner, grad_gate, grad_up, down_all, dh_own, dh_other, hid_pieces, cot_pieces
    )

    dh_other = swap(dh_other, CORE)
    cot_all = jnp.concatenate(cot_pieces, axis=0)
    hid_all = jnp.concatenate(hid_pieces, axis=0)
    grad_down = low(tn(inner, cot_all))
    grad_down, dh_other, dh_own, hid_all = fence(grad_down, dh_other, dh_own, hid_all)

    dh = ring(low(slot_sum(dh_own, dh_other, 3)), -1)
    down_x, down_y, down_keep = plane_sends(grad_down)
    down_fx, down_fy = swap(down_x, ACROSS), swap(down_y, ALONG)
    grad_gate_all = low(tn(grad_gate, hid_all))
    grad_up_all = low(tn(grad_up, hid_all))
    dh, grad_gate_all, grad_up_all = fence(dh, grad_gate_all, grad_up_all)

    dh = ring(low(slot_sum(dh_own, dh_other, 2) + wide(dh)), -1)
    out_part = low(nn(inner, down_all))
    dh, out_part, down_fx, down_fy = fence(dh, out_part, down_fx, down_fy)

    dh = ring(low(slot_sum(dh_own, dh_other, 1) + wide(dh)), -1)
    out_rows = out_part.shape[0] // 2
    out_own = out_part[:out_rows]
    out_other = swap(out_part[out_rows:], CORE)
    down_x, down_y = plane_second(down_keep, down_fx, down_fy)
    down_sx, down_sy = swap(down_x, ACROSS), swap(down_y, ALONG)
    grad_hidden_two = slot_sum(dh_own, dh_other, 0) + wide(dh)
    normed_two = resid_one * scale_two
    shared = grad_hidden_two * gain_second
    grad_resid = wide(grad_out) + scale_two * (
        shared - normed_two * jnp.mean(shared * normed_two, axis=-1, keepdims=True)
    )
    branch = low(grad_resid)
    gain_two_rows = jnp.sum(grad_hidden_two * normed_two, axis=0)
    branch, grad_resid, gain_two_rows, out_other, down_sx, down_sy = fence(
        branch, grad_resid, gain_two_rows, out_other, down_sx, down_sy
    )

    br_x, br_y, br_c = swap(branch, ACROSS), swap(branch, ALONG), swap(branch, CORE)
    out_sum = ring(low(slot_sum(out_own, out_other, 3)), -1)
    grad_down_w = plane_total(down_keep, down_fx, down_fy, down_sx, down_sy)
    br_x, br_y, br_c, out_sum = fence(br_x, br_y, br_c, out_sum)
    br_d1, br_d2 = swap(br_y[:half], ACROSS), swap(br_x[half:], ALONG)
    br_cx, br_cy = swap(br_x, CORE), swap(br_y, CORE)
    out_sum = ring(low(slot_sum(out_own, out_other, 2) + wide(out_sum)), -1)
    br_d1, br_d2, br_cx, br_cy, grad_gate_all = fence(br_d1, br_d2, br_cx, br_cy, grad_gate_all)
    br_c1, br_c2 = swap(br_d1, CORE), swap(br_d2, CORE)
    gate_x, gate_y, gate_keep = plane_sends(grad_gate_all)
    gate_fx, gate_fy = swap(gate_x, ACROSS), swap(gate_y, ALONG)

    pieces = (branch, br_x, br_y, br_d1, br_d2, br_c, br_cx, br_cy, br_c1, br_c2)
    grad_heads, grad_outs = heads_back(index, out_slots, (mixed_a, mixed_b), pieces)
    grad_heads, grad_outs, out_sum, grad_up_all = fence(grad_heads, grad_outs, out_sum, grad_up_all)

    def out_slot(k):
        return grad_outs[k // 2][k % 2 * DK : (k % 2 + 1) * DK]

    out_sum = ring(low(slot_sum(out_own, out_other, 1) + wide(out_sum)), -1)
    go_sum = ring(out_slot(3), -1)
    up_x, up_y, up_keep = plane_sends(grad_up_all)
    up_fx, up_fy = swap(up_x, ACROSS), swap(up_y, ALONG)
    dq_b, dk_b, dv_b, diag_b = attention_backward(
        qkv_b, grad_heads[1], lse_b, segment, bands[1][1]
    )
    dq_b, dk_b, dv_b, diag_b, go_sum, gate_fx, gate_fy, out_sum = fence(
        dq_b, dk_b, dv_b, diag_b, go_sum, gate_fx, gate_fy, out_sum
    )

    layer_out = low(resid_one + slot_sum(out_own, out_other, 0) + wide(out_sum))
    go_sum = ring(low(wide(out_slot(2)) + wide(go_sum)), -1)
    gate_x, gate_y = plane_second(gate_keep, gate_fx, gate_fy)
    gate_sx, gate_sy = swap(gate_x, ACROSS), swap(gate_y, ALONG)
    gq2, gq3, sums_b = qkv_grad(gain_first, hidden_one, dq_b, dk_b, dv_b, weight_b)
    gq2, gq3, sums_b, go_sum, up_fx, up_fy, qkv_a = fence(
        gq2, gq3, sums_b, go_sum, up_fx, up_fy, qkv_a
    )

    gq = ring(gq3, -1)
    go_sum = ring(low(wide(out_slot(1)) + wide(go_sum)), -1)
    up_x, up_y = plane_second(up_keep, up_fx, up_fy)
    up_sx, up_sy = swap(up_x, ACROSS), swap(up_y, ALONG)
    dq_a, dk_a, dv_a, diag_a = attention_backward(
        qkv_a, grad_heads[0], lse_a, segment, bands[0][1]
    )
    dq_a, dk_a, dv_a, diag_a, gq, go_sum, gate_sx, gate_sy, up_sx, up_sy = fence(
        dq_a, dk_a, dv_a, diag_a, gq, go_sum, gate_sx, gate_sy, up_sx, up_sy
    )

    gq = ring(low(wide(gq2) + wide(gq)), -1)
    back_own, back_other = spread(
        index, (dq_a, dk_a, dv_a, dq_b, dk_b, dv_b), (weight_a, weight_b)
    )
    back_own, back_other, dq_a = fence(back_own, back_other, dq_a)
    back_other = swap(back_other, CORE)
    gq0, gq1, sums_a = qkv_grad(gain_first, hidden_one, dq_a, dk_a, dv_a, weight_a)
    send_x, send_y, keep = plane_sends(back_own, back_other)
    gq, gq0, gq1, sums_a, send_x, send_y, keep = fence(
        gq, gq0, gq1, sums_a, send_x, send_y, keep
    )

    from_x, from_y = swap(send_x, ACROSS), swap(send_y, ALONG)
    gq = ring(low(wide(gq1) + wide(gq)), -1)
    diagonals = (diag_a, diag_b)
    table_rows = jnp.concatenate([bucket_sums(value) for value in diagonals], axis=0)
    gain_rows = jnp.stack([(sums_a + sums_b)[0], gain_two_rows]).reshape(2, 2 * CHIPS, 4, -1)
    gain_rows = jnp.moveaxis(gain_rows, 0, 2).reshape(2 * CHIPS, -1)
    gain_keep, gain_send = halves(gain_rows, ALONG)
    gain_rows = gain_keep + swap(gain_send, ALONG)
    table = table_rows[0] + sum(ring(table_rows[k], -k) for k in range(1, 4))
    send_x, send_y = plane_second(keep, from_x, from_y)
    send_x, send_y, gain_rows = fence(send_x, send_y, gain_rows)
    second_x, second_y = swap(send_x, ACROSS), swap(send_y, ALONG)
    for bits in (ACROSS, CORE):
        gain_keep, gain_send = halves(gain_rows, bits)
        gain_rows = gain_keep + swap(gain_send, bits)
    gain_slots = line_order(list(gain_rows.reshape(4, -1)))
    gain = gain_slots[0] + sum(ring(gain_slots[k], -k) for k in range(1, 4))
    grad_hidden_one = plane_total(keep, from_x, from_y, second_x, second_y)
    scale_one = lax.rsqrt(jnp.mean(inputs * inputs, axis=-1, keepdims=True) + EPSILON)
    normed_one = inputs * scale_one
    shared = grad_hidden_one * gain_first
    grad_tokens = low(
        grad_resid
        + scale_one * (shared - normed_one * jnp.mean(shared * normed_one, axis=-1, keepdims=True))
    )
    grad_qkv = wide(gq0) + wide(gq)
    grad_output_w = wide(out_slot(0)) + wide(go_sum)
    grad_gate_w = plane_total(gate_keep, gate_fx, gate_fy, gate_sx, gate_sy)
    grad_up_w = plane_total(up_keep, up_fx, up_fy, up_sx, up_sy)
    rows = first_gain.shape[0]
    return (
        layer_out[None],
        grad_tokens[None],
        gain[:rows],
        grad_qkv[:DK],
        grad_qkv[DK : 2 * DK],
        grad_qkv[2 * DK :],
        grad_output_w,
        table,
        gain[rows:],
        grad_gate_w,
        grad_up_w,
        grad_down_w,
    )


def rms_norm(values, gain):
    return values * lax.rsqrt(jnp.mean(values * values, axis=-1, keepdims=True) + EPSILON) * gain


def gated_gelu(gate, up_part):
    return jax.nn.gelu(gate, approximate=True) * up_part


def gather_rows(values):
    return lax.all_gather(values, "seq", axis=0, tiled=True)


def scatter_rows(values):
    return lax.psum_scatter(
        values.astype(jnp.bfloat16), "seq", scatter_dimension=0, tiled=True
    ).astype(jnp.float32)


def per_device_general(
    tokens,
    starts,
    first_gain,
    query_weight,
    key_weight,
    value_weight,
    output_weight,
    bias_table,
    second_gain,
    gate_weight,
    up_weight,
    down_weight,
    cotangent,
):
    segment = jnp.cumsum(lax.all_gather(starts, "seq", axis=1, tiled=True)[0], dtype=jnp.int32)
    inputs = tokens[0].astype(jnp.float32)
    grad_out = cotangent[0]
    head_count = H // lax.axis_size("seq")
    head_first = lax.axis_index("seq") * head_count
    query_low = query_weight.astype(jnp.bfloat16)
    key_low = key_weight.astype(jnp.bfloat16)
    value_low = value_weight.astype(jnp.bfloat16)
    output_low = output_weight.astype(jnp.bfloat16)
    gate_low = gate_weight.astype(jnp.bfloat16)
    up_low = up_weight.astype(jnp.bfloat16)
    down_low = down_weight.astype(jnp.bfloat16)
    first_low = first_gain.astype(jnp.bfloat16)
    second_low = second_gain.astype(jnp.bfloat16)
    table_low = bias_table.astype(jnp.bfloat16)
    query_part, key_part, value_part, output_part, gate_part, up_rows, down_part = (
        lax.all_gather(query_low, "fsdp", axis=0, tiled=True),
        lax.all_gather(key_low, "fsdp", axis=0, tiled=True),
        lax.all_gather(value_low, "fsdp", axis=0, tiled=True),
        lax.all_gather(output_low, "fsdp", axis=0, tiled=True),
        lax.all_gather(gate_low, "fsdp", axis=0, tiled=True),
        lax.all_gather(up_low, "fsdp", axis=0, tiled=True),
        lax.all_gather(down_low, "fsdp", axis=0, tiled=True),
    )
    gain_one, gain_two, table_full = (
        lax.all_gather(first_low, ("seq", "fsdp"), axis=0, tiled=True),
        lax.all_gather(second_low, ("seq", "fsdp"), axis=0, tiled=True),
        lax.all_gather(table_low, ("seq", "fsdp"), axis=0, tiled=True),
    )
    gain_first = gain_one.astype(jnp.float32)
    gain_second = gain_two.astype(jnp.float32)
    bias_rows = lax.dynamic_slice_in_dim(
        table_full.astype(jnp.float32).reshape(H, BUCKETS), head_first, head_count, 0
    )
    hidden_one = rms_norm(inputs, gain_first).astype(jnp.bfloat16)
    hidden_all = gather_rows(hidden_one)
    query_head = (
        low(nt(hidden_all, query_part))
    )
    key_head = (
        low(nt(hidden_all, key_part))
    )
    value_head = (
        low(nt(hidden_all, value_part))
    )
    pairs = head_count // 2
    pair = [slice(index * PAIR, (index + 1) * PAIR) for index in range(pairs)]
    bands = [bias_bands(bias_rows[2 * index : 2 * index + 2]) for index in range(pairs)]
    qkv = [
        jnp.concatenate([query_head[:, at], key_head[:, at], value_head[:, at]], axis=1)
        for at in pair
    ]
    forward = [attention_forward(qkv[i], segment, bands[i][0]) for i in range(pairs)]
    mixed = jnp.concatenate([out for out, _ in forward], axis=1)
    resid_one = inputs + scatter_rows(nn(mixed, output_part))
    hidden_two = rms_norm(resid_one, gain_second).astype(jnp.bfloat16)
    hidden_two_all = gather_rows(hidden_two)
    gate = nt(hidden_two_all, gate_part)
    up_part = nt(hidden_two_all, up_rows)
    inner = gated_gelu(gate, up_part).astype(jnp.bfloat16)
    layer_out = (resid_one + scatter_rows(nn(inner, down_part))).astype(jnp.bfloat16)
    grad_out_all = gather_rows(grad_out)
    grad_inner = nt(grad_out_all, down_part)
    grad_down = tn(inner, grad_out_all)
    grad_gate, grad_up = jax.vjp(gated_gelu, gate, up_part)[1](grad_inner)
    grad_gate = grad_gate.astype(jnp.bfloat16)
    grad_up = grad_up.astype(jnp.bfloat16)
    grad_gate_w = tn(grad_gate, hidden_two_all)
    grad_up_w = tn(grad_up, hidden_two_all)
    grad_hidden_two = scatter_rows(nn(grad_gate, gate_part) + nn(grad_up, up_rows))
    grad_norm_two, grad_gain_two = jax.vjp(rms_norm, resid_one, gain_second)[1](grad_hidden_two)
    grad_resid = grad_out.astype(jnp.float32) + grad_norm_two
    grad_branch = grad_resid.astype(jnp.bfloat16)
    branch_all = gather_rows(grad_branch)
    grad_output_w = tn(mixed, branch_all)
    grad_heads = (
        low(nt(branch_all, output_part))
    )
    back = [
        attention_backward(qkv[i], grad_heads[:, pair[i]], forward[i][1], segment, bands[i][1])
        for i in range(pairs)
    ]
    grad_query_seq, grad_key_seq, grad_value_seq = (
        jnp.concatenate([values[part] for values in back], axis=1) for part in range(3)
    )
    grad_bias = jnp.concatenate([bucket_sums(values[3]) for values in back], axis=0)
    grad_query_w = tn(grad_query_seq, hidden_all)
    grad_key_w = tn(grad_key_seq, hidden_all)
    grad_value_w = tn(grad_value_seq, hidden_all)
    grad_hidden_one = scatter_rows(
        nn(grad_query_seq, query_part)
        + nn(grad_key_seq, key_part)
        + nn(grad_value_seq, value_part)
    )
    grad_norm_one, grad_gain_one = jax.vjp(rms_norm, inputs, gain_first)[1](grad_hidden_one)
    grad_tokens = (grad_resid + grad_norm_one).astype(jnp.bfloat16)
    grad_table = lax.dynamic_update_slice_in_dim(
        jnp.zeros((H, BUCKETS), jnp.float32), grad_bias, head_first, 0
    ).reshape(-1)
    weight_grads = (
        lax.psum_scatter(
            grad_query_w.astype(jnp.bfloat16), "fsdp", scatter_dimension=0, tiled=True
        ).astype(jnp.float32),
        lax.psum_scatter(
            grad_key_w.astype(jnp.bfloat16), "fsdp", scatter_dimension=0, tiled=True
        ).astype(jnp.float32),
        lax.psum_scatter(
            grad_value_w.astype(jnp.bfloat16), "fsdp", scatter_dimension=0, tiled=True
        ).astype(jnp.float32),
        lax.psum_scatter(
            grad_output_w.astype(jnp.bfloat16), "fsdp", scatter_dimension=0, tiled=True
        ).astype(jnp.float32),
        lax.psum_scatter(
            grad_gate_w.astype(jnp.bfloat16), "fsdp", scatter_dimension=0, tiled=True
        ).astype(jnp.float32),
        lax.psum_scatter(
            grad_up_w.astype(jnp.bfloat16), "fsdp", scatter_dimension=0, tiled=True
        ).astype(jnp.float32),
        lax.psum_scatter(
            grad_down.astype(jnp.bfloat16), "fsdp", scatter_dimension=0, tiled=True
        ).astype(jnp.float32),
    )
    small_grads = (
        lax.psum_scatter(grad_gain_one, ("seq", "fsdp"), scatter_dimension=0, tiled=True),
        lax.psum_scatter(grad_gain_two, ("seq", "fsdp"), scatter_dimension=0, tiled=True),
        lax.psum_scatter(grad_table, ("seq", "fsdp"), scatter_dimension=0, tiled=True),
    )
    return (
        layer_out[None],
        grad_tokens[None],
        small_grads[0],
        weight_grads[0],
        weight_grads[1],
        weight_grads[2],
        weight_grads[3],
        small_grads[2],
        small_grads[1],
        weight_grads[4],
        weight_grads[5],
        weight_grads[6],
    )


def solution(mesh):
    rows = P(("seq", "fsdp"), None)
    row = P(("seq", "fsdp"))
    activations = P("fsdp", "seq", None)
    in_specs = (
        activations,
        P("fsdp", "seq"),
        row,
        rows,
        rows,
        rows,
        rows,
        row,
        row,
        rows,
        rows,
        rows,
        activations,
    )
    out_specs = (
        activations,
        activations,
        row,
        rows,
        rows,
        rows,
        rows,
        row,
        row,
        rows,
        rows,
        rows,
    )
    seq, fsdp = mesh.shape["seq"], mesh.shape["fsdp"]
    plan = per_device if seq == 2 * CHIPS and H == seq * fsdp else per_device_general
    return jax.shard_map(
        plan,
        mesh=mesh,
        in_specs=in_specs,
        out_specs=out_specs,
        check_vma=False,
    )
```

```python
import functools

import jax
import jax.numpy as jnp
from jax import lax
from jax.experimental import pallas as pl
from jax.experimental.pallas import tpu as pltpu
from jax.sharding import PartitionSpec as P

H = 32
DK = 64
BUCKETS = 32


EPSILON = 1e-06
NEGATIVE = -1000000000.0
BUCKET_EDGES = (12, 16, 23, 32, 46, 64, 91)
PRECISE = lax.Precision.HIGHEST
BLK = 256
PAIR = 128
GELU_SCALE = 0.7978845608028654
GELU_CUBE = 0.044715


def bucket_index(offset):
    distance = jnp.abs(offset)
    coarse = 8 + sum(((distance >= edge).astype(jnp.int32) for edge in BUCKET_EDGES))
    return jnp.where(distance < 8, distance, coarse) + 16 * (offset > 0).astype(jnp.int32)


def nt(left, right):
    return lax.dot_general(
        left, right, (((1,), (1,)), ((), ())), preferred_element_type=jnp.float32
    )


def nn(left, right):
    return jnp.dot(left, right, preferred_element_type=jnp.float32)


def tn(left, right):
    return lax.dot_general(
        left, right, (((0,), (0,)), ((), ())), preferred_element_type=jnp.float32
    )


def params(mib):
    return pltpu.CompilerParams(vmem_limit_bytes=mib * 1024 * 1024)


def cost(flops, bytes_accessed, transcendentals=0):
    return pl.CostEstimate(
        flops=flops, bytes_accessed=bytes_accessed, transcendentals=transcendentals
    )


def head_mask(values, head):
    lane = lax.broadcasted_iota(jnp.int32, values.shape, 1)
    keep = (lane < DK) if head == 0 else (lane >= DK)
    return jnp.where(keep, values, jnp.zeros_like(values))


def fill_strip(strip_ref, head, band_row, tiles):
    wide = jnp.broadcast_to(band_row, (BLK, band_row.shape[1]))
    rolled = pltpu.roll(wide, 0, 1, stride=1, stride_axis=0)
    span = (2 * tiles - 1) * BLK
    near = (tiles - 2) * BLK
    if near > 0:
        strip_ref[head, :, 0:near] = jnp.broadcast_to(band_row[:, 0:1], (BLK, near))
        strip_ref[head, :, near + 3 * BLK : span] = jnp.broadcast_to(
            band_row[:, 4 * BLK - 1 : 4 * BLK], (BLK, span - near - 3 * BLK)
        )
    strip_ref[head, :, near : near + 3 * BLK] = rolled[:, BLK:]


def forward_kernel(tiles, seg_row_ref, seg_col_ref, band_ref, q_ref, k_ref, v_ref, o_ref, lse_ref, strip_ref):
    blk = pl.program_id(0)

    @pl.when(blk == 0)
    def _():
        for head in range(2):
            fill_strip(strip_ref, head, band_ref[head : head + 1, :], tiles)

    keys = tiles * BLK
    start = pl.multiple_of((tiles - 1 - blk) * BLK, BLK)
    same = seg_col_ref[...] == seg_row_ref[...]
    total = jnp.zeros((BLK, PAIR), jnp.float32)
    rows = []
    for head in range(2):
        scores = nt(head_mask(q_ref[...], head), k_ref[...]) + strip_ref[head, :, pl.ds(start, keys)]
        scores = jnp.where(same, scores, NEGATIVE)
        top = jnp.max(scores, axis=1, keepdims=True)
        weight = jnp.exp(scores - top)
        norm = jnp.sum(weight, axis=1, keepdims=True)
        prob = (weight * (1.0 / norm)).astype(jnp.bfloat16)
        total = total + nn(prob, head_mask(v_ref[...], head))
        rows.append(jnp.transpose(jnp.broadcast_to(top + jnp.log(norm), (BLK, PAIR)))[0:1, :])
    o_ref[...] = total.astype(jnp.bfloat16)
    lse_ref[...] = jnp.concatenate(rows, axis=0)


def attention_forward(qkv, segment, band):
    seq_len = qkv.shape[0]
    tiles = seq_len // BLK
    return pl.pallas_call(
        functools.partial(forward_kernel, tiles),
        grid=(tiles,),
        in_specs=[
            pl.BlockSpec((1, seq_len), lambda b: (0, 0)),
            pl.BlockSpec((BLK, 1), lambda b: (b, 0)),
            pl.BlockSpec((2, 4 * BLK), lambda b: (0, 0)),
            pl.BlockSpec((BLK, PAIR), lambda b: (b, 0)),
            pl.BlockSpec((seq_len, PAIR), lambda b: (0, 1)),
            pl.BlockSpec((seq_len, PAIR), lambda b: (0, 2)),
        ],
        out_specs=[
            pl.BlockSpec((BLK, PAIR), lambda b: (b, 0)),
            pl.BlockSpec((2, BLK), lambda b: (0, b)),
        ],
        out_shape=[
            jax.ShapeDtypeStruct((seq_len, PAIR), jnp.bfloat16),
            jax.ShapeDtypeStruct((2, seq_len), jnp.float32),
        ],
        scratch_shapes=[pltpu.VMEM((2, BLK, (2 * tiles - 1) * BLK), jnp.float32)],
        compiler_params=params(32),
        cost_estimate=cost(
            8 * seq_len * seq_len * PAIR, 8 * seq_len * PAIR, 2 * seq_len * seq_len
        ),
        name="attention_forward",
    )(segment[None, :], segment[:, None], band, qkv, qkv, qkv)


def diagonal_sums(tile):
    wide = jnp.concatenate([tile, jnp.zeros_like(tile)], axis=1)
    width = 2 * BLK
    row = lax.broadcasted_iota(jnp.int32, wide.shape, 0)
    shift = 1
    while shift < BLK:
        wide = jnp.where((row & shift) != 0, pltpu.roll(wide, width - shift, 1), wide)
        shift *= 2
    return jnp.sum(wide, axis=0, keepdims=True)


def backward_kernel(tiles, seg_row_ref, seg_col_ref, band_ref, q_ref, k_ref, v_ref, do_ref, lse_ref,
                    dq_ref, dk_ref, dv_ref, diag_ref, strip_ref, dk_acc, dv_acc, bias_acc, p_ref, dp_ref):
    blk = pl.program_id(0)

    @pl.when(blk == 0)
    def _():
        for head in range(2):
            fill_strip(strip_ref, head, band_ref[head : head + 1, :], tiles)
        dk_acc[...] = jnp.zeros_like(dk_acc)
        dv_acc[...] = jnp.zeros_like(dv_acc)
        bias_acc[...] = jnp.zeros_like(bias_acc)

    seg_row = seg_row_ref[...]
    grad_q = jnp.zeros((BLK, PAIR), jnp.float32)
    for head in range(2):
        q_h = head_mask(q_ref[...], head)
        do_h = head_mask(do_ref[...], head)
        lse = lse_ref[head : head + 1, :]
        delta = jnp.zeros((1, BLK), jnp.float32)
        for tile in range(tiles):
            at = slice(tile * BLK, (tile + 1) * BLK)
            column = pl.multiple_of((blk - tile + tiles - 1) * BLK, BLK)
            scores = nt(k_ref[at, :], q_h) + strip_ref[head, :, pl.ds(column, BLK)]
            scores = jnp.where(seg_col_ref[at, :] == seg_row, scores, NEGATIVE)
            prob = jnp.exp(scores - lse)
            grad_p = nt(v_ref[at, :], do_h)
            delta = delta + jnp.sum(prob * grad_p, axis=0, keepdims=True)
            dv_acc[at, :] += nn(prob.astype(jnp.bfloat16), do_h)
            p_ref[at, :] = prob
            dp_ref[at, :] = grad_p
        for tile in range(tiles):
            at = slice(tile * BLK, (tile + 1) * BLK)
            grad_s = (p_ref[at, :] * (dp_ref[at, :] - delta)).astype(jnp.bfloat16)
            dk_acc[at, :] += nn(grad_s, q_h)
            grad_q = grad_q + tn(grad_s, head_mask(k_ref[at, :], head))
            away = jnp.clip(blk - tile, -2, 2) + 2
            bias_acc[head, away] += grad_s.astype(jnp.float32)
    dq_ref[...] = grad_q.astype(jnp.bfloat16)

    @pl.when(blk == tiles - 1)
    def _():
        dk_ref[...] = dk_acc[...].astype(jnp.bfloat16)
        dv_ref[...] = dv_acc[...].astype(jnp.bfloat16)
        for head in range(2):
            for away in range(5):
                diag_ref[head, away : away + 1, :] = diagonal_sums(bias_acc[head, away])


def attention_backward(qkv, grad_o, lse, segment, band_back):
    seq_len = qkv.shape[0]
    tiles = seq_len // BLK
    rows = pl.BlockSpec((BLK, PAIR), lambda b: (b, 0))
    whole = pl.BlockSpec((seq_len, PAIR), lambda b: (0, 0))
    result = jax.ShapeDtypeStruct((seq_len, PAIR), jnp.bfloat16)
    return pl.pallas_call(
        functools.partial(backward_kernel, tiles),
        grid=(tiles,),
        in_specs=[
            pl.BlockSpec((1, BLK), lambda b: (0, b)),
            pl.BlockSpec((seq_len, 1), lambda b: (0, 0)),
            pl.BlockSpec((2, 4 * BLK), lambda b: (0, 0)),
            rows,
            pl.BlockSpec((seq_len, PAIR), lambda b: (0, 1)),
            pl.BlockSpec((seq_len, PAIR), lambda b: (0, 2)),
            rows,
            pl.BlockSpec((2, BLK), lambda b: (0, b)),
        ],
        out_specs=[rows, whole, whole, pl.BlockSpec((2, 5, 2 * BLK), lambda b: (0, 0, 0))],
        out_shape=[
            result,
            result,
            result,
            jax.ShapeDtypeStruct((2, 5, 2 * BLK), jnp.float32),
        ],
        scratch_shapes=[
            pltpu.VMEM((2, BLK, (2 * tiles - 1) * BLK), jnp.float32),
            pltpu.VMEM((seq_len, PAIR), jnp.float32),
            pltpu.VMEM((seq_len, PAIR), jnp.float32),
            pltpu.VMEM((2, 5, BLK, BLK), jnp.float32),
            pltpu.VMEM((seq_len, BLK), jnp.float32),
            pltpu.VMEM((seq_len, BLK), jnp.float32),
        ],
        compiler_params=params(32),
        cost_estimate=cost(
            20 * seq_len * seq_len * PAIR, 16 * seq_len * PAIR, 2 * seq_len * seq_len
        ),
        name="attention_backward",
    )(segment[None, :], segment[:, None], band_back, qkv, qkv, qkv, grad_o, lse)


def one_hot_buckets(offset):
    return (bucket_index(offset)[..., None] == jnp.arange(BUCKETS, dtype=jnp.int32)).astype(
        jnp.float32
    )


def bias_bands(bias_rows):
    offset = jnp.arange(4 * BLK, dtype=jnp.int32) - 2 * BLK
    contract = (((1,), (1,)), ((), ()))
    ahead = lax.dot_general(bias_rows, one_hot_buckets(offset), contract, precision=PRECISE)
    behind = lax.dot_general(bias_rows, one_hot_buckets(-offset), contract, precision=PRECISE)
    return ahead, behind


def bucket_sums(diagonals):
    lane = jnp.arange(2 * BLK, dtype=jnp.int32)
    within = jnp.where(lane < BLK, lane, lane - 2 * BLK)
    away = (jnp.arange(5, dtype=jnp.int32) - 2) * BLK
    onehot = one_hot_buckets(-within[None, :] - away[:, None])
    return jnp.dot(diagonals.reshape(2, -1), onehot.reshape(-1, BUCKETS), precision=PRECISE)


CHIPS = 4
CORE, ACROSS, ALONG = 1, 2, 4
PLACES = ((6, 7), (0, 4), (5, 3), (1, 2))


def wide(values):
    return values.astype(jnp.float32)


def low(values):
    return values.astype(jnp.bfloat16)


def piece_rows(own_ref, piece, start, rows, total):
    base = (own_ref[0] ^ piece) * total + start
    return pl.ds(pl.multiple_of(base, rows), rows)


def gathered(refs):
    out = []
    for core in range(2):
        own, near_x, near_y, first, second = refs[5 * core : 5 * core + 5]
        out += [(core, 0, own), (2 + core, 0, near_x), (4 + core, 0, near_y)]
        out += [(6 + core, 0, first), (6 + core, first.shape[0], second)]
    return out


def join_slots(weight_ref, slots):
    for part in range(3):
        for index, slot in enumerate(slots):
            weight_ref[part * PAIR + index * DK : part * PAIR + (index + 1) * DK, :] = slot[
                part * DK : (part + 1) * DK, :
            ]


def norm_project_kernel(own_ref, gain_ref, slot_a, slot_b, *refs):
    hidden_ref, out_ref, weight_ref = refs[10:]
    total = refs[0].shape[0]
    for piece, start, ref in gathered(refs[:10]):
        values = wide(ref[...])
        scale = lax.rsqrt(jnp.mean(values * values, axis=-1, keepdims=True) + EPSILON)
        at = piece_rows(own_ref, piece, start, ref.shape[0], total)
        hidden_ref[at, :] = low(values * scale * gain_ref[...])
    join_slots(weight_ref, (slot_a, slot_b))
    for chunk in range(8 * total // BLK):
        at = slice(chunk * BLK, (chunk + 1) * BLK)
        out_ref[at, :] = low(nt(hidden_ref[at, :], weight_ref[...]))


VMEM = pl.BlockSpec(memory_space=pltpu.VMEM)
SMEM = pl.BlockSpec(memory_space=pltpu.SMEM)


def norm_project(own, gain, slots, pieces):
    rows, width = pieces[0].shape
    total, features = 8 * rows, 3 * PAIR
    return pl.pallas_call(
        norm_project_kernel,
        in_specs=[SMEM] + [VMEM] * 13,
        out_specs=[VMEM] * 3,
        out_shape=[
            jax.ShapeDtypeStruct((total, width), jnp.bfloat16),
            jax.ShapeDtypeStruct((total, features), jnp.bfloat16),
            jax.ShapeDtypeStruct((features, width), jnp.bfloat16),
        ],
        compiler_params=params(36),
        cost_estimate=cost(
            2 * total * width * features, 2 * (2 * total * width + features * (width + total))
        ),
        name="norm_project",
    )(own, gain[None, :], *slots, *pieces)


def project_kernel(hidden_ref, slot_a, slot_b, out_ref, weight_ref):
    @pl.when(pl.program_id(0) == 0)
    def _():
        join_slots(weight_ref, (slot_a, slot_b))

    out_ref[...] = low(nt(hidden_ref[...], weight_ref[...]))


def project(hidden, slots):
    total, width = hidden.shape
    features = 3 * PAIR
    slot = pl.BlockSpec((3 * DK, width), lambda b: (0, 0))
    return pl.pallas_call(
        project_kernel,
        grid=(total // BLK,),
        in_specs=[pl.BlockSpec((BLK, width), lambda b: (b, 0)), slot, slot],
        out_specs=[
            pl.BlockSpec((BLK, features), lambda b: (b, 0)),
            pl.BlockSpec((features, width), lambda b: (0, 0)),
        ],
        out_shape=[
            jax.ShapeDtypeStruct((total, features), jnp.bfloat16),
            jax.ShapeDtypeStruct((features, width), jnp.bfloat16),
        ],
        compiler_params=params(24),
        cost_estimate=cost(
            2 * total * width * features, 2 * (total * width + features * (width + total))
        ),
        name="project",
    )(hidden, *slots)


def spread_kernel(core, counts, own_ref, *refs):
    lefts, rights = refs[: counts[0]], refs[counts[0] : counts[0] + counts[1]]
    out, weight = refs[-2:]
    start = 0
    for right in rights:
        weight[start : start + right.shape[0], :] = right[...]
        start += right.shape[0]
    total = lefts[0].shape[0] // 8
    half = total // 2
    for chip in range(CHIPS):
        at = piece_rows(own_ref, 2 * chip + core, 0, total, total)
        values = None
        for index, left in enumerate(lefts):
            term = nn(left[at, :], weight[index * PAIR : (index + 1) * PAIR, :])
            values = term if values is None else values + term
        for index, place in enumerate(PLACES[chip]):
            out[place * half : (place + 1) * half, :] = low(
                values[index * half : (index + 1) * half, :]
            )


def spread(own, core, lefts, rights):
    total, width = lefts[0].shape[0] // 2, rights[0].shape[1]
    depth = sum(left.shape[1] for left in lefts)
    return pl.pallas_call(
        functools.partial(spread_kernel, core, (len(lefts), len(rights))),
        in_specs=[SMEM] + [VMEM] * (len(lefts) + len(rights)),
        out_specs=VMEM,
        out_shape=jax.ShapeDtypeStruct((total, width), jnp.bfloat16),
        scratch_shapes=[pltpu.VMEM((depth, width), jnp.bfloat16)],
        compiler_params=params(28),
        cost_estimate=cost(
            2 * total * width * depth, 2 * (total * width + depth * (width + total))
        ),
        name="spread",
    )(own, *lefts, *rights)


def heads_back_kernel(own_ref, weight_a0, weight_a1, weight_b0, weight_b1, mixed_a, mixed_b, *refs):
    heads_a, heads_b, grad_a, grad_b, whole, weight = refs[10:]
    total = refs[0].shape[0]
    for piece, start, ref in gathered(refs[:10]):
        whole[piece_rows(own_ref, piece, start, ref.shape[0], total), :] = ref[...]
    for index, ref in enumerate((weight_a0, weight_a1, weight_b0, weight_b1)):
        weight[index * DK : (index + 1) * DK, :] = ref[...]
    for chunk in range(8 * total // BLK):
        at = slice(chunk * BLK, (chunk + 1) * BLK)
        heads = low(nt(whole[at, :], weight[...]))
        heads_a[at, :] = heads[:, :PAIR]
        heads_b[at, :] = heads[:, PAIR:]
    grad_a[...] = low(tn(mixed_a[...], whole[...]))
    grad_b[...] = low(tn(mixed_b[...], whole[...]))


def heads_back(own, weights, mixed, pieces):
    rows, width = pieces[0].shape
    total = 8 * rows
    outs = pl.pallas_call(
        heads_back_kernel,
        in_specs=[SMEM] + [VMEM] * 16,
        out_specs=[VMEM] * 4,
        out_shape=[jax.ShapeDtypeStruct((total, PAIR), jnp.bfloat16)] * 2
        + [jax.ShapeDtypeStruct((PAIR, width), jnp.bfloat16)] * 2,
        scratch_shapes=[
            pltpu.VMEM((total, width), jnp.bfloat16),
            pltpu.VMEM((2 * PAIR, width), jnp.bfloat16),
        ],
        compiler_params=params(32),
        cost_estimate=cost(8 * total * width * PAIR, 2 * total * width),
        name="heads_back",
    )(own, *weights, *mixed, *pieces)
    return outs[:2], outs[2:]


def qkv_grad_kernel(gain_ref, hidden_ref, dq_ref, dk_ref, dv_ref, weight_ref, slot_a, slot_b, sum_ref):
    total = None
    for part, ref in enumerate((dq_ref, dk_ref, dv_ref)):
        grad = tn(ref[...], hidden_ref[...])
        slot_a[part * DK : (part + 1) * DK, :] = low(grad[:DK])
        slot_b[part * DK : (part + 1) * DK, :] = low(grad[DK:])
        at = slice(part * PAIR, (part + 1) * PAIR)
        term = jnp.sum(grad * wide(weight_ref[at, :]), axis=0, keepdims=True)
        total = term if total is None else total + term
    sum_ref[...] = total / gain_ref[...]


def qkv_grad(gain, hidden, dq, dk, dv, weight):
    total, width = hidden.shape
    cols = 512
    col = pl.BlockSpec((1, cols), lambda c: (0, c))
    back = pl.BlockSpec((total, PAIR), lambda c: (0, 0))
    slot = pl.BlockSpec((3 * DK, cols), lambda c: (0, c))
    return pl.pallas_call(
        qkv_grad_kernel,
        grid=(width // cols,),
        in_specs=[
            col,
            pl.BlockSpec((total, cols), lambda c: (0, c)),
            back,
            back,
            back,
            pl.BlockSpec((3 * PAIR, cols), lambda c: (0, c)),
        ],
        out_specs=[slot, slot, col],
        out_shape=[
            jax.ShapeDtypeStruct((3 * DK, width), jnp.bfloat16),
            jax.ShapeDtypeStruct((3 * DK, width), jnp.bfloat16),
            jax.ShapeDtypeStruct((1, width), jnp.float32),
        ],
        compiler_params=params(24),
        cost_estimate=cost(6 * total * width * PAIR, 2 * total * width + 12 * PAIR * width),
        name="qkv_grad",
    )(gain[None, :], hidden, dq, dk, dv, weight)


def assemble_kernel(own, *refs):
    outs = refs[6:]
    units = own.shape[0] // 3
    half = units // 2
    for part, weight in enumerate(outs):
        for chip in range(CHIPS):
            for index, place in enumerate(PLACES[chip]):
                ref, start = own, part * units + index * half
                if chip:
                    ref = refs[2 * chip - 2]
                    if start >= 3 * half:
                        ref, start = refs[2 * chip - 1], start - 3 * half
                weight[place * half : (place + 1) * half, :] = ref[start : start + half, :]


def assemble(own, *stacks):
    rows, width = own.shape
    return pl.pallas_call(
        assemble_kernel,
        in_specs=[VMEM] * 7,
        out_specs=[VMEM] * 3,
        out_shape=[jax.ShapeDtypeStruct((CHIPS * rows // 3, width), jnp.bfloat16)] * 3,
        compiler_params=params(28),
        cost_estimate=cost(0, 16 * rows * width),
        name="assemble",
    )(own, *stacks)


def feed_kernel(gate_w, up_w, down_w, *refs):
    hidden, cot, outs = refs[:2], refs[2:4], refs[4:]
    inner_ref, dgate_ref, dup_ref, grad_own, grad_other, out_own, out_other = outs
    rows = hidden[0].shape[0]
    values = jnp.concatenate([hidden[0][...], hidden[1][...]], axis=0)
    grads = jnp.concatenate([cot[0][...], cot[1][...]], axis=0)
    gate = nt(values, gate_w[...])
    up = nt(values, up_w[...])
    grad_m = nt(grads, down_w[...])
    square = gate * gate
    bend = jnp.tanh(GELU_SCALE * gate * (1.0 + GELU_CUBE * square))
    part = 0.5 * (1.0 + bend)
    act = gate * part
    slope = part + 0.5 * gate * (1.0 - bend * bend) * (
        GELU_SCALE * (1.0 + 3.0 * GELU_CUBE * square)
    )
    inner = low(act * up)
    inner_ref[...] = inner
    dgate = low(grad_m * up * slope)
    dup = low(grad_m * act)
    dgate_ref[...] = dgate
    dup_ref[...] = dup
    grad_h = low(nn(dgate, gate_w[...]) + nn(dup, up_w[...]))
    grad_own[...] = grad_h[:rows]
    grad_other[...] = grad_h[rows:]
    result = low(nn(inner, down_w[...]))
    out_own[...] = result[:rows]
    out_other[...] = result[rows:]


def feed(weights, hidden, cot):
    rows, width = hidden[0].shape
    total, units = 2 * rows, weights[0].shape[0]
    return pl.pallas_call(
        feed_kernel,
        in_specs=[VMEM] * 7,
        out_specs=[VMEM] * 7,
        out_shape=[jax.ShapeDtypeStruct((total, units), jnp.bfloat16)] * 3
        + [jax.ShapeDtypeStruct((rows, width), jnp.bfloat16)] * 4,
        compiler_params=params(24),
        cost_estimate=cost(12 * total * width * units, 2 * 4 * (total + units) * width),
        name="feed",
    )(*weights, *hidden, *cot)


def feed_grad_kernel(terms, *refs):
    lefts, pieces = refs[: 4 * terms], refs[4 * terms : 4 * terms + 8]
    outs, refs = refs[4 * terms + 8 : 5 * terms + 8], refs[5 * terms + 8 :]
    right = refs[0]
    rows = pieces[0].shape[0]
    for index, piece in enumerate(pieces):
        right[index * rows : (index + 1) * rows, :] = piece[...]
    for term in range(terms):
        left = jnp.concatenate([ref[...] for ref in lefts[4 * term : 4 * term + 4]], axis=0)
        outs[term][...] = low(tn(left, right[...]))


def feed_grad(lefts, pieces):
    terms = len(lefts)
    rows, width = pieces[0].shape
    units = lefts[0][0].shape[1]
    return pl.pallas_call(
        functools.partial(feed_grad_kernel, terms),
        in_specs=[VMEM] * (4 * terms + 8),
        out_specs=[VMEM] * terms,
        out_shape=[jax.ShapeDtypeStruct((units, width), jnp.bfloat16)] * terms,
        scratch_shapes=[pltpu.VMEM((8 * rows, width), jnp.bfloat16)],
        compiler_params=params(40),
        cost_estimate=cost(16 * terms * rows * width * units, 24 * rows * width),
        name="feed_grad",
    )(*[value for left in lefts for value in left], *pieces)


def fence(*values):
    return lax.optimization_barrier(values)


def swap(values, bits):
    return lax.ppermute(values, "seq", [(i, i ^ bits) for i in range(2 * CHIPS)])


def ring(values, step):
    n = lax.axis_size("fsdp")
    return lax.ppermute(values, "fsdp", [(i, (i + step) % n) for i in range(n)])


def line_order(slots):
    n = len(slots)
    order = (lax.axis_index("fsdp") - jnp.arange(n, dtype=jnp.int32)) % n
    return jnp.stack(slots)[order]


def both(values, other, bits):
    high = (lax.axis_index("seq") & bits) != 0
    return jnp.concatenate(
        [jnp.where(high, other, values), jnp.where(high, values, other)], axis=0
    )


def halves(values, bits):
    high = (lax.axis_index("seq") & bits) != 0
    size = values.shape[0] // 2
    lower, upper = values[:size], values[size:]
    return jnp.where(high, upper, lower), jnp.where(high, lower, upper)


def plane_sends(own, other=None):
    size = own.shape[0] // 4
    total = own if other is None else wide(own) + wide(other)
    return low(total[:size]), low(total[size : 2 * size]), total[2 * size :]


def plane_second(keep, from_x, from_y):
    size = keep.shape[0] // 4
    to_x = low(wide(keep[:size]) + wide(from_y[:size]))
    to_y = low(wide(keep[size : 2 * size]) + wide(from_x[size:]))
    return to_x, to_y


def plane_total(keep, from_x, from_y, second_x, second_y):
    size = keep.shape[0] // 4
    first = wide(keep[2 * size : 3 * size]) + wide(from_x[:size]) + wide(second_y)
    second = wide(keep[3 * size :]) + wide(from_y[size:]) + wide(second_x)
    return jnp.concatenate([first, second], axis=0)


def add(*values):
    return functools.reduce(lambda left, right: left + right, [wide(value) for value in values])


def per_device(
    tokens,
    starts,
    first_gain,
    query_weight,
    key_weight,
    value_weight,
    output_weight,
    bias_table,
    second_gain,
    gate_weight,
    up_weight,
    down_weight,
    cotangent,
):
    index = lax.axis_index("seq")[None]
    own = tokens[0]
    half = own.shape[0] // 2
    grad_out = cotangent[0]
    rows = first_gain.shape[0]
    buckets = bias_table.shape[0]
    qkv0 = low(jnp.concatenate([query_weight, key_weight, value_weight], axis=0))
    small = low(jnp.concatenate([first_gain, second_gain, bias_table]))
    own, qkv0, small, output_weight, gate_weight, up_weight, down_weight = fence(
        own, qkv0, small, output_weight, gate_weight, up_weight, down_weight
    )

    tok_x, tok_y, tok_c = swap(own, ACROSS), swap(own, ALONG), swap(own, CORE)
    qkv1 = ring(qkv0, 1)
    small_slots = [small] + [ring(small, k) for k in range(1, 4)]
    tok_x, tok_y, small_slots, output_weight, gate_weight, up_weight, down_weight = fence(
        tok_x, tok_y, small_slots, output_weight, gate_weight, up_weight, down_weight
    )

    gain_part = line_order([value[: 2 * rows] for value in small_slots]).reshape(-1)
    packed = jnp.concatenate([gain_part, low(starts[0])])[None]
    tok_d1, tok_d2 = swap(tok_y[:half], ACROSS), swap(tok_x[half:], ALONG)
    tok_cx, tok_cy = swap(tok_x, CORE), swap(tok_y, CORE)
    blocks = [packed] + [swap(packed, bits) for bits in range(1, 2 * CHIPS)]
    for bits in (CORE, ACROSS, ALONG):
        blocks = [both(blocks[i], blocks[i + 1], bits) for i in range(0, len(blocks), 2)]
    packed = blocks[0]
    feed0 = low(jnp.concatenate([gate_weight, up_weight, down_weight], axis=0))
    out0 = low(output_weight)
    packed, tok_d1, tok_d2, qkv1, feed0, out0 = fence(
        packed, tok_d1, tok_d2, qkv1, feed0, out0
    )

    tok_c1, tok_c2 = swap(tok_d1, CORE), swap(tok_d2, CORE)
    qkv2 = ring(qkv1, 1)
    gain_count = gain_part.shape[0]
    gains = wide(packed[:, :gain_count]).reshape(-1, 4, 2, rows)
    gain_first = gains[:, :, 0].reshape(-1)
    gain_second = gains[:, :, 1].reshape(-1)
    segment = jnp.cumsum(packed[:, gain_count:].reshape(-1).astype(jnp.int32), dtype=jnp.int32)
    tables = [wide(value[2 * rows :]) for value in small_slots]
    bands = [bias_bands(jnp.stack(tables[2 * p : 2 * p + 2])) for p in range(2)]
    segment, gain_first, gain_second, bands, tok_c1, tok_c2, feed0 = fence(
        segment, gain_first, gain_second, bands, tok_c1, tok_c2, feed0
    )

    feed_half = feed0.shape[0] // 2
    feed_top, feed_low = feed0[:feed_half], feed0[feed_half:]
    feed_xl, feed_yt = swap(feed_low, ACROSS), swap(feed_top, ALONG)
    tok_pieces = (own, tok_x, tok_y, tok_d1, tok_d2, tok_c, tok_cx, tok_cy, tok_c1, tok_c2)
    hidden_one, qkv_a, weight_a = norm_project(index, gain_first, (qkv0, qkv1), tok_pieces)
    hidden_one, qkv_a, weight_a, qkv2, out0, feed_top, feed_low = fence(
        hidden_one, qkv_a, weight_a, qkv2, out0, feed_top, feed_low
    )

    qkv3 = ring(qkv2, 1)
    out1 = ring(out0, 1)
    mixed_a, lse_a = attention_forward(qkv_a, segment, bands[0][0])
    mixed_a, lse_a, hidden_one, feed_xl, feed_yt = fence(
        mixed_a, lse_a, hidden_one, feed_xl, feed_yt
    )
    feed_dt, feed_dl = swap(feed_yt, ACROSS), swap(feed_xl, ALONG)
    hidden_one, qkv3, out1 = fence(hidden_one, qkv3, out1)

    out2 = ring(out1, 1)
    qkv_b, weight_b = project(hidden_one, (qkv2, qkv3))
    qkv_b, out2, grad_out, feed_dt, feed_dl, feed_top, feed_low = fence(
        qkv_b, out2, grad_out, feed_dt, feed_dl, feed_top, feed_low
    )

    out3 = ring(out2, 1)
    cot1 = ring(grad_out, 1)
    cot_c0 = swap(grad_out, CORE)
    feed_xt, feed_yl = swap(feed_top, ACROSS), swap(feed_low, ALONG)
    mixed_b, lse_b = attention_forward(qkv_b, segment, bands[1][0])
    mixed_b, lse_b, out3 = fence(mixed_b, lse_b, out3)
    out_slots = (out0, out1, out2, out3)
    part_other = spread(index, 1, (mixed_a, mixed_b), out_slots)
    part_other, mixed_b = fence(part_other, mixed_b)
    part_other = swap(part_other, CORE)
    mixed = (mixed_a, mixed_b)
    part_own = spread(index, 0, mixed, out_slots)
    part_own, part_other, feed_xt, feed_yl, cot1, cot_c0 = fence(
        part_own, part_other, feed_xt, feed_yl, cot1, cot_c0
    )

    send_x, send_y, keep = plane_sends(part_own, part_other)
    from_x, from_y = swap(send_x, ACROSS), swap(send_y, ALONG)
    cot2, cot_c1 = ring(cot1, 1), swap(cot1, CORE)
    weights = assemble(feed0, feed_xt, feed_xl, feed_yt, feed_yl, feed_dt, feed_dl)
    from_x, from_y, weights, cot2, cot_c1 = fence(from_x, from_y, weights, cot2, cot_c1)
    cot3, cot_c2 = ring(cot2, 1), swap(cot2, CORE)
    send_x, send_y = plane_second(keep, from_x, from_y)
    second_x, second_y = swap(send_x, ACROSS), swap(send_y, ALONG)
    inputs = wide(own)
    resid_one = inputs + plane_total(keep, from_x, from_y, second_x, second_y)

    scale_two = lax.rsqrt(jnp.mean(resid_one * resid_one, axis=-1, keepdims=True) + EPSILON)
    normed_two = resid_one * scale_two
    hid0 = low(normed_two * gain_second)
    hid0, cot_c2, resid_one, scale_two = fence(hid0, cot_c2, resid_one, scale_two)

    hid1, hid_c0 = ring(hid0, 1), swap(hid0, CORE)
    hid_c0, cot3 = fence(hid_c0, cot3)
    cot_c3 = swap(cot3, CORE)
    feed_a = feed(weights, (hid0, hid_c0), (grad_out, cot_c0))
    feed_a, hid1, cot_c3 = fence(feed_a, hid1, cot_c3)
    hid2, hid_c1 = ring(hid1, 1), swap(hid1, CORE)
    hid_c1, feed_a = fence(hid_c1, feed_a)
    grad_c0, out_c0 = swap(feed_a[4], CORE), swap(feed_a[6], CORE)
    feed_b = feed(weights, (hid1, hid_c1), (cot1, cot_c1))
    feed_b, hid2, grad_c0, out_c0 = fence(feed_b, hid2, grad_c0, out_c0)
    hid3, hid_c2 = ring(hid2, 1), swap(hid2, CORE)
    hid_c2, feed_b = fence(hid_c2, feed_b)
    grad_c1, out_c1 = swap(feed_b[4], CORE), swap(feed_b[6], CORE)
    feed_c = feed(weights, (hid2, hid_c2), (cot2, cot_c2))
    feed_c, hid3, grad_c1, out_c1 = fence(feed_c, hid3, grad_c1, out_c1)
    hid_c3 = swap(hid3, CORE)
    dh = ring(low(add(feed_b[3], grad_c1)), 1)
    hid_c3, feed_c = fence(hid_c3, feed_c)
    grad_c2, out_c2 = swap(feed_c[4], CORE), swap(feed_c[6], CORE)
    feed_d = feed(weights, (hid3, hid_c3), (cot3, cot_c3))
    feed_d, dh, grad_c2, out_c2 = fence(feed_d, dh, grad_c2, out_c2)
    dh = ring(low(add(feed_c[3], grad_c2, dh)), 1)
    grad_c3, out_c3 = swap(feed_d[4], CORE), swap(feed_d[6], CORE)
    parts = (feed_a, feed_b, feed_c, feed_d)
    hid_pieces = (hid0, hid_c0, hid1, hid_c1, hid2, hid_c2, hid3, hid_c3)
    cot_pieces = (grad_out, cot_c0, cot1, cot_c1, cot2, cot_c2, cot3, cot_c3)
    (grad_down,) = feed_grad([[part[0] for part in parts]], cot_pieces)
    grad_down, dh, grad_c3, out_c3, hid_pieces = fence(grad_down, dh, grad_c3, out_c3, hid_pieces)

    dh = ring(low(add(feed_d[3], grad_c3, dh)), 1)
    down_x, down_y, down_keep = plane_sends(grad_down)
    down_fx, down_fy = swap(down_x, ACROSS), swap(down_y, ALONG)
    grad_gate_all, grad_up_all = feed_grad(
        [[part[1] for part in parts], [part[2] for part in parts]], hid_pieces
    )
    dh, grad_gate_all, grad_up_all = fence(dh, grad_gate_all, grad_up_all)

    grad_hidden_two = add(feed_a[3], grad_c0, dh)
    normed_two = resid_one * scale_two
    shared = grad_hidden_two * gain_second
    grad_resid = wide(grad_out) + scale_two * (
        shared - normed_two * jnp.mean(shared * normed_two, axis=-1, keepdims=True)
    )
    branch = low(grad_resid)
    gain_two_rows = jnp.sum(grad_hidden_two * normed_two, axis=0)
    branch, grad_resid, gain_two_rows, down_fx, down_fy, feed_b = fence(
        branch, grad_resid, gain_two_rows, down_fx, down_fy, feed_b
    )

    br_x, br_y, br_c = swap(branch, ACROSS), swap(branch, ALONG), swap(branch, CORE)
    out_sum = ring(low(add(feed_b[5], out_c1)), 1)
    down_x, down_y = plane_second(down_keep, down_fx, down_fy)
    br_x, br_y, br_c, down_x, down_y, out_sum = fence(br_x, br_y, br_c, down_x, down_y, out_sum)
    br_d1, br_d2 = swap(br_y[:half], ACROSS), swap(br_x[half:], ALONG)
    br_cx, br_cy = swap(br_x, CORE), swap(br_y, CORE)
    out_send = low(add(feed_c[5], out_c2, out_sum))
    br_d1, br_d2, br_cx, br_cy, out_send = fence(br_d1, br_d2, br_cx, br_cy, out_send)
    br_c1, br_c2 = swap(br_d1, CORE), swap(br_d2, CORE)
    out_sum = ring(out_send, 1)
    gate_x, gate_y, gate_keep = plane_sends(grad_gate_all)
    br_c1, br_c2, gate_x, gate_y = fence(br_c1, br_c2, gate_x, gate_y)

    down_sx, down_sy = swap(down_x, ACROSS), swap(down_y, ALONG)
    pieces = (branch, br_x, br_y, br_d1, br_d2, br_c, br_cx, br_cy, br_c1, br_c2)
    grad_heads, grad_outs = heads_back(index, out_slots, mixed, pieces)
    grad_heads, grad_outs, out_sum, down_sx, down_sy, gate_x, gate_y = fence(
        grad_heads, grad_outs, out_sum, down_sx, down_sy, gate_x, gate_y
    )

    go0, go1 = grad_outs[0][:DK], grad_outs[0][DK:]
    go2, go3 = grad_outs[1][:DK], grad_outs[1][DK:]
    out_sum = ring(low(add(feed_d[5], out_c3, out_sum)), 1)
    go_sum = ring(go3, -1)
    gate_fx, gate_fy = swap(gate_x, ACROSS), swap(gate_y, ALONG)
    dq_b, dk_b, dv_b, diag_b = attention_backward(
        qkv_b, grad_heads[1], lse_b, segment, bands[1][1]
    )
    dq_b, dk_b, dv_b, diag_b, go_sum, gate_fx, gate_fy, out_sum, grad_up_all = fence(
        dq_b, dk_b, dv_b, diag_b, go_sum, gate_fx, gate_fy, out_sum, grad_up_all
    )

    go_sum = ring(low(add(go2, go_sum)), -1)
    gate_x, gate_y = plane_second(gate_keep, gate_fx, gate_fy)
    gate_sx, gate_sy = swap(gate_x, ACROSS), swap(gate_y, ALONG)
    up_x, up_y, up_keep = plane_sends(grad_up_all)
    gq2, gq3, sums_b = qkv_grad(gain_first, hidden_one, dq_b, dk_b, dv_b, weight_b)
    gq2, gq3, sums_b, qkv_a, go_sum, up_x, up_y = fence(
        gq2, gq3, sums_b, qkv_a, go_sum, up_x, up_y
    )

    gq = ring(gq3, -1)
    go_sum = ring(low(add(go1, go_sum)), -1)
    up_fx, up_fy = swap(up_x, ACROSS), swap(up_y, ALONG)
    dq_a, dk_a, dv_a, diag_a = attention_backward(
        qkv_a, grad_heads[0], lse_a, segment, bands[0][1]
    )
    dq_a, dk_a, dv_a, diag_a, gq, go_sum, gate_sx, gate_sy, up_fx, up_fy = fence(
        dq_a, dk_a, dv_a, diag_a, gq, go_sum, gate_sx, gate_sy, up_fx, up_fy
    )

    gq = ring(low(add(gq2, gq)), -1)
    up_x, up_y = plane_second(up_keep, up_fx, up_fy)
    up_sx, up_sy = swap(up_x, ACROSS), swap(up_y, ALONG)
    gq0, gq1, sums_a = qkv_grad(gain_first, hidden_one, dq_a, dk_a, dv_a, weight_a)
    gq0, gq1, sums_a, dq_a = fence(gq0, gq1, sums_a, dq_a)
    gain_rows = jnp.stack([(sums_a + sums_b)[0], gain_two_rows]).reshape(2, 2 * CHIPS, 4, -1)
    gain_rows = jnp.moveaxis(gain_rows, 0, 2).reshape(2 * CHIPS, -1)
    gain_keep, gain_send = halves(gain_rows, ALONG)
    gain_rows = gain_keep + swap(gain_send, ALONG)
    lefts = (dq_a, dk_a, dv_a, dq_b, dk_b, dv_b)
    back_other = spread(index, 1, lefts, (weight_a, weight_b))
    back_other, gain_rows, dq_b = fence(back_other, gain_rows, dq_b)
    back_other = swap(back_other, CORE)
    gain_keep, gain_send = halves(gain_rows, ACROSS)
    gain_rows = gain_keep + swap(gain_send, ACROSS)
    lefts = (dq_a, dk_a, dv_a, dq_b, dk_b, dv_b)
    back_own = spread(index, 0, lefts, (weight_a, weight_b))
    back_own, back_other, gain_rows = fence(back_own, back_other, gain_rows)
    send_x, send_y, keep = plane_sends(back_own, back_other)
    late = (feed_a, out_c0, out_sum, go0, down_keep, gate_keep, up_keep, resid_one)
    send_x, send_y, keep, gain_rows, gq, up_sx, up_sy, late = fence(
        send_x, send_y, keep, gain_rows, gq, up_sx, up_sy, late
    )

    from_x, from_y = swap(send_x, ACROSS), swap(send_y, ALONG)
    gq = low(add(gq1, gq))
    gq_first = ring(gq[: 2 * DK], -1)
    gain_keep, gain_send = halves(gain_rows, CORE)
    gain_rows = gain_keep + swap(gain_send, CORE)
    feed_a, out_c0, out_sum, go0, down_keep, gate_keep, up_keep, resid_one = late
    layer_out = low(resid_one + add(feed_a[5], out_c0, out_sum))
    grad_output_w = add(go0, go_sum)
    grad_down_w = plane_total(down_keep, down_fx, down_fy, down_sx, down_sy)
    grad_gate_w = plane_total(gate_keep, gate_fx, gate_fy, gate_sx, gate_sy)
    grad_up_w = plane_total(up_keep, up_fx, up_fy, up_sx, up_sy)
    tables_a, tables_b = bucket_sums(diag_a), bucket_sums(diag_b)
    table_slots = (tables_a[0], tables_a[1], tables_b[0], tables_b[1])
    gain_slots = line_order(list(gain_rows.reshape(4, -1)))
    sums = [jnp.concatenate([gain_slots[k], table_slots[k]]) for k in range(4)]
    done = (layer_out, grad_output_w, grad_down_w, grad_gate_w, grad_up_w)
    from_x, from_y, gq_first, sums, done = fence(from_x, from_y, gq_first, sums, done)
    layer_out, grad_output_w, grad_down_w, grad_gate_w, grad_up_w = done
    send_x, send_y = plane_second(keep, from_x, from_y)
    second_x, second_y = swap(send_x, ACROSS), swap(send_y, ALONG)
    gq_last = ring(gq[2 * DK :], -1)
    sums = sums[0] + sum(ring(sums[k], -k) for k in range(1, 4))
    grad_hidden_one = plane_total(keep, from_x, from_y, second_x, second_y)
    scale_one = lax.rsqrt(jnp.mean(inputs * inputs, axis=-1, keepdims=True) + EPSILON)
    normed_one = inputs * scale_one
    shared = grad_hidden_one * gain_first
    grad_tokens = low(
        grad_resid
        + scale_one * (shared - normed_one * jnp.mean(shared * normed_one, axis=-1, keepdims=True))
    )
    grad_qkv = [
        add(gq0[:DK], gq_first[:DK]),
        add(gq0[DK : 2 * DK], gq_first[DK:]),
        add(gq0[2 * DK :], gq_last),
    ]
    return (
        layer_out[None],
        grad_tokens[None],
        sums[:rows],
        *grad_qkv,
        grad_output_w,
        sums[2 * rows :],
        sums[rows : 2 * rows],
        grad_gate_w,
        grad_up_w,
        grad_down_w,
    )


def rms_norm(values, gain):
    return values * lax.rsqrt(jnp.mean(values * values, axis=-1, keepdims=True) + EPSILON) * gain


def gated_gelu(gate, up_part):
    return jax.nn.gelu(gate, approximate=True) * up_part


def gather_rows(values):
    return lax.all_gather(values, "seq", axis=0, tiled=True)


def scatter_rows(values):
    return lax.psum_scatter(
        values.astype(jnp.bfloat16), "seq", scatter_dimension=0, tiled=True
    ).astype(jnp.float32)


def per_device_general(
    tokens,
    starts,
    first_gain,
    query_weight,
    key_weight,
    value_weight,
    output_weight,
    bias_table,
    second_gain,
    gate_weight,
    up_weight,
    down_weight,
    cotangent,
):
    segment = jnp.cumsum(lax.all_gather(starts, "seq", axis=1, tiled=True)[0], dtype=jnp.int32)
    inputs = tokens[0].astype(jnp.float32)
    grad_out = cotangent[0]
    head_count = H // lax.axis_size("seq")
    head_first = lax.axis_index("seq") * head_count
    query_low = query_weight.astype(jnp.bfloat16)
    key_low = key_weight.astype(jnp.bfloat16)
    value_low = value_weight.astype(jnp.bfloat16)
    output_low = output_weight.astype(jnp.bfloat16)
    gate_low = gate_weight.astype(jnp.bfloat16)
    up_low = up_weight.astype(jnp.bfloat16)
    down_low = down_weight.astype(jnp.bfloat16)
    first_low = first_gain.astype(jnp.bfloat16)
    second_low = second_gain.astype(jnp.bfloat16)
    table_low = bias_table.astype(jnp.bfloat16)
    query_part, key_part, value_part, output_part, gate_part, up_rows, down_part = (
        lax.all_gather(query_low, "fsdp", axis=0, tiled=True),
        lax.all_gather(key_low, "fsdp", axis=0, tiled=True),
        lax.all_gather(value_low, "fsdp", axis=0, tiled=True),
        lax.all_gather(output_low, "fsdp", axis=0, tiled=True),
        lax.all_gather(gate_low, "fsdp", axis=0, tiled=True),
        lax.all_gather(up_low, "fsdp", axis=0, tiled=True),
        lax.all_gather(down_low, "fsdp", axis=0, tiled=True),
    )
    gain_one, gain_two, table_full = (
        lax.all_gather(first_low, ("seq", "fsdp"), axis=0, tiled=True),
        lax.all_gather(second_low, ("seq", "fsdp"), axis=0, tiled=True),
        lax.all_gather(table_low, ("seq", "fsdp"), axis=0, tiled=True),
    )
    gain_first = gain_one.astype(jnp.float32)
    gain_second = gain_two.astype(jnp.float32)
    bias_rows = lax.dynamic_slice_in_dim(
        table_full.astype(jnp.float32).reshape(H, BUCKETS), head_first, head_count, 0
    )
    hidden_one = rms_norm(inputs, gain_first).astype(jnp.bfloat16)
    hidden_all = gather_rows(hidden_one)
    query_head = (
        low(nt(hidden_all, query_part))
    )
    key_head = (
        low(nt(hidden_all, key_part))
    )
    value_head = (
        low(nt(hidden_all, value_part))
    )
    pairs = head_count // 2
    pair = [slice(index * PAIR, (index + 1) * PAIR) for index in range(pairs)]
    bands = [bias_bands(bias_rows[2 * index : 2 * index + 2]) for index in range(pairs)]
    qkv = [
        jnp.concatenate([query_head[:, at], key_head[:, at], value_head[:, at]], axis=1)
        for at in pair
    ]
    forward = [attention_forward(qkv[i], segment, bands[i][0]) for i in range(pairs)]
    mixed = jnp.concatenate([out for out, _ in forward], axis=1)
    resid_one = inputs + scatter_rows(nn(mixed, output_part))
    hidden_two = rms_norm(resid_one, gain_second).astype(jnp.bfloat16)
    hidden_two_all = gather_rows(hidden_two)
    gate = nt(hidden_two_all, gate_part)
    up_part = nt(hidden_two_all, up_rows)
    inner = gated_gelu(gate, up_part).astype(jnp.bfloat16)
    layer_out = (resid_one + scatter_rows(nn(inner, down_part))).astype(jnp.bfloat16)
    grad_out_all = gather_rows(grad_out)
    grad_inner = nt(grad_out_all, down_part)
    grad_down = tn(inner, grad_out_all)
    grad_gate, grad_up = jax.vjp(gated_gelu, gate, up_part)[1](grad_inner)
    grad_gate = grad_gate.astype(jnp.bfloat16)
    grad_up = grad_up.astype(jnp.bfloat16)
    grad_gate_w = tn(grad_gate, hidden_two_all)
    grad_up_w = tn(grad_up, hidden_two_all)
    grad_hidden_two = scatter_rows(nn(grad_gate, gate_part) + nn(grad_up, up_rows))
    grad_norm_two, grad_gain_two = jax.vjp(rms_norm, resid_one, gain_second)[1](grad_hidden_two)
    grad_resid = grad_out.astype(jnp.float32) + grad_norm_two
    grad_branch = grad_resid.astype(jnp.bfloat16)
    branch_all = gather_rows(grad_branch)
    grad_output_w = tn(mixed, branch_all)
    grad_heads = (
        low(nt(branch_all, output_part))
    )
    back = [
        attention_backward(qkv[i], grad_heads[:, pair[i]], forward[i][1], segment, bands[i][1])
        for i in range(pairs)
    ]
    grad_query_seq, grad_key_seq, grad_value_seq = (
        jnp.concatenate([values[part] for values in back], axis=1) for part in range(3)
    )
    grad_bias = jnp.concatenate([bucket_sums(values[3]) for values in back], axis=0)
    grad_query_w = tn(grad_query_seq, hidden_all)
    grad_key_w = tn(grad_key_seq, hidden_all)
    grad_value_w = tn(grad_value_seq, hidden_all)
    grad_hidden_one = scatter_rows(
        nn(grad_query_seq, query_part)
        + nn(grad_key_seq, key_part)
        + nn(grad_value_seq, value_part)
    )
    grad_norm_one, grad_gain_one = jax.vjp(rms_norm, inputs, gain_first)[1](grad_hidden_one)
    grad_tokens = (grad_resid + grad_norm_one).astype(jnp.bfloat16)
    grad_table = lax.dynamic_update_slice_in_dim(
        jnp.zeros((H, BUCKETS), jnp.float32), grad_bias, head_first, 0
    ).reshape(-1)
    weight_grads = (
        lax.psum_scatter(
            grad_query_w.astype(jnp.bfloat16), "fsdp", scatter_dimension=0, tiled=True
        ).astype(jnp.float32),
        lax.psum_scatter(
            grad_key_w.astype(jnp.bfloat16), "fsdp", scatter_dimension=0, tiled=True
        ).astype(jnp.float32),
        lax.psum_scatter(
            grad_value_w.astype(jnp.bfloat16), "fsdp", scatter_dimension=0, tiled=True
        ).astype(jnp.float32),
        lax.psum_scatter(
            grad_output_w.astype(jnp.bfloat16), "fsdp", scatter_dimension=0, tiled=True
        ).astype(jnp.float32),
        lax.psum_scatter(
            grad_gate_w.astype(jnp.bfloat16), "fsdp", scatter_dimension=0, tiled=True
        ).astype(jnp.float32),
        lax.psum_scatter(
            grad_up_w.astype(jnp.bfloat16), "fsdp", scatter_dimension=0, tiled=True
        ).astype(jnp.float32),
        lax.psum_scatter(
            grad_down.astype(jnp.bfloat16), "fsdp", scatter_dimension=0, tiled=True
        ).astype(jnp.float32),
    )
    small_grads = (
        lax.psum_scatter(grad_gain_one, ("seq", "fsdp"), scatter_dimension=0, tiled=True),
        lax.psum_scatter(grad_gain_two, ("seq", "fsdp"), scatter_dimension=0, tiled=True),
        lax.psum_scatter(grad_table, ("seq", "fsdp"), scatter_dimension=0, tiled=True),
    )
    return (
        layer_out[None],
        grad_tokens[None],
        small_grads[0],
        weight_grads[0],
        weight_grads[1],
        weight_grads[2],
        weight_grads[3],
        small_grads[2],
        small_grads[1],
        weight_grads[4],
        weight_grads[5],
        weight_grads[6],
    )


def solution(mesh):
    rows = P(("seq", "fsdp"), None)
    row = P(("seq", "fsdp"))
    activations = P("fsdp", "seq", None)
    in_specs = (
        activations,
        P("fsdp", "seq"),
        row,
        rows,
        rows,
        rows,
        rows,
        row,
        row,
        rows,
        rows,
        rows,
        activations,
    )
    out_specs = (
        activations,
        activations,
        row,
        rows,
        rows,
        rows,
        rows,
        row,
        row,
        rows,
        rows,
        rows,
    )
    seq, fsdp = mesh.shape["seq"], mesh.shape["fsdp"]
    plan = per_device if seq == 2 * CHIPS and H == seq * fsdp else per_device_general
    return jax.shard_map(
        plan,
        mesh=mesh,
        in_specs=in_specs,
        out_specs=out_specs,
        check_vma=False,
    )
```

```python
import functools

import jax
import jax.numpy as jnp
from jax import lax
from jax.experimental import pallas as pl
from jax.experimental.pallas import tpu as pltpu
from jax.sharding import PartitionSpec as P

H = 32
DK = 64
BUCKETS = 32


EPSILON = 1e-06
NEGATIVE = -1000000000.0
BUCKET_EDGES = (12, 16, 23, 32, 46, 64, 91)
PRECISE = lax.Precision.HIGHEST
BLK = 256
PAIR = 128
GELU_SCALE = 0.7978845608028654
GELU_CUBE = 0.044715


def bucket_index(offset):
    distance = jnp.abs(offset)
    coarse = 8 + sum(((distance >= edge).astype(jnp.int32) for edge in BUCKET_EDGES))
    return jnp.where(distance < 8, distance, coarse) + 16 * (offset > 0).astype(jnp.int32)


def nt(left, right):
    return lax.dot_general(
        left, right, (((1,), (1,)), ((), ())), preferred_element_type=jnp.float32
    )


def nn(left, right):
    return jnp.dot(left, right, preferred_element_type=jnp.float32)


def tn(left, right):
    return lax.dot_general(
        left, right, (((0,), (0,)), ((), ())), preferred_element_type=jnp.float32
    )


def params(mib):
    return pltpu.CompilerParams(vmem_limit_bytes=mib * 1024 * 1024)


def cost(flops, bytes_accessed, transcendentals=0):
    return pl.CostEstimate(
        flops=flops, bytes_accessed=bytes_accessed, transcendentals=transcendentals
    )


def head_mask(values, head):
    lane = lax.broadcasted_iota(jnp.int32, values.shape, 1)
    keep = (lane < DK) if head == 0 else (lane >= DK)
    return jnp.where(keep, values, jnp.zeros_like(values))


def fill_strip(strip_ref, head, band_row, tiles):
    wide = jnp.broadcast_to(band_row, (BLK, band_row.shape[1]))
    rolled = pltpu.roll(wide, 0, 1, stride=1, stride_axis=0)
    span = (2 * tiles - 1) * BLK
    near = (tiles - 2) * BLK
    if near > 0:
        strip_ref[head, :, 0:near] = jnp.broadcast_to(band_row[:, 0:1], (BLK, near))
        strip_ref[head, :, near + 3 * BLK : span] = jnp.broadcast_to(
            band_row[:, 4 * BLK - 1 : 4 * BLK], (BLK, span - near - 3 * BLK)
        )
    strip_ref[head, :, near : near + 3 * BLK] = rolled[:, BLK:]


def forward_kernel(tiles, seg_row_ref, seg_col_ref, band_ref, q_ref, k_ref, v_ref, o_ref, lse_ref, strip_ref):
    blk = pl.program_id(0)

    @pl.when(blk == 0)
    def _():
        for head in range(2):
            fill_strip(strip_ref, head, band_ref[head : head + 1, :], tiles)

    keys = tiles * BLK
    start = pl.multiple_of((tiles - 1 - blk) * BLK, BLK)
    same = seg_col_ref[...] == seg_row_ref[...]
    total = jnp.zeros((BLK, PAIR), jnp.float32)
    rows = []
    for head in range(2):
        scores = nt(head_mask(q_ref[...], head), k_ref[...]) + strip_ref[head, :, pl.ds(start, keys)]
        scores = jnp.where(same, scores, NEGATIVE)
        top = jnp.max(scores, axis=1, keepdims=True)
        weight = jnp.exp(scores - top)
        norm = jnp.sum(weight, axis=1, keepdims=True)
        prob = (weight * (1.0 / norm)).astype(jnp.bfloat16)
        total = total + nn(prob, head_mask(v_ref[...], head))
        rows.append(jnp.transpose(jnp.broadcast_to(top + jnp.log(norm), (BLK, PAIR)))[0:1, :])
    o_ref[...] = total.astype(jnp.bfloat16)
    lse_ref[...] = jnp.concatenate(rows, axis=0)


def attention_forward(qkv, segment, band):
    seq_len = qkv.shape[0]
    tiles = seq_len // BLK
    return pl.pallas_call(
        functools.partial(forward_kernel, tiles),
        grid=(tiles,),
        in_specs=[
            pl.BlockSpec((1, seq_len), lambda b: (0, 0)),
            pl.BlockSpec((BLK, 1), lambda b: (b, 0)),
            pl.BlockSpec((2, 4 * BLK), lambda b: (0, 0)),
            pl.BlockSpec((BLK, PAIR), lambda b: (b, 0)),
            pl.BlockSpec((seq_len, PAIR), lambda b: (0, 1)),
            pl.BlockSpec((seq_len, PAIR), lambda b: (0, 2)),
        ],
        out_specs=[
            pl.BlockSpec((BLK, PAIR), lambda b: (b, 0)),
            pl.BlockSpec((2, BLK), lambda b: (0, b)),
        ],
        out_shape=[
            jax.ShapeDtypeStruct((seq_len, PAIR), jnp.bfloat16),
            jax.ShapeDtypeStruct((2, seq_len), jnp.float32),
        ],
        scratch_shapes=[pltpu.VMEM((2, BLK, (2 * tiles - 1) * BLK), jnp.float32)],
        compiler_params=params(20),
        cost_estimate=cost(
            8 * seq_len * seq_len * PAIR, 8 * seq_len * PAIR, 2 * seq_len * seq_len
        ),
        name="attention_forward",
    )(segment[None, :], segment[:, None], band, qkv, qkv, qkv)


def diagonal_sums(tile):
    wide = jnp.concatenate([tile, jnp.zeros_like(tile)], axis=1)
    width = 2 * BLK
    row = lax.broadcasted_iota(jnp.int32, wide.shape, 0)
    shift = 1
    while shift < BLK:
        wide = jnp.where((row & shift) != 0, pltpu.roll(wide, width - shift, 1), wide)
        shift *= 2
    return jnp.sum(wide, axis=0, keepdims=True)


def backward_kernel(tiles, seg_row_ref, seg_col_ref, band_ref, q_ref, k_ref, v_ref, do_ref, lse_ref,
                    dq_ref, dk_ref, dv_ref, diag_ref, strip_ref, dk_acc, dv_acc, bias_acc, p_ref, dp_ref):
    blk = pl.program_id(0)

    @pl.when(blk == 0)
    def _():
        for head in range(2):
            fill_strip(strip_ref, head, band_ref[head : head + 1, :], tiles)
        dk_acc[...] = jnp.zeros_like(dk_acc)
        dv_acc[...] = jnp.zeros_like(dv_acc)
        bias_acc[...] = jnp.zeros_like(bias_acc)

    seg_row = seg_row_ref[...]
    grad_q = jnp.zeros((BLK, PAIR), jnp.float32)
    for head in range(2):
        q_h = head_mask(q_ref[...], head)
        do_h = head_mask(do_ref[...], head)
        lse = lse_ref[head : head + 1, :]
        delta = jnp.zeros((1, BLK), jnp.float32)
        for tile in range(tiles):
            at = slice(tile * BLK, (tile + 1) * BLK)
            column = pl.multiple_of((blk - tile + tiles - 1) * BLK, BLK)
            scores = nt(k_ref[at, :], q_h) + strip_ref[head, :, pl.ds(column, BLK)]
            scores = jnp.where(seg_col_ref[at, :] == seg_row, scores, NEGATIVE)
            prob = jnp.exp(scores - lse)
            grad_p = nt(v_ref[at, :], do_h)
            delta = delta + jnp.sum(prob * grad_p, axis=0, keepdims=True)
            dv_acc[at, :] += nn(prob.astype(jnp.bfloat16), do_h)
            p_ref[at, :] = prob
            dp_ref[at, :] = grad_p
        for tile in range(tiles):
            at = slice(tile * BLK, (tile + 1) * BLK)
            grad_s = (p_ref[at, :] * (dp_ref[at, :] - delta)).astype(jnp.bfloat16)
            dk_acc[at, :] += nn(grad_s, q_h)
            grad_q = grad_q + tn(grad_s, head_mask(k_ref[at, :], head))
            away = jnp.clip(blk - tile, -2, 2) + 2
            bias_acc[head, away] += grad_s.astype(jnp.float32)
    dq_ref[...] = grad_q.astype(jnp.bfloat16)

    @pl.when(blk == tiles - 1)
    def _():
        dk_ref[...] = dk_acc[...].astype(jnp.bfloat16)
        dv_ref[...] = dv_acc[...].astype(jnp.bfloat16)
        for head in range(2):
            for away in range(5):
                diag_ref[head, away : away + 1, :] = diagonal_sums(bias_acc[head, away])


def attention_backward(qkv, grad_o, lse, segment, band_back):
    seq_len = qkv.shape[0]
    tiles = seq_len // BLK
    rows = pl.BlockSpec((BLK, PAIR), lambda b: (b, 0))
    whole = pl.BlockSpec((seq_len, PAIR), lambda b: (0, 0))
    result = jax.ShapeDtypeStruct((seq_len, PAIR), jnp.bfloat16)
    return pl.pallas_call(
        functools.partial(backward_kernel, tiles),
        grid=(tiles,),
        in_specs=[
            pl.BlockSpec((1, BLK), lambda b: (0, b)),
            pl.BlockSpec((seq_len, 1), lambda b: (0, 0)),
            pl.BlockSpec((2, 4 * BLK), lambda b: (0, 0)),
            rows,
            pl.BlockSpec((seq_len, PAIR), lambda b: (0, 1)),
            pl.BlockSpec((seq_len, PAIR), lambda b: (0, 2)),
            rows,
            pl.BlockSpec((2, BLK), lambda b: (0, b)),
        ],
        out_specs=[rows, whole, whole, pl.BlockSpec((2, 5, 2 * BLK), lambda b: (0, 0, 0))],
        out_shape=[
            result,
            result,
            result,
            jax.ShapeDtypeStruct((2, 5, 2 * BLK), jnp.float32),
        ],
        scratch_shapes=[
            pltpu.VMEM((2, BLK, (2 * tiles - 1) * BLK), jnp.float32),
            pltpu.VMEM((seq_len, PAIR), jnp.float32),
            pltpu.VMEM((seq_len, PAIR), jnp.float32),
            pltpu.VMEM((2, 5, BLK, BLK), jnp.float32),
            pltpu.VMEM((seq_len, BLK), jnp.float32),
            pltpu.VMEM((seq_len, BLK), jnp.float32),
        ],
        compiler_params=params(20),
        cost_estimate=cost(
            20 * seq_len * seq_len * PAIR, 16 * seq_len * PAIR, 2 * seq_len * seq_len
        ),
        name="attention_backward",
    )(segment[None, :], segment[:, None], band_back, qkv, qkv, qkv, grad_o, lse)


def one_hot_buckets(offset):
    return (bucket_index(offset)[..., None] == jnp.arange(BUCKETS, dtype=jnp.int32)).astype(
        jnp.float32
    )


def bias_bands(bias_rows):
    offset = jnp.arange(4 * BLK, dtype=jnp.int32) - 2 * BLK
    contract = (((1,), (1,)), ((), ()))
    ahead = lax.dot_general(bias_rows, one_hot_buckets(offset), contract, precision=PRECISE)
    behind = lax.dot_general(bias_rows, one_hot_buckets(-offset), contract, precision=PRECISE)
    return ahead, behind


def bucket_sums(diagonals):
    lane = jnp.arange(2 * BLK, dtype=jnp.int32)
    within = jnp.where(lane < BLK, lane, lane - 2 * BLK)
    away = (jnp.arange(5, dtype=jnp.int32) - 2) * BLK
    onehot = one_hot_buckets(-within[None, :] - away[:, None])
    return jnp.dot(diagonals.reshape(2, -1), onehot.reshape(-1, BUCKETS), precision=PRECISE)


CHIPS = 4
CORE, ACROSS, ALONG = 1, 2, 4
PLACES = ((6, 7), (0, 4), (5, 3), (1, 2))


def wide(values):
    return values.astype(jnp.float32)


def low(values):
    return values.astype(jnp.bfloat16)


def piece_rows(own_ref, piece, start, rows, total):
    base = (own_ref[0] ^ piece) * total + start
    return pl.ds(pl.multiple_of(base, rows), rows)


def gathered(refs):
    out = []
    for core in range(2):
        own, near_x, near_y, first, second = refs[5 * core : 5 * core + 5]
        out += [(core, 0, own), (2 + core, 0, near_x), (4 + core, 0, near_y)]
        out += [(6 + core, 0, first), (6 + core, first.shape[0], second)]
    return out


def join_slots(weight_ref, slots):
    for part in range(3):
        for index, slot in enumerate(slots):
            weight_ref[part * PAIR + index * DK : part * PAIR + (index + 1) * DK, :] = slot[
                part * DK : (part + 1) * DK, :
            ]


def norm_project_kernel(own_ref, gain_ref, slot_a, slot_b, *refs):
    hidden_ref, out_ref, weight_ref = refs[10:]
    total = refs[0].shape[0]
    for piece, start, ref in gathered(refs[:10]):
        values = wide(ref[...])
        scale = lax.rsqrt(jnp.mean(values * values, axis=-1, keepdims=True) + EPSILON)
        at = piece_rows(own_ref, piece, start, ref.shape[0], total)
        hidden_ref[at, :] = low(values * scale * gain_ref[...])
    join_slots(weight_ref, (slot_a, slot_b))
    for chunk in range(8 * total // BLK):
        at = slice(chunk * BLK, (chunk + 1) * BLK)
        out_ref[at, :] = low(nt(hidden_ref[at, :], weight_ref[...]))


VMEM = pl.BlockSpec(memory_space=pltpu.VMEM)
SMEM = pl.BlockSpec(memory_space=pltpu.SMEM)


def norm_project(own, gain, slots, pieces):
    rows, width = pieces[0].shape
    total, features = 8 * rows, 3 * PAIR
    return pl.pallas_call(
        norm_project_kernel,
        in_specs=[SMEM] + [VMEM] * 13,
        out_specs=[VMEM] * 3,
        out_shape=[
            jax.ShapeDtypeStruct((total, width), jnp.bfloat16),
            jax.ShapeDtypeStruct((total, features), jnp.bfloat16),
            jax.ShapeDtypeStruct((features, width), jnp.bfloat16),
        ],
        compiler_params=params(60),
        cost_estimate=cost(
            2 * total * width * features, 2 * (2 * total * width + features * (width + total))
        ),
        name="norm_project",
    )(own, gain[None, :], *slots, *pieces)


def project_kernel(hidden_ref, slot_a, slot_b, out_ref, weight_ref):
    @pl.when(pl.program_id(0) == 0)
    def _():
        join_slots(weight_ref, (slot_a, slot_b))

    out_ref[...] = low(nt(hidden_ref[...], weight_ref[...]))


def project(hidden, slots):
    total, width = hidden.shape
    features = 3 * PAIR
    slot = pl.BlockSpec((3 * DK, width), lambda b: (0, 0))
    return pl.pallas_call(
        project_kernel,
        grid=(total // BLK,),
        in_specs=[pl.BlockSpec((BLK, width), lambda b: (b, 0)), slot, slot],
        out_specs=[
            pl.BlockSpec((BLK, features), lambda b: (b, 0)),
            pl.BlockSpec((features, width), lambda b: (0, 0)),
        ],
        out_shape=[
            jax.ShapeDtypeStruct((total, features), jnp.bfloat16),
            jax.ShapeDtypeStruct((features, width), jnp.bfloat16),
        ],
        compiler_params=params(12),
        cost_estimate=cost(
            2 * total * width * features, 2 * (total * width + features * (width + total))
        ),
        name="project",
    )(hidden, *slots)


def spread_kernel(core, counts, own_ref, *refs):
    lefts, rights = refs[: counts[0]], refs[counts[0] : counts[0] + counts[1]]
    out, weight = refs[-2:]
    start = 0
    for right in rights:
        weight[start : start + right.shape[0], :] = right[...]
        start += right.shape[0]
    total = lefts[0].shape[0] // 8
    half = total // 2
    for chip in range(CHIPS):
        at = piece_rows(own_ref, 2 * chip + core, 0, total, total)
        values = None
        for index, left in enumerate(lefts):
            term = nn(left[at, :], weight[index * PAIR : (index + 1) * PAIR, :])
            values = term if values is None else values + term
        for index, place in enumerate(PLACES[chip]):
            out[place * half : (place + 1) * half, :] = low(
                values[index * half : (index + 1) * half, :]
            )


def spread(own, core, lefts, rights):
    total, width = lefts[0].shape[0] // 2, rights[0].shape[1]
    depth = sum(left.shape[1] for left in lefts)
    return pl.pallas_call(
        functools.partial(spread_kernel, core, (len(lefts), len(rights))),
        in_specs=[SMEM] + [VMEM] * (len(lefts) + len(rights)),
        out_specs=VMEM,
        out_shape=jax.ShapeDtypeStruct((total, width), jnp.bfloat16),
        scratch_shapes=[pltpu.VMEM((depth, width), jnp.bfloat16)],
        compiler_params=params(14),
        cost_estimate=cost(
            2 * total * width * depth, 2 * (total * width + depth * (width + total))
        ),
        name="spread",
    )(own, *lefts, *rights)


def heads_back_kernel(own_ref, weight_a0, weight_a1, weight_b0, weight_b1, mixed_a, mixed_b, *refs):
    heads_a, heads_b, grad_a, grad_b, whole, weight = refs[10:]
    total = refs[0].shape[0]
    for piece, start, ref in gathered(refs[:10]):
        whole[piece_rows(own_ref, piece, start, ref.shape[0], total), :] = ref[...]
    for index, ref in enumerate((weight_a0, weight_a1, weight_b0, weight_b1)):
        weight[index * DK : (index + 1) * DK, :] = ref[...]
    for chunk in range(8 * total // BLK):
        at = slice(chunk * BLK, (chunk + 1) * BLK)
        heads = low(nt(whole[at, :], weight[...]))
        heads_a[at, :] = heads[:, :PAIR]
        heads_b[at, :] = heads[:, PAIR:]
    grad_a[...] = low(tn(mixed_a[...], whole[...]))
    grad_b[...] = low(tn(mixed_b[...], whole[...]))


def heads_back(own, weights, mixed, pieces):
    rows, width = pieces[0].shape
    total = 8 * rows
    outs = pl.pallas_call(
        heads_back_kernel,
        in_specs=[SMEM] + [VMEM] * 16,
        out_specs=[VMEM] * 4,
        out_shape=[jax.ShapeDtypeStruct((total, PAIR), jnp.bfloat16)] * 2
        + [jax.ShapeDtypeStruct((PAIR, width), jnp.bfloat16)] * 2,
        scratch_shapes=[
            pltpu.VMEM((total, width), jnp.bfloat16),
            pltpu.VMEM((2 * PAIR, width), jnp.bfloat16),
        ],
        compiler_params=params(20),
        cost_estimate=cost(8 * total * width * PAIR, 2 * total * width),
        name="heads_back",
    )(own, *weights, *mixed, *pieces)
    return outs[:2], outs[2:]


def qkv_grad_kernel(gain_ref, hidden_ref, dq_ref, dk_ref, dv_ref, weight_ref, slot_a, slot_b, sum_ref):
    total = None
    for part, ref in enumerate((dq_ref, dk_ref, dv_ref)):
        grad = tn(ref[...], hidden_ref[...])
        slot_a[part * DK : (part + 1) * DK, :] = low(grad[:DK])
        slot_b[part * DK : (part + 1) * DK, :] = low(grad[DK:])
        at = slice(part * PAIR, (part + 1) * PAIR)
        term = jnp.sum(grad * wide(weight_ref[at, :]), axis=0, keepdims=True)
        total = term if total is None else total + term
    sum_ref[...] = total / gain_ref[...]


def qkv_grad(gain, hidden, dq, dk, dv, weight):
    total, width = hidden.shape
    cols = 512
    col = pl.BlockSpec((1, cols), lambda c: (0, c))
    back = pl.BlockSpec((total, PAIR), lambda c: (0, 0))
    slot = pl.BlockSpec((3 * DK, cols), lambda c: (0, c))
    return pl.pallas_call(
        qkv_grad_kernel,
        grid=(width // cols,),
        in_specs=[
            col,
            pl.BlockSpec((total, cols), lambda c: (0, c)),
            back,
            back,
            back,
            pl.BlockSpec((3 * PAIR, cols), lambda c: (0, c)),
        ],
        out_specs=[slot, slot, col],
        out_shape=[
            jax.ShapeDtypeStruct((3 * DK, width), jnp.bfloat16),
            jax.ShapeDtypeStruct((3 * DK, width), jnp.bfloat16),
            jax.ShapeDtypeStruct((1, width), jnp.float32),
        ],
        compiler_params=params(12),
        cost_estimate=cost(6 * total * width * PAIR, 2 * total * width + 12 * PAIR * width),
        name="qkv_grad",
    )(gain[None, :], hidden, dq, dk, dv, weight)


def assemble_kernel(own, *refs):
    outs = refs[6:]
    units = own.shape[0] // 3
    half = units // 2
    for part, weight in enumerate(outs):
        for chip in range(CHIPS):
            for index, place in enumerate(PLACES[chip]):
                ref, start = own, part * units + index * half
                if chip:
                    ref = refs[2 * chip - 2]
                    if start >= 3 * half:
                        ref, start = refs[2 * chip - 1], start - 3 * half
                weight[place * half : (place + 1) * half, :] = ref[start : start + half, :]


def assemble(own, *stacks):
    rows, width = own.shape
    return pl.pallas_call(
        assemble_kernel,
        in_specs=[VMEM] * 7,
        out_specs=[VMEM] * 3,
        out_shape=[jax.ShapeDtypeStruct((CHIPS * rows // 3, width), jnp.bfloat16)] * 3,
        compiler_params=params(20),
        cost_estimate=cost(0, 16 * rows * width),
        name="assemble",
    )(own, *stacks)


def feed_kernel(gate_w, up_w, down_w, *refs):
    hidden, cot, outs = refs[:2], refs[2:4], refs[4:]
    inner_ref, dgate_ref, dup_ref, grad_own, grad_other, out_own, out_other = outs
    rows = hidden[0].shape[0]
    values = jnp.concatenate([hidden[0][...], hidden[1][...]], axis=0)
    grads = jnp.concatenate([cot[0][...], cot[1][...]], axis=0)
    gate = nt(values, gate_w[...])
    up = nt(values, up_w[...])
    grad_m = nt(grads, down_w[...])
    square = gate * gate
    bend = jnp.tanh(GELU_SCALE * gate * (1.0 + GELU_CUBE * square))
    part = 0.5 * (1.0 + bend)
    act = gate * part
    slope = part + 0.5 * gate * (1.0 - bend * bend) * (
        GELU_SCALE * (1.0 + 3.0 * GELU_CUBE * square)
    )
    inner = low(act * up)
    inner_ref[...] = inner
    dgate = low(grad_m * up * slope)
    dup = low(grad_m * act)
    dgate_ref[...] = dgate
    dup_ref[...] = dup
    grad_h = low(nn(dgate, gate_w[...]) + nn(dup, up_w[...]))
    grad_own[...] = grad_h[:rows]
    grad_other[...] = grad_h[rows:]
    result = low(nn(inner, down_w[...]))
    out_own[...] = result[:rows]
    out_other[...] = result[rows:]


def feed(weights, hidden, cot):
    rows, width = hidden[0].shape
    total, units = 2 * rows, weights[0].shape[0]
    return pl.pallas_call(
        feed_kernel,
        in_specs=[VMEM] * 7,
        out_specs=[VMEM] * 7,
        out_shape=[jax.ShapeDtypeStruct((total, units), jnp.bfloat16)] * 3
        + [jax.ShapeDtypeStruct((rows, width), jnp.bfloat16)] * 4,
        compiler_params=params(24),
        cost_estimate=cost(12 * total * width * units, 2 * 4 * (total + units) * width),
        name="feed",
    )(*weights, *hidden, *cot)


def feed_grad_kernel(terms, *refs):
    lefts, pieces = refs[: 4 * terms], refs[4 * terms : 4 * terms + 8]
    outs, right = refs[-4:-1], refs[-1]
    rows = pieces[0].shape[0]
    for index, piece in enumerate(pieces):
        right[index * rows : (index + 1) * rows, :] = piece[...]
    for term in range(terms):
        left = jnp.concatenate([ref[...] for ref in lefts[4 * term : 4 * term + 4]], axis=0)
        grad = low(tn(left, right[...]))
        start = 0
        for out in outs:
            size = out.shape[0] // terms
            out[term * size : (term + 1) * size, :] = grad[start : start + size]
            start += size


def feed_grad(lefts, pieces):
    terms = len(lefts)
    rows, width = pieces[0].shape
    units = lefts[0][0].shape[1]
    return pl.pallas_call(
        functools.partial(feed_grad_kernel, terms),
        in_specs=[VMEM] * (4 * terms + 8),
        out_specs=[VMEM] * 3,
        out_shape=[
            jax.ShapeDtypeStruct((terms * units // part, width), jnp.bfloat16)
            for part in (4, 4, 2)
        ],
        scratch_shapes=[pltpu.VMEM((8 * rows, width), jnp.bfloat16)],
        compiler_params=params(48),
        cost_estimate=cost(16 * terms * rows * width * units, 24 * rows * width),
        name="feed_grad",
    )(*[value for left in lefts for value in left], *pieces)


def second_kernel(terms, keep, from_x, from_y, to_x, to_y):
    size = to_x.shape[0] // terms
    for term in range(terms):
        out = slice(term * size, (term + 1) * size)
        base = 4 * term * size
        pair = 2 * term * size
        to_x[out, :] = low(wide(keep[base : base + size, :]) + wide(from_y[pair : pair + size, :]))
        to_y[out, :] = low(
            wide(keep[base + size : base + 2 * size, :])
            + wide(from_x[pair + size : pair + 2 * size, :])
        )


def second(terms, keep, from_x, from_y):
    shape = jax.ShapeDtypeStruct((from_x.shape[0] // 2, from_x.shape[1]), jnp.bfloat16)
    return pl.pallas_call(
        functools.partial(second_kernel, terms),
        in_specs=[VMEM] * 3,
        out_specs=[VMEM] * 2,
        out_shape=[shape, shape],
        compiler_params=params(12),
        cost_estimate=cost(0, 6 * from_x.shape[0] * from_x.shape[1]),
        name="second",
    )(keep, from_x, from_y)


def totals_kernel(terms, *refs):
    outs = refs[5 * len(terms) :]
    done = 0
    for index, count in enumerate(terms):
        keep, from_x, from_y, second_x, second_y = refs[5 * index : 5 * index + 5]
        for term in range(count):
            out = outs[done]
            done += 1
            size = out.shape[0] // 2
            base, pair, one = 4 * term * size, 2 * term * size, term * size
            out[:size, :] = (
                wide(keep[base + 2 * size : base + 3 * size, :])
                + wide(from_x[pair : pair + size, :])
                + wide(second_y[one : one + size, :])
            )
            out[size:, :] = (
                wide(keep[base + 3 * size : base + 4 * size, :])
                + wide(from_y[pair + size : pair + 2 * size, :])
                + wide(second_x[one : one + size, :])
            )


def totals(terms, *groups):
    shapes = [
        (2 * group[3].shape[0] // count, group[3].shape[1])
        for count, group in zip(terms, groups)
        for _ in range(count)
    ]
    return pl.pallas_call(
        functools.partial(totals_kernel, terms),
        in_specs=[VMEM] * (5 * len(groups)),
        out_specs=[VMEM] * len(shapes),
        out_shape=[jax.ShapeDtypeStruct(shape, jnp.float32) for shape in shapes],
        compiler_params=params(56),
        cost_estimate=cost(0, 10 * sum(rows * width for rows, width in shapes)),
        name="totals",
    )(*[value for group in groups for value in group])


def fence(*values):
    return lax.optimization_barrier(values)


def swap(values, bits):
    return lax.ppermute(values, "seq", [(i, i ^ bits) for i in range(2 * CHIPS)])


def ring(values, step):
    n = lax.axis_size("fsdp")
    return lax.ppermute(values, "fsdp", [(i, (i + step) % n) for i in range(n)])


def line_order(slots):
    n = len(slots)
    order = (lax.axis_index("fsdp") - jnp.arange(n, dtype=jnp.int32)) % n
    return jnp.stack(slots)[order]


def both(values, other, bits):
    high = (lax.axis_index("seq") & bits) != 0
    return jnp.concatenate(
        [jnp.where(high, other, values), jnp.where(high, values, other)], axis=0
    )


def halves(values, bits):
    high = (lax.axis_index("seq") & bits) != 0
    size = values.shape[0] // 2
    lower, upper = values[:size], values[size:]
    return jnp.where(high, upper, lower), jnp.where(high, lower, upper)


def plane_sends(own, other=None):
    size = own.shape[0] // 4
    total = own if other is None else wide(own) + wide(other)
    return low(total[:size]), low(total[size : 2 * size]), total[2 * size :]


def plane_total(keep, from_x, from_y, second_x, second_y):
    size = keep.shape[0] // 4
    first = wide(keep[2 * size : 3 * size]) + wide(from_x[:size]) + wide(second_y)
    second = wide(keep[3 * size :]) + wide(from_y[size:]) + wide(second_x)
    return jnp.concatenate([first, second], axis=0)


def add(*values):
    return functools.reduce(lambda left, right: left + right, [wide(value) for value in values])


def per_device(
    tokens,
    starts,
    first_gain,
    query_weight,
    key_weight,
    value_weight,
    output_weight,
    bias_table,
    second_gain,
    gate_weight,
    up_weight,
    down_weight,
    cotangent,
):
    index = lax.axis_index("seq")[None]
    own = tokens[0]
    half = own.shape[0] // 2
    grad_out = cotangent[0]
    rows = first_gain.shape[0]
    buckets = bias_table.shape[0]
    qkv0 = low(jnp.concatenate([query_weight, key_weight, value_weight], axis=0))
    small = low(jnp.concatenate([first_gain, second_gain, bias_table]))
    own, qkv0, small, output_weight, gate_weight, up_weight, down_weight = fence(
        own, qkv0, small, output_weight, gate_weight, up_weight, down_weight
    )

    tok_x, tok_y = swap(own, ACROSS), swap(own, ALONG)
    small_slots = [small] + [ring(small, k) for k in range(1, 4)]
    small_slots, own, qkv0, output_weight, gate_weight, up_weight, down_weight = fence(
        small_slots, own, qkv0, output_weight, gate_weight, up_weight, down_weight
    )
    qkv1 = ring(qkv0, 1)
    gain_part = line_order([value[: 2 * rows] for value in small_slots]).reshape(-1)
    packed = jnp.concatenate([gain_part, low(starts[0])])[None]
    packed = both(packed, swap(packed, CORE), CORE)
    packed, output_weight, gate_weight, up_weight, down_weight = fence(
        packed, output_weight, gate_weight, up_weight, down_weight
    )
    near = both(packed, swap(packed, ACROSS), ACROSS)
    far = both(swap(packed, ALONG), swap(packed, ALONG | ACROSS), ACROSS)
    packed = both(near, far, ALONG)
    packed, tok_x, tok_y, output_weight, gate_weight, up_weight, down_weight = fence(
        packed, tok_x, tok_y, output_weight, gate_weight, up_weight, down_weight
    )

    tok_d1, tok_d2 = swap(tok_y[:half], ACROSS), swap(tok_x[half:], ALONG)
    tok_cx, tok_cy = swap(tok_x, CORE), swap(tok_y, CORE)
    out0 = low(output_weight)
    gain_count = gain_part.shape[0]
    gains = wide(packed[:, :gain_count]).reshape(-1, 4, 2, rows)
    gain_first = gains[:, :, 0].reshape(-1)
    gain_second = gains[:, :, 1].reshape(-1)
    segment = jnp.cumsum(packed[:, gain_count:].reshape(-1).astype(jnp.int32), dtype=jnp.int32)
    tables = [wide(value[2 * rows :]) for value in small_slots]
    bands = [bias_bands(jnp.stack(tables[2 * p : 2 * p + 2])) for p in range(2)]
    tok_d1, tok_d2, tok_cx, tok_cy, segment, gain_first, gain_second, bands, out0, own = fence(
        tok_d1, tok_d2, tok_cx, tok_cy, segment, gain_first, gain_second, bands, out0, own
    )

    tok_c, tok_c1, tok_c2 = swap(own, CORE), swap(tok_d1, CORE), swap(tok_d2, CORE)
    feed0 = low(jnp.concatenate([gate_weight, up_weight, down_weight], axis=0))
    tok_c, tok_c1, tok_c2, feed0, qkv1, out0 = fence(tok_c, tok_c1, tok_c2, feed0, qkv1, out0)

    qkv2, out1 = ring(qkv1, 1), ring(out0, 1)
    feed_half = feed0.shape[0] // 2
    feed_top, feed_low = feed0[:feed_half], feed0[feed_half:]
    feed_xl, feed_yt = swap(feed_low, ACROSS), swap(feed_top, ALONG)
    tok_pieces = (own, tok_x, tok_y, tok_d1, tok_d2, tok_c, tok_cx, tok_cy, tok_c1, tok_c2)
    hidden_one, qkv_a, weight_a = norm_project(index, gain_first, (qkv0, qkv1), tok_pieces)
    hidden_one, qkv_a, weight_a, qkv2, out1, grad_out, feed_xl, feed_yt, feed_top, feed_low = fence(
        hidden_one, qkv_a, weight_a, qkv2, out1, grad_out, feed_xl, feed_yt, feed_top, feed_low
    )

    qkv3, out2 = ring(qkv2, 1), ring(out1, 1)
    feed_xt, feed_yl = swap(feed_top, ACROSS), swap(feed_low, ALONG)
    mixed_a, lse_a = attention_forward(qkv_a, segment, bands[0][0])
    mixed_a, lse_a, hidden_one, qkv3, out2, feed_xt, feed_yl, feed_xl, feed_yt = fence(
        mixed_a, lse_a, hidden_one, qkv3, out2, feed_xt, feed_yl, feed_xl, feed_yt
    )

    feed_dt, feed_dl = swap(feed_yt, ACROSS), swap(feed_xl, ALONG)
    out3, cot1 = ring(out2, 1), ring(grad_out, 1)
    qkv_b, weight_b = project(hidden_one, (qkv2, qkv3))
    mixed_b, lse_b = attention_forward(qkv_b, segment, bands[1][0])
    mixed_b, lse_b, out3, grad_out = fence(mixed_b, lse_b, out3, grad_out)
    cot_c0 = swap(grad_out, CORE)
    out_slots = (out0, out1, out2, out3)
    mixed = (mixed_a, mixed_b)
    part_other = spread(index, 1, mixed, out_slots)
    part_other, mixed, feed_dt, feed_dl, cot1, cot_c0 = fence(
        part_other, mixed, feed_dt, feed_dl, cot1, cot_c0
    )
    part_other, cot2, cot_c1 = swap(part_other, CORE), ring(cot1, 1), swap(cot1, CORE)
    part_own = spread(index, 0, mixed, out_slots)
    part_own, part_other, cot_c1 = fence(part_own, part_other, cot_c1)

    send_x, send_y, keep = plane_sends(part_own, part_other)
    send_x, send_y, keep = fence(send_x, send_y, keep)
    from_x, from_y = swap(send_x, ACROSS), swap(send_y, ALONG)
    weights = assemble(feed0, feed_xt, feed_xl, feed_yt, feed_yl, feed_dt, feed_dl)
    from_x, from_y, weights, cot2 = fence(from_x, from_y, weights, cot2)
    send_x, send_y = fence(*second(1, keep, from_x, from_y))
    second_x, second_y = swap(send_x, ACROSS), swap(send_y, ALONG)
    cot3, cot_c2 = ring(cot2, 1), swap(cot2, CORE)
    second_x, second_y, cot3, cot_c2 = fence(second_x, second_y, cot3, cot_c2)
    inputs = wide(own)
    resid_one = inputs + plane_total(keep, from_x, from_y, second_x, second_y)

    scale_two = lax.rsqrt(jnp.mean(resid_one * resid_one, axis=-1, keepdims=True) + EPSILON)
    normed_two = resid_one * scale_two
    hid0 = low(normed_two * gain_second)
    hid0, resid_one, scale_two = fence(hid0, resid_one, scale_two)

    hid1, hid_c0, cot_c3 = ring(hid0, 1), swap(hid0, CORE), swap(cot3, CORE)
    hid_c0, cot_c3 = fence(hid_c0, cot_c3)
    feed_a = feed(weights, (hid0, hid_c0), (grad_out, cot_c0))
    feed_a, hid1 = fence(feed_a, hid1)
    hid2, hid_c1 = ring(hid1, 1), swap(hid1, CORE)
    hid_c1, feed_a = fence(hid_c1, feed_a)
    grad_c0, out_c0 = swap(feed_a[4], CORE), swap(feed_a[6], CORE)
    feed_b = feed(weights, (hid1, hid_c1), (cot1, cot_c1))
    feed_b, hid2, grad_c0, out_c0 = fence(feed_b, hid2, grad_c0, out_c0)
    hid3, hid_c2 = ring(hid2, 1), swap(hid2, CORE)
    hid_c2, feed_b = fence(hid_c2, feed_b)
    grad_c1, out_c1 = swap(feed_b[4], CORE), swap(feed_b[6], CORE)
    feed_c = feed(weights, (hid2, hid_c2), (cot2, cot_c2))
    feed_c, hid3, grad_c1, out_c1 = fence(feed_c, hid3, grad_c1, out_c1)
    hid_c3 = swap(hid3, CORE)
    dh = ring(low(add(feed_b[3], grad_c1)), 1)
    hid_c3, feed_c = fence(hid_c3, feed_c)
    grad_c2, out_c2 = swap(feed_c[4], CORE), swap(feed_c[6], CORE)
    feed_d = feed(weights, (hid3, hid_c3), (cot3, cot_c3))
    feed_d, dh, grad_c2, out_c2 = fence(feed_d, dh, grad_c2, out_c2)
    dh = ring(low(add(feed_c[3], grad_c2, dh)), 1)
    grad_c3, out_c3 = swap(feed_d[4], CORE), swap(feed_d[6], CORE)
    parts = (feed_a, feed_b, feed_c, feed_d)
    hid_pieces = (hid0, hid_c0, hid1, hid_c1, hid2, hid_c2, hid3, hid_c3)
    cot_pieces = (grad_out, cot_c0, cot1, cot_c1, cot2, cot_c2, cot3, cot_c3)
    grad_down = feed_grad([[part[0] for part in parts]], cot_pieces)
    grad_down, dh, grad_c3, out_c3, hid_pieces = fence(grad_down, dh, grad_c3, out_c3, hid_pieces)

    dh = ring(low(add(feed_d[3], grad_c3, dh)), 1)
    down_x, down_y, down_keep = grad_down
    down_fx, down_fy = swap(down_x, ACROSS), swap(down_y, ALONG)
    grad_both = feed_grad(
        [[part[1] for part in parts], [part[2] for part in parts]], hid_pieces
    )
    dh, grad_both = fence(dh, grad_both)

    grad_hidden_two = add(feed_a[3], grad_c0, dh)
    normed_two = resid_one * scale_two
    shared = grad_hidden_two * gain_second
    grad_resid = wide(grad_out) + scale_two * (
        shared - normed_two * jnp.mean(shared * normed_two, axis=-1, keepdims=True)
    )
    branch = low(grad_resid)
    gain_two_rows = jnp.sum(grad_hidden_two * normed_two, axis=0)
    branch, grad_resid, gain_two_rows, down_fx, down_fy, feed_b = fence(
        branch, grad_resid, gain_two_rows, down_fx, down_fy, feed_b
    )

    br_x, br_y, br_c = swap(branch, ACROSS), swap(branch, ALONG), swap(branch, CORE)
    out_sum = ring(low(add(feed_b[5], out_c1)), 1)
    down_x, down_y = second(1, down_keep, down_fx, down_fy)
    br_x, br_y, br_c, down_x, down_y, out_sum = fence(br_x, br_y, br_c, down_x, down_y, out_sum)
    br_d1, br_d2 = swap(br_y[:half], ACROSS), swap(br_x[half:], ALONG)
    br_cx, br_cy = swap(br_x, CORE), swap(br_y, CORE)
    out_sum = ring(low(add(feed_c[5], out_c2, out_sum)), 1)
    br_d1, br_d2, br_cx, br_cy = fence(br_d1, br_d2, br_cx, br_cy)

    br_c1, br_c2 = swap(br_d1, CORE), swap(br_d2, CORE)
    down_sx, down_sy = swap(down_x, ACROSS), swap(down_y, ALONG)
    pieces = (branch, br_x, br_y, br_d1, br_d2, br_c, br_cx, br_cy, br_c1, br_c2)
    grad_heads, grad_outs = heads_back(index, out_slots, mixed, pieces)
    out_send = low(add(feed_d[5], out_c3, out_sum))
    grad_heads, grad_outs, grad_both, down_sx, down_sy, out_send = fence(
        grad_heads, grad_outs, grad_both, down_sx, down_sy, out_send
    )

    go0, go1 = grad_outs[0][:DK], grad_outs[0][DK:]
    go2, go3 = grad_outs[1][:DK], grad_outs[1][DK:]
    both_x, both_y, both_keep = grad_both
    both_fx, both_fy = swap(both_x, ACROSS), swap(both_y, ALONG)
    go_sum, out_sum = ring(go3, -1), ring(out_send, 1)
    dq_b, dk_b, dv_b, diag_b = attention_backward(
        qkv_b, grad_heads[1], lse_b, segment, bands[1][1]
    )
    dq_b, dk_b, dv_b, diag_b, go_sum, out_sum = fence(
        dq_b, dk_b, dv_b, diag_b, go_sum, out_sum
    )

    go_sum = ring(low(add(go2, go_sum)), -1)
    gq2, gq3, sums_b = qkv_grad(gain_first, hidden_one, dq_b, dk_b, dv_b, weight_b)
    gq2, gq3, sums_b, both_fx, both_fy, go_sum = fence(
        gq2, gq3, sums_b, both_fx, both_fy, go_sum
    )
    both_x, both_y = second(2, both_keep, both_fx, both_fy)
    go_send = low(add(go1, go_sum))
    gq2, gq3, qkv_a, both_x, both_y, go_send = fence(gq2, gq3, qkv_a, both_x, both_y, go_send)

    gq, go_sum = ring(gq3, -1), ring(go_send, -1)
    both_sx, both_sy = swap(both_x, ACROSS), swap(both_y, ALONG)
    dq_a, dk_a, dv_a, diag_a = attention_backward(
        qkv_a, grad_heads[0], lse_a, segment, bands[0][1]
    )
    dq_a, dk_a, dv_a, diag_a, gq, both_sx, both_sy, go_sum = fence(
        dq_a, dk_a, dv_a, diag_a, gq, both_sx, both_sy, go_sum
    )

    gq = ring(low(add(gq2, gq)), -1)
    lefts = (dq_a, dk_a, dv_a, dq_b, dk_b, dv_b)
    back_other = spread(index, 1, lefts, (weight_a, weight_b))
    back_other, lefts = fence(back_other, lefts)
    back_other = swap(back_other, CORE)
    gq0, gq1, sums_a = qkv_grad(gain_first, hidden_one, *lefts[:3], weight_a)
    back_own = spread(index, 0, lefts, (weight_a, weight_b))
    gain_rows = jnp.stack([(sums_a + sums_b)[0], gain_two_rows]).reshape(2, 2, 2, 2, 4, -1)
    gain_rows = jnp.transpose(gain_rows, (3, 1, 2, 4, 0, 5)).reshape(2 * CHIPS, -1)
    back_own, back_other, gq0, gq1, gain_rows = fence(
        back_own, back_other, gq0, gq1, gain_rows
    )
    send_x, send_y, keep = plane_sends(back_own, back_other)
    send_x, send_y, keep, gain_rows = fence(send_x, send_y, keep, gain_rows)

    from_x, from_y = swap(send_x, ACROSS), swap(send_y, ALONG)
    gain_keep, gain_send = halves(gain_rows, CORE)
    gain_rows = gain_keep + swap(gain_send, CORE)
    from_x, from_y, gain_rows, gq, gq1 = fence(from_x, from_y, gain_rows, gq, gq1)
    gq = ring(low(add(gq1, gq)), -1)
    send_x, send_y = second(1, keep, from_x, from_y)
    second_x, second_y = swap(send_x, ACROSS), swap(send_y, ALONG)
    gain_keep, gain_send = halves(gain_rows, ALONG)
    gain_rows = gain_keep + swap(gain_send, ALONG)
    late = (down_keep, both_keep, resid_one, diag_a)
    second_x, second_y, gain_rows, late = fence(second_x, second_y, gain_rows, late)
    down_keep, both_keep, resid_one, diag_a = late
    gain_keep, gain_send = halves(gain_rows, ACROSS)
    gain_rows = gain_keep + swap(gain_send, ACROSS)
    tables_a, tables_b = bucket_sums(diag_a), bucket_sums(diag_b)
    table_slots = (tables_a[0], tables_a[1], tables_b[0], tables_b[1])
    gain_slots = line_order(list(gain_rows.reshape(4, -1)))
    sums = [jnp.concatenate([gain_slots[k], table_slots[k]]) for k in range(4)]
    sums = sums[0] + sum(ring(sums[k], -k) for k in range(1, 4))
    grad_down_w, grad_gate_w, grad_up_w = totals(
        (1, 2),
        (down_keep, down_fx, down_fy, down_sx, down_sy),
        (both_keep, both_fx, both_fy, both_sx, both_sy),
    )
    layer_out = low(resid_one + add(feed_a[5], out_c0, out_sum))
    grad_hidden_one = plane_total(keep, from_x, from_y, second_x, second_y)
    scale_one = lax.rsqrt(jnp.mean(inputs * inputs, axis=-1, keepdims=True) + EPSILON)
    normed_one = inputs * scale_one
    shared = grad_hidden_one * gain_first
    grad_tokens = low(
        grad_resid
        + scale_one * (shared - normed_one * jnp.mean(shared * normed_one, axis=-1, keepdims=True))
    )
    grad_qkv = add(gq0, gq)
    grad_output_w = add(go0, go_sum)
    return (
        layer_out[None],
        grad_tokens[None],
        sums[:rows],
        grad_qkv[:DK],
        grad_qkv[DK : 2 * DK],
        grad_qkv[2 * DK :],
        grad_output_w,
        sums[2 * rows :],
        sums[rows : 2 * rows],
        grad_gate_w,
        grad_up_w,
        grad_down_w,
    )


def rms_norm(values, gain):
    return values * lax.rsqrt(jnp.mean(values * values, axis=-1, keepdims=True) + EPSILON) * gain


def gated_gelu(gate, up_part):
    return jax.nn.gelu(gate, approximate=True) * up_part


def gather_rows(values):
    return lax.all_gather(values, "seq", axis=0, tiled=True)


def scatter_rows(values):
    return lax.psum_scatter(
        values.astype(jnp.bfloat16), "seq", scatter_dimension=0, tiled=True
    ).astype(jnp.float32)


def per_device_general(
    tokens,
    starts,
    first_gain,
    query_weight,
    key_weight,
    value_weight,
    output_weight,
    bias_table,
    second_gain,
    gate_weight,
    up_weight,
    down_weight,
    cotangent,
):
    segment = jnp.cumsum(lax.all_gather(starts, "seq", axis=1, tiled=True)[0], dtype=jnp.int32)
    inputs = tokens[0].astype(jnp.float32)
    grad_out = cotangent[0]
    head_count = H // lax.axis_size("seq")
    head_first = lax.axis_index("seq") * head_count
    query_low = query_weight.astype(jnp.bfloat16)
    key_low = key_weight.astype(jnp.bfloat16)
    value_low = value_weight.astype(jnp.bfloat16)
    output_low = output_weight.astype(jnp.bfloat16)
    gate_low = gate_weight.astype(jnp.bfloat16)
    up_low = up_weight.astype(jnp.bfloat16)
    down_low = down_weight.astype(jnp.bfloat16)
    first_low = first_gain.astype(jnp.bfloat16)
    second_low = second_gain.astype(jnp.bfloat16)
    table_low = bias_table.astype(jnp.bfloat16)
    query_part, key_part, value_part, output_part, gate_part, up_rows, down_part = (
        lax.all_gather(query_low, "fsdp", axis=0, tiled=True),
        lax.all_gather(key_low, "fsdp", axis=0, tiled=True),
        lax.all_gather(value_low, "fsdp", axis=0, tiled=True),
        lax.all_gather(output_low, "fsdp", axis=0, tiled=True),
        lax.all_gather(gate_low, "fsdp", axis=0, tiled=True),
        lax.all_gather(up_low, "fsdp", axis=0, tiled=True),
        lax.all_gather(down_low, "fsdp", axis=0, tiled=True),
    )
    gain_one, gain_two, table_full = (
        lax.all_gather(first_low, ("seq", "fsdp"), axis=0, tiled=True),
        lax.all_gather(second_low, ("seq", "fsdp"), axis=0, tiled=True),
        lax.all_gather(table_low, ("seq", "fsdp"), axis=0, tiled=True),
    )
    gain_first = gain_one.astype(jnp.float32)
    gain_second = gain_two.astype(jnp.float32)
    bias_rows = lax.dynamic_slice_in_dim(
        table_full.astype(jnp.float32).reshape(H, BUCKETS), head_first, head_count, 0
    )
    hidden_one = rms_norm(inputs, gain_first).astype(jnp.bfloat16)
    hidden_all = gather_rows(hidden_one)
    query_head = (
        low(nt(hidden_all, query_part))
    )
    key_head = (
        low(nt(hidden_all, key_part))
    )
    value_head = (
        low(nt(hidden_all, value_part))
    )
    pairs = head_count // 2
    pair = [slice(index * PAIR, (index + 1) * PAIR) for index in range(pairs)]
    bands = [bias_bands(bias_rows[2 * index : 2 * index + 2]) for index in range(pairs)]
    qkv = [
        jnp.concatenate([query_head[:, at], key_head[:, at], value_head[:, at]], axis=1)
        for at in pair
    ]
    forward = [attention_forward(qkv[i], segment, bands[i][0]) for i in range(pairs)]
    mixed = jnp.concatenate([out for out, _ in forward], axis=1)
    resid_one = inputs + scatter_rows(nn(mixed, output_part))
    hidden_two = rms_norm(resid_one, gain_second).astype(jnp.bfloat16)
    hidden_two_all = gather_rows(hidden_two)
    gate = nt(hidden_two_all, gate_part)
    up_part = nt(hidden_two_all, up_rows)
    inner = gated_gelu(gate, up_part).astype(jnp.bfloat16)
    layer_out = (resid_one + scatter_rows(nn(inner, down_part))).astype(jnp.bfloat16)
    grad_out_all = gather_rows(grad_out)
    grad_inner = nt(grad_out_all, down_part)
    grad_down = tn(inner, grad_out_all)
    grad_gate, grad_up = jax.vjp(gated_gelu, gate, up_part)[1](grad_inner)
    grad_gate = grad_gate.astype(jnp.bfloat16)
    grad_up = grad_up.astype(jnp.bfloat16)
    grad_gate_w = tn(grad_gate, hidden_two_all)
    grad_up_w = tn(grad_up, hidden_two_all)
    grad_hidden_two = scatter_rows(nn(grad_gate, gate_part) + nn(grad_up, up_rows))
    grad_norm_two, grad_gain_two = jax.vjp(rms_norm, resid_one, gain_second)[1](grad_hidden_two)
    grad_resid = grad_out.astype(jnp.float32) + grad_norm_two
    grad_branch = grad_resid.astype(jnp.bfloat16)
    branch_all = gather_rows(grad_branch)
    grad_output_w = tn(mixed, branch_all)
    grad_heads = (
        low(nt(branch_all, output_part))
    )
    back = [
        attention_backward(qkv[i], grad_heads[:, pair[i]], forward[i][1], segment, bands[i][1])
        for i in range(pairs)
    ]
    grad_query_seq, grad_key_seq, grad_value_seq = (
        jnp.concatenate([values[part] for values in back], axis=1) for part in range(3)
    )
    grad_bias = jnp.concatenate([bucket_sums(values[3]) for values in back], axis=0)
    grad_query_w = tn(grad_query_seq, hidden_all)
    grad_key_w = tn(grad_key_seq, hidden_all)
    grad_value_w = tn(grad_value_seq, hidden_all)
    grad_hidden_one = scatter_rows(
        nn(grad_query_seq, query_part)
        + nn(grad_key_seq, key_part)
        + nn(grad_value_seq, value_part)
    )
    grad_norm_one, grad_gain_one = jax.vjp(rms_norm, inputs, gain_first)[1](grad_hidden_one)
    grad_tokens = (grad_resid + grad_norm_one).astype(jnp.bfloat16)
    grad_table = lax.dynamic_update_slice_in_dim(
        jnp.zeros((H, BUCKETS), jnp.float32), grad_bias, head_first, 0
    ).reshape(-1)
    weight_grads = (
        lax.psum_scatter(
            grad_query_w.astype(jnp.bfloat16), "fsdp", scatter_dimension=0, tiled=True
        ).astype(jnp.float32),
        lax.psum_scatter(
            grad_key_w.astype(jnp.bfloat16), "fsdp", scatter_dimension=0, tiled=True
        ).astype(jnp.float32),
        lax.psum_scatter(
            grad_value_w.astype(jnp.bfloat16), "fsdp", scatter_dimension=0, tiled=True
        ).astype(jnp.float32),
        lax.psum_scatter(
            grad_output_w.astype(jnp.bfloat16), "fsdp", scatter_dimension=0, tiled=True
        ).astype(jnp.float32),
        lax.psum_scatter(
            grad_gate_w.astype(jnp.bfloat16), "fsdp", scatter_dimension=0, tiled=True
        ).astype(jnp.float32),
        lax.psum_scatter(
            grad_up_w.astype(jnp.bfloat16), "fsdp", scatter_dimension=0, tiled=True
        ).astype(jnp.float32),
        lax.psum_scatter(
            grad_down.astype(jnp.bfloat16), "fsdp", scatter_dimension=0, tiled=True
        ).astype(jnp.float32),
    )
    small_grads = (
        lax.psum_scatter(grad_gain_one, ("seq", "fsdp"), scatter_dimension=0, tiled=True),
        lax.psum_scatter(grad_gain_two, ("seq", "fsdp"), scatter_dimension=0, tiled=True),
        lax.psum_scatter(grad_table, ("seq", "fsdp"), scatter_dimension=0, tiled=True),
    )
    return (
        layer_out[None],
        grad_tokens[None],
        small_grads[0],
        weight_grads[0],
        weight_grads[1],
        weight_grads[2],
        weight_grads[3],
        small_grads[2],
        small_grads[1],
        weight_grads[4],
        weight_grads[5],
        weight_grads[6],
    )


def solution(mesh):
    rows = P(("seq", "fsdp"), None)
    row = P(("seq", "fsdp"))
    activations = P("fsdp", "seq", None)
    in_specs = (
        activations,
        P("fsdp", "seq"),
        row,
        rows,
        rows,
        rows,
        rows,
        row,
        row,
        rows,
        rows,
        rows,
        activations,
    )
    out_specs = (
        activations,
        activations,
        row,
        rows,
        rows,
        rows,
        rows,
        row,
        row,
        rows,
        rows,
        rows,
    )
    seq, fsdp = mesh.shape["seq"], mesh.shape["fsdp"]
    plan = per_device if seq == 2 * CHIPS and H == seq * fsdp else per_device_general
    return jax.shard_map(
        plan,
        mesh=mesh,
        in_specs=in_specs,
        out_specs=out_specs,
        check_vma=False,
    )
```

```python
import functools

import jax
import jax.numpy as jnp
from jax import lax
from jax.experimental import pallas as pl
from jax.experimental.pallas import tpu as pltpu
from jax.sharding import PartitionSpec as P

H = 32
DK = 64
BUCKETS = 32


EPSILON = 1e-06
NEGATIVE = -1000000000.0
BUCKET_EDGES = (12, 16, 23, 32, 46, 64, 91)
PRECISE = lax.Precision.HIGHEST
BLK = 256
PAIR = 128
GELU_SCALE = 0.7978845608028654
GELU_CUBE = 0.044715


def bucket_index(offset):
    distance = jnp.abs(offset)
    coarse = 8 + sum(((distance >= edge).astype(jnp.int32) for edge in BUCKET_EDGES))
    return jnp.where(distance < 8, distance, coarse) + 16 * (offset > 0).astype(jnp.int32)


def nt(left, right):
    return lax.dot_general(
        left, right, (((1,), (1,)), ((), ())), preferred_element_type=jnp.float32
    )


def nn(left, right):
    return jnp.dot(left, right, preferred_element_type=jnp.float32)


def tn(left, right):
    return lax.dot_general(
        left, right, (((0,), (0,)), ((), ())), preferred_element_type=jnp.float32
    )


def params(mib):
    return pltpu.CompilerParams(vmem_limit_bytes=mib * 1024 * 1024)


def cost(flops, bytes_accessed, transcendentals=0):
    return pl.CostEstimate(
        flops=flops, bytes_accessed=bytes_accessed, transcendentals=transcendentals
    )


def head_mask(values, head):
    lane = lax.broadcasted_iota(jnp.int32, values.shape, 1)
    keep = (lane < DK) if head == 0 else (lane >= DK)
    return jnp.where(keep, values, jnp.zeros_like(values))


def fill_strip(strip_ref, head, band_row, tiles):
    wide = jnp.broadcast_to(band_row, (BLK, band_row.shape[1]))
    rolled = pltpu.roll(wide, 0, 1, stride=1, stride_axis=0)
    span = (2 * tiles - 1) * BLK
    near = (tiles - 2) * BLK
    if near > 0:
        strip_ref[head, :, 0:near] = jnp.broadcast_to(band_row[:, 0:1], (BLK, near))
        strip_ref[head, :, near + 3 * BLK : span] = jnp.broadcast_to(
            band_row[:, 4 * BLK - 1 : 4 * BLK], (BLK, span - near - 3 * BLK)
        )
    strip_ref[head, :, near : near + 3 * BLK] = rolled[:, BLK:]


def forward_kernel(tiles, seg_row_ref, seg_col_ref, band_ref, q_ref, k_ref, v_ref, o_ref, lse_ref, strip_ref):
    blk = pl.program_id(0)

    @pl.when(blk == 0)
    def _():
        for head in range(2):
            fill_strip(strip_ref, head, band_ref[head : head + 1, :], tiles)

    keys = tiles * BLK
    start = pl.multiple_of((tiles - 1 - blk) * BLK, BLK)
    same = seg_col_ref[...] == seg_row_ref[...]
    total = jnp.zeros((BLK, PAIR), jnp.float32)
    rows = []
    for head in range(2):
        scores = nt(head_mask(q_ref[...], head), k_ref[...]) + strip_ref[head, :, pl.ds(start, keys)]
        scores = jnp.where(same, scores, NEGATIVE)
        top = jnp.max(scores, axis=1, keepdims=True)
        weight = jnp.exp(scores - top)
        norm = jnp.sum(weight, axis=1, keepdims=True)
        prob = (weight * (1.0 / norm)).astype(jnp.bfloat16)
        total = total + nn(prob, head_mask(v_ref[...], head))
        rows.append(jnp.transpose(jnp.broadcast_to(top + jnp.log(norm), (BLK, PAIR)))[0:1, :])
    o_ref[...] = total.astype(jnp.bfloat16)
    lse_ref[...] = jnp.concatenate(rows, axis=0)


def attention_forward(qkv, segment, band):
    seq_len = qkv.shape[0]
    tiles = seq_len // BLK
    return pl.pallas_call(
        functools.partial(forward_kernel, tiles),
        grid=(tiles,),
        in_specs=[
            pl.BlockSpec((1, seq_len), lambda b: (0, 0)),
            pl.BlockSpec((BLK, 1), lambda b: (b, 0)),
            pl.BlockSpec((2, 4 * BLK), lambda b: (0, 0)),
            pl.BlockSpec((BLK, PAIR), lambda b: (b, 0)),
            pl.BlockSpec((seq_len, PAIR), lambda b: (0, 1)),
            pl.BlockSpec((seq_len, PAIR), lambda b: (0, 2)),
        ],
        out_specs=[
            pl.BlockSpec((BLK, PAIR), lambda b: (b, 0)),
            pl.BlockSpec((2, BLK), lambda b: (0, b)),
        ],
        out_shape=[
            jax.ShapeDtypeStruct((seq_len, PAIR), jnp.bfloat16),
            jax.ShapeDtypeStruct((2, seq_len), jnp.float32),
        ],
        scratch_shapes=[pltpu.VMEM((2, BLK, (2 * tiles - 1) * BLK), jnp.float32)],
        compiler_params=params(20),
        cost_estimate=cost(
            8 * seq_len * seq_len * PAIR, 8 * seq_len * PAIR, 2 * seq_len * seq_len
        ),
        name="attention_forward",
    )(segment[None, :], segment[:, None], band, qkv, qkv, qkv)


def diagonal_sums(tile):
    wide = jnp.concatenate([tile, jnp.zeros_like(tile)], axis=1)
    width = 2 * BLK
    row = lax.broadcasted_iota(jnp.int32, wide.shape, 0)
    shift = 1
    while shift < BLK:
        wide = jnp.where((row & shift) != 0, pltpu.roll(wide, width - shift, 1), wide)
        shift *= 2
    return jnp.sum(wide, axis=0, keepdims=True)


def backward_kernel(tiles, seg_row_ref, seg_col_ref, band_ref, q_ref, k_ref, v_ref, do_ref, lse_ref,
                    dq_ref, dk_ref, dv_ref, diag_ref, strip_ref, dk_acc, dv_acc, bias_acc, p_ref, dp_ref):
    blk = pl.program_id(0)

    @pl.when(blk == 0)
    def _():
        for head in range(2):
            fill_strip(strip_ref, head, band_ref[head : head + 1, :], tiles)
        dk_acc[...] = jnp.zeros_like(dk_acc)
        dv_acc[...] = jnp.zeros_like(dv_acc)
        bias_acc[...] = jnp.zeros_like(bias_acc)

    seg_row = seg_row_ref[...]
    grad_q = jnp.zeros((BLK, PAIR), jnp.float32)
    for head in range(2):
        q_h = head_mask(q_ref[...], head)
        do_h = head_mask(do_ref[...], head)
        lse = lse_ref[head : head + 1, :]
        delta = jnp.zeros((1, BLK), jnp.float32)
        for tile in range(tiles):
            at = slice(tile * BLK, (tile + 1) * BLK)
            column = pl.multiple_of((blk - tile + tiles - 1) * BLK, BLK)
            scores = nt(k_ref[at, :], q_h) + strip_ref[head, :, pl.ds(column, BLK)]
            scores = jnp.where(seg_col_ref[at, :] == seg_row, scores, NEGATIVE)
            prob = jnp.exp(scores - lse)
            grad_p = nt(v_ref[at, :], do_h)
            delta = delta + jnp.sum(prob * grad_p, axis=0, keepdims=True)
            dv_acc[at, :] += nn(prob.astype(jnp.bfloat16), do_h)
            p_ref[at, :] = prob
            dp_ref[at, :] = grad_p
        for tile in range(tiles):
            at = slice(tile * BLK, (tile + 1) * BLK)
            grad_s = (p_ref[at, :] * (dp_ref[at, :] - delta)).astype(jnp.bfloat16)
            dk_acc[at, :] += nn(grad_s, q_h)
            grad_q = grad_q + tn(grad_s, head_mask(k_ref[at, :], head))
            away = jnp.clip(blk - tile, -2, 2) + 2
            bias_acc[head, away] += grad_s.astype(jnp.float32)
    dq_ref[...] = grad_q.astype(jnp.bfloat16)

    @pl.when(blk == tiles - 1)
    def _():
        dk_ref[...] = dk_acc[...].astype(jnp.bfloat16)
        dv_ref[...] = dv_acc[...].astype(jnp.bfloat16)
        for head in range(2):
            for away in range(5):
                diag_ref[head, away : away + 1, :] = diagonal_sums(bias_acc[head, away])


def attention_backward(qkv, grad_o, lse, segment, band_back):
    seq_len = qkv.shape[0]
    tiles = seq_len // BLK
    rows = pl.BlockSpec((BLK, PAIR), lambda b: (b, 0))
    whole = pl.BlockSpec((seq_len, PAIR), lambda b: (0, 0))
    result = jax.ShapeDtypeStruct((seq_len, PAIR), jnp.bfloat16)
    return pl.pallas_call(
        functools.partial(backward_kernel, tiles),
        grid=(tiles,),
        in_specs=[
            pl.BlockSpec((1, BLK), lambda b: (0, b)),
            pl.BlockSpec((seq_len, 1), lambda b: (0, 0)),
            pl.BlockSpec((2, 4 * BLK), lambda b: (0, 0)),
            rows,
            pl.BlockSpec((seq_len, PAIR), lambda b: (0, 1)),
            pl.BlockSpec((seq_len, PAIR), lambda b: (0, 2)),
            rows,
            pl.BlockSpec((2, BLK), lambda b: (0, b)),
        ],
        out_specs=[rows, whole, whole, pl.BlockSpec((2, 5, 2 * BLK), lambda b: (0, 0, 0))],
        out_shape=[
            result,
            result,
            result,
            jax.ShapeDtypeStruct((2, 5, 2 * BLK), jnp.float32),
        ],
        scratch_shapes=[
            pltpu.VMEM((2, BLK, (2 * tiles - 1) * BLK), jnp.float32),
            pltpu.VMEM((seq_len, PAIR), jnp.float32),
            pltpu.VMEM((seq_len, PAIR), jnp.float32),
            pltpu.VMEM((2, 5, BLK, BLK), jnp.float32),
            pltpu.VMEM((seq_len, BLK), jnp.float32),
            pltpu.VMEM((seq_len, BLK), jnp.float32),
        ],
        compiler_params=params(20),
        cost_estimate=cost(
            20 * seq_len * seq_len * PAIR, 16 * seq_len * PAIR, 2 * seq_len * seq_len
        ),
        name="attention_backward",
    )(segment[None, :], segment[:, None], band_back, qkv, qkv, qkv, grad_o, lse)


def one_hot_buckets(offset):
    return (bucket_index(offset)[..., None] == jnp.arange(BUCKETS, dtype=jnp.int32)).astype(
        jnp.float32
    )


def bias_bands(bias_rows):
    offset = jnp.arange(4 * BLK, dtype=jnp.int32) - 2 * BLK
    contract = (((1,), (1,)), ((), ()))
    ahead = lax.dot_general(bias_rows, one_hot_buckets(offset), contract, precision=PRECISE)
    behind = lax.dot_general(bias_rows, one_hot_buckets(-offset), contract, precision=PRECISE)
    return ahead, behind


def bucket_sums(diagonals):
    lane = jnp.arange(2 * BLK, dtype=jnp.int32)
    within = jnp.where(lane < BLK, lane, lane - 2 * BLK)
    away = (jnp.arange(5, dtype=jnp.int32) - 2) * BLK
    onehot = one_hot_buckets(-within[None, :] - away[:, None])
    return jnp.dot(diagonals.reshape(2, -1), onehot.reshape(-1, BUCKETS), precision=PRECISE)


CHIPS = 4
CORE, ACROSS, ALONG = 1, 2, 4
PLACES = ((6, 7), (0, 4), (5, 3), (1, 2))


def wide(values):
    return values.astype(jnp.float32)


def low(values):
    return values.astype(jnp.bfloat16)


def piece_rows(own_ref, piece, start, rows, total):
    base = (own_ref[0] ^ piece) * total + start
    return pl.ds(pl.multiple_of(base, rows), rows)


def gathered(refs):
    out = []
    for core in range(2):
        own, near_x, near_y, first, second = refs[5 * core : 5 * core + 5]
        out += [(core, 0, own), (2 + core, 0, near_x), (4 + core, 0, near_y)]
        out += [(6 + core, 0, first), (6 + core, first.shape[0], second)]
    return out


def join_slots(weight_ref, slots):
    for part in range(3):
        for index, slot in enumerate(slots):
            weight_ref[part * PAIR + index * DK : part * PAIR + (index + 1) * DK, :] = slot[
                part * DK : (part + 1) * DK, :
            ]


def norm_project_kernel(own_ref, gain_ref, slot_a, slot_b, *refs):
    hidden_ref, out_ref, weight_ref = refs[10:]
    total = refs[0].shape[0]
    for piece, start, ref in gathered(refs[:10]):
        values = wide(ref[...])
        scale = lax.rsqrt(jnp.mean(values * values, axis=-1, keepdims=True) + EPSILON)
        at = piece_rows(own_ref, piece, start, ref.shape[0], total)
        hidden_ref[at, :] = low(values * scale * gain_ref[...])
    join_slots(weight_ref, (slot_a, slot_b))
    for chunk in range(8 * total // BLK):
        at = slice(chunk * BLK, (chunk + 1) * BLK)
        out_ref[at, :] = low(nt(hidden_ref[at, :], weight_ref[...]))


VMEM = pl.BlockSpec(memory_space=pltpu.VMEM)
SMEM = pl.BlockSpec(memory_space=pltpu.SMEM)


def norm_project(own, gain, slots, pieces):
    rows, width = pieces[0].shape
    total, features = 8 * rows, 3 * PAIR
    return pl.pallas_call(
        norm_project_kernel,
        in_specs=[SMEM] + [VMEM] * 13,
        out_specs=[VMEM] * 3,
        out_shape=[
            jax.ShapeDtypeStruct((total, width), jnp.bfloat16),
            jax.ShapeDtypeStruct((total, features), jnp.bfloat16),
            jax.ShapeDtypeStruct((features, width), jnp.bfloat16),
        ],
        compiler_params=params(60),
        cost_estimate=cost(
            2 * total * width * features, 2 * (2 * total * width + features * (width + total))
        ),
        name="norm_project",
    )(own, gain[None, :], *slots, *pieces)


def project_kernel(hidden_ref, slot_a, slot_b, out_ref, weight_ref):
    @pl.when(pl.program_id(0) == 0)
    def _():
        join_slots(weight_ref, (slot_a, slot_b))

    out_ref[...] = low(nt(hidden_ref[...], weight_ref[...]))


def project(hidden, slots):
    total, width = hidden.shape
    features = 3 * PAIR
    slot = pl.BlockSpec((slots[0].shape[0], width), lambda b: (0, 0))
    return pl.pallas_call(
        project_kernel,
        grid=(total // BLK,),
        in_specs=[pl.BlockSpec((BLK, width), lambda b: (b, 0)), slot, slot],
        out_specs=[
            pl.BlockSpec((BLK, features), lambda b: (b, 0)),
            pl.BlockSpec((features, width), lambda b: (0, 0)),
        ],
        out_shape=[
            jax.ShapeDtypeStruct((total, features), jnp.bfloat16),
            jax.ShapeDtypeStruct((features, width), jnp.bfloat16),
        ],
        compiler_params=params(12),
        cost_estimate=cost(
            2 * total * width * features, 2 * (total * width + features * (width + total))
        ),
        name="project",
    )(hidden, *slots)


def spread_rows(core, own_ref, lefts, weight, out):
    total = lefts[0].shape[0] // 8
    half = total // 2
    for chip in range(CHIPS):
        at = piece_rows(own_ref, 2 * chip + core, 0, total, total)
        values = None
        for index, left in enumerate(lefts):
            term = nn(left[at, :], weight[index * PAIR : (index + 1) * PAIR, :])
            values = term if values is None else values + term
        for index, place in enumerate(PLACES[chip]):
            out[place * half : (place + 1) * half, :] = low(
                values[index * half : (index + 1) * half, :]
            )


def spread_kernel(core, counts, own_ref, *refs):
    lefts, rights = refs[: counts[0]], refs[counts[0] : counts[0] + counts[1]]
    out, weight = refs[-2:]
    start = 0
    for right in rights:
        weight[start : start + right.shape[0], :] = right[...]
        start += right.shape[0]
    spread_rows(core, own_ref, lefts, weight, out)


def spread(own, core, lefts, rights, limit):
    total, width = lefts[0].shape[0] // 2, rights[0].shape[1]
    depth = sum(right.shape[0] for right in rights)
    return pl.pallas_call(
        functools.partial(spread_kernel, core, (len(lefts), len(rights))),
        in_specs=[SMEM] + [VMEM] * (len(lefts) + len(rights)),
        out_specs=VMEM,
        out_shape=jax.ShapeDtypeStruct((total, width), jnp.bfloat16),
        scratch_shapes=[pltpu.VMEM((depth, width), jnp.bfloat16)],
        compiler_params=params(limit),
        cost_estimate=cost(
            2 * total * width * depth, 2 * (total * width + depth * (width + total))
        ),
        name="spread",
    )(own, *lefts, *rights)


def last_kernel(own_ref, gain_ref, hidden_ref, *refs):
    lefts, rights = refs[:6], refs[6:8]
    out, slot_a, slot_b, sum_ref, weight = refs[8:]
    for index, right in enumerate(rights):
        weight[3 * PAIR * index : 3 * PAIR * (index + 1), :] = right[...]
    spread_rows(0, own_ref, lefts, weight, out)
    width = out.shape[1]
    for start in range(0, width, 512):
        cols = slice(start, start + 512)
        total = None
        for part in range(3):
            grad = tn(lefts[part][...], hidden_ref[:, cols])
            slot_a[part * DK : (part + 1) * DK, cols] = low(grad[:DK])
            slot_b[part * DK : (part + 1) * DK, cols] = low(grad[DK:])
            at = slice(part * PAIR, (part + 1) * PAIR)
            term = jnp.sum(grad * wide(weight[at, cols]), axis=0, keepdims=True)
            total = term if total is None else total + term
        sum_ref[:, cols] = total / gain_ref[:, cols]


def last(own, gain, hidden, lefts, rights):
    total, width = hidden.shape
    return pl.pallas_call(
        last_kernel,
        in_specs=[SMEM] + [VMEM] * 10,
        out_specs=[VMEM] * 4,
        out_shape=[
            jax.ShapeDtypeStruct((total // 2, width), jnp.bfloat16),
            jax.ShapeDtypeStruct((3 * DK, width), jnp.bfloat16),
            jax.ShapeDtypeStruct((3 * DK, width), jnp.bfloat16),
            jax.ShapeDtypeStruct((1, width), jnp.float32),
        ],
        scratch_shapes=[pltpu.VMEM((6 * PAIR, width), jnp.bfloat16)],
        compiler_params=params(56),
        cost_estimate=cost(12 * total * width * PAIR, 6 * total * width),
        name="last",
    )(own, gain[None, :], hidden, *lefts, *rights)


def heads_back_kernel(own_ref, weight_a0, weight_a1, weight_b0, weight_b1, mixed_a, mixed_b, *refs):
    heads_a, heads_b, grad_a, grad_b, whole, weight = refs[10:]
    total = refs[0].shape[0]
    for piece, start, ref in gathered(refs[:10]):
        whole[piece_rows(own_ref, piece, start, ref.shape[0], total), :] = ref[...]
    for index, ref in enumerate((weight_a0, weight_a1, weight_b0, weight_b1)):
        weight[index * DK : (index + 1) * DK, :] = ref[...]
    for chunk in range(8 * total // BLK):
        at = slice(chunk * BLK, (chunk + 1) * BLK)
        heads = low(nt(whole[at, :], weight[...]))
        heads_a[at, :] = heads[:, :PAIR]
        heads_b[at, :] = heads[:, PAIR:]
    grad_a[...] = low(tn(mixed_a[...], whole[...]))
    grad_b[...] = low(tn(mixed_b[...], whole[...]))


def heads_back(own, weights, mixed, pieces):
    rows, width = pieces[0].shape
    total = 8 * rows
    outs = pl.pallas_call(
        heads_back_kernel,
        in_specs=[SMEM] + [VMEM] * 16,
        out_specs=[VMEM] * 4,
        out_shape=[jax.ShapeDtypeStruct((total, PAIR), jnp.bfloat16)] * 2
        + [jax.ShapeDtypeStruct((PAIR, width), jnp.bfloat16)] * 2,
        scratch_shapes=[
            pltpu.VMEM((total, width), jnp.bfloat16),
            pltpu.VMEM((2 * PAIR, width), jnp.bfloat16),
        ],
        compiler_params=params(20),
        cost_estimate=cost(8 * total * width * PAIR, 2 * total * width),
        name="heads_back",
    )(own, *weights, *mixed, *pieces)
    return outs[:2], outs[2:]


def qkv_grad_kernel(gain_ref, hidden_ref, dq_ref, dk_ref, dv_ref, weight_ref, slot_a, slot_b, sum_ref):
    total = None
    for part, ref in enumerate((dq_ref, dk_ref, dv_ref)):
        grad = tn(ref[...], hidden_ref[...])
        slot_a[part * DK : (part + 1) * DK, :] = low(grad[:DK])
        slot_b[part * DK : (part + 1) * DK, :] = low(grad[DK:])
        at = slice(part * PAIR, (part + 1) * PAIR)
        term = jnp.sum(grad * wide(weight_ref[at, :]), axis=0, keepdims=True)
        total = term if total is None else total + term
    sum_ref[...] = total / gain_ref[...]


def qkv_grad(gain, hidden, dq, dk, dv, weight):
    total, width = hidden.shape
    cols = 512
    col = pl.BlockSpec((1, cols), lambda c: (0, c))
    back = pl.BlockSpec((total, PAIR), lambda c: (0, 0))
    slot = pl.BlockSpec((3 * DK, cols), lambda c: (0, c))
    return pl.pallas_call(
        qkv_grad_kernel,
        grid=(width // cols,),
        in_specs=[
            col,
            pl.BlockSpec((total, cols), lambda c: (0, c)),
            back,
            back,
            back,
            pl.BlockSpec((3 * PAIR, cols), lambda c: (0, c)),
        ],
        out_specs=[slot, slot, col],
        out_shape=[
            jax.ShapeDtypeStruct((3 * DK, width), jnp.bfloat16),
            jax.ShapeDtypeStruct((3 * DK, width), jnp.bfloat16),
            jax.ShapeDtypeStruct((1, width), jnp.float32),
        ],
        compiler_params=params(12),
        cost_estimate=cost(6 * total * width * PAIR, 2 * total * width + 12 * PAIR * width),
        name="qkv_grad",
    )(gain[None, :], hidden, dq, dk, dv, weight)


def assemble_kernel(own, *refs):
    outs = refs[6:]
    units = own.shape[0] // 3
    half = units // 2
    for part, weight in enumerate(outs):
        for chip in range(CHIPS):
            for index, place in enumerate(PLACES[chip]):
                ref, start = own, part * units + index * half
                if chip:
                    ref = refs[2 * chip - 2]
                    if start >= 3 * half:
                        ref, start = refs[2 * chip - 1], start - 3 * half
                weight[place * half : (place + 1) * half, :] = ref[start : start + half, :]


def assemble(own, *stacks):
    rows, width = own.shape
    return pl.pallas_call(
        assemble_kernel,
        in_specs=[VMEM] * 7,
        out_specs=[VMEM] * 3,
        out_shape=[jax.ShapeDtypeStruct((CHIPS * rows // 3, width), jnp.bfloat16)] * 3,
        compiler_params=params(20),
        cost_estimate=cost(0, 16 * rows * width),
        name="assemble",
    )(own, *stacks)


def feed_kernel(gate_w, up_w, down_w, *refs):
    hidden, cot, outs = refs[:2], refs[2:4], refs[4:]
    inner_ref, dgate_ref, dup_ref, grad_own, grad_other, out_own, out_other = outs
    rows = hidden[0].shape[0]
    values = jnp.concatenate([hidden[0][...], hidden[1][...]], axis=0)
    grads = jnp.concatenate([cot[0][...], cot[1][...]], axis=0)
    gate = nt(values, gate_w[...])
    up = nt(values, up_w[...])
    grad_m = nt(grads, down_w[...])
    square = gate * gate
    bend = jnp.tanh(GELU_SCALE * gate * (1.0 + GELU_CUBE * square))
    part = 0.5 * (1.0 + bend)
    act = gate * part
    slope = part + 0.5 * gate * (1.0 - bend * bend) * (
        GELU_SCALE * (1.0 + 3.0 * GELU_CUBE * square)
    )
    inner = low(act * up)
    inner_ref[...] = inner
    dgate = low(grad_m * up * slope)
    dup = low(grad_m * act)
    dgate_ref[...] = dgate
    dup_ref[...] = dup
    grad_h = low(nn(dgate, gate_w[...]) + nn(dup, up_w[...]))
    grad_own[...] = grad_h[:rows]
    grad_other[...] = grad_h[rows:]
    result = low(nn(inner, down_w[...]))
    out_own[...] = result[:rows]
    out_other[...] = result[rows:]


def feed(weights, hidden, cot):
    rows, width = hidden[0].shape
    total, units = 2 * rows, weights[0].shape[0]
    return pl.pallas_call(
        feed_kernel,
        in_specs=[VMEM] * 7,
        out_specs=[VMEM] * 7,
        out_shape=[jax.ShapeDtypeStruct((total, units), jnp.bfloat16)] * 3
        + [jax.ShapeDtypeStruct((rows, width), jnp.bfloat16)] * 4,
        compiler_params=params(24),
        cost_estimate=cost(12 * total * width * units, 2 * 4 * (total + units) * width),
        name="feed",
    )(*weights, *hidden, *cot)


def feed_grad_kernel(terms, *refs):
    lefts, pieces = refs[: 4 * terms], refs[4 * terms : 4 * terms + 8]
    outs, right = refs[-4:-1], refs[-1]
    rows = pieces[0].shape[0]
    for index, piece in enumerate(pieces):
        right[index * rows : (index + 1) * rows, :] = piece[...]
    for term in range(terms):
        left = jnp.concatenate([ref[...] for ref in lefts[4 * term : 4 * term + 4]], axis=0)
        grad = low(tn(left, right[...]))
        start = 0
        for out in outs:
            size = out.shape[0] // terms
            out[term * size : (term + 1) * size, :] = grad[start : start + size]
            start += size


def feed_grad(lefts, pieces):
    terms = len(lefts)
    rows, width = pieces[0].shape
    units = lefts[0][0].shape[1]
    return pl.pallas_call(
        functools.partial(feed_grad_kernel, terms),
        in_specs=[VMEM] * (4 * terms + 8),
        out_specs=[VMEM] * 3,
        out_shape=[
            jax.ShapeDtypeStruct((terms * units // part, width), jnp.bfloat16)
            for part in (4, 4, 2)
        ],
        scratch_shapes=[pltpu.VMEM((8 * rows, width), jnp.bfloat16)],
        compiler_params=params(48),
        cost_estimate=cost(16 * terms * rows * width * units, 24 * rows * width),
        name="feed_grad",
    )(*[value for left in lefts for value in left], *pieces)


def second_kernel(terms, keep, from_x, from_y, to_x, to_y):
    size = to_x.shape[0] // terms
    for term in range(terms):
        out = slice(term * size, (term + 1) * size)
        base = 4 * term * size
        pair = 2 * term * size
        to_x[out, :] = low(wide(keep[base : base + size, :]) + wide(from_y[pair : pair + size, :]))
        to_y[out, :] = low(
            wide(keep[base + size : base + 2 * size, :])
            + wide(from_x[pair + size : pair + 2 * size, :])
        )


def second(terms, keep, from_x, from_y):
    shape = jax.ShapeDtypeStruct((from_x.shape[0] // 2, from_x.shape[1]), jnp.bfloat16)
    return pl.pallas_call(
        functools.partial(second_kernel, terms),
        in_specs=[VMEM] * 3,
        out_specs=[VMEM] * 2,
        out_shape=[shape, shape],
        compiler_params=params(12),
        cost_estimate=cost(0, 6 * from_x.shape[0] * from_x.shape[1]),
        name="second",
    )(keep, from_x, from_y)


def totals_kernel(terms, *refs):
    outs = refs[5 * len(terms) :]
    done = 0
    for index, count in enumerate(terms):
        keep, from_x, from_y, second_x, second_y = refs[5 * index : 5 * index + 5]
        for term in range(count):
            out = outs[done]
            done += 1
            size = out.shape[0] // 2
            base, pair, one = 4 * term * size, 2 * term * size, term * size
            out[:size, :] = (
                wide(keep[base + 2 * size : base + 3 * size, :])
                + wide(from_x[pair : pair + size, :])
                + wide(second_y[one : one + size, :])
            )
            out[size:, :] = (
                wide(keep[base + 3 * size : base + 4 * size, :])
                + wide(from_y[pair + size : pair + 2 * size, :])
                + wide(second_x[one : one + size, :])
            )


def totals(terms, *groups):
    shapes = [
        (2 * group[3].shape[0] // count, group[3].shape[1])
        for count, group in zip(terms, groups)
        for _ in range(count)
    ]
    return pl.pallas_call(
        functools.partial(totals_kernel, terms),
        in_specs=[VMEM] * (5 * len(groups)),
        out_specs=[VMEM] * len(shapes),
        out_shape=[jax.ShapeDtypeStruct(shape, jnp.float32) for shape in shapes],
        compiler_params=params(56),
        cost_estimate=cost(0, 10 * sum(rows * width for rows, width in shapes)),
        name="totals",
    )(*[value for group in groups for value in group])


def sends_kernel(own_ref, other_ref, to_x, to_y, keep):
    size = to_x.shape[0]
    to_x[...] = low(wide(own_ref[:size, :]) + wide(other_ref[:size, :]))
    to_y[...] = low(wide(own_ref[size : 2 * size, :]) + wide(other_ref[size : 2 * size, :]))
    keep[...] = wide(own_ref[2 * size :, :]) + wide(other_ref[2 * size :, :])


def sends(own, other, limit):
    rows, width = own.shape
    shape = jax.ShapeDtypeStruct((rows // 4, width), jnp.bfloat16)
    return pl.pallas_call(
        sends_kernel,
        in_specs=[VMEM] * 2,
        out_specs=[VMEM] * 3,
        out_shape=[shape, shape, jax.ShapeDtypeStruct((rows // 2, width), jnp.float32)],
        compiler_params=params(limit),
        cost_estimate=cost(0, 7 * rows * width),
        name="sends",
    )(own, other)


def fence(*values):
    return lax.optimization_barrier(values)


def swap(values, bits):
    return lax.ppermute(values, "seq", [(i, i ^ bits) for i in range(2 * CHIPS)])


def ring(values, step):
    n = lax.axis_size("fsdp")
    return lax.ppermute(values, "fsdp", [(i, (i + step) % n) for i in range(n)])


def line_order(slots):
    n = len(slots)
    order = (lax.axis_index("fsdp") - jnp.arange(n, dtype=jnp.int32)) % n
    return jnp.stack(slots)[order]


def both(values, other, bits):
    high = (lax.axis_index("seq") & bits) != 0
    return jnp.concatenate(
        [jnp.where(high, other, values), jnp.where(high, values, other)], axis=0
    )


def halves(values, bits):
    high = (lax.axis_index("seq") & bits) != 0
    size = values.shape[0] // 2
    lower, upper = values[:size], values[size:]
    return jnp.where(high, upper, lower), jnp.where(high, lower, upper)


def plane_total(keep, from_x, from_y, second_x, second_y):
    size = keep.shape[0] // 4
    first = wide(keep[2 * size : 3 * size]) + wide(from_x[:size]) + wide(second_y)
    second = wide(keep[3 * size :]) + wide(from_y[size:]) + wide(second_x)
    return jnp.concatenate([first, second], axis=0)


def add(*values):
    return functools.reduce(lambda left, right: left + right, [wide(value) for value in values])


def per_device(
    tokens,
    starts,
    first_gain,
    query_weight,
    key_weight,
    value_weight,
    output_weight,
    bias_table,
    second_gain,
    gate_weight,
    up_weight,
    down_weight,
    cotangent,
):
    index = lax.axis_index("seq")[None]
    own = tokens[0]
    half = own.shape[0] // 2
    grad_out = cotangent[0]
    rows = first_gain.shape[0]
    buckets = bias_table.shape[0]
    qkv0 = low(
        jnp.concatenate([query_weight, key_weight, value_weight, output_weight], axis=0)
    )
    small = low(jnp.concatenate([first_gain, second_gain, bias_table]))
    own, qkv0, small, gate_weight, up_weight, down_weight = fence(
        own, qkv0, small, gate_weight, up_weight, down_weight
    )

    tok_x, tok_y = swap(own, ACROSS), swap(own, ALONG)
    small_slots = [small] + [ring(small, k) for k in range(1, 4)]
    small_slots, own, qkv0, gate_weight, up_weight, down_weight = fence(
        small_slots, own, qkv0, gate_weight, up_weight, down_weight
    )
    qkv1 = ring(qkv0, 1)
    gain_part = line_order([value[: 2 * rows] for value in small_slots]).reshape(-1)
    packed = jnp.concatenate([gain_part, low(starts[0])])[None]
    packed = both(packed, swap(packed, CORE), CORE)
    packed, gate_weight, up_weight, down_weight = fence(
        packed, gate_weight, up_weight, down_weight
    )
    near = both(packed, swap(packed, ACROSS), ACROSS)
    far = both(swap(packed, ALONG), swap(packed, ALONG | ACROSS), ACROSS)
    packed = both(near, far, ALONG)
    packed, tok_x, tok_y, gate_weight, up_weight, down_weight = fence(
        packed, tok_x, tok_y, gate_weight, up_weight, down_weight
    )

    tok_d1, tok_d2 = swap(tok_y[:half], ACROSS), swap(tok_x[half:], ALONG)
    tok_cx, tok_cy = swap(tok_x, CORE), swap(tok_y, CORE)
    gain_count = gain_part.shape[0]
    gains = wide(packed[:, :gain_count]).reshape(-1, 4, 2, rows)
    gain_first = gains[:, :, 0].reshape(-1)
    gain_second = gains[:, :, 1].reshape(-1)
    segment = jnp.cumsum(packed[:, gain_count:].reshape(-1).astype(jnp.int32), dtype=jnp.int32)
    tables = [wide(value[2 * rows :]) for value in small_slots]
    bands = [bias_bands(jnp.stack(tables[2 * p : 2 * p + 2])) for p in range(2)]
    tok_d1, tok_d2, tok_cx, tok_cy, segment, gain_first, gain_second, bands, own = fence(
        tok_d1, tok_d2, tok_cx, tok_cy, segment, gain_first, gain_second, bands, own
    )

    tok_c, tok_c1, tok_c2 = swap(own, CORE), swap(tok_d1, CORE), swap(tok_d2, CORE)
    feed0 = low(jnp.concatenate([gate_weight, up_weight, down_weight], axis=0))
    tok_c, tok_c1, tok_c2, feed0, qkv1 = fence(tok_c, tok_c1, tok_c2, feed0, qkv1)

    qkv2 = ring(qkv1, 1)
    feed_half = feed0.shape[0] // 2
    feed_top, feed_low = feed0[:feed_half], feed0[feed_half:]
    feed_xl, feed_yt = swap(feed_low, ACROSS), swap(feed_top, ALONG)
    feed_top, feed_low = fence(feed_top, feed_low)
    feed_xt, feed_yl = swap(feed_top, ACROSS), swap(feed_low, ALONG)
    tok_pieces = (own, tok_x, tok_y, tok_d1, tok_d2, tok_c, tok_cx, tok_cy, tok_c1, tok_c2)
    hidden_one, qkv_a, weight_a = norm_project(index, gain_first, (qkv0, qkv1), tok_pieces)
    hidden_one, qkv_a, weight_a, qkv2, grad_out, feed_xl, feed_yt = fence(
        hidden_one, qkv_a, weight_a, qkv2, grad_out, feed_xl, feed_yt
    )

    qkv3 = ring(qkv2, 1)
    feed_dt, feed_dl = swap(feed_yt, ACROSS), swap(feed_xl, ALONG)
    mixed_a, lse_a = attention_forward(qkv_a, segment, bands[0][0])
    out0, out1, out2 = (value[3 * DK :] for value in (qkv0, qkv1, qkv2))
    mixed_a, lse_a, hidden_one, qkv3, feed_xt, feed_yl, out0, out1, out2 = fence(
        mixed_a, lse_a, hidden_one, qkv3, feed_xt, feed_yl, out0, out1, out2
    )

    cot1 = ring(grad_out, 1)
    qkv_b, weight_b = project(hidden_one, (qkv2, qkv3))
    out3 = qkv3[3 * DK :]
    mixed_b, lse_b = attention_forward(qkv_b, segment, bands[1][0])
    mixed_b, lse_b, out3, grad_out = fence(mixed_b, lse_b, out3, grad_out)
    cot_c0 = swap(grad_out, CORE)
    out_slots = (out0, out1, out2, out3)
    mixed = (mixed_a, mixed_b)
    part_other = spread(index, 1, mixed, out_slots, 14)
    part_other, mixed, feed_dt, feed_dl, cot1, cot_c0 = fence(
        part_other, mixed, feed_dt, feed_dl, cot1, cot_c0
    )
    part_other, cot2, cot_c1 = swap(part_other, CORE), ring(cot1, 1), swap(cot1, CORE)
    part_own = spread(index, 0, mixed, out_slots, 14)
    part_own, part_other, cot_c1 = fence(part_own, part_other, cot_c1)

    send_x, send_y, keep = sends(part_own, part_other, 12)
    send_x, send_y, keep = fence(send_x, send_y, keep)
    from_x, from_y = swap(send_x, ACROSS), swap(send_y, ALONG)
    weights = assemble(feed0, feed_xt, feed_xl, feed_yt, feed_yl, feed_dt, feed_dl)
    from_x, from_y, weights, cot2 = fence(from_x, from_y, weights, cot2)
    send_x, send_y = fence(*second(1, keep, from_x, from_y))
    second_x, second_y = swap(send_x, ACROSS), swap(send_y, ALONG)
    cot3, cot_c2 = ring(cot2, 1), swap(cot2, CORE)
    second_x, second_y, cot3, cot_c2 = fence(second_x, second_y, cot3, cot_c2)
    inputs = wide(own)
    resid_one = inputs + plane_total(keep, from_x, from_y, second_x, second_y)

    scale_two = lax.rsqrt(jnp.mean(resid_one * resid_one, axis=-1, keepdims=True) + EPSILON)
    normed_two = resid_one * scale_two
    hid0 = low(normed_two * gain_second)
    hid0, resid_one, scale_two = fence(hid0, resid_one, scale_two)

    hid1, hid_c0, cot_c3 = ring(hid0, 1), swap(hid0, CORE), swap(cot3, CORE)
    hid_c0, cot_c3 = fence(hid_c0, cot_c3)
    feed_a = feed(weights, (hid0, hid_c0), (grad_out, cot_c0))
    feed_a, hid1 = fence(feed_a, hid1)
    hid2, hid_c1 = ring(hid1, 1), swap(hid1, CORE)
    hid_c1, feed_a = fence(hid_c1, feed_a)
    grad_c0, out_c0 = swap(feed_a[4], CORE), swap(feed_a[6], CORE)
    feed_b = feed(weights, (hid1, hid_c1), (cot1, cot_c1))
    feed_b, hid2, grad_c0, out_c0 = fence(feed_b, hid2, grad_c0, out_c0)
    hid3, hid_c2 = ring(hid2, 1), swap(hid2, CORE)
    hid_c2, feed_b = fence(hid_c2, feed_b)
    grad_c1, out_c1 = swap(feed_b[4], CORE), swap(feed_b[6], CORE)
    feed_c = feed(weights, (hid2, hid_c2), (cot2, cot_c2))
    feed_c, hid3, grad_c1, out_c1 = fence(feed_c, hid3, grad_c1, out_c1)
    hid_c3 = swap(hid3, CORE)
    dh = ring(low(add(feed_b[3], grad_c1)), 1)
    hid_c3, feed_c = fence(hid_c3, feed_c)
    grad_c2, out_c2 = swap(feed_c[4], CORE), swap(feed_c[6], CORE)
    feed_d = feed(weights, (hid3, hid_c3), (cot3, cot_c3))
    feed_d, dh, grad_c2, out_c2 = fence(feed_d, dh, grad_c2, out_c2)
    dh = ring(low(add(feed_c[3], grad_c2, dh)), 1)
    grad_c3, out_c3 = swap(feed_d[4], CORE), swap(feed_d[6], CORE)
    parts = (feed_a, feed_b, feed_c, feed_d)
    hid_pieces = (hid0, hid_c0, hid1, hid_c1, hid2, hid_c2, hid3, hid_c3)
    cot_pieces = (grad_out, cot_c0, cot1, cot_c1, cot2, cot_c2, cot3, cot_c3)
    grad_down = feed_grad([[part[0] for part in parts]], cot_pieces)
    grad_down, dh, grad_c3, out_c3, hid_pieces = fence(grad_down, dh, grad_c3, out_c3, hid_pieces)

    dh, out_sum = ring(low(add(feed_d[3], grad_c3, dh)), 1), low(add(feed_b[5], out_c1))
    out_sum = ring(out_sum, 1)
    down_x, down_y, down_keep = grad_down
    down_fx, down_fy = swap(down_x, ACROSS), swap(down_y, ALONG)
    grad_both = feed_grad(
        [[part[1] for part in parts], [part[2] for part in parts]], hid_pieces
    )
    dh, grad_both = fence(dh, grad_both)

    grad_hidden_two = add(feed_a[3], grad_c0, dh)
    normed_two = resid_one * scale_two
    shared = grad_hidden_two * gain_second
    grad_resid = wide(grad_out) + scale_two * (
        shared - normed_two * jnp.mean(shared * normed_two, axis=-1, keepdims=True)
    )
    branch = low(grad_resid)
    gain_two_rows = jnp.sum(grad_hidden_two * normed_two, axis=0)
    branch, grad_resid, gain_two_rows, down_fx, down_fy = fence(
        branch, grad_resid, gain_two_rows, down_fx, down_fy
    )

    br_x, br_y, br_c = swap(branch, ACROSS), swap(branch, ALONG), swap(branch, CORE)
    down_x, down_y = second(1, down_keep, down_fx, down_fy)
    out_send = low(add(feed_c[5], out_c2, out_sum))
    br_x, br_y, br_c, down_x, down_y, out_send = fence(
        br_x, br_y, br_c, down_x, down_y, out_send
    )
    br_d1, br_d2 = swap(br_y[:half], ACROSS), swap(br_x[half:], ALONG)
    br_cx, br_cy = swap(br_x, CORE), swap(br_y, CORE)
    out_sum = ring(out_send, 1)
    br_d1, br_d2, br_cx, br_cy = fence(br_d1, br_d2, br_cx, br_cy)

    br_c1, br_c2 = swap(br_d1, CORE), swap(br_d2, CORE)
    down_sx, down_sy = swap(down_x, ACROSS), swap(down_y, ALONG)
    pieces = (branch, br_x, br_y, br_d1, br_d2, br_c, br_cx, br_cy, br_c1, br_c2)
    grad_heads, grad_outs = heads_back(index, out_slots, mixed, pieces)
    grad_heads, grad_outs, grad_both, down_sx, down_sy, out_sum = fence(
        grad_heads, grad_outs, grad_both, down_sx, down_sy, out_sum
    )

    go0, go1 = grad_outs[0][:DK], grad_outs[0][DK:]
    go2, go3 = grad_outs[1][:DK], grad_outs[1][DK:]
    both_x, both_y, both_keep = grad_both
    both_fx, both_fy = swap(both_x, ACROSS), swap(both_y, ALONG)
    out_sum = ring(low(add(feed_d[5], out_c3, out_sum)), 1)
    dq_b, dk_b, dv_b, diag_b = attention_backward(
        qkv_b, grad_heads[1], lse_b, segment, bands[1][1]
    )
    dq_b, dk_b, dv_b, diag_b, go3, out_sum = fence(dq_b, dk_b, dv_b, diag_b, go3, out_sum)

    go_sum = ring(go3, -1)
    gq2, gq3, sums_b = qkv_grad(gain_first, hidden_one, dq_b, dk_b, dv_b, weight_b)
    gq2, gq3, sums_b, both_fx, both_fy, go_sum = fence(
        gq2, gq3, sums_b, both_fx, both_fy, go_sum
    )
    both_x, both_y = second(2, both_keep, both_fx, both_fy)
    go_send = low(add(go2, go_sum))
    gq2, gq3, qkv_a, both_x, both_y, go_send = fence(gq2, gq3, qkv_a, both_x, both_y, go_send)

    gq, go_sum = ring(gq3, -1), ring(go_send, -1)
    both_sx, both_sy = swap(both_x, ACROSS), swap(both_y, ALONG)
    dq_a, dk_a, dv_a, diag_a = attention_backward(
        qkv_a, grad_heads[0], lse_a, segment, bands[0][1]
    )
    dq_a, dk_a, dv_a, diag_a, gq, both_sx, both_sy, go_sum = fence(
        dq_a, dk_a, dv_a, diag_a, gq, both_sx, both_sy, go_sum
    )

    gq = ring(low(add(gq2, gq)), -1)
    lefts = (dq_a, dk_a, dv_a, dq_b, dk_b, dv_b)
    back_other = spread(index, 1, lefts, (weight_a, weight_b), 14)
    back_other, lefts = fence(back_other, lefts)
    back_other = swap(back_other, CORE)
    back_own, gq0, gq1, sums_a = last(index, gain_first, hidden_one, lefts, (weight_a, weight_b))
    back_own, back_other, gq0, gq1, sums_a = fence(back_own, back_other, gq0, gq1, sums_a)
    send_x, send_y, keep = sends(back_own, back_other, 56)
    gain_rows = jnp.stack([(sums_a + sums_b)[0], gain_two_rows]).reshape(2, 2, 2, 2, 4, -1)
    gain_rows = jnp.transpose(gain_rows, (3, 1, 2, 4, 0, 5)).reshape(2 * CHIPS, -1)
    send_x, send_y, keep, gq1, gain_rows, go_sum = fence(
        send_x, send_y, keep, gq1, gain_rows, go_sum
    )

    from_x, from_y = swap(send_x, ACROSS), swap(send_y, ALONG)
    gain_keep, gain_send = halves(gain_rows, CORE)
    gain_rows = gain_keep + swap(gain_send, CORE)
    gain_rows, gq1 = fence(gain_rows, gq1)
    gq_send = low(add(gq1, gq))
    gq_first = ring(gq_send[: 2 * DK], -1)
    gain_keep, gain_send = halves(gain_rows, ALONG)
    gain_rows = gain_keep + swap(gain_send, ALONG)
    last_send = jnp.concatenate([gq_send[2 * DK :], low(add(go1, go_sum))], axis=0)
    from_x, from_y, gain_rows, gq_first, last_send = fence(
        from_x, from_y, gain_rows, gq_first, last_send
    )
    send_x, send_y = second(1, keep, from_x, from_y)
    second_x, second_y = swap(send_x, ACROSS), swap(send_y, ALONG)
    gq_last = ring(last_send, -1)
    gain_keep, gain_send = halves(gain_rows, ACROSS)
    gain_rows = gain_keep + swap(gain_send, ACROSS)
    late = (down_keep, both_keep, resid_one, diag_a, gq_first, go0, gq0, out_sum)
    second_x, second_y, gain_rows, late = fence(second_x, second_y, gain_rows, late)
    down_keep, both_keep, resid_one, diag_a, gq_first, go0, gq0, out_sum = late
    tables_a, tables_b = bucket_sums(diag_a), bucket_sums(diag_b)
    table_slots = (tables_a[0], tables_a[1], tables_b[0], tables_b[1])
    gain_slots = line_order(list(gain_rows.reshape(4, -1)))
    sums = [jnp.concatenate([gain_slots[k], table_slots[k]]) for k in range(4)]
    sums = sums[0] + sum(ring(sums[k], -k) for k in range(1, 4))
    grad_down_w, grad_gate_w, grad_up_w = totals(
        (1, 2),
        (down_keep, down_fx, down_fy, down_sx, down_sy),
        (both_keep, both_fx, both_fy, both_sx, both_sy),
    )
    layer_out = low(resid_one + add(feed_a[5], out_c0, out_sum))
    grad_hidden_one = plane_total(keep, from_x, from_y, second_x, second_y)
    scale_one = lax.rsqrt(jnp.mean(inputs * inputs, axis=-1, keepdims=True) + EPSILON)
    normed_one = inputs * scale_one
    shared = grad_hidden_one * gain_first
    grad_tokens = low(
        grad_resid
        + scale_one * (shared - normed_one * jnp.mean(shared * normed_one, axis=-1, keepdims=True))
    )
    gq_last, sums = fence(gq_last, sums)
    grad_q, grad_k = add(gq0[:DK], gq_first[:DK]), add(gq0[DK : 2 * DK], gq_first[DK:])
    grad_v, grad_output_w = add(gq0[2 * DK :], gq_last[:DK]), add(go0, gq_last[DK:])
    return (
        layer_out[None],
        grad_tokens[None],
        sums[:rows],
        grad_q,
        grad_k,
        grad_v,
        grad_output_w,
        sums[2 * rows :],
        sums[rows : 2 * rows],
        grad_gate_w,
        grad_up_w,
        grad_down_w,
    )


def rms_norm(values, gain):
    return values * lax.rsqrt(jnp.mean(values * values, axis=-1, keepdims=True) + EPSILON) * gain


def gated_gelu(gate, up_part):
    return jax.nn.gelu(gate, approximate=True) * up_part


def gather_rows(values):
    return lax.all_gather(values, "seq", axis=0, tiled=True)


def scatter_rows(values):
    return lax.psum_scatter(
        values.astype(jnp.bfloat16), "seq", scatter_dimension=0, tiled=True
    ).astype(jnp.float32)


def per_device_general(
    tokens,
    starts,
    first_gain,
    query_weight,
    key_weight,
    value_weight,
    output_weight,
    bias_table,
    second_gain,
    gate_weight,
    up_weight,
    down_weight,
    cotangent,
):
    segment = jnp.cumsum(lax.all_gather(starts, "seq", axis=1, tiled=True)[0], dtype=jnp.int32)
    inputs = tokens[0].astype(jnp.float32)
    grad_out = cotangent[0]
    head_count = H // lax.axis_size("seq")
    head_first = lax.axis_index("seq") * head_count
    query_low = query_weight.astype(jnp.bfloat16)
    key_low = key_weight.astype(jnp.bfloat16)
    value_low = value_weight.astype(jnp.bfloat16)
    output_low = output_weight.astype(jnp.bfloat16)
    gate_low = gate_weight.astype(jnp.bfloat16)
    up_low = up_weight.astype(jnp.bfloat16)
    down_low = down_weight.astype(jnp.bfloat16)
    first_low = first_gain.astype(jnp.bfloat16)
    second_low = second_gain.astype(jnp.bfloat16)
    table_low = bias_table.astype(jnp.bfloat16)
    query_part, key_part, value_part, output_part, gate_part, up_rows, down_part = (
        lax.all_gather(query_low, "fsdp", axis=0, tiled=True),
        lax.all_gather(key_low, "fsdp", axis=0, tiled=True),
        lax.all_gather(value_low, "fsdp", axis=0, tiled=True),
        lax.all_gather(output_low, "fsdp", axis=0, tiled=True),
        lax.all_gather(gate_low, "fsdp", axis=0, tiled=True),
        lax.all_gather(up_low, "fsdp", axis=0, tiled=True),
        lax.all_gather(down_low, "fsdp", axis=0, tiled=True),
    )
    gain_one, gain_two, table_full = (
        lax.all_gather(first_low, ("seq", "fsdp"), axis=0, tiled=True),
        lax.all_gather(second_low, ("seq", "fsdp"), axis=0, tiled=True),
        lax.all_gather(table_low, ("seq", "fsdp"), axis=0, tiled=True),
    )
    gain_first = gain_one.astype(jnp.float32)
    gain_second = gain_two.astype(jnp.float32)
    bias_rows = lax.dynamic_slice_in_dim(
        table_full.astype(jnp.float32).reshape(H, BUCKETS), head_first, head_count, 0
    )
    hidden_one = rms_norm(inputs, gain_first).astype(jnp.bfloat16)
    hidden_all = gather_rows(hidden_one)
    query_head = (
        low(nt(hidden_all, query_part))
    )
    key_head = (
        low(nt(hidden_all, key_part))
    )
    value_head = (
        low(nt(hidden_all, value_part))
    )
    pairs = head_count // 2
    pair = [slice(index * PAIR, (index + 1) * PAIR) for index in range(pairs)]
    bands = [bias_bands(bias_rows[2 * index : 2 * index + 2]) for index in range(pairs)]
    qkv = [
        jnp.concatenate([query_head[:, at], key_head[:, at], value_head[:, at]], axis=1)
        for at in pair
    ]
    forward = [attention_forward(qkv[i], segment, bands[i][0]) for i in range(pairs)]
    mixed = jnp.concatenate([out for out, _ in forward], axis=1)
    resid_one = inputs + scatter_rows(nn(mixed, output_part))
    hidden_two = rms_norm(resid_one, gain_second).astype(jnp.bfloat16)
    hidden_two_all = gather_rows(hidden_two)
    gate = nt(hidden_two_all, gate_part)
    up_part = nt(hidden_two_all, up_rows)
    inner = gated_gelu(gate, up_part).astype(jnp.bfloat16)
    layer_out = (resid_one + scatter_rows(nn(inner, down_part))).astype(jnp.bfloat16)
    grad_out_all = gather_rows(grad_out)
    grad_inner = nt(grad_out_all, down_part)
    grad_down = tn(inner, grad_out_all)
    grad_gate, grad_up = jax.vjp(gated_gelu, gate, up_part)[1](grad_inner)
    grad_gate = grad_gate.astype(jnp.bfloat16)
    grad_up = grad_up.astype(jnp.bfloat16)
    grad_gate_w = tn(grad_gate, hidden_two_all)
    grad_up_w = tn(grad_up, hidden_two_all)
    grad_hidden_two = scatter_rows(nn(grad_gate, gate_part) + nn(grad_up, up_rows))
    grad_norm_two, grad_gain_two = jax.vjp(rms_norm, resid_one, gain_second)[1](grad_hidden_two)
    grad_resid = grad_out.astype(jnp.float32) + grad_norm_two
    grad_branch = grad_resid.astype(jnp.bfloat16)
    branch_all = gather_rows(grad_branch)
    grad_output_w = tn(mixed, branch_all)
    grad_heads = (
        low(nt(branch_all, output_part))
    )
    back = [
        attention_backward(qkv[i], grad_heads[:, pair[i]], forward[i][1], segment, bands[i][1])
        for i in range(pairs)
    ]
    grad_query_seq, grad_key_seq, grad_value_seq = (
        jnp.concatenate([values[part] for values in back], axis=1) for part in range(3)
    )
    grad_bias = jnp.concatenate([bucket_sums(values[3]) for values in back], axis=0)
    grad_query_w = tn(grad_query_seq, hidden_all)
    grad_key_w = tn(grad_key_seq, hidden_all)
    grad_value_w = tn(grad_value_seq, hidden_all)
    grad_hidden_one = scatter_rows(
        nn(grad_query_seq, query_part)
        + nn(grad_key_seq, key_part)
        + nn(grad_value_seq, value_part)
    )
    grad_norm_one, grad_gain_one = jax.vjp(rms_norm, inputs, gain_first)[1](grad_hidden_one)
    grad_tokens = (grad_resid + grad_norm_one).astype(jnp.bfloat16)
    grad_table = lax.dynamic_update_slice_in_dim(
        jnp.zeros((H, BUCKETS), jnp.float32), grad_bias, head_first, 0
    ).reshape(-1)
    weight_grads = (
        lax.psum_scatter(
            grad_query_w.astype(jnp.bfloat16), "fsdp", scatter_dimension=0, tiled=True
        ).astype(jnp.float32),
        lax.psum_scatter(
            grad_key_w.astype(jnp.bfloat16), "fsdp", scatter_dimension=0, tiled=True
        ).astype(jnp.float32),
        lax.psum_scatter(
            grad_value_w.astype(jnp.bfloat16), "fsdp", scatter_dimension=0, tiled=True
        ).astype(jnp.float32),
        lax.psum_scatter(
            grad_output_w.astype(jnp.bfloat16), "fsdp", scatter_dimension=0, tiled=True
        ).astype(jnp.float32),
        lax.psum_scatter(
            grad_gate_w.astype(jnp.bfloat16), "fsdp", scatter_dimension=0, tiled=True
        ).astype(jnp.float32),
        lax.psum_scatter(
            grad_up_w.astype(jnp.bfloat16), "fsdp", scatter_dimension=0, tiled=True
        ).astype(jnp.float32),
        lax.psum_scatter(
            grad_down.astype(jnp.bfloat16), "fsdp", scatter_dimension=0, tiled=True
        ).astype(jnp.float32),
    )
    small_grads = (
        lax.psum_scatter(grad_gain_one, ("seq", "fsdp"), scatter_dimension=0, tiled=True),
        lax.psum_scatter(grad_gain_two, ("seq", "fsdp"), scatter_dimension=0, tiled=True),
        lax.psum_scatter(grad_table, ("seq", "fsdp"), scatter_dimension=0, tiled=True),
    )
    return (
        layer_out[None],
        grad_tokens[None],
        small_grads[0],
        weight_grads[0],
        weight_grads[1],
        weight_grads[2],
        weight_grads[3],
        small_grads[2],
        small_grads[1],
        weight_grads[4],
        weight_grads[5],
        weight_grads[6],
    )


def solution(mesh):
    rows = P(("seq", "fsdp"), None)
    row = P(("seq", "fsdp"))
    activations = P("fsdp", "seq", None)
    in_specs = (
        activations,
        P("fsdp", "seq"),
        row,
        rows,
        rows,
        rows,
        rows,
        row,
        row,
        rows,
        rows,
        rows,
        activations,
    )
    out_specs = (
        activations,
        activations,
        row,
        rows,
        rows,
        rows,
        rows,
        row,
        row,
        rows,
        rows,
        rows,
    )
    seq, fsdp = mesh.shape["seq"], mesh.shape["fsdp"]
    plan = per_device if seq == 2 * CHIPS and H == seq * fsdp else per_device_general
    return jax.shard_map(
        plan,
        mesh=mesh,
        in_specs=in_specs,
        out_specs=out_specs,
        check_vma=False,
    )
```

```python
import functools

import jax
import jax.numpy as jnp
from jax import lax
from jax.experimental import pallas as pl
from jax.experimental.pallas import tpu as pltpu
from jax.sharding import PartitionSpec as P

H = 32
DK = 64
BUCKETS = 32


EPSILON = 1e-06
NEGATIVE = -1000000000.0
BUCKET_EDGES = (12, 16, 23, 32, 46, 64, 91)
PRECISE = lax.Precision.HIGHEST
BLK = 256
PAIR = 128
GELU_SCALE = 0.7978845608028654
GELU_CUBE = 0.044715


def bucket_index(offset):
    distance = jnp.abs(offset)
    coarse = 8 + sum(((distance >= edge).astype(jnp.int32) for edge in BUCKET_EDGES))
    return jnp.where(distance < 8, distance, coarse) + 16 * (offset > 0).astype(jnp.int32)


def nt(left, right):
    return lax.dot_general(
        left, right, (((1,), (1,)), ((), ())), preferred_element_type=jnp.float32
    )


def nn(left, right):
    return jnp.dot(left, right, preferred_element_type=jnp.float32)


def tn(left, right):
    return lax.dot_general(
        left, right, (((0,), (0,)), ((), ())), preferred_element_type=jnp.float32
    )


def params(mib):
    return pltpu.CompilerParams(vmem_limit_bytes=mib * 1024 * 1024)


def cost(flops, bytes_accessed, transcendentals=0):
    return pl.CostEstimate(
        flops=flops, bytes_accessed=bytes_accessed, transcendentals=transcendentals
    )


def head_mask(values, head):
    lane = lax.broadcasted_iota(jnp.int32, values.shape, 1)
    keep = (lane < DK) if head == 0 else (lane >= DK)
    return jnp.where(keep, values, jnp.zeros_like(values))


def fill_strip(strip_ref, head, band_row, tiles):
    wide = jnp.broadcast_to(band_row, (BLK, band_row.shape[1]))
    rolled = pltpu.roll(wide, 0, 1, stride=1, stride_axis=0)
    span = (2 * tiles - 1) * BLK
    near = (tiles - 2) * BLK
    if near > 0:
        strip_ref[head, :, 0:near] = jnp.broadcast_to(band_row[:, 0:1], (BLK, near))
        strip_ref[head, :, near + 3 * BLK : span] = jnp.broadcast_to(
            band_row[:, 4 * BLK - 1 : 4 * BLK], (BLK, span - near - 3 * BLK)
        )
    strip_ref[head, :, near : near + 3 * BLK] = rolled[:, BLK:]


def forward_kernel(tiles, seg_row_ref, seg_col_ref, band_ref, q_ref, k_ref, v_ref, o_ref, lse_ref, strip_ref):
    blk = pl.program_id(0)

    @pl.when(blk == 0)
    def _():
        for head in range(2):
            fill_strip(strip_ref, head, band_ref[head : head + 1, :], tiles)

    keys = tiles * BLK
    start = pl.multiple_of((tiles - 1 - blk) * BLK, BLK)
    same = seg_col_ref[...] == seg_row_ref[...]
    total = jnp.zeros((BLK, PAIR), jnp.float32)
    rows = []
    for head in range(2):
        scores = nt(head_mask(q_ref[...], head), k_ref[...]) + strip_ref[head, :, pl.ds(start, keys)]
        scores = jnp.where(same, scores, NEGATIVE)
        top = jnp.max(scores, axis=1, keepdims=True)
        weight = jnp.exp(scores - top)
        norm = jnp.sum(weight, axis=1, keepdims=True)
        prob = (weight * (1.0 / norm)).astype(jnp.bfloat16)
        total = total + nn(prob, head_mask(v_ref[...], head))
        rows.append(jnp.transpose(jnp.broadcast_to(top + jnp.log(norm), (BLK, PAIR)))[0:1, :])
    o_ref[...] = total.astype(jnp.bfloat16)
    lse_ref[...] = jnp.concatenate(rows, axis=0)


def attention_forward(qkv, segment, band):
    seq_len = qkv.shape[0]
    tiles = seq_len // BLK
    return pl.pallas_call(
        functools.partial(forward_kernel, tiles),
        grid=(tiles,),
        in_specs=[
            pl.BlockSpec((1, seq_len), lambda b: (0, 0)),
            pl.BlockSpec((BLK, 1), lambda b: (b, 0)),
            pl.BlockSpec((2, 4 * BLK), lambda b: (0, 0)),
            pl.BlockSpec((BLK, PAIR), lambda b: (b, 0)),
            pl.BlockSpec((seq_len, PAIR), lambda b: (0, 1)),
            pl.BlockSpec((seq_len, PAIR), lambda b: (0, 2)),
        ],
        out_specs=[
            pl.BlockSpec((BLK, PAIR), lambda b: (b, 0)),
            pl.BlockSpec((2, BLK), lambda b: (0, b)),
        ],
        out_shape=[
            jax.ShapeDtypeStruct((seq_len, PAIR), jnp.bfloat16),
            jax.ShapeDtypeStruct((2, seq_len), jnp.float32),
        ],
        scratch_shapes=[pltpu.VMEM((2, BLK, (2 * tiles - 1) * BLK), jnp.float32)],
        compiler_params=params(20),
        cost_estimate=cost(
            8 * seq_len * seq_len * PAIR, 8 * seq_len * PAIR, 2 * seq_len * seq_len
        ),
        name="attention_forward",
    )(segment[None, :], segment[:, None], band, qkv, qkv, qkv)


def diagonal_sums(tile):
    width = 2 * BLK
    wide = jnp.concatenate([tile, jnp.zeros_like(tile)], axis=1)
    total = wide[:8]
    for start in range(8, BLK, 8):
        total = total + pltpu.roll(wide[start : start + 8], width - start, 1)
    row = lax.broadcasted_iota(jnp.int32, total.shape, 0)
    for shift in (1, 2, 4):
        total = jnp.where((row & shift) != 0, pltpu.roll(total, width - shift, 1), total)
    return jnp.sum(total, axis=0, keepdims=True)


def backward_kernel(tiles, seg_row_ref, seg_col_ref, band_ref, q_ref, k_ref, v_ref, do_ref, o_ref, lse_ref,
                    dq_ref, dk_ref, dv_ref, diag_ref, strip_ref, dk_acc, dv_acc, bias_acc,
                    score_ref, grad_ref, prob_ref, back_ref):
    blk = pl.program_id(0)

    @pl.when(blk == 0)
    def _():
        for head in range(2):
            fill_strip(strip_ref, head, band_ref[head : head + 1, :], tiles)
        dk_acc[...] = jnp.zeros_like(dk_acc)
        dv_acc[...] = jnp.zeros_like(dv_acc)
        bias_acc[...] = jnp.zeros_like(bias_acc)

    seg_row = seg_row_ref[...]
    product = jnp.transpose(
        do_ref[...].astype(jnp.float32) * o_ref[...].astype(jnp.float32)
    )
    grad_q = jnp.zeros((BLK, PAIR), jnp.float32)
    for head in range(2):
        q_h = head_mask(q_ref[...], head)
        do_h = head_mask(do_ref[...], head)
        lse = lse_ref[head : head + 1, :]
        delta = jnp.sum(product[head * DK : (head + 1) * DK, :], axis=0, keepdims=True)
        score_ref[...] = nt(k_ref[...], q_h)
        grad_ref[...] = nt(v_ref[...], do_h)
        for tile in range(tiles):
            at = slice(tile * BLK, (tile + 1) * BLK)
            column = pl.multiple_of((blk - tile + tiles - 1) * BLK, BLK)
            scores = score_ref[at, :] + strip_ref[head, :, pl.ds(column, BLK)]
            scores = jnp.where(seg_col_ref[at, :] == seg_row, scores, NEGATIVE)
            prob = jnp.exp(scores - lse)
            prob_ref[at, :] = prob.astype(jnp.bfloat16)
            grad_s = (prob * (grad_ref[at, :] - delta)).astype(jnp.bfloat16)
            back_ref[at, :] = grad_s
            away = jnp.clip(blk - tile, -2, 2) + 2
            bias_acc[head, away] += grad_s.astype(jnp.float32)
        dv_acc[...] += nn(prob_ref[...], do_h)
        dk_acc[...] += nn(back_ref[...], q_h)
        grad_q = grad_q + tn(back_ref[...], head_mask(k_ref[...], head))
    dq_ref[...] = grad_q.astype(jnp.bfloat16)

    @pl.when(blk == tiles - 1)
    def _():
        dk_ref[...] = dk_acc[...].astype(jnp.bfloat16)
        dv_ref[...] = dv_acc[...].astype(jnp.bfloat16)
        for head in range(2):
            for away in (0, 4):
                far = jnp.sum(bias_acc[head, away], axis=0, keepdims=True)
                diag_ref[head, away : away + 1, :] = jnp.concatenate(
                    [far, jnp.zeros_like(far)], axis=1
                )
            for away in (1, 2, 3):
                diag_ref[head, away : away + 1, :] = diagonal_sums(bias_acc[head, away])


def attention_backward(qkv, grad_o, mixed, lse, segment, band_back):
    seq_len = qkv.shape[0]
    tiles = seq_len // BLK
    rows = pl.BlockSpec((BLK, PAIR), lambda b: (b, 0))
    whole = pl.BlockSpec((seq_len, PAIR), lambda b: (0, 0))
    result = jax.ShapeDtypeStruct((seq_len, PAIR), jnp.bfloat16)
    return pl.pallas_call(
        functools.partial(backward_kernel, tiles),
        grid=(tiles,),
        in_specs=[
            pl.BlockSpec((1, BLK), lambda b: (0, b)),
            pl.BlockSpec((seq_len, 1), lambda b: (0, 0)),
            pl.BlockSpec((2, 4 * BLK), lambda b: (0, 0)),
            rows,
            pl.BlockSpec((seq_len, PAIR), lambda b: (0, 1)),
            pl.BlockSpec((seq_len, PAIR), lambda b: (0, 2)),
            rows,
            rows,
            pl.BlockSpec((2, BLK), lambda b: (0, b)),
        ],
        out_specs=[rows, whole, whole, pl.BlockSpec((2, 5, 2 * BLK), lambda b: (0, 0, 0))],
        out_shape=[
            result,
            result,
            result,
            jax.ShapeDtypeStruct((2, 5, 2 * BLK), jnp.float32),
        ],
        scratch_shapes=[
            pltpu.VMEM((2, BLK, (2 * tiles - 1) * BLK), jnp.float32),
            pltpu.VMEM((seq_len, PAIR), jnp.float32),
            pltpu.VMEM((seq_len, PAIR), jnp.float32),
            pltpu.VMEM((2, 5, BLK, BLK), jnp.float32),
            pltpu.VMEM((seq_len, BLK), jnp.float32),
            pltpu.VMEM((seq_len, BLK), jnp.float32),
            pltpu.VMEM((seq_len, BLK), jnp.bfloat16),
            pltpu.VMEM((seq_len, BLK), jnp.bfloat16),
        ],
        compiler_params=params(20),
        cost_estimate=cost(
            20 * seq_len * seq_len * PAIR, 16 * seq_len * PAIR, 2 * seq_len * seq_len
        ),
        name="attention_backward",
    )(segment[None, :], segment[:, None], band_back, qkv, qkv, qkv, grad_o, mixed, lse)


def one_hot_buckets(offset):
    return (bucket_index(offset)[..., None] == jnp.arange(BUCKETS, dtype=jnp.int32)).astype(
        jnp.float32
    )


def bias_bands(bias_rows):
    offset = jnp.arange(4 * BLK, dtype=jnp.int32) - 2 * BLK
    contract = (((1,), (1,)), ((), ()))
    ahead = lax.dot_general(bias_rows, one_hot_buckets(offset), contract, precision=PRECISE)
    behind = lax.dot_general(bias_rows, one_hot_buckets(-offset), contract, precision=PRECISE)
    return ahead, behind


def bucket_sums(diagonals):
    lane = jnp.arange(2 * BLK, dtype=jnp.int32)
    within = jnp.where(lane < BLK, lane, lane - 2 * BLK)
    away = (jnp.arange(5, dtype=jnp.int32) - 2) * BLK
    onehot = one_hot_buckets(-within[None, :] - away[:, None])
    return jnp.dot(diagonals.reshape(2, -1), onehot.reshape(-1, BUCKETS), precision=PRECISE)


CHIPS = 4
CORE, ACROSS, ALONG = 1, 2, 4
PLACES = ((6, 7), (0, 4), (5, 3), (1, 2))


def wide(values):
    return values.astype(jnp.float32)


def low(values):
    return values.astype(jnp.bfloat16)


def piece_rows(own_ref, piece, start, rows, total):
    base = (own_ref[0] ^ piece) * total + start
    return pl.ds(pl.multiple_of(base, rows), rows)


def gathered(refs):
    out = []
    for core in range(2):
        own, near_x, near_y, first, second = refs[5 * core : 5 * core + 5]
        out += [(core, 0, own), (2 + core, 0, near_x), (4 + core, 0, near_y)]
        out += [(6 + core, 0, first), (6 + core, first.shape[0], second)]
    return out


def join_slots(weight_ref, slots):
    for part in range(3):
        for index, slot in enumerate(slots):
            weight_ref[part * PAIR + index * DK : part * PAIR + (index + 1) * DK, :] = slot[
                part * DK : (part + 1) * DK, :
            ]


def norm_project_kernel(own_ref, gain_ref, slot_a, slot_b, *refs):
    hidden_ref, out_ref, weight_ref = refs[10:]
    total = refs[0].shape[0]
    for piece, start, ref in gathered(refs[:10]):
        values = wide(ref[...])
        scale = lax.rsqrt(jnp.mean(values * values, axis=-1, keepdims=True) + EPSILON)
        at = piece_rows(own_ref, piece, start, ref.shape[0], total)
        hidden_ref[at, :] = low(values * scale * gain_ref[...])
    join_slots(weight_ref, (slot_a, slot_b))
    for chunk in range(8 * total // BLK):
        at = slice(chunk * BLK, (chunk + 1) * BLK)
        out_ref[at, :] = low(nt(hidden_ref[at, :], weight_ref[...]))


VMEM = pl.BlockSpec(memory_space=pltpu.VMEM)
SMEM = pl.BlockSpec(memory_space=pltpu.SMEM)


def norm_project(own, gain, slots, pieces):
    rows, width = pieces[0].shape
    total, features = 8 * rows, 3 * PAIR
    return pl.pallas_call(
        norm_project_kernel,
        in_specs=[SMEM] + [VMEM] * 13,
        out_specs=[VMEM] * 3,
        out_shape=[
            jax.ShapeDtypeStruct((total, width), jnp.bfloat16),
            jax.ShapeDtypeStruct((total, features), jnp.bfloat16),
            jax.ShapeDtypeStruct((features, width), jnp.bfloat16),
        ],
        compiler_params=params(60),
        cost_estimate=cost(
            2 * total * width * features, 2 * (2 * total * width + features * (width + total))
        ),
        name="norm_project",
    )(own, gain[None, :], *slots, *pieces)


def project_kernel(hidden_ref, slot_a, slot_b, out_ref, weight_ref):
    @pl.when(pl.program_id(0) == 0)
    def _():
        join_slots(weight_ref, (slot_a, slot_b))

    out_ref[...] = low(nt(hidden_ref[...], weight_ref[...]))


def project(hidden, slots):
    total, width = hidden.shape
    features = 3 * PAIR
    slot = pl.BlockSpec((slots[0].shape[0], width), lambda b: (0, 0))
    return pl.pallas_call(
        project_kernel,
        grid=(total // BLK,),
        in_specs=[pl.BlockSpec((BLK, width), lambda b: (b, 0)), slot, slot],
        out_specs=[
            pl.BlockSpec((BLK, features), lambda b: (b, 0)),
            pl.BlockSpec((features, width), lambda b: (0, 0)),
        ],
        out_shape=[
            jax.ShapeDtypeStruct((total, features), jnp.bfloat16),
            jax.ShapeDtypeStruct((features, width), jnp.bfloat16),
        ],
        compiler_params=params(12),
        cost_estimate=cost(
            2 * total * width * features, 2 * (total * width + features * (width + total))
        ),
        name="project",
    )(hidden, *slots)


def spread_rows(core, own_ref, lefts, weight, out):
    total = lefts[0].shape[0] // 8
    half = total // 2
    for chip in range(CHIPS):
        at = piece_rows(own_ref, 2 * chip + core, 0, total, total)
        values = None
        for index, left in enumerate(lefts):
            term = nn(left[at, :], weight[index * PAIR : (index + 1) * PAIR, :])
            values = term if values is None else values + term
        for index, place in enumerate(PLACES[chip]):
            out[place * half : (place + 1) * half, :] = low(
                values[index * half : (index + 1) * half, :]
            )


def spread_kernel(core, counts, own_ref, *refs):
    lefts, rights = refs[: counts[0]], refs[counts[0] : counts[0] + counts[1]]
    out, weight = refs[-2:]
    start = 0
    for right in rights:
        weight[start : start + right.shape[0], :] = right[...]
        start += right.shape[0]
    spread_rows(core, own_ref, lefts, weight, out)


def spread(own, core, lefts, rights, limit):
    total, width = lefts[0].shape[0] // 2, rights[0].shape[1]
    depth = sum(right.shape[0] for right in rights)
    return pl.pallas_call(
        functools.partial(spread_kernel, core, (len(lefts), len(rights))),
        in_specs=[SMEM] + [VMEM] * (len(lefts) + len(rights)),
        out_specs=VMEM,
        out_shape=jax.ShapeDtypeStruct((total, width), jnp.bfloat16),
        scratch_shapes=[pltpu.VMEM((depth, width), jnp.bfloat16)],
        compiler_params=params(limit),
        cost_estimate=cost(
            2 * total * width * depth, 2 * (total * width + depth * (width + total))
        ),
        name="spread",
    )(own, *lefts, *rights)


def last_kernel(own_ref, gain_ref, hidden_ref, *refs):
    lefts, rights = refs[:6], refs[6:8]
    out, slot_a, slot_b, sum_ref, weight = refs[8:]
    for index, right in enumerate(rights):
        weight[3 * PAIR * index : 3 * PAIR * (index + 1), :] = right[...]
    spread_rows(0, own_ref, lefts, weight, out)
    width = out.shape[1]
    for start in range(0, width, 512):
        cols = slice(start, start + 512)
        total = None
        for part in range(3):
            grad = tn(lefts[part][...], hidden_ref[:, cols])
            slot_a[part * DK : (part + 1) * DK, cols] = low(grad[:DK])
            slot_b[part * DK : (part + 1) * DK, cols] = low(grad[DK:])
            at = slice(part * PAIR, (part + 1) * PAIR)
            term = jnp.sum(grad * wide(weight[at, cols]), axis=0, keepdims=True)
            total = term if total is None else total + term
        sum_ref[:, cols] = total / gain_ref[:, cols]


def last(own, gain, hidden, lefts, rights):
    total, width = hidden.shape
    return pl.pallas_call(
        last_kernel,
        in_specs=[SMEM] + [VMEM] * 10,
        out_specs=[VMEM] * 4,
        out_shape=[
            jax.ShapeDtypeStruct((total // 2, width), jnp.bfloat16),
            jax.ShapeDtypeStruct((3 * DK, width), jnp.bfloat16),
            jax.ShapeDtypeStruct((3 * DK, width), jnp.bfloat16),
            jax.ShapeDtypeStruct((1, width), jnp.float32),
        ],
        scratch_shapes=[pltpu.VMEM((6 * PAIR, width), jnp.bfloat16)],
        compiler_params=params(56),
        cost_estimate=cost(12 * total * width * PAIR, 6 * total * width),
        name="last",
    )(own, gain[None, :], hidden, *lefts, *rights)


def heads_back_kernel(own_ref, weight_a0, weight_a1, weight_b0, weight_b1, mixed_a, mixed_b, *refs):
    heads_a, heads_b, grad_a, grad_b, whole, weight = refs[10:]
    total = refs[0].shape[0]
    for piece, start, ref in gathered(refs[:10]):
        whole[piece_rows(own_ref, piece, start, ref.shape[0], total), :] = ref[...]
    for index, ref in enumerate((weight_a0, weight_a1, weight_b0, weight_b1)):
        weight[index * DK : (index + 1) * DK, :] = ref[...]
    for chunk in range(8 * total // BLK):
        at = slice(chunk * BLK, (chunk + 1) * BLK)
        heads = low(nt(whole[at, :], weight[...]))
        heads_a[at, :] = heads[:, :PAIR]
        heads_b[at, :] = heads[:, PAIR:]
    grad_a[...] = low(tn(mixed_a[...], whole[...]))
    grad_b[...] = low(tn(mixed_b[...], whole[...]))


def heads_back(own, weights, mixed, pieces):
    rows, width = pieces[0].shape
    total = 8 * rows
    outs = pl.pallas_call(
        heads_back_kernel,
        in_specs=[SMEM] + [VMEM] * 16,
        out_specs=[VMEM] * 4,
        out_shape=[jax.ShapeDtypeStruct((total, PAIR), jnp.bfloat16)] * 2
        + [jax.ShapeDtypeStruct((PAIR, width), jnp.bfloat16)] * 2,
        scratch_shapes=[
            pltpu.VMEM((total, width), jnp.bfloat16),
            pltpu.VMEM((2 * PAIR, width), jnp.bfloat16),
        ],
        compiler_params=params(20),
        cost_estimate=cost(8 * total * width * PAIR, 2 * total * width),
        name="heads_back",
    )(own, *weights, *mixed, *pieces)
    return outs[:2], outs[2:]


def qkv_grad_kernel(gain_ref, hidden_ref, dq_ref, dk_ref, dv_ref, weight_ref, slot_a, slot_b, sum_ref):
    total = None
    for part, ref in enumerate((dq_ref, dk_ref, dv_ref)):
        grad = tn(ref[...], hidden_ref[...])
        slot_a[part * DK : (part + 1) * DK, :] = low(grad[:DK])
        slot_b[part * DK : (part + 1) * DK, :] = low(grad[DK:])
        at = slice(part * PAIR, (part + 1) * PAIR)
        term = jnp.sum(grad * wide(weight_ref[at, :]), axis=0, keepdims=True)
        total = term if total is None else total + term
    sum_ref[...] = total / gain_ref[...]


def qkv_grad(gain, hidden, dq, dk, dv, weight):
    total, width = hidden.shape
    cols = 512
    col = pl.BlockSpec((1, cols), lambda c: (0, c))
    back = pl.BlockSpec((total, PAIR), lambda c: (0, 0))
    slot = pl.BlockSpec((3 * DK, cols), lambda c: (0, c))
    return pl.pallas_call(
        qkv_grad_kernel,
        grid=(width // cols,),
        in_specs=[
            col,
            pl.BlockSpec((total, cols), lambda c: (0, c)),
            back,
            back,
            back,
            pl.BlockSpec((3 * PAIR, cols), lambda c: (0, c)),
        ],
        out_specs=[slot, slot, col],
        out_shape=[
            jax.ShapeDtypeStruct((3 * DK, width), jnp.bfloat16),
            jax.ShapeDtypeStruct((3 * DK, width), jnp.bfloat16),
            jax.ShapeDtypeStruct((1, width), jnp.float32),
        ],
        compiler_params=params(12),
        cost_estimate=cost(6 * total * width * PAIR, 2 * total * width + 12 * PAIR * width),
        name="qkv_grad",
    )(gain[None, :], hidden, dq, dk, dv, weight)


def assemble_kernel(own, *refs):
    outs = refs[6:]
    units = own.shape[0] // 3
    half = units // 2
    for part, weight in enumerate(outs):
        for chip in range(CHIPS):
            for index, place in enumerate(PLACES[chip]):
                ref, start = own, part * units + index * half
                if chip:
                    ref = refs[2 * chip - 2]
                    if start >= 3 * half:
                        ref, start = refs[2 * chip - 1], start - 3 * half
                weight[place * half : (place + 1) * half, :] = ref[start : start + half, :]


def assemble(own, *stacks):
    rows, width = own.shape
    return pl.pallas_call(
        assemble_kernel,
        in_specs=[VMEM] * 7,
        out_specs=[VMEM] * 3,
        out_shape=[jax.ShapeDtypeStruct((CHIPS * rows // 3, width), jnp.bfloat16)] * 3,
        compiler_params=params(20),
        cost_estimate=cost(0, 16 * rows * width),
        name="assemble",
    )(own, *stacks)


def feed_kernel(gate_w, up_w, down_w, *refs):
    hidden, cot, outs = refs[:2], refs[2:4], refs[4:]
    inner_ref, dgate_ref, dup_ref, grad_own, grad_other, out_own, out_other = outs
    rows = hidden[0].shape[0]
    values = jnp.concatenate([hidden[0][...], hidden[1][...]], axis=0)
    grads = jnp.concatenate([cot[0][...], cot[1][...]], axis=0)
    gate = nt(values, gate_w[...])
    up = nt(values, up_w[...])
    grad_m = nt(grads, down_w[...])
    square = gate * gate
    bend = jnp.tanh(GELU_SCALE * gate * (1.0 + GELU_CUBE * square))
    part = 0.5 * (1.0 + bend)
    act = gate * part
    slope = part + 0.5 * gate * (1.0 - bend * bend) * (
        GELU_SCALE * (1.0 + 3.0 * GELU_CUBE * square)
    )
    inner = low(act * up)
    inner_ref[...] = inner
    dgate = low(grad_m * up * slope)
    dup = low(grad_m * act)
    dgate_ref[...] = dgate
    dup_ref[...] = dup
    grad_h = low(nn(dgate, gate_w[...]) + nn(dup, up_w[...]))
    grad_own[...] = grad_h[:rows]
    grad_other[...] = grad_h[rows:]
    result = low(nn(inner, down_w[...]))
    out_own[...] = result[:rows]
    out_other[...] = result[rows:]


def feed(weights, hidden, cot):
    rows, width = hidden[0].shape
    total, units = 2 * rows, weights[0].shape[0]
    return pl.pallas_call(
        feed_kernel,
        in_specs=[VMEM] * 7,
        out_specs=[VMEM] * 7,
        out_shape=[jax.ShapeDtypeStruct((total, units), jnp.bfloat16)] * 3
        + [jax.ShapeDtypeStruct((rows, width), jnp.bfloat16)] * 4,
        compiler_params=params(24),
        cost_estimate=cost(12 * total * width * units, 2 * 4 * (total + units) * width),
        name="feed",
    )(*weights, *hidden, *cot)


def feed_grad_kernel(terms, *refs):
    lefts, pieces = refs[: 4 * terms], refs[4 * terms : 4 * terms + 8]
    outs, right = refs[-4:-1], refs[-1]
    rows = pieces[0].shape[0]
    for index, piece in enumerate(pieces):
        right[index * rows : (index + 1) * rows, :] = piece[...]
    for term in range(terms):
        left = jnp.concatenate([ref[...] for ref in lefts[4 * term : 4 * term + 4]], axis=0)
        grad = low(tn(left, right[...]))
        start = 0
        for out in outs:
            size = out.shape[0] // terms
            out[term * size : (term + 1) * size, :] = grad[start : start + size]
            start += size


def feed_grad(lefts, pieces):
    terms = len(lefts)
    rows, width = pieces[0].shape
    units = lefts[0][0].shape[1]
    return pl.pallas_call(
        functools.partial(feed_grad_kernel, terms),
        in_specs=[VMEM] * (4 * terms + 8),
        out_specs=[VMEM] * 3,
        out_shape=[
            jax.ShapeDtypeStruct((terms * units // part, width), jnp.bfloat16)
            for part in (4, 4, 2)
        ],
        scratch_shapes=[pltpu.VMEM((8 * rows, width), jnp.bfloat16)],
        compiler_params=params(48),
        cost_estimate=cost(16 * terms * rows * width * units, 24 * rows * width),
        name="feed_grad",
    )(*[value for left in lefts for value in left], *pieces)


def second_kernel(terms, keep, from_x, from_y, to_x, to_y):
    size = to_x.shape[0] // terms
    for term in range(terms):
        out = slice(term * size, (term + 1) * size)
        base = 4 * term * size
        pair = 2 * term * size
        to_x[out, :] = low(wide(keep[base : base + size, :]) + wide(from_y[pair : pair + size, :]))
        to_y[out, :] = low(
            wide(keep[base + size : base + 2 * size, :])
            + wide(from_x[pair + size : pair + 2 * size, :])
        )


def second(terms, keep, from_x, from_y):
    shape = jax.ShapeDtypeStruct((from_x.shape[0] // 2, from_x.shape[1]), jnp.bfloat16)
    return pl.pallas_call(
        functools.partial(second_kernel, terms),
        in_specs=[VMEM] * 3,
        out_specs=[VMEM] * 2,
        out_shape=[shape, shape],
        compiler_params=params(12),
        cost_estimate=cost(0, 6 * from_x.shape[0] * from_x.shape[1]),
        name="second",
    )(keep, from_x, from_y)


def totals_kernel(terms, *refs):
    outs = refs[5 * len(terms) :]
    done = 0
    for index, count in enumerate(terms):
        keep, from_x, from_y, second_x, second_y = refs[5 * index : 5 * index + 5]
        for term in range(count):
            out = outs[done]
            done += 1
            size = out.shape[0] // 2
            base, pair, one = 4 * term * size, 2 * term * size, term * size
            out[:size, :] = (
                wide(keep[base + 2 * size : base + 3 * size, :])
                + wide(from_x[pair : pair + size, :])
                + wide(second_y[one : one + size, :])
            )
            out[size:, :] = (
                wide(keep[base + 3 * size : base + 4 * size, :])
                + wide(from_y[pair + size : pair + 2 * size, :])
                + wide(second_x[one : one + size, :])
            )


def totals(terms, *groups):
    shapes = [
        (2 * group[3].shape[0] // count, group[3].shape[1])
        for count, group in zip(terms, groups)
        for _ in range(count)
    ]
    return pl.pallas_call(
        functools.partial(totals_kernel, terms),
        in_specs=[VMEM] * (5 * len(groups)),
        out_specs=[VMEM] * len(shapes),
        out_shape=[jax.ShapeDtypeStruct(shape, jnp.float32) for shape in shapes],
        compiler_params=params(56),
        cost_estimate=cost(0, 10 * sum(rows * width for rows, width in shapes)),
        name="totals",
    )(*[value for group in groups for value in group])


def sends_kernel(own_ref, other_ref, to_x, to_y, keep):
    size = to_x.shape[0]
    to_x[...] = low(wide(own_ref[:size, :]) + wide(other_ref[:size, :]))
    to_y[...] = low(wide(own_ref[size : 2 * size, :]) + wide(other_ref[size : 2 * size, :]))
    keep[...] = wide(own_ref[2 * size :, :]) + wide(other_ref[2 * size :, :])


def sends(own, other, limit):
    rows, width = own.shape
    shape = jax.ShapeDtypeStruct((rows // 4, width), jnp.bfloat16)
    return pl.pallas_call(
        sends_kernel,
        in_specs=[VMEM] * 2,
        out_specs=[VMEM] * 3,
        out_shape=[shape, shape, jax.ShapeDtypeStruct((rows // 2, width), jnp.float32)],
        compiler_params=params(limit),
        cost_estimate=cost(0, 7 * rows * width),
        name="sends",
    )(own, other)


def fence(*values):
    return lax.optimization_barrier(values)


def swap(values, bits):
    return lax.ppermute(values, "seq", [(i, i ^ bits) for i in range(2 * CHIPS)])


def ring(values, step):
    n = lax.axis_size("fsdp")
    return lax.ppermute(values, "fsdp", [(i, (i + step) % n) for i in range(n)])


def line_order(slots):
    n = len(slots)
    order = (lax.axis_index("fsdp") - jnp.arange(n, dtype=jnp.int32)) % n
    return jnp.stack(slots)[order]


def both(values, other, bits):
    high = (lax.axis_index("seq") & bits) != 0
    return jnp.concatenate(
        [jnp.where(high, other, values), jnp.where(high, values, other)], axis=0
    )


def halves(values, bits):
    high = (lax.axis_index("seq") & bits) != 0
    size = values.shape[0] // 2
    lower, upper = values[:size], values[size:]
    return jnp.where(high, upper, lower), jnp.where(high, lower, upper)


def plane_total(keep, from_x, from_y, second_x, second_y):
    size = keep.shape[0] // 4
    first = wide(keep[2 * size : 3 * size]) + wide(from_x[:size]) + wide(second_y)
    second = wide(keep[3 * size :]) + wide(from_y[size:]) + wide(second_x)
    return jnp.concatenate([first, second], axis=0)


def add(*values):
    return functools.reduce(lambda left, right: left + right, [wide(value) for value in values])


def per_device(
    tokens,
    starts,
    first_gain,
    query_weight,
    key_weight,
    value_weight,
    output_weight,
    bias_table,
    second_gain,
    gate_weight,
    up_weight,
    down_weight,
    cotangent,
):
    index = lax.axis_index("seq")[None]
    own = tokens[0]
    half = own.shape[0] // 2
    grad_out = cotangent[0]
    rows = first_gain.shape[0]
    buckets = bias_table.shape[0]
    qkv0 = low(
        jnp.concatenate([query_weight, key_weight, value_weight, output_weight], axis=0)
    )
    small = low(jnp.concatenate([first_gain, second_gain, bias_table]))
    own, qkv0, small, gate_weight, up_weight, down_weight = fence(
        own, qkv0, small, gate_weight, up_weight, down_weight
    )

    tok_x, tok_y = swap(own, ACROSS), swap(own, ALONG)
    small_slots = [small] + [ring(small, k) for k in range(1, 4)]
    small_slots, own, qkv0, gate_weight, up_weight, down_weight = fence(
        small_slots, own, qkv0, gate_weight, up_weight, down_weight
    )
    qkv1 = ring(qkv0, 1)
    gain_part = line_order([value[: 2 * rows] for value in small_slots]).reshape(-1)
    packed = jnp.concatenate([gain_part, low(starts[0])])[None]
    packed = both(packed, swap(packed, CORE), CORE)
    packed, gate_weight, up_weight, down_weight = fence(
        packed, gate_weight, up_weight, down_weight
    )
    near = both(packed, swap(packed, ACROSS), ACROSS)
    far = both(swap(packed, ALONG), swap(packed, ALONG | ACROSS), ACROSS)
    packed = both(near, far, ALONG)
    packed, tok_x, tok_y, gate_weight, up_weight, down_weight = fence(
        packed, tok_x, tok_y, gate_weight, up_weight, down_weight
    )

    tok_d1, tok_d2 = swap(tok_y[:half], ACROSS), swap(tok_x[half:], ALONG)
    tok_cx, tok_cy = swap(tok_x, CORE), swap(tok_y, CORE)
    gain_count = gain_part.shape[0]
    gains = wide(packed[:, :gain_count]).reshape(-1, 4, 2, rows)
    gain_first = gains[:, :, 0].reshape(-1)
    gain_second = gains[:, :, 1].reshape(-1)
    segment = jnp.cumsum(packed[:, gain_count:].reshape(-1).astype(jnp.int32), dtype=jnp.int32)
    tables = [wide(value[2 * rows :]) for value in small_slots]
    bands = [bias_bands(jnp.stack(tables[2 * p : 2 * p + 2])) for p in range(2)]
    tok_d1, tok_d2, tok_cx, tok_cy, segment, gain_first, gain_second, bands, own = fence(
        tok_d1, tok_d2, tok_cx, tok_cy, segment, gain_first, gain_second, bands, own
    )

    tok_c, tok_c1, tok_c2 = swap(own, CORE), swap(tok_d1, CORE), swap(tok_d2, CORE)
    feed0 = low(jnp.concatenate([gate_weight, up_weight, down_weight], axis=0))
    tok_c, tok_c1, tok_c2, feed0, qkv1 = fence(tok_c, tok_c1, tok_c2, feed0, qkv1)

    qkv2 = ring(qkv1, 1)
    feed_half = feed0.shape[0] // 2
    feed_top, feed_low = feed0[:feed_half], feed0[feed_half:]
    feed_xl, feed_yt = swap(feed_low, ACROSS), swap(feed_top, ALONG)
    feed_top, feed_low = fence(feed_top, feed_low)
    feed_xt, feed_yl = swap(feed_top, ACROSS), swap(feed_low, ALONG)
    tok_pieces = (own, tok_x, tok_y, tok_d1, tok_d2, tok_c, tok_cx, tok_cy, tok_c1, tok_c2)
    hidden_one, qkv_a, weight_a = norm_project(index, gain_first, (qkv0, qkv1), tok_pieces)
    hidden_one, qkv_a, weight_a, qkv2, grad_out, feed_xl, feed_yt = fence(
        hidden_one, qkv_a, weight_a, qkv2, grad_out, feed_xl, feed_yt
    )

    qkv3 = ring(qkv2, 1)
    feed_dt, feed_dl = swap(feed_yt, ACROSS), swap(feed_xl, ALONG)
    mixed_a, lse_a = attention_forward(qkv_a, segment, bands[0][0])
    out0, out1, out2 = (value[3 * DK :] for value in (qkv0, qkv1, qkv2))
    mixed_a, lse_a, hidden_one, qkv3, feed_xt, feed_yl, out0, out1, out2 = fence(
        mixed_a, lse_a, hidden_one, qkv3, feed_xt, feed_yl, out0, out1, out2
    )

    cot1 = ring(grad_out, 1)
    qkv_b, weight_b = project(hidden_one, (qkv2, qkv3))
    out3 = qkv3[3 * DK :]
    mixed_b, lse_b = attention_forward(qkv_b, segment, bands[1][0])
    mixed_b, lse_b, out3, grad_out = fence(mixed_b, lse_b, out3, grad_out)
    cot_c0 = swap(grad_out, CORE)
    out_slots = (out0, out1, out2, out3)
    mixed = (mixed_a, mixed_b)
    part_other = spread(index, 1, mixed, out_slots, 14)
    part_other, mixed, feed_dt, feed_dl, cot1, cot_c0 = fence(
        part_other, mixed, feed_dt, feed_dl, cot1, cot_c0
    )
    part_other, cot2, cot_c1 = swap(part_other, CORE), ring(cot1, 1), swap(cot1, CORE)
    part_own = spread(index, 0, mixed, out_slots, 14)
    part_own, part_other, cot_c1 = fence(part_own, part_other, cot_c1)

    send_x, send_y, keep = sends(part_own, part_other, 12)
    send_x, send_y, keep = fence(send_x, send_y, keep)
    from_x, from_y = swap(send_x, ACROSS), swap(send_y, ALONG)
    weights = assemble(feed0, feed_xt, feed_xl, feed_yt, feed_yl, feed_dt, feed_dl)
    from_x, from_y, weights, cot2 = fence(from_x, from_y, weights, cot2)
    send_x, send_y = fence(*second(1, keep, from_x, from_y))
    second_x, second_y = swap(send_x, ACROSS), swap(send_y, ALONG)
    cot3, cot_c2 = ring(cot2, 1), swap(cot2, CORE)
    second_x, second_y, cot3, cot_c2 = fence(second_x, second_y, cot3, cot_c2)
    inputs = wide(own)
    resid_one = inputs + plane_total(keep, from_x, from_y, second_x, second_y)

    scale_two = lax.rsqrt(jnp.mean(resid_one * resid_one, axis=-1, keepdims=True) + EPSILON)
    normed_two = resid_one * scale_two
    hid0 = low(normed_two * gain_second)
    hid0, resid_one, scale_two = fence(hid0, resid_one, scale_two)

    hid1, hid_c0, cot_c3 = ring(hid0, 1), swap(hid0, CORE), swap(cot3, CORE)
    hid_c0, cot_c3 = fence(hid_c0, cot_c3)
    feed_a = feed(weights, (hid0, hid_c0), (grad_out, cot_c0))
    feed_a, hid1 = fence(feed_a, hid1)
    hid2, hid_c1 = ring(hid1, 1), swap(hid1, CORE)
    hid_c1, feed_a = fence(hid_c1, feed_a)
    grad_c0, out_c0 = swap(feed_a[4], CORE), swap(feed_a[6], CORE)
    feed_b = feed(weights, (hid1, hid_c1), (cot1, cot_c1))
    feed_b, hid2, grad_c0, out_c0 = fence(feed_b, hid2, grad_c0, out_c0)
    hid3, hid_c2 = ring(hid2, 1), swap(hid2, CORE)
    hid_c2, feed_b = fence(hid_c2, feed_b)
    grad_c1, out_c1 = swap(feed_b[4], CORE), swap(feed_b[6], CORE)
    feed_c = feed(weights, (hid2, hid_c2), (cot2, cot_c2))
    feed_c, hid3, grad_c1, out_c1 = fence(feed_c, hid3, grad_c1, out_c1)
    hid_c3 = swap(hid3, CORE)
    dh = ring(low(add(feed_b[3], grad_c1)), 1)
    hid_c3, feed_c = fence(hid_c3, feed_c)
    grad_c2, out_c2 = swap(feed_c[4], CORE), swap(feed_c[6], CORE)
    feed_d = feed(weights, (hid3, hid_c3), (cot3, cot_c3))
    feed_d, dh, grad_c2, out_c2 = fence(feed_d, dh, grad_c2, out_c2)
    dh = ring(low(add(feed_c[3], grad_c2, dh)), 1)
    grad_c3, out_c3 = swap(feed_d[4], CORE), swap(feed_d[6], CORE)
    parts = (feed_a, feed_b, feed_c, feed_d)
    hid_pieces = (hid0, hid_c0, hid1, hid_c1, hid2, hid_c2, hid3, hid_c3)
    cot_pieces = (grad_out, cot_c0, cot1, cot_c1, cot2, cot_c2, cot3, cot_c3)
    grad_down = feed_grad([[part[0] for part in parts]], cot_pieces)
    grad_down, dh, grad_c3, out_c3, hid_pieces = fence(grad_down, dh, grad_c3, out_c3, hid_pieces)

    dh, out_sum = ring(low(add(feed_d[3], grad_c3, dh)), 1), low(add(feed_b[5], out_c1))
    out_sum = ring(out_sum, 1)
    down_x, down_y, down_keep = grad_down
    down_fx, down_fy = swap(down_x, ACROSS), swap(down_y, ALONG)
    grad_both = feed_grad(
        [[part[1] for part in parts], [part[2] for part in parts]], hid_pieces
    )
    dh, grad_both = fence(dh, grad_both)

    grad_hidden_two = add(feed_a[3], grad_c0, dh)
    normed_two = resid_one * scale_two
    shared = grad_hidden_two * gain_second
    grad_resid = wide(grad_out) + scale_two * (
        shared - normed_two * jnp.mean(shared * normed_two, axis=-1, keepdims=True)
    )
    branch = low(grad_resid)
    gain_two_rows = jnp.sum(grad_hidden_two * normed_two, axis=0)
    branch, grad_resid, gain_two_rows, down_fx, down_fy = fence(
        branch, grad_resid, gain_two_rows, down_fx, down_fy
    )

    br_x, br_y, br_c = swap(branch, ACROSS), swap(branch, ALONG), swap(branch, CORE)
    down_x, down_y = second(1, down_keep, down_fx, down_fy)
    out_send = low(add(feed_c[5], out_c2, out_sum))
    br_x, br_y, br_c, down_x, down_y, out_send = fence(
        br_x, br_y, br_c, down_x, down_y, out_send
    )
    br_d1, br_d2 = swap(br_y[:half], ACROSS), swap(br_x[half:], ALONG)
    br_cx, br_cy = swap(br_x, CORE), swap(br_y, CORE)
    out_sum = ring(out_send, 1)
    br_d1, br_d2, br_cx, br_cy = fence(br_d1, br_d2, br_cx, br_cy)

    br_c1, br_c2 = swap(br_d1, CORE), swap(br_d2, CORE)
    down_sx, down_sy = swap(down_x, ACROSS), swap(down_y, ALONG)
    pieces = (branch, br_x, br_y, br_d1, br_d2, br_c, br_cx, br_cy, br_c1, br_c2)
    grad_heads, grad_outs = heads_back(index, out_slots, mixed, pieces)
    grad_heads, grad_outs, grad_both, down_sx, down_sy, out_sum = fence(
        grad_heads, grad_outs, grad_both, down_sx, down_sy, out_sum
    )

    go0, go1 = grad_outs[0][:DK], grad_outs[0][DK:]
    go2, go3 = grad_outs[1][:DK], grad_outs[1][DK:]
    both_x, both_y, both_keep = grad_both
    both_fx, both_fy = swap(both_x, ACROSS), swap(both_y, ALONG)
    out_sum = ring(low(add(feed_d[5], out_c3, out_sum)), 1)
    dq_b, dk_b, dv_b, diag_b = attention_backward(
        qkv_b, grad_heads[1], mixed[1], lse_b, segment, bands[1][1]
    )
    dq_b, dk_b, dv_b, diag_b, go3 = fence(dq_b, dk_b, dv_b, diag_b, go3)

    go_sum = ring(go3, -1)
    gq2, gq3, sums_b = qkv_grad(gain_first, hidden_one, dq_b, dk_b, dv_b, weight_b)
    gq2, gq3, sums_b, qkv_a, out_sum = fence(gq2, gq3, sums_b, qkv_a, out_sum)

    gq = ring(gq3, -1)
    dq_a, dk_a, dv_a, diag_a = attention_backward(
        qkv_a, grad_heads[0], mixed[0], lse_a, segment, bands[0][1]
    )
    dq_a, dk_a, dv_a, diag_a, both_fx, both_fy = fence(
        dq_a, dk_a, dv_a, diag_a, both_fx, both_fy
    )

    both_x, both_y = second(2, both_keep, both_fx, both_fy)
    both_sx, both_sy = swap(both_x, ACROSS), swap(both_y, ALONG)
    lefts = (dq_a, dk_a, dv_a, dq_b, dk_b, dv_b)
    back_other = spread(index, 1, lefts, (weight_a, weight_b), 14)
    back_other, lefts, gq, go_sum = fence(back_other, lefts, gq, go_sum)
    gq, go_sum = ring(low(add(gq2, gq)), -1), ring(low(add(go2, go_sum)), -1)
    back_other = swap(back_other, CORE)
    back_own, gq0, gq1, sums_a = last(index, gain_first, hidden_one, lefts, (weight_a, weight_b))
    back_own, back_other, gq0, gq1, sums_a, both_sx, both_sy = fence(
        back_own, back_other, gq0, gq1, sums_a, both_sx, both_sy
    )
    send_x, send_y, keep = sends(back_own, back_other, 56)
    gain_rows = jnp.stack([(sums_a + sums_b)[0], gain_two_rows]).reshape(2, 2, 2, 2, 4, -1)
    gain_rows = jnp.transpose(gain_rows, (3, 1, 2, 4, 0, 5)).reshape(2 * CHIPS, -1)
    send_x, send_y, keep, gq1, gain_rows = fence(send_x, send_y, keep, gq1, gain_rows)

    from_x, from_y = swap(send_x, ACROSS), swap(send_y, ALONG)
    gain_keep, gain_send = halves(gain_rows, CORE)
    gain_rows = gain_keep + swap(gain_send, CORE)
    gain_rows, gq1 = fence(gain_rows, gq1)
    gq_send = low(add(gq1, gq))
    gq_first = ring(gq_send[: 2 * DK], -1)
    gain_keep, gain_send = halves(gain_rows, ALONG)
    gain_rows = gain_keep + swap(gain_send, ALONG)
    last_send = jnp.concatenate([gq_send[2 * DK :], low(add(go1, go_sum))], axis=0)
    from_x, from_y, gain_rows, gq_first, last_send = fence(
        from_x, from_y, gain_rows, gq_first, last_send
    )
    send_x, send_y = second(1, keep, from_x, from_y)
    second_x, second_y = swap(send_x, ACROSS), swap(send_y, ALONG)
    gq_last = ring(last_send, -1)
    gain_keep, gain_send = halves(gain_rows, ACROSS)
    gain_rows = gain_keep + swap(gain_send, ACROSS)
    late = (down_keep, both_keep, resid_one, diag_a, gq_first, go0, gq0, out_sum)
    second_x, second_y, gain_rows, late = fence(second_x, second_y, gain_rows, late)
    down_keep, both_keep, resid_one, diag_a, gq_first, go0, gq0, out_sum = late
    tables_a, tables_b = bucket_sums(diag_a), bucket_sums(diag_b)
    table_slots = (tables_a[0], tables_a[1], tables_b[0], tables_b[1])
    gain_slots = line_order(list(gain_rows.reshape(4, -1)))
    sums = [jnp.concatenate([gain_slots[k], table_slots[k]]) for k in range(4)]
    sums = sums[0] + sum(ring(sums[k], -k) for k in range(1, 4))
    grad_down_w, grad_gate_w, grad_up_w = totals(
        (1, 2),
        (down_keep, down_fx, down_fy, down_sx, down_sy),
        (both_keep, both_fx, both_fy, both_sx, both_sy),
    )
    layer_out = low(resid_one + add(feed_a[5], out_c0, out_sum))
    grad_hidden_one = plane_total(keep, from_x, from_y, second_x, second_y)
    scale_one = lax.rsqrt(jnp.mean(inputs * inputs, axis=-1, keepdims=True) + EPSILON)
    normed_one = inputs * scale_one
    shared = grad_hidden_one * gain_first
    grad_tokens = low(
        grad_resid
        + scale_one * (shared - normed_one * jnp.mean(shared * normed_one, axis=-1, keepdims=True))
    )
    gq_last, sums = fence(gq_last, sums)
    grad_q, grad_k = add(gq0[:DK], gq_first[:DK]), add(gq0[DK : 2 * DK], gq_first[DK:])
    grad_v, grad_output_w = add(gq0[2 * DK :], gq_last[:DK]), add(go0, gq_last[DK:])
    return (
        layer_out[None],
        grad_tokens[None],
        sums[:rows],
        grad_q,
        grad_k,
        grad_v,
        grad_output_w,
        sums[2 * rows :],
        sums[rows : 2 * rows],
        grad_gate_w,
        grad_up_w,
        grad_down_w,
    )


def rms_norm(values, gain):
    return values * lax.rsqrt(jnp.mean(values * values, axis=-1, keepdims=True) + EPSILON) * gain


def gated_gelu(gate, up_part):
    return jax.nn.gelu(gate, approximate=True) * up_part


def gather_rows(values):
    return lax.all_gather(values, "seq", axis=0, tiled=True)


def scatter_rows(values):
    return lax.psum_scatter(
        values.astype(jnp.bfloat16), "seq", scatter_dimension=0, tiled=True
    ).astype(jnp.float32)


def per_device_general(
    tokens,
    starts,
    first_gain,
    query_weight,
    key_weight,
    value_weight,
    output_weight,
    bias_table,
    second_gain,
    gate_weight,
    up_weight,
    down_weight,
    cotangent,
):
    segment = jnp.cumsum(lax.all_gather(starts, "seq", axis=1, tiled=True)[0], dtype=jnp.int32)
    inputs = tokens[0].astype(jnp.float32)
    grad_out = cotangent[0]
    head_count = H // lax.axis_size("seq")
    head_first = lax.axis_index("seq") * head_count
    query_low = query_weight.astype(jnp.bfloat16)
    key_low = key_weight.astype(jnp.bfloat16)
    value_low = value_weight.astype(jnp.bfloat16)
    output_low = output_weight.astype(jnp.bfloat16)
    gate_low = gate_weight.astype(jnp.bfloat16)
    up_low = up_weight.astype(jnp.bfloat16)
    down_low = down_weight.astype(jnp.bfloat16)
    first_low = first_gain.astype(jnp.bfloat16)
    second_low = second_gain.astype(jnp.bfloat16)
    table_low = bias_table.astype(jnp.bfloat16)
    query_part, key_part, value_part, output_part, gate_part, up_rows, down_part = (
        lax.all_gather(query_low, "fsdp", axis=0, tiled=True),
        lax.all_gather(key_low, "fsdp", axis=0, tiled=True),
        lax.all_gather(value_low, "fsdp", axis=0, tiled=True),
        lax.all_gather(output_low, "fsdp", axis=0, tiled=True),
        lax.all_gather(gate_low, "fsdp", axis=0, tiled=True),
        lax.all_gather(up_low, "fsdp", axis=0, tiled=True),
        lax.all_gather(down_low, "fsdp", axis=0, tiled=True),
    )
    gain_one, gain_two, table_full = (
        lax.all_gather(first_low, ("seq", "fsdp"), axis=0, tiled=True),
        lax.all_gather(second_low, ("seq", "fsdp"), axis=0, tiled=True),
        lax.all_gather(table_low, ("seq", "fsdp"), axis=0, tiled=True),
    )
    gain_first = gain_one.astype(jnp.float32)
    gain_second = gain_two.astype(jnp.float32)
    bias_rows = lax.dynamic_slice_in_dim(
        table_full.astype(jnp.float32).reshape(H, BUCKETS), head_first, head_count, 0
    )
    hidden_one = rms_norm(inputs, gain_first).astype(jnp.bfloat16)
    hidden_all = gather_rows(hidden_one)
    query_head = (
        low(nt(hidden_all, query_part))
    )
    key_head = (
        low(nt(hidden_all, key_part))
    )
    value_head = (
        low(nt(hidden_all, value_part))
    )
    pairs = head_count // 2
    pair = [slice(index * PAIR, (index + 1) * PAIR) for index in range(pairs)]
    bands = [bias_bands(bias_rows[2 * index : 2 * index + 2]) for index in range(pairs)]
    qkv = [
        jnp.concatenate([query_head[:, at], key_head[:, at], value_head[:, at]], axis=1)
        for at in pair
    ]
    forward = [attention_forward(qkv[i], segment, bands[i][0]) for i in range(pairs)]
    mixed = jnp.concatenate([out for out, _ in forward], axis=1)
    resid_one = inputs + scatter_rows(nn(mixed, output_part))
    hidden_two = rms_norm(resid_one, gain_second).astype(jnp.bfloat16)
    hidden_two_all = gather_rows(hidden_two)
    gate = nt(hidden_two_all, gate_part)
    up_part = nt(hidden_two_all, up_rows)
    inner = gated_gelu(gate, up_part).astype(jnp.bfloat16)
    layer_out = (resid_one + scatter_rows(nn(inner, down_part))).astype(jnp.bfloat16)
    grad_out_all = gather_rows(grad_out)
    grad_inner = nt(grad_out_all, down_part)
    grad_down = tn(inner, grad_out_all)
    grad_gate, grad_up = jax.vjp(gated_gelu, gate, up_part)[1](grad_inner)
    grad_gate = grad_gate.astype(jnp.bfloat16)
    grad_up = grad_up.astype(jnp.bfloat16)
    grad_gate_w = tn(grad_gate, hidden_two_all)
    grad_up_w = tn(grad_up, hidden_two_all)
    grad_hidden_two = scatter_rows(nn(grad_gate, gate_part) + nn(grad_up, up_rows))
    grad_norm_two, grad_gain_two = jax.vjp(rms_norm, resid_one, gain_second)[1](grad_hidden_two)
    grad_resid = grad_out.astype(jnp.float32) + grad_norm_two
    grad_branch = grad_resid.astype(jnp.bfloat16)
    branch_all = gather_rows(grad_branch)
    grad_output_w = tn(mixed, branch_all)
    grad_heads = (
        low(nt(branch_all, output_part))
    )
    back = [
        attention_backward(
            qkv[i], grad_heads[:, pair[i]], forward[i][0], forward[i][1], segment, bands[i][1]
        )
        for i in range(pairs)
    ]
    grad_query_seq, grad_key_seq, grad_value_seq = (
        jnp.concatenate([values[part] for values in back], axis=1) for part in range(3)
    )
    grad_bias = jnp.concatenate([bucket_sums(values[3]) for values in back], axis=0)
    grad_query_w = tn(grad_query_seq, hidden_all)
    grad_key_w = tn(grad_key_seq, hidden_all)
    grad_value_w = tn(grad_value_seq, hidden_all)
    grad_hidden_one = scatter_rows(
        nn(grad_query_seq, query_part)
        + nn(grad_key_seq, key_part)
        + nn(grad_value_seq, value_part)
    )
    grad_norm_one, grad_gain_one = jax.vjp(rms_norm, inputs, gain_first)[1](grad_hidden_one)
    grad_tokens = (grad_resid + grad_norm_one).astype(jnp.bfloat16)
    grad_table = lax.dynamic_update_slice_in_dim(
        jnp.zeros((H, BUCKETS), jnp.float32), grad_bias, head_first, 0
    ).reshape(-1)
    weight_grads = (
        lax.psum_scatter(
            grad_query_w.astype(jnp.bfloat16), "fsdp", scatter_dimension=0, tiled=True
        ).astype(jnp.float32),
        lax.psum_scatter(
            grad_key_w.astype(jnp.bfloat16), "fsdp", scatter_dimension=0, tiled=True
        ).astype(jnp.float32),
        lax.psum_scatter(
            grad_value_w.astype(jnp.bfloat16), "fsdp", scatter_dimension=0, tiled=True
        ).astype(jnp.float32),
        lax.psum_scatter(
            grad_output_w.astype(jnp.bfloat16), "fsdp", scatter_dimension=0, tiled=True
        ).astype(jnp.float32),
        lax.psum_scatter(
            grad_gate_w.astype(jnp.bfloat16), "fsdp", scatter_dimension=0, tiled=True
        ).astype(jnp.float32),
        lax.psum_scatter(
            grad_up_w.astype(jnp.bfloat16), "fsdp", scatter_dimension=0, tiled=True
        ).astype(jnp.float32),
        lax.psum_scatter(
            grad_down.astype(jnp.bfloat16), "fsdp", scatter_dimension=0, tiled=True
        ).astype(jnp.float32),
    )
    small_grads = (
        lax.psum_scatter(grad_gain_one, ("seq", "fsdp"), scatter_dimension=0, tiled=True),
        lax.psum_scatter(grad_gain_two, ("seq", "fsdp"), scatter_dimension=0, tiled=True),
        lax.psum_scatter(grad_table, ("seq", "fsdp"), scatter_dimension=0, tiled=True),
    )
    return (
        layer_out[None],
        grad_tokens[None],
        small_grads[0],
        weight_grads[0],
        weight_grads[1],
        weight_grads[2],
        weight_grads[3],
        small_grads[2],
        small_grads[1],
        weight_grads[4],
        weight_grads[5],
        weight_grads[6],
    )


def solution(mesh):
    rows = P(("seq", "fsdp"), None)
    row = P(("seq", "fsdp"))
    activations = P("fsdp", "seq", None)
    in_specs = (
        activations,
        P("fsdp", "seq"),
        row,
        rows,
        rows,
        rows,
        rows,
        row,
        row,
        rows,
        rows,
        rows,
        activations,
    )
    out_specs = (
        activations,
        activations,
        row,
        rows,
        rows,
        rows,
        rows,
        row,
        row,
        rows,
        rows,
        rows,
    )
    seq, fsdp = mesh.shape["seq"], mesh.shape["fsdp"]
    plan = per_device if seq == 2 * CHIPS and H == seq * fsdp else per_device_general
    return jax.shard_map(
        plan,
        mesh=mesh,
        in_specs=in_specs,
        out_specs=out_specs,
        check_vma=False,
    )
```

```python
import functools

import jax
import jax.numpy as jnp
from jax import lax
from jax.experimental import pallas as pl
from jax.experimental.pallas import tpu as pltpu
from jax.sharding import PartitionSpec as P

H = 32
DK = 64
BUCKETS = 32


EPSILON = 1e-06
NEGATIVE = -1000000000.0
BUCKET_EDGES = (12, 16, 23, 32, 46, 64, 91)
PRECISE = lax.Precision.HIGHEST
BLK = 256
PAIR = 128
GELU_SCALE = 0.7978845608028654
GELU_CUBE = 0.044715


def bucket_index(offset):
    distance = jnp.abs(offset)
    coarse = 8 + sum(((distance >= edge).astype(jnp.int32) for edge in BUCKET_EDGES))
    return jnp.where(distance < 8, distance, coarse) + 16 * (offset > 0).astype(jnp.int32)


def nt(left, right):
    return lax.dot_general(
        left, right, (((1,), (1,)), ((), ())), preferred_element_type=jnp.float32
    )


def nn(left, right):
    return jnp.dot(left, right, preferred_element_type=jnp.float32)


def tn(left, right):
    return lax.dot_general(
        left, right, (((0,), (0,)), ((), ())), preferred_element_type=jnp.float32
    )


def params(mib):
    return pltpu.CompilerParams(vmem_limit_bytes=mib * 1024 * 1024)


def cost(flops, bytes_accessed, transcendentals=0):
    return pl.CostEstimate(
        flops=flops, bytes_accessed=bytes_accessed, transcendentals=transcendentals
    )


def head_mask(values, head):
    lane = lax.broadcasted_iota(jnp.int32, values.shape, 1)
    keep = (lane < DK) if head == 0 else (lane >= DK)
    return jnp.where(keep, values, jnp.zeros_like(values))


def fill_strip(strip_ref, head, band_row, tiles):
    wide = jnp.broadcast_to(band_row, (BLK, band_row.shape[1]))
    rolled = pltpu.roll(wide, 0, 1, stride=1, stride_axis=0)
    span = (2 * tiles - 1) * BLK
    near = (tiles - 2) * BLK
    if near > 0:
        strip_ref[head, :, 0:near] = jnp.broadcast_to(band_row[:, 0:1], (BLK, near))
        strip_ref[head, :, near + 3 * BLK : span] = jnp.broadcast_to(
            band_row[:, 4 * BLK - 1 : 4 * BLK], (BLK, span - near - 3 * BLK)
        )
    strip_ref[head, :, near : near + 3 * BLK] = rolled[:, BLK:]


def forward_kernel(tiles, seg_row_ref, seg_col_ref, band_ref, q_ref, k_ref, v_ref, o_ref, lse_ref, strip_ref):
    blk = pl.program_id(0)

    @pl.when(blk == 0)
    def _():
        for head in range(2):
            fill_strip(strip_ref, head, band_ref[head : head + 1, :], tiles)

    keys = tiles * BLK
    start = pl.multiple_of((tiles - 1 - blk) * BLK, BLK)
    same = seg_col_ref[...] == seg_row_ref[...]
    total = jnp.zeros((BLK, PAIR), jnp.float32)
    rows = []
    for head in range(2):
        scores = nt(head_mask(q_ref[...], head), k_ref[...]) + strip_ref[head, :, pl.ds(start, keys)]
        scores = jnp.where(same, scores, NEGATIVE)
        top = jnp.max(scores, axis=1, keepdims=True)
        weight = jnp.exp(scores - top)
        norm = jnp.sum(weight, axis=1, keepdims=True)
        prob = (weight * (1.0 / norm)).astype(jnp.bfloat16)
        total = total + nn(prob, head_mask(v_ref[...], head))
        rows.append(jnp.transpose(jnp.broadcast_to(top + jnp.log(norm), (BLK, PAIR)))[0:1, :])
    o_ref[...] = total.astype(jnp.bfloat16)
    lse_ref[...] = jnp.concatenate(rows, axis=0)


def attention_forward(qkv, segment, band):
    seq_len = qkv.shape[0]
    tiles = seq_len // BLK
    return pl.pallas_call(
        functools.partial(forward_kernel, tiles),
        grid=(tiles,),
        in_specs=[
            pl.BlockSpec((1, seq_len), lambda b: (0, 0)),
            pl.BlockSpec((BLK, 1), lambda b: (b, 0)),
            pl.BlockSpec((2, 4 * BLK), lambda b: (0, 0)),
            pl.BlockSpec((BLK, PAIR), lambda b: (b, 0)),
            pl.BlockSpec((seq_len, PAIR), lambda b: (0, 1)),
            pl.BlockSpec((seq_len, PAIR), lambda b: (0, 2)),
        ],
        out_specs=[
            pl.BlockSpec((BLK, PAIR), lambda b: (b, 0)),
            pl.BlockSpec((2, BLK), lambda b: (0, b)),
        ],
        out_shape=[
            jax.ShapeDtypeStruct((seq_len, PAIR), jnp.bfloat16),
            jax.ShapeDtypeStruct((2, seq_len), jnp.float32),
        ],
        scratch_shapes=[pltpu.VMEM((2, BLK, (2 * tiles - 1) * BLK), jnp.float32)],
        compiler_params=params(20),
        cost_estimate=cost(
            8 * seq_len * seq_len * PAIR, 8 * seq_len * PAIR, 2 * seq_len * seq_len
        ),
        name="attention_forward",
    )(segment[None, :], segment[:, None], band, qkv, qkv, qkv)


def diagonal_sums(tile):
    width = 2 * BLK
    wide = jnp.concatenate([tile, jnp.zeros_like(tile)], axis=1)
    total = wide[:8]
    for start in range(8, BLK, 8):
        total = total + pltpu.roll(wide[start : start + 8], width - start, 1)
    row = lax.broadcasted_iota(jnp.int32, total.shape, 0)
    for shift in (1, 2, 4):
        total = jnp.where((row & shift) != 0, pltpu.roll(total, width - shift, 1), total)
    return jnp.sum(total, axis=0, keepdims=True)


def backward_kernel(tiles, seg_row_ref, seg_col_ref, band_ref, q_ref, k_ref, v_ref, do_ref, o_ref, lse_ref,
                    dq_ref, dk_ref, dv_ref, diag_ref, strip_ref, dk_acc, dv_acc, bias_acc,
                    score_ref, grad_ref, prob_ref, back_ref):
    blk = pl.program_id(0)

    @pl.when(blk == 0)
    def _():
        for head in range(2):
            fill_strip(strip_ref, head, band_ref[head : head + 1, :], tiles)
        dk_acc[...] = jnp.zeros_like(dk_acc)
        dv_acc[...] = jnp.zeros_like(dv_acc)
        bias_acc[...] = jnp.zeros_like(bias_acc)

    seg_row = seg_row_ref[...]
    product = jnp.transpose(
        do_ref[...].astype(jnp.float32) * o_ref[...].astype(jnp.float32)
    )
    grad_q = jnp.zeros((BLK, PAIR), jnp.float32)
    for head in range(2):
        q_h = head_mask(q_ref[...], head)
        do_h = head_mask(do_ref[...], head)
        lse = lse_ref[head : head + 1, :]
        delta = jnp.sum(product[head * DK : (head + 1) * DK, :], axis=0, keepdims=True)
        score_ref[...] = nt(k_ref[...], q_h)
        grad_ref[...] = nt(v_ref[...], do_h)
        for tile in range(tiles):
            at = slice(tile * BLK, (tile + 1) * BLK)
            column = pl.multiple_of((blk - tile + tiles - 1) * BLK, BLK)
            scores = score_ref[at, :] + strip_ref[head, :, pl.ds(column, BLK)]
            scores = jnp.where(seg_col_ref[at, :] == seg_row, scores, NEGATIVE)
            prob = jnp.exp(scores - lse)
            prob_ref[at, :] = prob.astype(jnp.bfloat16)
            grad_s = (prob * (grad_ref[at, :] - delta)).astype(jnp.bfloat16)
            back_ref[at, :] = grad_s
            away = jnp.clip(blk - tile, -2, 2) + 2
            bias_acc[head, away] += grad_s.astype(jnp.float32)
        dv_acc[...] += nn(prob_ref[...], do_h)
        dk_acc[...] += nn(back_ref[...], q_h)
        grad_q = grad_q + tn(back_ref[...], head_mask(k_ref[...], head))
    dq_ref[...] = grad_q.astype(jnp.bfloat16)

    @pl.when(blk == tiles - 1)
    def _():
        dk_ref[...] = dk_acc[...].astype(jnp.bfloat16)
        dv_ref[...] = dv_acc[...].astype(jnp.bfloat16)
        for head in range(2):
            for away in (0, 4):
                far = jnp.sum(bias_acc[head, away], axis=0, keepdims=True)
                diag_ref[head, away : away + 1, :] = jnp.concatenate(
                    [far, jnp.zeros_like(far)], axis=1
                )
            for away in (1, 2, 3):
                diag_ref[head, away : away + 1, :] = diagonal_sums(bias_acc[head, away])


def attention_backward(qkv, grad_o, mixed, lse, segment, band_back):
    seq_len = qkv.shape[0]
    tiles = seq_len // BLK
    rows = pl.BlockSpec((BLK, PAIR), lambda b: (b, 0))
    whole = pl.BlockSpec((seq_len, PAIR), lambda b: (0, 0))
    result = jax.ShapeDtypeStruct((seq_len, PAIR), jnp.bfloat16)
    return pl.pallas_call(
        functools.partial(backward_kernel, tiles),
        grid=(tiles,),
        in_specs=[
            pl.BlockSpec((1, BLK), lambda b: (0, b)),
            pl.BlockSpec((seq_len, 1), lambda b: (0, 0)),
            pl.BlockSpec((2, 4 * BLK), lambda b: (0, 0)),
            rows,
            pl.BlockSpec((seq_len, PAIR), lambda b: (0, 1)),
            pl.BlockSpec((seq_len, PAIR), lambda b: (0, 2)),
            rows,
            rows,
            pl.BlockSpec((2, BLK), lambda b: (0, b)),
        ],
        out_specs=[rows, whole, whole, pl.BlockSpec((2, 5, 2 * BLK), lambda b: (0, 0, 0))],
        out_shape=[
            result,
            result,
            result,
            jax.ShapeDtypeStruct((2, 5, 2 * BLK), jnp.float32),
        ],
        scratch_shapes=[
            pltpu.VMEM((2, BLK, (2 * tiles - 1) * BLK), jnp.float32),
            pltpu.VMEM((seq_len, PAIR), jnp.float32),
            pltpu.VMEM((seq_len, PAIR), jnp.float32),
            pltpu.VMEM((2, 5, BLK, BLK), jnp.float32),
            pltpu.VMEM((seq_len, BLK), jnp.float32),
            pltpu.VMEM((seq_len, BLK), jnp.float32),
            pltpu.VMEM((seq_len, BLK), jnp.bfloat16),
            pltpu.VMEM((seq_len, BLK), jnp.bfloat16),
        ],
        compiler_params=params(20),
        cost_estimate=cost(
            20 * seq_len * seq_len * PAIR, 16 * seq_len * PAIR, 2 * seq_len * seq_len
        ),
        name="attention_backward",
    )(segment[None, :], segment[:, None], band_back, qkv, qkv, qkv, grad_o, mixed, lse)


def one_hot_buckets(offset):
    return (bucket_index(offset)[..., None] == jnp.arange(BUCKETS, dtype=jnp.int32)).astype(
        jnp.float32
    )


def bias_bands(bias_rows):
    offset = jnp.arange(4 * BLK, dtype=jnp.int32) - 2 * BLK
    contract = (((1,), (1,)), ((), ()))
    ahead = lax.dot_general(bias_rows, one_hot_buckets(offset), contract, precision=PRECISE)
    behind = lax.dot_general(bias_rows, one_hot_buckets(-offset), contract, precision=PRECISE)
    return ahead, behind


def bucket_sums(diagonals):
    lane = jnp.arange(2 * BLK, dtype=jnp.int32)
    within = jnp.where(lane < BLK, lane, lane - 2 * BLK)
    away = (jnp.arange(5, dtype=jnp.int32) - 2) * BLK
    onehot = one_hot_buckets(-within[None, :] - away[:, None])
    return jnp.dot(diagonals.reshape(2, -1), onehot.reshape(-1, BUCKETS), precision=PRECISE)


CHIPS = 4
CORE, ACROSS, ALONG = 1, 2, 4
PLACES = ((6, 7), (0, 4), (5, 3), (1, 2))


def wide(values):
    return values.astype(jnp.float32)


def low(values):
    return values.astype(jnp.bfloat16)


def piece_rows(own_ref, piece, start, rows, total):
    base = (own_ref[0] ^ piece) * total + start
    return pl.ds(pl.multiple_of(base, rows), rows)


def gathered(refs):
    out = []
    for core in range(2):
        own, near_x, near_y, first, second = refs[5 * core : 5 * core + 5]
        out += [(core, 0, own), (2 + core, 0, near_x), (4 + core, 0, near_y)]
        out += [(6 + core, 0, first), (6 + core, first.shape[0], second)]
    return out


def join_slots(weight_ref, slots):
    for part in range(3):
        for index, slot in enumerate(slots):
            weight_ref[part * PAIR + index * DK : part * PAIR + (index + 1) * DK, :] = slot[
                part * DK : (part + 1) * DK, :
            ]


def norm_project_kernel(own_ref, gain_ref, slot_a, slot_b, *refs):
    hidden_ref, out_ref, weight_ref = refs[10:]
    total = refs[0].shape[0]
    for piece, start, ref in gathered(refs[:10]):
        values = wide(ref[...])
        scale = lax.rsqrt(jnp.mean(values * values, axis=-1, keepdims=True) + EPSILON)
        at = piece_rows(own_ref, piece, start, ref.shape[0], total)
        hidden_ref[at, :] = low(values * scale * gain_ref[...])
    join_slots(weight_ref, (slot_a, slot_b))
    for chunk in range(8 * total // BLK):
        at = slice(chunk * BLK, (chunk + 1) * BLK)
        out_ref[at, :] = low(nt(hidden_ref[at, :], weight_ref[...]))


VMEM = pl.BlockSpec(memory_space=pltpu.VMEM)
SMEM = pl.BlockSpec(memory_space=pltpu.SMEM)


def norm_project(own, gain, slots, pieces):
    rows, width = pieces[0].shape
    total, features = 8 * rows, 3 * PAIR
    return pl.pallas_call(
        norm_project_kernel,
        in_specs=[SMEM] + [VMEM] * 13,
        out_specs=[VMEM] * 3,
        out_shape=[
            jax.ShapeDtypeStruct((total, width), jnp.bfloat16),
            jax.ShapeDtypeStruct((total, features), jnp.bfloat16),
            jax.ShapeDtypeStruct((features, width), jnp.bfloat16),
        ],
        compiler_params=params(60),
        cost_estimate=cost(
            2 * total * width * features, 2 * (2 * total * width + features * (width + total))
        ),
        name="norm_project",
    )(own, gain[None, :], *slots, *pieces)


def project_kernel(hidden_ref, slot_a, slot_b, out_ref, weight_ref):
    @pl.when(pl.program_id(0) == 0)
    def _():
        join_slots(weight_ref, (slot_a, slot_b))

    out_ref[...] = low(nt(hidden_ref[...], weight_ref[...]))


def project(hidden, slots):
    total, width = hidden.shape
    features = 3 * PAIR
    slot = pl.BlockSpec((slots[0].shape[0], width), lambda b: (0, 0))
    return pl.pallas_call(
        project_kernel,
        grid=(total // BLK,),
        in_specs=[pl.BlockSpec((BLK, width), lambda b: (b, 0)), slot, slot],
        out_specs=[
            pl.BlockSpec((BLK, features), lambda b: (b, 0)),
            pl.BlockSpec((features, width), lambda b: (0, 0)),
        ],
        out_shape=[
            jax.ShapeDtypeStruct((total, features), jnp.bfloat16),
            jax.ShapeDtypeStruct((features, width), jnp.bfloat16),
        ],
        compiler_params=params(12),
        cost_estimate=cost(
            2 * total * width * features, 2 * (total * width + features * (width + total))
        ),
        name="project",
    )(hidden, *slots)


def spread_rows(core, own_ref, lefts, weight, out):
    total = lefts[0].shape[0] // 8
    half = total // 2
    for chip in range(CHIPS):
        at = piece_rows(own_ref, 2 * chip + core, 0, total, total)
        values = None
        for index, left in enumerate(lefts):
            term = nn(left[at, :], weight[index * PAIR : (index + 1) * PAIR, :])
            values = term if values is None else values + term
        for index, place in enumerate(PLACES[chip]):
            out[place * half : (place + 1) * half, :] = low(
                values[index * half : (index + 1) * half, :]
            )


def spread_kernel(core, counts, own_ref, *refs):
    lefts, rights = refs[: counts[0]], refs[counts[0] : counts[0] + counts[1]]
    out, weight = refs[-2:]
    start = 0
    for right in rights:
        weight[start : start + right.shape[0], :] = right[...]
        start += right.shape[0]
    spread_rows(core, own_ref, lefts, weight, out)


def spread(own, core, lefts, rights, limit):
    total, width = lefts[0].shape[0] // 2, rights[0].shape[1]
    depth = sum(right.shape[0] for right in rights)
    return pl.pallas_call(
        functools.partial(spread_kernel, core, (len(lefts), len(rights))),
        in_specs=[SMEM] + [VMEM] * (len(lefts) + len(rights)),
        out_specs=VMEM,
        out_shape=jax.ShapeDtypeStruct((total, width), jnp.bfloat16),
        scratch_shapes=[pltpu.VMEM((depth, width), jnp.bfloat16)],
        compiler_params=params(limit),
        cost_estimate=cost(
            2 * total * width * depth, 2 * (total * width + depth * (width + total))
        ),
        name="spread",
    )(own, *lefts, *rights)


def last_kernel(own_ref, gain_ref, hidden_ref, *refs):
    lefts, rights = refs[:6], refs[6:8]
    out, slot_a, slot_b, sum_ref, weight = refs[8:]
    for index, right in enumerate(rights):
        weight[3 * PAIR * index : 3 * PAIR * (index + 1), :] = right[...]
    spread_rows(0, own_ref, lefts, weight, out)
    width = out.shape[1]
    for start in range(0, width, 512):
        cols = slice(start, start + 512)
        total = None
        for part in range(3):
            grad = tn(lefts[part][...], hidden_ref[:, cols])
            slot_a[part * DK : (part + 1) * DK, cols] = low(grad[:DK])
            slot_b[part * DK : (part + 1) * DK, cols] = low(grad[DK:])
            at = slice(part * PAIR, (part + 1) * PAIR)
            term = jnp.sum(grad * wide(weight[at, cols]), axis=0, keepdims=True)
            total = term if total is None else total + term
        sum_ref[:, cols] = total / gain_ref[:, cols]


def last(own, gain, hidden, lefts, rights):
    total, width = hidden.shape
    return pl.pallas_call(
        last_kernel,
        in_specs=[SMEM] + [VMEM] * 10,
        out_specs=[VMEM] * 4,
        out_shape=[
            jax.ShapeDtypeStruct((total // 2, width), jnp.bfloat16),
            jax.ShapeDtypeStruct((3 * DK, width), jnp.bfloat16),
            jax.ShapeDtypeStruct((3 * DK, width), jnp.bfloat16),
            jax.ShapeDtypeStruct((1, width), jnp.float32),
        ],
        scratch_shapes=[pltpu.VMEM((6 * PAIR, width), jnp.bfloat16)],
        compiler_params=params(56),
        cost_estimate=cost(12 * total * width * PAIR, 6 * total * width),
        name="last",
    )(own, gain[None, :], hidden, *lefts, *rights)


def heads_back_kernel(own_ref, weight_a0, weight_a1, weight_b0, weight_b1, mixed_a, mixed_b, *refs):
    heads_a, heads_b, grad_a, grad_b, whole, weight = refs[10:]
    total = refs[0].shape[0]
    for piece, start, ref in gathered(refs[:10]):
        whole[piece_rows(own_ref, piece, start, ref.shape[0], total), :] = ref[...]
    for index, ref in enumerate((weight_a0, weight_a1, weight_b0, weight_b1)):
        weight[index * DK : (index + 1) * DK, :] = ref[...]
    for chunk in range(8 * total // BLK):
        at = slice(chunk * BLK, (chunk + 1) * BLK)
        heads = low(nt(whole[at, :], weight[...]))
        heads_a[at, :] = heads[:, :PAIR]
        heads_b[at, :] = heads[:, PAIR:]
    grad_a[...] = low(tn(mixed_a[...], whole[...]))
    grad_b[...] = low(tn(mixed_b[...], whole[...]))


def heads_back(own, weights, mixed, pieces):
    rows, width = pieces[0].shape
    total = 8 * rows
    outs = pl.pallas_call(
        heads_back_kernel,
        in_specs=[SMEM] + [VMEM] * 16,
        out_specs=[VMEM] * 4,
        out_shape=[jax.ShapeDtypeStruct((total, PAIR), jnp.bfloat16)] * 2
        + [jax.ShapeDtypeStruct((PAIR, width), jnp.bfloat16)] * 2,
        scratch_shapes=[
            pltpu.VMEM((total, width), jnp.bfloat16),
            pltpu.VMEM((2 * PAIR, width), jnp.bfloat16),
        ],
        compiler_params=params(20),
        cost_estimate=cost(8 * total * width * PAIR, 2 * total * width),
        name="heads_back",
    )(own, *weights, *mixed, *pieces)
    return outs[:2], outs[2:]


def qkv_grad_kernel(gain_ref, hidden_ref, dq_ref, dk_ref, dv_ref, weight_ref, slot_a, slot_b, sum_ref):
    total = None
    for part, ref in enumerate((dq_ref, dk_ref, dv_ref)):
        grad = tn(ref[...], hidden_ref[...])
        slot_a[part * DK : (part + 1) * DK, :] = low(grad[:DK])
        slot_b[part * DK : (part + 1) * DK, :] = low(grad[DK:])
        at = slice(part * PAIR, (part + 1) * PAIR)
        term = jnp.sum(grad * wide(weight_ref[at, :]), axis=0, keepdims=True)
        total = term if total is None else total + term
    sum_ref[...] = total / gain_ref[...]


def qkv_grad(gain, hidden, dq, dk, dv, weight):
    total, width = hidden.shape
    cols = 512
    col = pl.BlockSpec((1, cols), lambda c: (0, c))
    back = pl.BlockSpec((total, PAIR), lambda c: (0, 0))
    slot = pl.BlockSpec((3 * DK, cols), lambda c: (0, c))
    return pl.pallas_call(
        qkv_grad_kernel,
        grid=(width // cols,),
        in_specs=[
            col,
            pl.BlockSpec((total, cols), lambda c: (0, c)),
            back,
            back,
            back,
            pl.BlockSpec((3 * PAIR, cols), lambda c: (0, c)),
        ],
        out_specs=[slot, slot, col],
        out_shape=[
            jax.ShapeDtypeStruct((3 * DK, width), jnp.bfloat16),
            jax.ShapeDtypeStruct((3 * DK, width), jnp.bfloat16),
            jax.ShapeDtypeStruct((1, width), jnp.float32),
        ],
        compiler_params=params(12),
        cost_estimate=cost(6 * total * width * PAIR, 2 * total * width + 12 * PAIR * width),
        name="qkv_grad",
    )(gain[None, :], hidden, dq, dk, dv, weight)


def assemble_kernel(own, *refs):
    outs = refs[6:]
    units = own.shape[0] // 3
    half = units // 2
    for part, weight in enumerate(outs):
        for chip in range(CHIPS):
            for index, place in enumerate(PLACES[chip]):
                ref, start = own, part * units + index * half
                if chip:
                    ref = refs[2 * chip - 2]
                    if start >= 3 * half:
                        ref, start = refs[2 * chip - 1], start - 3 * half
                weight[place * half : (place + 1) * half, :] = ref[start : start + half, :]


def assemble(own, *stacks):
    rows, width = own.shape
    return pl.pallas_call(
        assemble_kernel,
        in_specs=[VMEM] * 7,
        out_specs=[VMEM] * 3,
        out_shape=[jax.ShapeDtypeStruct((CHIPS * rows // 3, width), jnp.bfloat16)] * 3,
        compiler_params=params(20),
        cost_estimate=cost(0, 16 * rows * width),
        name="assemble",
    )(own, *stacks)


def feed_kernel(gate_w, up_w, down_w, *refs):
    hidden, cot, outs = refs[:2], refs[2:4], refs[4:]
    inner_ref, dgate_ref, dup_ref, grad_own, grad_other, out_own, out_other = outs
    rows = hidden[0].shape[0]
    values = jnp.concatenate([hidden[0][...], hidden[1][...]], axis=0)
    grads = jnp.concatenate([cot[0][...], cot[1][...]], axis=0)
    gate = nt(values, gate_w[...])
    up = nt(values, up_w[...])
    grad_m = nt(grads, down_w[...])
    square = gate * gate
    bend = jnp.tanh(GELU_SCALE * gate * (1.0 + GELU_CUBE * square))
    part = 0.5 * (1.0 + bend)
    act = gate * part
    slope = part + 0.5 * gate * (1.0 - bend * bend) * (
        GELU_SCALE * (1.0 + 3.0 * GELU_CUBE * square)
    )
    inner = low(act * up)
    inner_ref[...] = inner
    dgate = low(grad_m * up * slope)
    dup = low(grad_m * act)
    dgate_ref[...] = dgate
    dup_ref[...] = dup
    grad_h = low(nn(dgate, gate_w[...]) + nn(dup, up_w[...]))
    grad_own[...] = grad_h[:rows]
    grad_other[...] = grad_h[rows:]
    result = low(nn(inner, down_w[...]))
    out_own[...] = result[:rows]
    out_other[...] = result[rows:]


def feed(weights, hidden, cot):
    rows, width = hidden[0].shape
    total, units = 2 * rows, weights[0].shape[0]
    return pl.pallas_call(
        feed_kernel,
        in_specs=[VMEM] * 7,
        out_specs=[VMEM] * 7,
        out_shape=[jax.ShapeDtypeStruct((total, units), jnp.bfloat16)] * 3
        + [jax.ShapeDtypeStruct((rows, width), jnp.bfloat16)] * 4,
        compiler_params=params(24),
        cost_estimate=cost(12 * total * width * units, 2 * 4 * (total + units) * width),
        name="feed",
    )(*weights, *hidden, *cot)


def feed_grad_kernel(terms, *refs):
    lefts, pieces = refs[: 4 * terms], refs[4 * terms : 4 * terms + 8]
    outs, right = refs[-4:-1], refs[-1]
    rows = pieces[0].shape[0]
    for index, piece in enumerate(pieces):
        right[index * rows : (index + 1) * rows, :] = piece[...]
    for term in range(terms):
        left = jnp.concatenate([ref[...] for ref in lefts[4 * term : 4 * term + 4]], axis=0)
        grad = low(tn(left, right[...]))
        start = 0
        for out in outs:
            size = out.shape[0] // terms
            out[term * size : (term + 1) * size, :] = grad[start : start + size]
            start += size


def feed_grad(lefts, pieces):
    terms = len(lefts)
    rows, width = pieces[0].shape
    units = lefts[0][0].shape[1]
    return pl.pallas_call(
        functools.partial(feed_grad_kernel, terms),
        in_specs=[VMEM] * (4 * terms + 8),
        out_specs=[VMEM] * 3,
        out_shape=[
            jax.ShapeDtypeStruct((terms * units // part, width), jnp.bfloat16)
            for part in (4, 4, 2)
        ],
        scratch_shapes=[pltpu.VMEM((8 * rows, width), jnp.bfloat16)],
        compiler_params=params(48),
        cost_estimate=cost(16 * terms * rows * width * units, 24 * rows * width),
        name="feed_grad",
    )(*[value for left in lefts for value in left], *pieces)


def second_kernel(terms, keep, from_x, from_y, to_x, to_y):
    size = to_x.shape[0] // terms
    for term in range(terms):
        out = slice(term * size, (term + 1) * size)
        base = 4 * term * size
        pair = 2 * term * size
        to_x[out, :] = low(wide(keep[base : base + size, :]) + wide(from_y[pair : pair + size, :]))
        to_y[out, :] = low(
            wide(keep[base + size : base + 2 * size, :])
            + wide(from_x[pair + size : pair + 2 * size, :])
        )


def second(terms, keep, from_x, from_y):
    shape = jax.ShapeDtypeStruct((from_x.shape[0] // 2, from_x.shape[1]), jnp.bfloat16)
    return pl.pallas_call(
        functools.partial(second_kernel, terms),
        in_specs=[VMEM] * 3,
        out_specs=[VMEM] * 2,
        out_shape=[shape, shape],
        compiler_params=params(12),
        cost_estimate=cost(0, 6 * from_x.shape[0] * from_x.shape[1]),
        name="second",
    )(keep, from_x, from_y)


def totals_kernel(terms, *refs):
    outs = refs[5 * len(terms) :]
    done = 0
    for index, count in enumerate(terms):
        keep, from_x, from_y, second_x, second_y = refs[5 * index : 5 * index + 5]
        for term in range(count):
            out = outs[done]
            done += 1
            size = out.shape[0] // 2
            base, pair, one = 4 * term * size, 2 * term * size, term * size
            out[:size, :] = (
                wide(keep[base + 2 * size : base + 3 * size, :])
                + wide(from_x[pair : pair + size, :])
                + wide(second_y[one : one + size, :])
            )
            out[size:, :] = (
                wide(keep[base + 3 * size : base + 4 * size, :])
                + wide(from_y[pair + size : pair + 2 * size, :])
                + wide(second_x[one : one + size, :])
            )


def totals(terms, *groups):
    shapes = [
        (2 * group[3].shape[0] // count, group[3].shape[1])
        for count, group in zip(terms, groups)
        for _ in range(count)
    ]
    return pl.pallas_call(
        functools.partial(totals_kernel, terms),
        in_specs=[VMEM] * (5 * len(groups)),
        out_specs=[VMEM] * len(shapes),
        out_shape=[jax.ShapeDtypeStruct(shape, jnp.float32) for shape in shapes],
        compiler_params=params(56),
        cost_estimate=cost(0, 10 * sum(rows * width for rows, width in shapes)),
        name="totals",
    )(*[value for group in groups for value in group])


def finish_kernel(own_qkv, own_out, first, second_ref, grad_q, grad_k, grad_v, grad_o):
    size = grad_q.shape[0]
    grad_q[...] = wide(own_qkv[:size, :]) + wide(first[:size, :])
    grad_k[...] = wide(own_qkv[size : 2 * size, :]) + wide(first[size:, :])
    grad_v[...] = wide(own_qkv[2 * size :, :]) + wide(second_ref[:size, :])
    grad_o[...] = wide(own_out[...]) + wide(second_ref[size:, :])


def finish(own_qkv, own_out, first, second_part):
    rows, width = own_out.shape
    cols = 1024
    return pl.pallas_call(
        finish_kernel,
        grid=(width // cols,),
        in_specs=[
            pl.BlockSpec((value.shape[0], cols), lambda c: (0, c))
            for value in (own_qkv, own_out, first, second_part)
        ],
        out_specs=[pl.BlockSpec((rows, cols), lambda c: (0, c))] * 4,
        out_shape=[jax.ShapeDtypeStruct((rows, width), jnp.float32)] * 4,
        compiler_params=params(56),
        cost_estimate=cost(0, 24 * rows * width),
        name="finish",
    )(own_qkv, own_out, first, second_part)


def sends_kernel(own_ref, other_ref, to_x, to_y, keep):
    size = to_x.shape[0]
    to_x[...] = low(wide(own_ref[:size, :]) + wide(other_ref[:size, :]))
    to_y[...] = low(wide(own_ref[size : 2 * size, :]) + wide(other_ref[size : 2 * size, :]))
    keep[...] = wide(own_ref[2 * size :, :]) + wide(other_ref[2 * size :, :])


def sends(own, other, limit):
    rows, width = own.shape
    shape = jax.ShapeDtypeStruct((rows // 4, width), jnp.bfloat16)
    return pl.pallas_call(
        sends_kernel,
        in_specs=[VMEM] * 2,
        out_specs=[VMEM] * 3,
        out_shape=[shape, shape, jax.ShapeDtypeStruct((rows // 2, width), jnp.float32)],
        compiler_params=params(limit),
        cost_estimate=cost(0, 7 * rows * width),
        name="sends",
    )(own, other)


def fence(*values):
    return lax.optimization_barrier(values)


def swap(values, bits):
    return lax.ppermute(values, "seq", [(i, i ^ bits) for i in range(2 * CHIPS)])


def ring(values, step):
    n = lax.axis_size("fsdp")
    return lax.ppermute(values, "fsdp", [(i, (i + step) % n) for i in range(n)])


def line_order(slots):
    n = len(slots)
    order = (lax.axis_index("fsdp") - jnp.arange(n, dtype=jnp.int32)) % n
    return jnp.stack(slots)[order]


def both(values, other, bits):
    high = (lax.axis_index("seq") & bits) != 0
    return jnp.concatenate(
        [jnp.where(high, other, values), jnp.where(high, values, other)], axis=0
    )


def halves(values, bits):
    high = (lax.axis_index("seq") & bits) != 0
    size = values.shape[0] // 2
    lower, upper = values[:size], values[size:]
    return jnp.where(high, upper, lower), jnp.where(high, lower, upper)


def plane_total(keep, from_x, from_y, second_x, second_y):
    size = keep.shape[0] // 4
    first = wide(keep[2 * size : 3 * size]) + wide(from_x[:size]) + wide(second_y)
    second = wide(keep[3 * size :]) + wide(from_y[size:]) + wide(second_x)
    return jnp.concatenate([first, second], axis=0)


def add(*values):
    return functools.reduce(lambda left, right: left + right, [wide(value) for value in values])


def per_device(
    tokens,
    starts,
    first_gain,
    query_weight,
    key_weight,
    value_weight,
    output_weight,
    bias_table,
    second_gain,
    gate_weight,
    up_weight,
    down_weight,
    cotangent,
):
    index = lax.axis_index("seq")[None]
    own = tokens[0]
    half = own.shape[0] // 2
    grad_out = cotangent[0]
    rows = first_gain.shape[0]
    buckets = bias_table.shape[0]
    qkv0 = low(
        jnp.concatenate([query_weight, key_weight, value_weight, output_weight], axis=0)
    )
    small = low(jnp.concatenate([first_gain, second_gain, bias_table]))
    own, qkv0, small, gate_weight, up_weight, down_weight = fence(
        own, qkv0, small, gate_weight, up_weight, down_weight
    )

    tok_x, tok_y = swap(own, ACROSS), swap(own, ALONG)
    small_slots = [small] + [ring(small, k) for k in range(1, 4)]
    small_slots, own, qkv0, gate_weight, up_weight, down_weight = fence(
        small_slots, own, qkv0, gate_weight, up_weight, down_weight
    )
    qkv1 = ring(qkv0, 1)
    gain_part = line_order([value[: 2 * rows] for value in small_slots]).reshape(-1)
    packed = jnp.concatenate([gain_part, low(starts[0])])[None]
    packed = both(packed, swap(packed, CORE), CORE)
    packed, gate_weight, up_weight, down_weight = fence(
        packed, gate_weight, up_weight, down_weight
    )
    near = both(packed, swap(packed, ACROSS), ACROSS)
    far = both(swap(packed, ALONG), swap(packed, ALONG | ACROSS), ACROSS)
    packed = both(near, far, ALONG)
    packed, tok_x, tok_y, gate_weight, up_weight, down_weight = fence(
        packed, tok_x, tok_y, gate_weight, up_weight, down_weight
    )

    tok_d1, tok_d2 = swap(tok_y[:half], ACROSS), swap(tok_x[half:], ALONG)
    tok_cx, tok_cy = swap(tok_x, CORE), swap(tok_y, CORE)
    gain_count = gain_part.shape[0]
    gains = wide(packed[:, :gain_count]).reshape(-1, 4, 2, rows)
    gain_first = gains[:, :, 0].reshape(-1)
    gain_second = gains[:, :, 1].reshape(-1)
    segment = jnp.cumsum(packed[:, gain_count:].reshape(-1).astype(jnp.int32), dtype=jnp.int32)
    tables = [wide(value[2 * rows :]) for value in small_slots]
    bands = [bias_bands(jnp.stack(tables[2 * p : 2 * p + 2])) for p in range(2)]
    tok_d1, tok_d2, tok_cx, tok_cy, segment, gain_first, gain_second, bands, own = fence(
        tok_d1, tok_d2, tok_cx, tok_cy, segment, gain_first, gain_second, bands, own
    )

    tok_c, tok_c1, tok_c2 = swap(own, CORE), swap(tok_d1, CORE), swap(tok_d2, CORE)
    feed0 = low(jnp.concatenate([gate_weight, up_weight, down_weight], axis=0))
    tok_c, tok_c1, tok_c2, feed0, qkv1 = fence(tok_c, tok_c1, tok_c2, feed0, qkv1)

    qkv2 = ring(qkv1, 1)
    feed_half = feed0.shape[0] // 2
    feed_top, feed_low = feed0[:feed_half], feed0[feed_half:]
    feed_xl, feed_yt = swap(feed_low, ACROSS), swap(feed_top, ALONG)
    feed_top, feed_low = fence(feed_top, feed_low)
    feed_xt, feed_yl = swap(feed_top, ACROSS), swap(feed_low, ALONG)
    tok_pieces = (own, tok_x, tok_y, tok_d1, tok_d2, tok_c, tok_cx, tok_cy, tok_c1, tok_c2)
    hidden_one, qkv_a, weight_a = norm_project(index, gain_first, (qkv0, qkv1), tok_pieces)
    hidden_one, qkv_a, weight_a, qkv2, grad_out, feed_xl, feed_yt = fence(
        hidden_one, qkv_a, weight_a, qkv2, grad_out, feed_xl, feed_yt
    )

    qkv3 = ring(qkv2, 1)
    feed_dt, feed_dl = swap(feed_yt, ACROSS), swap(feed_xl, ALONG)
    mixed_a, lse_a = attention_forward(qkv_a, segment, bands[0][0])
    out0, out1, out2 = (value[3 * DK :] for value in (qkv0, qkv1, qkv2))
    mixed_a, lse_a, hidden_one, qkv3, feed_xt, feed_yl, out0, out1, out2 = fence(
        mixed_a, lse_a, hidden_one, qkv3, feed_xt, feed_yl, out0, out1, out2
    )

    cot1 = ring(grad_out, 1)
    qkv_b, weight_b = project(hidden_one, (qkv2, qkv3))
    out3 = qkv3[3 * DK :]
    mixed_b, lse_b = attention_forward(qkv_b, segment, bands[1][0])
    mixed_b, lse_b, out3, grad_out = fence(mixed_b, lse_b, out3, grad_out)
    cot_c0 = swap(grad_out, CORE)
    out_slots = (out0, out1, out2, out3)
    mixed = (mixed_a, mixed_b)
    part_other = spread(index, 1, mixed, out_slots, 14)
    part_other, mixed, feed_dt, feed_dl, cot1, cot_c0 = fence(
        part_other, mixed, feed_dt, feed_dl, cot1, cot_c0
    )
    part_other, cot2, cot_c1 = swap(part_other, CORE), ring(cot1, 1), swap(cot1, CORE)
    part_own = spread(index, 0, mixed, out_slots, 14)
    part_own, part_other, cot_c1 = fence(part_own, part_other, cot_c1)

    send_x, send_y, keep = sends(part_own, part_other, 12)
    send_x, send_y, keep = fence(send_x, send_y, keep)
    from_x, from_y = swap(send_x, ACROSS), swap(send_y, ALONG)
    weights = assemble(feed0, feed_xt, feed_xl, feed_yt, feed_yl, feed_dt, feed_dl)
    from_x, from_y, weights, cot2 = fence(from_x, from_y, weights, cot2)
    send_x, send_y = fence(*second(1, keep, from_x, from_y))
    second_x, second_y = swap(send_x, ACROSS), swap(send_y, ALONG)
    cot3, cot_c2 = ring(cot2, 1), swap(cot2, CORE)
    second_x, second_y, cot3, cot_c2 = fence(second_x, second_y, cot3, cot_c2)
    inputs = wide(own)
    resid_one = inputs + plane_total(keep, from_x, from_y, second_x, second_y)

    scale_two = lax.rsqrt(jnp.mean(resid_one * resid_one, axis=-1, keepdims=True) + EPSILON)
    normed_two = resid_one * scale_two
    hid0 = low(normed_two * gain_second)
    hid0, resid_one, scale_two = fence(hid0, resid_one, scale_two)

    hid1, hid_c0, cot_c3 = ring(hid0, 1), swap(hid0, CORE), swap(cot3, CORE)
    hid_c0, cot_c3 = fence(hid_c0, cot_c3)
    feed_a = feed(weights, (hid0, hid_c0), (grad_out, cot_c0))
    feed_a, hid1 = fence(feed_a, hid1)
    hid2, hid_c1 = ring(hid1, 1), swap(hid1, CORE)
    hid_c1, feed_a = fence(hid_c1, feed_a)
    grad_c0, out_c0 = swap(feed_a[4], CORE), swap(feed_a[6], CORE)
    feed_b = feed(weights, (hid1, hid_c1), (cot1, cot_c1))
    feed_b, hid2, grad_c0, out_c0 = fence(feed_b, hid2, grad_c0, out_c0)
    hid3, hid_c2 = ring(hid2, 1), swap(hid2, CORE)
    hid_c2, feed_b = fence(hid_c2, feed_b)
    grad_c1, out_c1 = swap(feed_b[4], CORE), swap(feed_b[6], CORE)
    feed_c = feed(weights, (hid2, hid_c2), (cot2, cot_c2))
    feed_c, hid3, grad_c1, out_c1 = fence(feed_c, hid3, grad_c1, out_c1)
    hid_c3 = swap(hid3, CORE)
    dh = ring(low(add(feed_b[3], grad_c1)), 1)
    hid_c3, feed_c = fence(hid_c3, feed_c)
    grad_c2, out_c2 = swap(feed_c[4], CORE), swap(feed_c[6], CORE)
    feed_d = feed(weights, (hid3, hid_c3), (cot3, cot_c3))
    feed_d, dh, grad_c2, out_c2 = fence(feed_d, dh, grad_c2, out_c2)
    dh = ring(low(add(feed_c[3], grad_c2, dh)), 1)
    grad_c3, out_c3 = swap(feed_d[4], CORE), swap(feed_d[6], CORE)
    parts = (feed_a, feed_b, feed_c, feed_d)
    hid_pieces = (hid0, hid_c0, hid1, hid_c1, hid2, hid_c2, hid3, hid_c3)
    cot_pieces = (grad_out, cot_c0, cot1, cot_c1, cot2, cot_c2, cot3, cot_c3)
    grad_down = feed_grad([[part[0] for part in parts]], cot_pieces)
    grad_down, dh, grad_c3, out_c3, hid_pieces = fence(grad_down, dh, grad_c3, out_c3, hid_pieces)

    dh, out_sum = ring(low(add(feed_d[3], grad_c3, dh)), 1), low(add(feed_b[5], out_c1))
    out_sum = ring(out_sum, 1)
    down_x, down_y, down_keep = grad_down
    down_fx, down_fy = swap(down_x, ACROSS), swap(down_y, ALONG)
    grad_both = feed_grad(
        [[part[1] for part in parts], [part[2] for part in parts]], hid_pieces
    )
    dh, grad_both = fence(dh, grad_both)

    grad_hidden_two = add(feed_a[3], grad_c0, dh)
    normed_two = resid_one * scale_two
    shared = grad_hidden_two * gain_second
    grad_resid = wide(grad_out) + scale_two * (
        shared - normed_two * jnp.mean(shared * normed_two, axis=-1, keepdims=True)
    )
    branch = low(grad_resid)
    gain_two_rows = jnp.sum(grad_hidden_two * normed_two, axis=0)
    branch, grad_resid, gain_two_rows, down_fx, down_fy = fence(
        branch, grad_resid, gain_two_rows, down_fx, down_fy
    )

    br_x, br_y, br_c = swap(branch, ACROSS), swap(branch, ALONG), swap(branch, CORE)
    down_x, down_y = second(1, down_keep, down_fx, down_fy)
    out_send = low(add(feed_c[5], out_c2, out_sum))
    br_x, br_y, br_c, down_x, down_y, out_send = fence(
        br_x, br_y, br_c, down_x, down_y, out_send
    )
    br_d1, br_d2 = swap(br_y[:half], ACROSS), swap(br_x[half:], ALONG)
    br_cx, br_cy = swap(br_x, CORE), swap(br_y, CORE)
    out_sum = ring(out_send, 1)
    br_d1, br_d2, br_cx, br_cy = fence(br_d1, br_d2, br_cx, br_cy)

    br_c1, br_c2 = swap(br_d1, CORE), swap(br_d2, CORE)
    down_sx, down_sy = swap(down_x, ACROSS), swap(down_y, ALONG)
    pieces = (branch, br_x, br_y, br_d1, br_d2, br_c, br_cx, br_cy, br_c1, br_c2)
    grad_heads, grad_outs = heads_back(index, out_slots, mixed, pieces)
    grad_heads, grad_outs, grad_both, out_sum = fence(
        grad_heads, grad_outs, grad_both, out_sum
    )

    go0, go1 = grad_outs[0][:DK], grad_outs[0][DK:]
    go2, go3 = grad_outs[1][:DK], grad_outs[1][DK:]
    both_x, both_y, both_keep = grad_both
    both_fx, both_fy = swap(both_x, ACROSS), swap(both_y, ALONG)
    out_sum = ring(low(add(feed_d[5], out_c3, out_sum)), 1)
    dq_b, dk_b, dv_b, diag_b = attention_backward(
        qkv_b, grad_heads[1], mixed[1], lse_b, segment, bands[1][1]
    )
    dq_b, dk_b, dv_b, diag_b, go3 = fence(dq_b, dk_b, dv_b, diag_b, go3)

    go_sum = ring(go3, -1)
    gq2, gq3, sums_b = qkv_grad(gain_first, hidden_one, dq_b, dk_b, dv_b, weight_b)
    gq2, gq3, sums_b, qkv_a, out_sum = fence(gq2, gq3, sums_b, qkv_a, out_sum)

    gq = ring(gq3, -1)
    dq_a, dk_a, dv_a, diag_a = attention_backward(
        qkv_a, grad_heads[0], mixed[0], lse_a, segment, bands[0][1]
    )
    dq_a, dk_a, dv_a, diag_a, both_fx, both_fy = fence(
        dq_a, dk_a, dv_a, diag_a, both_fx, both_fy
    )

    both_x, both_y = second(2, both_keep, both_fx, both_fy)
    both_sx, both_sy = swap(both_x, ACROSS), swap(both_y, ALONG)
    lefts = (dq_a, dk_a, dv_a, dq_b, dk_b, dv_b)
    back_other = spread(index, 1, lefts, (weight_a, weight_b), 14)
    back_other, lefts, gq, go_sum, down_sx, down_sy = fence(
        back_other, lefts, gq, go_sum, down_sx, down_sy
    )
    gq = ring(low(add(gq2, gq)), -1)
    back_other = swap(back_other, CORE)
    back_own, gq0, gq1, sums_a = last(index, gain_first, hidden_one, lefts, (weight_a, weight_b))
    back_own, back_other, gq0, gq1, sums_a, both_sx, both_sy, go_sum = fence(
        back_own, back_other, gq0, gq1, sums_a, both_sx, both_sy, go_sum
    )
    send_x, send_y, keep = sends(back_own, back_other, 56)
    gain_rows = jnp.stack([(sums_a + sums_b)[0], gain_two_rows]).reshape(2, 2, 2, 2, 4, -1)
    gain_rows = jnp.transpose(gain_rows, (3, 1, 2, 4, 0, 5)).reshape(2 * CHIPS, -1)
    send_x, send_y, keep, gq1, gain_rows, go_sum = fence(
        send_x, send_y, keep, gq1, gain_rows, go_sum
    )
    go_sum = ring(low(add(go2, go_sum)), -1)

    from_x, from_y = swap(send_x, ACROSS), swap(send_y, ALONG)
    gain_keep, gain_send = halves(gain_rows, CORE)
    gain_rows = gain_keep + swap(gain_send, CORE)
    gain_rows, gq1 = fence(gain_rows, gq1)
    gq_send = low(add(gq1, gq))
    gq_first = ring(gq_send[: 2 * DK], -1)
    gain_keep, gain_send = halves(gain_rows, ALONG)
    gain_rows = gain_keep + swap(gain_send, ALONG)
    last_send = jnp.concatenate([gq_send[2 * DK :], low(add(go1, go_sum))], axis=0)
    from_x, from_y, gain_rows, gq_first, last_send = fence(
        from_x, from_y, gain_rows, gq_first, last_send
    )
    send_x, send_y = second(1, keep, from_x, from_y)
    second_x, second_y = swap(send_x, ACROSS), swap(send_y, ALONG)
    gq_last = ring(last_send, -1)
    gain_keep, gain_send = halves(gain_rows, ACROSS)
    gain_rows = gain_keep + swap(gain_send, ACROSS)
    late = (down_keep, both_keep, resid_one, diag_a, gq_first, go0, gq0, out_sum)
    second_x, second_y, gain_rows, late = fence(second_x, second_y, gain_rows, late)
    down_keep, both_keep, resid_one, diag_a, gq_first, go0, gq0, out_sum = late
    tables_a, tables_b = bucket_sums(diag_a), bucket_sums(diag_b)
    table_slots = (tables_a[0], tables_a[1], tables_b[0], tables_b[1])
    gain_slots = line_order(list(gain_rows.reshape(4, -1)))
    sums = [jnp.concatenate([gain_slots[k], table_slots[k]]) for k in range(4)]
    sums = sums[0] + sum(ring(sums[k], -k) for k in range(1, 4))
    grad_down_w, grad_gate_w, grad_up_w = totals(
        (1, 2),
        (down_keep, down_fx, down_fy, down_sx, down_sy),
        (both_keep, both_fx, both_fy, both_sx, both_sy),
    )
    layer_out = low(resid_one + add(feed_a[5], out_c0, out_sum))
    grad_hidden_one = plane_total(keep, from_x, from_y, second_x, second_y)
    scale_one = lax.rsqrt(jnp.mean(inputs * inputs, axis=-1, keepdims=True) + EPSILON)
    normed_one = inputs * scale_one
    shared = grad_hidden_one * gain_first
    grad_tokens = low(
        grad_resid
        + scale_one * (shared - normed_one * jnp.mean(shared * normed_one, axis=-1, keepdims=True))
    )
    gq_last, sums = fence(gq_last, sums)
    grad_q, grad_k, grad_v, grad_output_w = finish(gq0, go0, gq_first, gq_last)
    return (
        layer_out[None],
        grad_tokens[None],
        sums[:rows],
        grad_q,
        grad_k,
        grad_v,
        grad_output_w,
        sums[2 * rows :],
        sums[rows : 2 * rows],
        grad_gate_w,
        grad_up_w,
        grad_down_w,
    )


def rms_norm(values, gain):
    return values * lax.rsqrt(jnp.mean(values * values, axis=-1, keepdims=True) + EPSILON) * gain


def gated_gelu(gate, up_part):
    return jax.nn.gelu(gate, approximate=True) * up_part


def gather_rows(values):
    return lax.all_gather(values, "seq", axis=0, tiled=True)


def scatter_rows(values):
    return lax.psum_scatter(
        values.astype(jnp.bfloat16), "seq", scatter_dimension=0, tiled=True
    ).astype(jnp.float32)


def per_device_general(
    tokens,
    starts,
    first_gain,
    query_weight,
    key_weight,
    value_weight,
    output_weight,
    bias_table,
    second_gain,
    gate_weight,
    up_weight,
    down_weight,
    cotangent,
):
    segment = jnp.cumsum(lax.all_gather(starts, "seq", axis=1, tiled=True)[0], dtype=jnp.int32)
    inputs = tokens[0].astype(jnp.float32)
    grad_out = cotangent[0]
    head_count = H // lax.axis_size("seq")
    head_first = lax.axis_index("seq") * head_count
    query_low = query_weight.astype(jnp.bfloat16)
    key_low = key_weight.astype(jnp.bfloat16)
    value_low = value_weight.astype(jnp.bfloat16)
    output_low = output_weight.astype(jnp.bfloat16)
    gate_low = gate_weight.astype(jnp.bfloat16)
    up_low = up_weight.astype(jnp.bfloat16)
    down_low = down_weight.astype(jnp.bfloat16)
    first_low = first_gain.astype(jnp.bfloat16)
    second_low = second_gain.astype(jnp.bfloat16)
    table_low = bias_table.astype(jnp.bfloat16)
    query_part, key_part, value_part, output_part, gate_part, up_rows, down_part = (
        lax.all_gather(query_low, "fsdp", axis=0, tiled=True),
        lax.all_gather(key_low, "fsdp", axis=0, tiled=True),
        lax.all_gather(value_low, "fsdp", axis=0, tiled=True),
        lax.all_gather(output_low, "fsdp", axis=0, tiled=True),
        lax.all_gather(gate_low, "fsdp", axis=0, tiled=True),
        lax.all_gather(up_low, "fsdp", axis=0, tiled=True),
        lax.all_gather(down_low, "fsdp", axis=0, tiled=True),
    )
    gain_one, gain_two, table_full = (
        lax.all_gather(first_low, ("seq", "fsdp"), axis=0, tiled=True),
        lax.all_gather(second_low, ("seq", "fsdp"), axis=0, tiled=True),
        lax.all_gather(table_low, ("seq", "fsdp"), axis=0, tiled=True),
    )
    gain_first = gain_one.astype(jnp.float32)
    gain_second = gain_two.astype(jnp.float32)
    bias_rows = lax.dynamic_slice_in_dim(
        table_full.astype(jnp.float32).reshape(H, BUCKETS), head_first, head_count, 0
    )
    hidden_one = rms_norm(inputs, gain_first).astype(jnp.bfloat16)
    hidden_all = gather_rows(hidden_one)
    query_head = (
        low(nt(hidden_all, query_part))
    )
    key_head = (
        low(nt(hidden_all, key_part))
    )
    value_head = (
        low(nt(hidden_all, value_part))
    )
    pairs = head_count // 2
    pair = [slice(index * PAIR, (index + 1) * PAIR) for index in range(pairs)]
    bands = [bias_bands(bias_rows[2 * index : 2 * index + 2]) for index in range(pairs)]
    qkv = [
        jnp.concatenate([query_head[:, at], key_head[:, at], value_head[:, at]], axis=1)
        for at in pair
    ]
    forward = [attention_forward(qkv[i], segment, bands[i][0]) for i in range(pairs)]
    mixed = jnp.concatenate([out for out, _ in forward], axis=1)
    resid_one = inputs + scatter_rows(nn(mixed, output_part))
    hidden_two = rms_norm(resid_one, gain_second).astype(jnp.bfloat16)
    hidden_two_all = gather_rows(hidden_two)
    gate = nt(hidden_two_all, gate_part)
    up_part = nt(hidden_two_all, up_rows)
    inner = gated_gelu(gate, up_part).astype(jnp.bfloat16)
    layer_out = (resid_one + scatter_rows(nn(inner, down_part))).astype(jnp.bfloat16)
    grad_out_all = gather_rows(grad_out)
    grad_inner = nt(grad_out_all, down_part)
    grad_down = tn(inner, grad_out_all)
    grad_gate, grad_up = jax.vjp(gated_gelu, gate, up_part)[1](grad_inner)
    grad_gate = grad_gate.astype(jnp.bfloat16)
    grad_up = grad_up.astype(jnp.bfloat16)
    grad_gate_w = tn(grad_gate, hidden_two_all)
    grad_up_w = tn(grad_up, hidden_two_all)
    grad_hidden_two = scatter_rows(nn(grad_gate, gate_part) + nn(grad_up, up_rows))
    grad_norm_two, grad_gain_two = jax.vjp(rms_norm, resid_one, gain_second)[1](grad_hidden_two)
    grad_resid = grad_out.astype(jnp.float32) + grad_norm_two
    grad_branch = grad_resid.astype(jnp.bfloat16)
    branch_all = gather_rows(grad_branch)
    grad_output_w = tn(mixed, branch_all)
    grad_heads = (
        low(nt(branch_all, output_part))
    )
    back = [
        attention_backward(
            qkv[i], grad_heads[:, pair[i]], forward[i][0], forward[i][1], segment, bands[i][1]
        )
        for i in range(pairs)
    ]
    grad_query_seq, grad_key_seq, grad_value_seq = (
        jnp.concatenate([values[part] for values in back], axis=1) for part in range(3)
    )
    grad_bias = jnp.concatenate([bucket_sums(values[3]) for values in back], axis=0)
    grad_query_w = tn(grad_query_seq, hidden_all)
    grad_key_w = tn(grad_key_seq, hidden_all)
    grad_value_w = tn(grad_value_seq, hidden_all)
    grad_hidden_one = scatter_rows(
        nn(grad_query_seq, query_part)
        + nn(grad_key_seq, key_part)
        + nn(grad_value_seq, value_part)
    )
    grad_norm_one, grad_gain_one = jax.vjp(rms_norm, inputs, gain_first)[1](grad_hidden_one)
    grad_tokens = (grad_resid + grad_norm_one).astype(jnp.bfloat16)
    grad_table = lax.dynamic_update_slice_in_dim(
        jnp.zeros((H, BUCKETS), jnp.float32), grad_bias, head_first, 0
    ).reshape(-1)
    weight_grads = (
        lax.psum_scatter(
            grad_query_w.astype(jnp.bfloat16), "fsdp", scatter_dimension=0, tiled=True
        ).astype(jnp.float32),
        lax.psum_scatter(
            grad_key_w.astype(jnp.bfloat16), "fsdp", scatter_dimension=0, tiled=True
        ).astype(jnp.float32),
        lax.psum_scatter(
            grad_value_w.astype(jnp.bfloat16), "fsdp", scatter_dimension=0, tiled=True
        ).astype(jnp.float32),
        lax.psum_scatter(
            grad_output_w.astype(jnp.bfloat16), "fsdp", scatter_dimension=0, tiled=True
        ).astype(jnp.float32),
        lax.psum_scatter(
            grad_gate_w.astype(jnp.bfloat16), "fsdp", scatter_dimension=0, tiled=True
        ).astype(jnp.float32),
        lax.psum_scatter(
            grad_up_w.astype(jnp.bfloat16), "fsdp", scatter_dimension=0, tiled=True
        ).astype(jnp.float32),
        lax.psum_scatter(
            grad_down.astype(jnp.bfloat16), "fsdp", scatter_dimension=0, tiled=True
        ).astype(jnp.float32),
    )
    small_grads = (
        lax.psum_scatter(grad_gain_one, ("seq", "fsdp"), scatter_dimension=0, tiled=True),
        lax.psum_scatter(grad_gain_two, ("seq", "fsdp"), scatter_dimension=0, tiled=True),
        lax.psum_scatter(grad_table, ("seq", "fsdp"), scatter_dimension=0, tiled=True),
    )
    return (
        layer_out[None],
        grad_tokens[None],
        small_grads[0],
        weight_grads[0],
        weight_grads[1],
        weight_grads[2],
        weight_grads[3],
        small_grads[2],
        small_grads[1],
        weight_grads[4],
        weight_grads[5],
        weight_grads[6],
    )


def solution(mesh):
    rows = P(("seq", "fsdp"), None)
    row = P(("seq", "fsdp"))
    activations = P("fsdp", "seq", None)
    in_specs = (
        activations,
        P("fsdp", "seq"),
        row,
        rows,
        rows,
        rows,
        rows,
        row,
        row,
        rows,
        rows,
        rows,
        activations,
    )
    out_specs = (
        activations,
        activations,
        row,
        rows,
        rows,
        rows,
        rows,
        row,
        row,
        rows,
        rows,
        rows,
    )
    seq, fsdp = mesh.shape["seq"], mesh.shape["fsdp"]
    plan = per_device if seq == 2 * CHIPS and H == seq * fsdp else per_device_general
    return jax.shard_map(
        plan,
        mesh=mesh,
        in_specs=in_specs,
        out_specs=out_specs,
        check_vma=False,
    )
```

```python
import functools

import jax
import jax.numpy as jnp
from jax import lax
from jax.experimental import pallas as pl
from jax.experimental.pallas import tpu as pltpu
from jax.sharding import PartitionSpec as P

H = 32
DK = 64
BUCKETS = 32


EPSILON = 1e-06
NEGATIVE = -1000000000.0
BUCKET_EDGES = (12, 16, 23, 32, 46, 64, 91)
PRECISE = lax.Precision.HIGHEST
BLK = 256
PAIR = 128
GELU_SCALE = 0.7978845608028654
GELU_CUBE = 0.044715


def bucket_index(offset):
    distance = jnp.abs(offset)
    coarse = 8 + sum(((distance >= edge).astype(jnp.int32) for edge in BUCKET_EDGES))
    return jnp.where(distance < 8, distance, coarse) + 16 * (offset > 0).astype(jnp.int32)


def nt(left, right):
    return lax.dot_general(
        left, right, (((1,), (1,)), ((), ())), preferred_element_type=jnp.float32
    )


def nn(left, right):
    return jnp.dot(left, right, preferred_element_type=jnp.float32)


def tn(left, right):
    return lax.dot_general(
        left, right, (((0,), (0,)), ((), ())), preferred_element_type=jnp.float32
    )


def params(mib):
    return pltpu.CompilerParams(vmem_limit_bytes=mib * 1024 * 1024)


def cost(flops, bytes_accessed, transcendentals=0):
    return pl.CostEstimate(
        flops=flops, bytes_accessed=bytes_accessed, transcendentals=transcendentals
    )


def head_mask(values, head):
    lane = lax.broadcasted_iota(jnp.int32, values.shape, 1)
    keep = (lane < DK) if head == 0 else (lane >= DK)
    return jnp.where(keep, values, jnp.zeros_like(values))


def fill_strip(strip_ref, head, band_row, tiles):
    wide = jnp.broadcast_to(band_row, (BLK, band_row.shape[1]))
    rolled = pltpu.roll(wide, 0, 1, stride=1, stride_axis=0)
    span = (2 * tiles - 1) * BLK
    near = (tiles - 2) * BLK
    if near > 0:
        strip_ref[head, :, 0:near] = jnp.broadcast_to(band_row[:, 0:1], (BLK, near))
        strip_ref[head, :, near + 3 * BLK : span] = jnp.broadcast_to(
            band_row[:, 4 * BLK - 1 : 4 * BLK], (BLK, span - near - 3 * BLK)
        )
    strip_ref[head, :, near : near + 3 * BLK] = rolled[:, BLK:]


def forward_kernel(tiles, seg_row_ref, seg_col_ref, band_ref, q_ref, k_ref, v_ref, o_ref, lse_ref, strip_ref):
    blk = pl.program_id(0)

    @pl.when(blk == 0)
    def _():
        for head in range(2):
            fill_strip(strip_ref, head, band_ref[head : head + 1, :], tiles)

    keys = tiles * BLK
    start = pl.multiple_of((tiles - 1 - blk) * BLK, BLK)
    same = seg_col_ref[...] == seg_row_ref[...]
    total = jnp.zeros((BLK, PAIR), jnp.float32)
    rows = []
    for head in range(2):
        scores = nt(head_mask(q_ref[...], head), k_ref[...]) + strip_ref[head, :, pl.ds(start, keys)]
        scores = jnp.where(same, scores, NEGATIVE)
        top = jnp.max(scores, axis=1, keepdims=True)
        weight = jnp.exp(scores - top)
        norm = jnp.sum(weight, axis=1, keepdims=True)
        mixed = nn(weight.astype(jnp.bfloat16), head_mask(v_ref[...], head))
        total = total + mixed * (1.0 / norm)
        rows.append(jnp.transpose(jnp.broadcast_to(top + jnp.log(norm), (BLK, PAIR)))[0:1, :])
    o_ref[...] = total.astype(jnp.bfloat16)
    lse_ref[...] = jnp.concatenate(rows, axis=0)


def attention_forward(qkv, segment, band):
    seq_len = qkv.shape[0]
    tiles = seq_len // BLK
    return pl.pallas_call(
        functools.partial(forward_kernel, tiles),
        grid=(tiles,),
        in_specs=[
            pl.BlockSpec((1, seq_len), lambda b: (0, 0)),
            pl.BlockSpec((BLK, 1), lambda b: (b, 0)),
            pl.BlockSpec((2, 4 * BLK), lambda b: (0, 0)),
            pl.BlockSpec((BLK, PAIR), lambda b: (b, 0)),
            pl.BlockSpec((seq_len, PAIR), lambda b: (0, 1)),
            pl.BlockSpec((seq_len, PAIR), lambda b: (0, 2)),
        ],
        out_specs=[
            pl.BlockSpec((BLK, PAIR), lambda b: (b, 0)),
            pl.BlockSpec((2, BLK), lambda b: (0, b)),
        ],
        out_shape=[
            jax.ShapeDtypeStruct((seq_len, PAIR), jnp.bfloat16),
            jax.ShapeDtypeStruct((2, seq_len), jnp.float32),
        ],
        scratch_shapes=[pltpu.VMEM((2, BLK, (2 * tiles - 1) * BLK), jnp.float32)],
        compiler_params=params(20),
        cost_estimate=cost(
            8 * seq_len * seq_len * PAIR, 8 * seq_len * PAIR, 2 * seq_len * seq_len
        ),
        name="attention_forward",
    )(segment[None, :], segment[:, None], band, qkv, qkv, qkv)


def diagonal_sums(tile):
    width = 2 * BLK
    wide = jnp.concatenate([tile, jnp.zeros_like(tile)], axis=1)
    total = wide[:8]
    for start in range(8, BLK, 8):
        total = total + pltpu.roll(wide[start : start + 8], width - start, 1)
    row = lax.broadcasted_iota(jnp.int32, total.shape, 0)
    for shift in (1, 2, 4):
        total = jnp.where((row & shift) != 0, pltpu.roll(total, width - shift, 1), total)
    return jnp.sum(total, axis=0, keepdims=True)


def backward_kernel(tiles, seg_row_ref, seg_col_ref, band_ref, q_ref, k_ref, v_ref, do_ref, o_ref, lse_ref,
                    dq_ref, dk_ref, dv_ref, diag_ref, strip_ref, dk_acc, dv_acc, bias_acc,
                    score_ref, grad_ref, prob_ref, back_ref):
    blk = pl.program_id(0)

    @pl.when(blk == 0)
    def _():
        for head in range(2):
            fill_strip(strip_ref, head, band_ref[head : head + 1, :], tiles)
        dk_acc[...] = jnp.zeros_like(dk_acc)
        dv_acc[...] = jnp.zeros_like(dv_acc)
        bias_acc[...] = jnp.zeros_like(bias_acc)

    seg_row = seg_row_ref[...]
    product = jnp.transpose(
        do_ref[...].astype(jnp.float32) * o_ref[...].astype(jnp.float32)
    )
    grad_q = jnp.zeros((BLK, PAIR), jnp.float32)
    for head in range(2):
        q_h = head_mask(q_ref[...], head)
        do_h = head_mask(do_ref[...], head)
        lse = lse_ref[head : head + 1, :]
        delta = jnp.sum(product[head * DK : (head + 1) * DK, :], axis=0, keepdims=True)
        score_ref[...] = nt(k_ref[...], q_h)
        grad_ref[...] = nt(v_ref[...], do_h)
        for tile in range(tiles):
            at = slice(tile * BLK, (tile + 1) * BLK)
            column = pl.multiple_of((blk - tile + tiles - 1) * BLK, BLK)
            scores = score_ref[at, :] + strip_ref[head, :, pl.ds(column, BLK)]
            scores = jnp.where(seg_col_ref[at, :] == seg_row, scores, NEGATIVE)
            prob = jnp.exp(scores - lse)
            prob_ref[at, :] = prob.astype(jnp.bfloat16)
            grad_s = (prob * (grad_ref[at, :] - delta)).astype(jnp.bfloat16)
            back_ref[at, :] = grad_s
            away = jnp.clip(blk - tile, -2, 2) + 2
            bias_acc[head, away] += grad_s.astype(jnp.float32)
        dv_acc[...] += nn(prob_ref[...], do_h)
        dk_acc[...] += nn(back_ref[...], q_h)
        grad_q = grad_q + tn(back_ref[...], head_mask(k_ref[...], head))
    dq_ref[...] = grad_q.astype(jnp.bfloat16)

    @pl.when(blk == tiles - 1)
    def _():
        dk_ref[...] = dk_acc[...].astype(jnp.bfloat16)
        dv_ref[...] = dv_acc[...].astype(jnp.bfloat16)
        for head in range(2):
            for away in (0, 4):
                far = jnp.sum(bias_acc[head, away], axis=0, keepdims=True)
                diag_ref[head, away : away + 1, :] = jnp.concatenate(
                    [far, jnp.zeros_like(far)], axis=1
                )
            for away in (1, 2, 3):
                diag_ref[head, away : away + 1, :] = diagonal_sums(bias_acc[head, away])


def attention_backward(qkv, grad_o, mixed, lse, segment, band_back):
    seq_len = qkv.shape[0]
    tiles = seq_len // BLK
    rows = pl.BlockSpec((BLK, PAIR), lambda b: (b, 0))
    whole = pl.BlockSpec((seq_len, PAIR), lambda b: (0, 0))
    result = jax.ShapeDtypeStruct((seq_len, PAIR), jnp.bfloat16)
    return pl.pallas_call(
        functools.partial(backward_kernel, tiles),
        grid=(tiles,),
        in_specs=[
            pl.BlockSpec((1, BLK), lambda b: (0, b)),
            pl.BlockSpec((seq_len, 1), lambda b: (0, 0)),
            pl.BlockSpec((2, 4 * BLK), lambda b: (0, 0)),
            rows,
            pl.BlockSpec((seq_len, PAIR), lambda b: (0, 1)),
            pl.BlockSpec((seq_len, PAIR), lambda b: (0, 2)),
            rows,
            rows,
            pl.BlockSpec((2, BLK), lambda b: (0, b)),
        ],
        out_specs=[rows, whole, whole, pl.BlockSpec((2, 5, 2 * BLK), lambda b: (0, 0, 0))],
        out_shape=[
            result,
            result,
            result,
            jax.ShapeDtypeStruct((2, 5, 2 * BLK), jnp.float32),
        ],
        scratch_shapes=[
            pltpu.VMEM((2, BLK, (2 * tiles - 1) * BLK), jnp.float32),
            pltpu.VMEM((seq_len, PAIR), jnp.float32),
            pltpu.VMEM((seq_len, PAIR), jnp.float32),
            pltpu.VMEM((2, 5, BLK, BLK), jnp.float32),
            pltpu.VMEM((seq_len, BLK), jnp.float32),
            pltpu.VMEM((seq_len, BLK), jnp.float32),
            pltpu.VMEM((seq_len, BLK), jnp.bfloat16),
            pltpu.VMEM((seq_len, BLK), jnp.bfloat16),
        ],
        compiler_params=params(20),
        cost_estimate=cost(
            20 * seq_len * seq_len * PAIR, 16 * seq_len * PAIR, 2 * seq_len * seq_len
        ),
        name="attention_backward",
    )(segment[None, :], segment[:, None], band_back, qkv, qkv, qkv, grad_o, mixed, lse)


def one_hot_buckets(offset):
    return (bucket_index(offset)[..., None] == jnp.arange(BUCKETS, dtype=jnp.int32)).astype(
        jnp.float32
    )


def bias_bands(bias_rows):
    offset = jnp.arange(4 * BLK, dtype=jnp.int32) - 2 * BLK
    contract = (((1,), (1,)), ((), ()))
    ahead = lax.dot_general(bias_rows, one_hot_buckets(offset), contract, precision=PRECISE)
    behind = lax.dot_general(bias_rows, one_hot_buckets(-offset), contract, precision=PRECISE)
    return ahead, behind


def bucket_sums(diagonals):
    lane = jnp.arange(2 * BLK, dtype=jnp.int32)
    within = jnp.where(lane < BLK, lane, lane - 2 * BLK)
    away = (jnp.arange(5, dtype=jnp.int32) - 2) * BLK
    onehot = one_hot_buckets(-within[None, :] - away[:, None])
    return jnp.dot(diagonals.reshape(2, -1), onehot.reshape(-1, BUCKETS), precision=PRECISE)


CHIPS = 4
CORE, ACROSS, ALONG = 1, 2, 4
PLACES = ((6, 7), (0, 4), (5, 3), (1, 2))


def wide(values):
    return values.astype(jnp.float32)


def low(values):
    return values.astype(jnp.bfloat16)


def piece_rows(own_ref, piece, start, rows, total):
    base = (own_ref[0] ^ piece) * total + start
    return pl.ds(pl.multiple_of(base, rows), rows)


def gathered(refs):
    out = []
    for core in range(2):
        own, near_x, near_y, first, second = refs[5 * core : 5 * core + 5]
        out += [(core, 0, own), (2 + core, 0, near_x), (4 + core, 0, near_y)]
        out += [(6 + core, 0, first), (6 + core, first.shape[0], second)]
    return out


def join_slots(weight_ref, slots):
    for part in range(3):
        for index, slot in enumerate(slots):
            weight_ref[part * PAIR + index * DK : part * PAIR + (index + 1) * DK, :] = slot[
                part * DK : (part + 1) * DK, :
            ]


def norm_project_kernel(own_ref, gain_ref, slot_a, slot_b, *refs):
    hidden_ref, out_ref, weight_ref = refs[10:]
    total = refs[0].shape[0]
    for piece, start, ref in gathered(refs[:10]):
        values = wide(ref[...])
        scale = lax.rsqrt(jnp.mean(values * values, axis=-1, keepdims=True) + EPSILON)
        at = piece_rows(own_ref, piece, start, ref.shape[0], total)
        hidden_ref[at, :] = low(values * scale * gain_ref[...])
    join_slots(weight_ref, (slot_a, slot_b))
    for chunk in range(8 * total // BLK):
        at = slice(chunk * BLK, (chunk + 1) * BLK)
        out_ref[at, :] = low(nt(hidden_ref[at, :], weight_ref[...]))


VMEM = pl.BlockSpec(memory_space=pltpu.VMEM)
SMEM = pl.BlockSpec(memory_space=pltpu.SMEM)


def norm_project(own, gain, slots, pieces):
    rows, width = pieces[0].shape
    total, features = 8 * rows, 3 * PAIR
    return pl.pallas_call(
        norm_project_kernel,
        in_specs=[SMEM] + [VMEM] * 13,
        out_specs=[VMEM] * 3,
        out_shape=[
            jax.ShapeDtypeStruct((total, width), jnp.bfloat16),
            jax.ShapeDtypeStruct((total, features), jnp.bfloat16),
            jax.ShapeDtypeStruct((features, width), jnp.bfloat16),
        ],
        compiler_params=params(60),
        cost_estimate=cost(
            2 * total * width * features, 2 * (2 * total * width + features * (width + total))
        ),
        name="norm_project",
    )(own, gain[None, :], *slots, *pieces)


def project_kernel(hidden_ref, slot_a, slot_b, out_ref, weight_ref):
    @pl.when(pl.program_id(0) == 0)
    def _():
        join_slots(weight_ref, (slot_a, slot_b))

    out_ref[...] = low(nt(hidden_ref[...], weight_ref[...]))


def project(hidden, slots):
    total, width = hidden.shape
    features = 3 * PAIR
    slot = pl.BlockSpec((slots[0].shape[0], width), lambda b: (0, 0))
    return pl.pallas_call(
        project_kernel,
        grid=(total // BLK,),
        in_specs=[pl.BlockSpec((BLK, width), lambda b: (b, 0)), slot, slot],
        out_specs=[
            pl.BlockSpec((BLK, features), lambda b: (b, 0)),
            pl.BlockSpec((features, width), lambda b: (0, 0)),
        ],
        out_shape=[
            jax.ShapeDtypeStruct((total, features), jnp.bfloat16),
            jax.ShapeDtypeStruct((features, width), jnp.bfloat16),
        ],
        compiler_params=params(12),
        cost_estimate=cost(
            2 * total * width * features, 2 * (total * width + features * (width + total))
        ),
        name="project",
    )(hidden, *slots)


def spread_rows(core, own_ref, lefts, weight, out):
    total = lefts[0].shape[0] // 8
    half = total // 2
    for chip in range(CHIPS):
        at = piece_rows(own_ref, 2 * chip + core, 0, total, total)
        values = None
        for index, left in enumerate(lefts):
            term = nn(left[at, :], weight[index * PAIR : (index + 1) * PAIR, :])
            values = term if values is None else values + term
        for index, place in enumerate(PLACES[chip]):
            out[place * half : (place + 1) * half, :] = low(
                values[index * half : (index + 1) * half, :]
            )


def spread_kernel(core, counts, own_ref, *refs):
    lefts, rights = refs[: counts[0]], refs[counts[0] : counts[0] + counts[1]]
    out, weight = refs[-2:]
    start = 0
    for right in rights:
        weight[start : start + right.shape[0], :] = right[...]
        start += right.shape[0]
    spread_rows(core, own_ref, lefts, weight, out)


def spread(own, core, lefts, rights, limit):
    total, width = lefts[0].shape[0] // 2, rights[0].shape[1]
    depth = sum(right.shape[0] for right in rights)
    return pl.pallas_call(
        functools.partial(spread_kernel, core, (len(lefts), len(rights))),
        in_specs=[SMEM] + [VMEM] * (len(lefts) + len(rights)),
        out_specs=VMEM,
        out_shape=jax.ShapeDtypeStruct((total, width), jnp.bfloat16),
        scratch_shapes=[pltpu.VMEM((depth, width), jnp.bfloat16)],
        compiler_params=params(limit),
        cost_estimate=cost(
            2 * total * width * depth, 2 * (total * width + depth * (width + total))
        ),
        name="spread",
    )(own, *lefts, *rights)


def last_kernel(own_ref, gain_ref, hidden_ref, *refs):
    lefts, rights = refs[:6], refs[6:8]
    out, slot_a, slot_b, sum_ref, weight = refs[8:]
    for index, right in enumerate(rights):
        weight[3 * PAIR * index : 3 * PAIR * (index + 1), :] = right[...]
    spread_rows(0, own_ref, lefts, weight, out)
    width = out.shape[1]
    for start in range(0, width, 512):
        cols = slice(start, start + 512)
        total = None
        for part in range(3):
            grad = tn(lefts[part][...], hidden_ref[:, cols])
            slot_a[part * DK : (part + 1) * DK, cols] = low(grad[:DK])
            slot_b[part * DK : (part + 1) * DK, cols] = low(grad[DK:])
            at = slice(part * PAIR, (part + 1) * PAIR)
            term = jnp.sum(grad * wide(weight[at, cols]), axis=0, keepdims=True)
            total = term if total is None else total + term
        sum_ref[:, cols] = total / gain_ref[:, cols]


def last(own, gain, hidden, lefts, rights):
    total, width = hidden.shape
    return pl.pallas_call(
        last_kernel,
        in_specs=[SMEM] + [VMEM] * 10,
        out_specs=[VMEM] * 4,
        out_shape=[
            jax.ShapeDtypeStruct((total // 2, width), jnp.bfloat16),
            jax.ShapeDtypeStruct((3 * DK, width), jnp.bfloat16),
            jax.ShapeDtypeStruct((3 * DK, width), jnp.bfloat16),
            jax.ShapeDtypeStruct((1, width), jnp.float32),
        ],
        scratch_shapes=[pltpu.VMEM((6 * PAIR, width), jnp.bfloat16)],
        compiler_params=params(56),
        cost_estimate=cost(12 * total * width * PAIR, 6 * total * width),
        name="last",
    )(own, gain[None, :], hidden, *lefts, *rights)


def heads_back_kernel(own_ref, weight_a0, weight_a1, weight_b0, weight_b1, mixed_a, mixed_b, *refs):
    heads_a, heads_b, grad_a, grad_b, whole, weight = refs[10:]
    total = refs[0].shape[0]
    for piece, start, ref in gathered(refs[:10]):
        whole[piece_rows(own_ref, piece, start, ref.shape[0], total), :] = ref[...]
    for index, ref in enumerate((weight_a0, weight_a1, weight_b0, weight_b1)):
        weight[index * DK : (index + 1) * DK, :] = ref[...]
    for chunk in range(8 * total // BLK):
        at = slice(chunk * BLK, (chunk + 1) * BLK)
        heads = low(nt(whole[at, :], weight[...]))
        heads_a[at, :] = heads[:, :PAIR]
        heads_b[at, :] = heads[:, PAIR:]
    grad_a[...] = low(tn(mixed_a[...], whole[...]))
    grad_b[...] = low(tn(mixed_b[...], whole[...]))


def heads_back(own, weights, mixed, pieces):
    rows, width = pieces[0].shape
    total = 8 * rows
    outs = pl.pallas_call(
        heads_back_kernel,
        in_specs=[SMEM] + [VMEM] * 16,
        out_specs=[VMEM] * 4,
        out_shape=[jax.ShapeDtypeStruct((total, PAIR), jnp.bfloat16)] * 2
        + [jax.ShapeDtypeStruct((PAIR, width), jnp.bfloat16)] * 2,
        scratch_shapes=[
            pltpu.VMEM((total, width), jnp.bfloat16),
            pltpu.VMEM((2 * PAIR, width), jnp.bfloat16),
        ],
        compiler_params=params(20),
        cost_estimate=cost(8 * total * width * PAIR, 2 * total * width),
        name="heads_back",
    )(own, *weights, *mixed, *pieces)
    return outs[:2], outs[2:]


def qkv_grad_kernel(gain_ref, hidden_ref, dq_ref, dk_ref, dv_ref, weight_ref, slot_a, slot_b, sum_ref):
    total = None
    for part, ref in enumerate((dq_ref, dk_ref, dv_ref)):
        grad = tn(ref[...], hidden_ref[...])
        slot_a[part * DK : (part + 1) * DK, :] = low(grad[:DK])
        slot_b[part * DK : (part + 1) * DK, :] = low(grad[DK:])
        at = slice(part * PAIR, (part + 1) * PAIR)
        term = jnp.sum(grad * wide(weight_ref[at, :]), axis=0, keepdims=True)
        total = term if total is None else total + term
    sum_ref[...] = total / gain_ref[...]


def qkv_grad(gain, hidden, dq, dk, dv, weight):
    total, width = hidden.shape
    cols = 512
    col = pl.BlockSpec((1, cols), lambda c: (0, c))
    back = pl.BlockSpec((total, PAIR), lambda c: (0, 0))
    slot = pl.BlockSpec((3 * DK, cols), lambda c: (0, c))
    return pl.pallas_call(
        qkv_grad_kernel,
        grid=(width // cols,),
        in_specs=[
            col,
            pl.BlockSpec((total, cols), lambda c: (0, c)),
            back,
            back,
            back,
            pl.BlockSpec((3 * PAIR, cols), lambda c: (0, c)),
        ],
        out_specs=[slot, slot, col],
        out_shape=[
            jax.ShapeDtypeStruct((3 * DK, width), jnp.bfloat16),
            jax.ShapeDtypeStruct((3 * DK, width), jnp.bfloat16),
            jax.ShapeDtypeStruct((1, width), jnp.float32),
        ],
        compiler_params=params(12),
        cost_estimate=cost(6 * total * width * PAIR, 2 * total * width + 12 * PAIR * width),
        name="qkv_grad",
    )(gain[None, :], hidden, dq, dk, dv, weight)


def assemble_kernel(own, *refs):
    outs = refs[6:]
    units = own.shape[0] // 3
    half = units // 2
    for part, weight in enumerate(outs):
        for chip in range(CHIPS):
            for index, place in enumerate(PLACES[chip]):
                ref, start = own, part * units + index * half
                if chip:
                    ref = refs[2 * chip - 2]
                    if start >= 3 * half:
                        ref, start = refs[2 * chip - 1], start - 3 * half
                weight[place * half : (place + 1) * half, :] = ref[start : start + half, :]


def assemble(own, *stacks):
    rows, width = own.shape
    return pl.pallas_call(
        assemble_kernel,
        in_specs=[VMEM] * 7,
        out_specs=[VMEM] * 3,
        out_shape=[jax.ShapeDtypeStruct((CHIPS * rows // 3, width), jnp.bfloat16)] * 3,
        compiler_params=params(20),
        cost_estimate=cost(0, 16 * rows * width),
        name="assemble",
    )(own, *stacks)


def feed_kernel(gate_w, up_w, down_w, *refs):
    hidden, cot, outs = refs[:2], refs[2:4], refs[4:]
    inner_ref, dgate_ref, dup_ref, grad_own, grad_other, out_own, out_other = outs
    rows = hidden[0].shape[0]
    values = jnp.concatenate([hidden[0][...], hidden[1][...]], axis=0)
    grads = jnp.concatenate([cot[0][...], cot[1][...]], axis=0)
    gate = nt(values, gate_w[...])
    up = nt(values, up_w[...])
    grad_m = nt(grads, down_w[...])
    square = gate * gate
    bend = jnp.tanh(GELU_SCALE * gate * (1.0 + GELU_CUBE * square))
    part = 0.5 * (1.0 + bend)
    act = gate * part
    slope = part + 0.5 * gate * (1.0 - bend * bend) * (
        GELU_SCALE * (1.0 + 3.0 * GELU_CUBE * square)
    )
    inner = low(act * up)
    inner_ref[...] = inner
    dgate = low(grad_m * up * slope)
    dup = low(grad_m * act)
    dgate_ref[...] = dgate
    dup_ref[...] = dup
    grad_h = low(nn(dgate, gate_w[...]) + nn(dup, up_w[...]))
    grad_own[...] = grad_h[:rows]
    grad_other[...] = grad_h[rows:]
    result = low(nn(inner, down_w[...]))
    out_own[...] = result[:rows]
    out_other[...] = result[rows:]


def feed(weights, hidden, cot):
    rows, width = hidden[0].shape
    total, units = 2 * rows, weights[0].shape[0]
    return pl.pallas_call(
        feed_kernel,
        in_specs=[VMEM] * 7,
        out_specs=[VMEM] * 7,
        out_shape=[jax.ShapeDtypeStruct((total, units), jnp.bfloat16)] * 3
        + [jax.ShapeDtypeStruct((rows, width), jnp.bfloat16)] * 4,
        compiler_params=params(24),
        cost_estimate=cost(12 * total * width * units, 2 * 4 * (total + units) * width),
        name="feed",
    )(*weights, *hidden, *cot)


def feed_grad_kernel(terms, *refs):
    lefts, pieces = refs[: 4 * terms], refs[4 * terms : 4 * terms + 8]
    outs, right = refs[-4:-1], refs[-1]
    rows = pieces[0].shape[0]
    for index, piece in enumerate(pieces):
        right[index * rows : (index + 1) * rows, :] = piece[...]
    for term in range(terms):
        left = jnp.concatenate([ref[...] for ref in lefts[4 * term : 4 * term + 4]], axis=0)
        grad = low(tn(left, right[...]))
        start = 0
        for out in outs:
            size = out.shape[0] // terms
            out[term * size : (term + 1) * size, :] = grad[start : start + size]
            start += size


def feed_grad(lefts, pieces):
    terms = len(lefts)
    rows, width = pieces[0].shape
    units = lefts[0][0].shape[1]
    return pl.pallas_call(
        functools.partial(feed_grad_kernel, terms),
        in_specs=[VMEM] * (4 * terms + 8),
        out_specs=[VMEM] * 3,
        out_shape=[
            jax.ShapeDtypeStruct((terms * units // part, width), jnp.bfloat16)
            for part in (4, 4, 2)
        ],
        scratch_shapes=[pltpu.VMEM((8 * rows, width), jnp.bfloat16)],
        compiler_params=params(48),
        cost_estimate=cost(16 * terms * rows * width * units, 24 * rows * width),
        name="feed_grad",
    )(*[value for left in lefts for value in left], *pieces)


def second_kernel(terms, keep, from_x, from_y, to_x, to_y):
    size = to_x.shape[0] // terms
    for term in range(terms):
        out = slice(term * size, (term + 1) * size)
        base = 4 * term * size
        pair = 2 * term * size
        to_x[out, :] = low(wide(keep[base : base + size, :]) + wide(from_y[pair : pair + size, :]))
        to_y[out, :] = low(
            wide(keep[base + size : base + 2 * size, :])
            + wide(from_x[pair + size : pair + 2 * size, :])
        )


def second(terms, keep, from_x, from_y):
    shape = jax.ShapeDtypeStruct((from_x.shape[0] // 2, from_x.shape[1]), jnp.bfloat16)
    return pl.pallas_call(
        functools.partial(second_kernel, terms),
        in_specs=[VMEM] * 3,
        out_specs=[VMEM] * 2,
        out_shape=[shape, shape],
        compiler_params=params(12),
        cost_estimate=cost(0, 6 * from_x.shape[0] * from_x.shape[1]),
        name="second",
    )(keep, from_x, from_y)


def totals_kernel(terms, *refs):
    outs = refs[5 * len(terms) :]
    done = 0
    for index, count in enumerate(terms):
        keep, from_x, from_y, second_x, second_y = refs[5 * index : 5 * index + 5]
        for term in range(count):
            out = outs[done]
            done += 1
            size = out.shape[0] // 2
            base, pair, one = 4 * term * size, 2 * term * size, term * size
            out[:size, :] = (
                wide(keep[base + 2 * size : base + 3 * size, :])
                + wide(from_x[pair : pair + size, :])
                + wide(second_y[one : one + size, :])
            )
            out[size:, :] = (
                wide(keep[base + 3 * size : base + 4 * size, :])
                + wide(from_y[pair + size : pair + 2 * size, :])
                + wide(second_x[one : one + size, :])
            )


def totals(terms, *groups):
    shapes = [
        (2 * group[3].shape[0] // count, group[3].shape[1])
        for count, group in zip(terms, groups)
        for _ in range(count)
    ]
    return pl.pallas_call(
        functools.partial(totals_kernel, terms),
        in_specs=[VMEM] * (5 * len(groups)),
        out_specs=[VMEM] * len(shapes),
        out_shape=[jax.ShapeDtypeStruct(shape, jnp.float32) for shape in shapes],
        compiler_params=params(56),
        cost_estimate=cost(0, 10 * sum(rows * width for rows, width in shapes)),
        name="totals",
    )(*[value for group in groups for value in group])


def finish_kernel(own_qkv, own_out, first, second_ref, grad_q, grad_k, grad_v, grad_o):
    size = grad_q.shape[0]
    grad_q[...] = wide(own_qkv[:size, :]) + wide(first[:size, :])
    grad_k[...] = wide(own_qkv[size : 2 * size, :]) + wide(first[size:, :])
    grad_v[...] = wide(own_qkv[2 * size :, :]) + wide(second_ref[:size, :])
    grad_o[...] = wide(own_out[...]) + wide(second_ref[size:, :])


def finish(own_qkv, own_out, first, second_part):
    rows, width = own_out.shape
    cols = 1024
    return pl.pallas_call(
        finish_kernel,
        grid=(width // cols,),
        in_specs=[
            pl.BlockSpec((value.shape[0], cols), lambda c: (0, c))
            for value in (own_qkv, own_out, first, second_part)
        ],
        out_specs=[pl.BlockSpec((rows, cols), lambda c: (0, c))] * 4,
        out_shape=[jax.ShapeDtypeStruct((rows, width), jnp.float32)] * 4,
        compiler_params=params(56),
        cost_estimate=cost(0, 24 * rows * width),
        name="finish",
    )(own_qkv, own_out, first, second_part)


def sends_kernel(own_ref, other_ref, to_x, to_y, keep):
    size = to_x.shape[0]
    to_x[...] = low(wide(own_ref[:size, :]) + wide(other_ref[:size, :]))
    to_y[...] = low(wide(own_ref[size : 2 * size, :]) + wide(other_ref[size : 2 * size, :]))
    keep[...] = wide(own_ref[2 * size :, :]) + wide(other_ref[2 * size :, :])


def sends(own, other, limit):
    rows, width = own.shape
    shape = jax.ShapeDtypeStruct((rows // 4, width), jnp.bfloat16)
    return pl.pallas_call(
        sends_kernel,
        in_specs=[VMEM] * 2,
        out_specs=[VMEM] * 3,
        out_shape=[shape, shape, jax.ShapeDtypeStruct((rows // 2, width), jnp.float32)],
        compiler_params=params(limit),
        cost_estimate=cost(0, 7 * rows * width),
        name="sends",
    )(own, other)


def fence(*values):
    return lax.optimization_barrier(values)


def swap(values, bits):
    return lax.ppermute(values, "seq", [(i, i ^ bits) for i in range(2 * CHIPS)])


def ring(values, step):
    n = lax.axis_size("fsdp")
    return lax.ppermute(values, "fsdp", [(i, (i + step) % n) for i in range(n)])


def line_order(slots):
    n = len(slots)
    order = (lax.axis_index("fsdp") - jnp.arange(n, dtype=jnp.int32)) % n
    return jnp.stack(slots)[order]


def both(values, other, bits):
    high = (lax.axis_index("seq") & bits) != 0
    return jnp.concatenate(
        [jnp.where(high, other, values), jnp.where(high, values, other)], axis=0
    )


def halves(values, bits):
    high = (lax.axis_index("seq") & bits) != 0
    size = values.shape[0] // 2
    lower, upper = values[:size], values[size:]
    return jnp.where(high, upper, lower), jnp.where(high, lower, upper)


def plane_total(keep, from_x, from_y, second_x, second_y):
    size = keep.shape[0] // 4
    first = wide(keep[2 * size : 3 * size]) + wide(from_x[:size]) + wide(second_y)
    second = wide(keep[3 * size :]) + wide(from_y[size:]) + wide(second_x)
    return jnp.concatenate([first, second], axis=0)


def add(*values):
    return functools.reduce(lambda left, right: left + right, [wide(value) for value in values])


def per_device(
    tokens,
    starts,
    first_gain,
    query_weight,
    key_weight,
    value_weight,
    output_weight,
    bias_table,
    second_gain,
    gate_weight,
    up_weight,
    down_weight,
    cotangent,
):
    index = lax.axis_index("seq")[None]
    own = tokens[0]
    half = own.shape[0] // 2
    grad_out = cotangent[0]
    rows = first_gain.shape[0]
    buckets = bias_table.shape[0]
    qkv0 = low(
        jnp.concatenate([query_weight, key_weight, value_weight, output_weight], axis=0)
    )
    small = low(jnp.concatenate([first_gain, second_gain, bias_table]))
    own, qkv0, small, gate_weight, up_weight, down_weight = fence(
        own, qkv0, small, gate_weight, up_weight, down_weight
    )

    tok_x, tok_y = swap(own, ACROSS), swap(own, ALONG)
    small_slots = [small] + [ring(small, k) for k in range(1, 4)]
    small_slots, own, qkv0, gate_weight, up_weight, down_weight = fence(
        small_slots, own, qkv0, gate_weight, up_weight, down_weight
    )
    qkv1 = ring(qkv0, 1)
    gain_part = line_order([value[: 2 * rows] for value in small_slots]).reshape(-1)
    packed = jnp.concatenate([gain_part, low(starts[0])])[None]
    packed = both(packed, swap(packed, CORE), CORE)
    packed, gate_weight, up_weight, down_weight = fence(
        packed, gate_weight, up_weight, down_weight
    )
    near = both(packed, swap(packed, ACROSS), ACROSS)
    far = both(swap(packed, ALONG), swap(packed, ALONG | ACROSS), ACROSS)
    packed = both(near, far, ALONG)
    packed, tok_x, tok_y, gate_weight, up_weight, down_weight = fence(
        packed, tok_x, tok_y, gate_weight, up_weight, down_weight
    )

    tok_d1, tok_d2 = swap(tok_y[:half], ACROSS), swap(tok_x[half:], ALONG)
    tok_cx, tok_cy = swap(tok_x, CORE), swap(tok_y, CORE)
    gain_count = gain_part.shape[0]
    gains = wide(packed[:, :gain_count]).reshape(-1, 4, 2, rows)
    gain_first = gains[:, :, 0].reshape(-1)
    gain_second = gains[:, :, 1].reshape(-1)
    segment = jnp.cumsum(packed[:, gain_count:].reshape(-1).astype(jnp.int32), dtype=jnp.int32)
    tables = [wide(value[2 * rows :]) for value in small_slots]
    bands = [bias_bands(jnp.stack(tables[2 * p : 2 * p + 2])) for p in range(2)]
    tok_d1, tok_d2, tok_cx, tok_cy, segment, gain_first, gain_second, bands, own = fence(
        tok_d1, tok_d2, tok_cx, tok_cy, segment, gain_first, gain_second, bands, own
    )

    tok_c, tok_c1, tok_c2 = swap(own, CORE), swap(tok_d1, CORE), swap(tok_d2, CORE)
    feed0 = low(jnp.concatenate([gate_weight, up_weight, down_weight], axis=0))
    tok_c, tok_c1, tok_c2, feed0, qkv1 = fence(tok_c, tok_c1, tok_c2, feed0, qkv1)

    qkv2 = ring(qkv1, 1)
    feed_half = feed0.shape[0] // 2
    feed_top, feed_low = feed0[:feed_half], feed0[feed_half:]
    feed_xl, feed_yt = swap(feed_low, ACROSS), swap(feed_top, ALONG)
    feed_top, feed_low = fence(feed_top, feed_low)
    feed_xt, feed_yl = swap(feed_top, ACROSS), swap(feed_low, ALONG)
    tok_pieces = (own, tok_x, tok_y, tok_d1, tok_d2, tok_c, tok_cx, tok_cy, tok_c1, tok_c2)
    hidden_one, qkv_a, weight_a = norm_project(index, gain_first, (qkv0, qkv1), tok_pieces)
    hidden_one, qkv_a, weight_a, qkv2, grad_out, feed_xl, feed_yt = fence(
        hidden_one, qkv_a, weight_a, qkv2, grad_out, feed_xl, feed_yt
    )

    qkv3 = ring(qkv2, 1)
    feed_dt, feed_dl = swap(feed_yt, ACROSS), swap(feed_xl, ALONG)
    mixed_a, lse_a = attention_forward(qkv_a, segment, bands[0][0])
    out0, out1, out2 = (value[3 * DK :] for value in (qkv0, qkv1, qkv2))
    mixed_a, lse_a, hidden_one, qkv3, feed_xt, feed_yl, out0, out1, out2 = fence(
        mixed_a, lse_a, hidden_one, qkv3, feed_xt, feed_yl, out0, out1, out2
    )

    cot1 = ring(grad_out, 1)
    qkv_b, weight_b = project(hidden_one, (qkv2, qkv3))
    out3 = qkv3[3 * DK :]
    mixed_b, lse_b = attention_forward(qkv_b, segment, bands[1][0])
    mixed_b, lse_b, out3, grad_out = fence(mixed_b, lse_b, out3, grad_out)
    cot_c0 = swap(grad_out, CORE)
    out_slots = (out0, out1, out2, out3)
    mixed = (mixed_a, mixed_b)
    part_other = spread(index, 1, mixed, out_slots, 14)
    part_other, mixed, feed_dt, feed_dl, cot1, cot_c0 = fence(
        part_other, mixed, feed_dt, feed_dl, cot1, cot_c0
    )
    part_other, cot2, cot_c1 = swap(part_other, CORE), ring(cot1, 1), swap(cot1, CORE)
    part_own = spread(index, 0, mixed, out_slots, 14)
    part_own, part_other, cot_c1 = fence(part_own, part_other, cot_c1)

    send_x, send_y, keep = sends(part_own, part_other, 12)
    send_x, send_y, keep = fence(send_x, send_y, keep)
    from_x, from_y = swap(send_x, ACROSS), swap(send_y, ALONG)
    weights = assemble(feed0, feed_xt, feed_xl, feed_yt, feed_yl, feed_dt, feed_dl)
    from_x, from_y, weights, cot2 = fence(from_x, from_y, weights, cot2)
    send_x, send_y = fence(*second(1, keep, from_x, from_y))
    second_x, second_y = swap(send_x, ACROSS), swap(send_y, ALONG)
    cot3, cot_c2 = ring(cot2, 1), swap(cot2, CORE)
    second_x, second_y, cot3, cot_c2 = fence(second_x, second_y, cot3, cot_c2)
    inputs = wide(own)
    resid_one = inputs + plane_total(keep, from_x, from_y, second_x, second_y)

    scale_two = lax.rsqrt(jnp.mean(resid_one * resid_one, axis=-1, keepdims=True) + EPSILON)
    normed_two = resid_one * scale_two
    hid0 = low(normed_two * gain_second)
    hid0, resid_one, scale_two = fence(hid0, resid_one, scale_two)

    hid1, hid_c0, cot_c3 = ring(hid0, 1), swap(hid0, CORE), swap(cot3, CORE)
    hid_c0, cot_c3 = fence(hid_c0, cot_c3)
    feed_a = feed(weights, (hid0, hid_c0), (grad_out, cot_c0))
    feed_a, hid1 = fence(feed_a, hid1)
    hid2, hid_c1 = ring(hid1, 1), swap(hid1, CORE)
    hid_c1, feed_a = fence(hid_c1, feed_a)
    grad_c0, out_c0 = swap(feed_a[4], CORE), swap(feed_a[6], CORE)
    feed_b = feed(weights, (hid1, hid_c1), (cot1, cot_c1))
    feed_b, hid2, grad_c0, out_c0 = fence(feed_b, hid2, grad_c0, out_c0)
    hid3, hid_c2 = ring(hid2, 1), swap(hid2, CORE)
    hid_c2, feed_b = fence(hid_c2, feed_b)
    grad_c1, out_c1 = swap(feed_b[4], CORE), swap(feed_b[6], CORE)
    feed_c = feed(weights, (hid2, hid_c2), (cot2, cot_c2))
    feed_c, hid3, grad_c1, out_c1 = fence(feed_c, hid3, grad_c1, out_c1)
    hid_c3 = swap(hid3, CORE)
    dh = ring(low(add(feed_b[3], grad_c1)), 1)
    hid_c3, feed_c = fence(hid_c3, feed_c)
    grad_c2, out_c2 = swap(feed_c[4], CORE), swap(feed_c[6], CORE)
    feed_d = feed(weights, (hid3, hid_c3), (cot3, cot_c3))
    feed_d, dh, grad_c2, out_c2 = fence(feed_d, dh, grad_c2, out_c2)
    dh = ring(low(add(feed_c[3], grad_c2, dh)), 1)
    grad_c3, out_c3 = swap(feed_d[4], CORE), swap(feed_d[6], CORE)
    parts = (feed_a, feed_b, feed_c, feed_d)
    hid_pieces = (hid0, hid_c0, hid1, hid_c1, hid2, hid_c2, hid3, hid_c3)
    cot_pieces = (grad_out, cot_c0, cot1, cot_c1, cot2, cot_c2, cot3, cot_c3)
    grad_down = feed_grad([[part[0] for part in parts]], cot_pieces)
    grad_down, dh, grad_c3, out_c3, hid_pieces = fence(grad_down, dh, grad_c3, out_c3, hid_pieces)

    dh, out_sum = ring(low(add(feed_d[3], grad_c3, dh)), 1), low(add(feed_b[5], out_c1))
    out_sum = ring(out_sum, 1)
    down_x, down_y, down_keep = grad_down
    down_fx, down_fy = swap(down_x, ACROSS), swap(down_y, ALONG)
    grad_both = feed_grad(
        [[part[1] for part in parts], [part[2] for part in parts]], hid_pieces
    )
    dh, grad_both = fence(dh, grad_both)

    grad_hidden_two = add(feed_a[3], grad_c0, dh)
    normed_two = resid_one * scale_two
    shared = grad_hidden_two * gain_second
    grad_resid = wide(grad_out) + scale_two * (
        shared - normed_two * jnp.mean(shared * normed_two, axis=-1, keepdims=True)
    )
    branch = low(grad_resid)
    gain_two_rows = jnp.sum(grad_hidden_two * normed_two, axis=0)
    branch, grad_resid, gain_two_rows, down_fx, down_fy = fence(
        branch, grad_resid, gain_two_rows, down_fx, down_fy
    )

    br_x, br_y, br_c = swap(branch, ACROSS), swap(branch, ALONG), swap(branch, CORE)
    down_x, down_y = second(1, down_keep, down_fx, down_fy)
    out_send = low(add(feed_c[5], out_c2, out_sum))
    br_x, br_y, br_c, down_x, down_y, out_send = fence(
        br_x, br_y, br_c, down_x, down_y, out_send
    )
    br_d1, br_d2 = swap(br_y[:half], ACROSS), swap(br_x[half:], ALONG)
    br_cx, br_cy = swap(br_x, CORE), swap(br_y, CORE)
    out_sum = ring(out_send, 1)
    br_d1, br_d2, br_cx, br_cy = fence(br_d1, br_d2, br_cx, br_cy)

    br_c1, br_c2 = swap(br_d1, CORE), swap(br_d2, CORE)
    down_sx, down_sy = swap(down_x, ACROSS), swap(down_y, ALONG)
    pieces = (branch, br_x, br_y, br_d1, br_d2, br_c, br_cx, br_cy, br_c1, br_c2)
    grad_heads, grad_outs = heads_back(index, out_slots, mixed, pieces)
    grad_heads, grad_outs, grad_both, out_sum = fence(
        grad_heads, grad_outs, grad_both, out_sum
    )

    go0, go1 = grad_outs[0][:DK], grad_outs[0][DK:]
    go2, go3 = grad_outs[1][:DK], grad_outs[1][DK:]
    both_x, both_y, both_keep = grad_both
    both_fx, both_fy = swap(both_x, ACROSS), swap(both_y, ALONG)
    out_sum = ring(low(add(feed_d[5], out_c3, out_sum)), 1)
    dq_b, dk_b, dv_b, diag_b = attention_backward(
        qkv_b, grad_heads[1], mixed[1], lse_b, segment, bands[1][1]
    )
    dq_b, dk_b, dv_b, diag_b, go3 = fence(dq_b, dk_b, dv_b, diag_b, go3)

    go_sum = ring(go3, -1)
    gq2, gq3, sums_b = qkv_grad(gain_first, hidden_one, dq_b, dk_b, dv_b, weight_b)
    gq2, gq3, sums_b, qkv_a, out_sum = fence(gq2, gq3, sums_b, qkv_a, out_sum)

    gq = ring(gq3, -1)
    dq_a, dk_a, dv_a, diag_a = attention_backward(
        qkv_a, grad_heads[0], mixed[0], lse_a, segment, bands[0][1]
    )
    dq_a, dk_a, dv_a, diag_a, both_fx, both_fy = fence(
        dq_a, dk_a, dv_a, diag_a, both_fx, both_fy
    )

    both_x, both_y = second(2, both_keep, both_fx, both_fy)
    both_sx, both_sy = swap(both_x, ACROSS), swap(both_y, ALONG)
    lefts = (dq_a, dk_a, dv_a, dq_b, dk_b, dv_b)
    back_other = spread(index, 1, lefts, (weight_a, weight_b), 14)
    back_other, lefts, gq, go_sum, down_sx, down_sy = fence(
        back_other, lefts, gq, go_sum, down_sx, down_sy
    )
    gq = ring(low(add(gq2, gq)), -1)
    back_other = swap(back_other, CORE)
    back_own, gq0, gq1, sums_a = last(index, gain_first, hidden_one, lefts, (weight_a, weight_b))
    back_own, back_other, gq0, gq1, sums_a, both_sx, both_sy, go_sum = fence(
        back_own, back_other, gq0, gq1, sums_a, both_sx, both_sy, go_sum
    )
    send_x, send_y, keep = sends(back_own, back_other, 16)
    gain_rows = jnp.stack([(sums_a + sums_b)[0], gain_two_rows]).reshape(2, 2, 2, 2, 4, -1)
    gain_rows = jnp.transpose(gain_rows, (3, 1, 2, 4, 0, 5)).reshape(2 * CHIPS, -1)
    send_x, send_y, keep, gq1, gain_rows, go_sum = fence(
        send_x, send_y, keep, gq1, gain_rows, go_sum
    )
    go_sum = ring(low(add(go2, go_sum)), -1)

    from_x, from_y = swap(send_x, ACROSS), swap(send_y, ALONG)
    gain_keep, gain_send = halves(gain_rows, CORE)
    gain_rows = gain_keep + swap(gain_send, CORE)
    gain_rows, gq1 = fence(gain_rows, gq1)
    gq_send = low(add(gq1, gq))
    gq_first = ring(gq_send[: 2 * DK], -1)
    gain_keep, gain_send = halves(gain_rows, ALONG)
    gain_rows = gain_keep + swap(gain_send, ALONG)
    last_send = jnp.concatenate([gq_send[2 * DK :], low(add(go1, go_sum))], axis=0)
    from_x, from_y, gain_rows, gq_first, last_send = fence(
        from_x, from_y, gain_rows, gq_first, last_send
    )
    send_x, send_y = second(1, keep, from_x, from_y)
    second_x, second_y = swap(send_x, ACROSS), swap(send_y, ALONG)
    gq_last = ring(last_send, -1)
    gain_keep, gain_send = halves(gain_rows, ACROSS)
    gain_rows = gain_keep + swap(gain_send, ACROSS)
    late = (down_keep, both_keep, resid_one, diag_a, gq_first, go0, gq0, out_sum)
    second_x, second_y, gain_rows, late = fence(second_x, second_y, gain_rows, late)
    down_keep, both_keep, resid_one, diag_a, gq_first, go0, gq0, out_sum = late
    tables_a, tables_b = bucket_sums(diag_a), bucket_sums(diag_b)
    table_slots = (tables_a[0], tables_a[1], tables_b[0], tables_b[1])
    gain_slots = line_order(list(gain_rows.reshape(4, -1)))
    sums = [jnp.concatenate([gain_slots[k], table_slots[k]]) for k in range(4)]
    sums = sums[0] + sum(ring(sums[k], -k) for k in range(1, 4))
    grad_down_w, grad_gate_w, grad_up_w = totals(
        (1, 2),
        (down_keep, down_fx, down_fy, down_sx, down_sy),
        (both_keep, both_fx, both_fy, both_sx, both_sy),
    )
    layer_out = low(resid_one + add(feed_a[5], out_c0, out_sum))
    grad_hidden_one = plane_total(keep, from_x, from_y, second_x, second_y)
    scale_one = lax.rsqrt(jnp.mean(inputs * inputs, axis=-1, keepdims=True) + EPSILON)
    normed_one = inputs * scale_one
    shared = grad_hidden_one * gain_first
    grad_tokens = low(
        grad_resid
        + scale_one * (shared - normed_one * jnp.mean(shared * normed_one, axis=-1, keepdims=True))
    )
    gq_last, sums = fence(gq_last, sums)
    grad_q, grad_k, grad_v, grad_output_w = finish(gq0, go0, gq_first, gq_last)
    return (
        layer_out[None],
        grad_tokens[None],
        sums[:rows],
        grad_q,
        grad_k,
        grad_v,
        grad_output_w,
        sums[2 * rows :],
        sums[rows : 2 * rows],
        grad_gate_w,
        grad_up_w,
        grad_down_w,
    )


def rms_norm(values, gain):
    return values * lax.rsqrt(jnp.mean(values * values, axis=-1, keepdims=True) + EPSILON) * gain


def gated_gelu(gate, up_part):
    return jax.nn.gelu(gate, approximate=True) * up_part


def gather_rows(values):
    return lax.all_gather(values, "seq", axis=0, tiled=True)


def scatter_rows(values):
    return lax.psum_scatter(
        values.astype(jnp.bfloat16), "seq", scatter_dimension=0, tiled=True
    ).astype(jnp.float32)


def per_device_general(
    tokens,
    starts,
    first_gain,
    query_weight,
    key_weight,
    value_weight,
    output_weight,
    bias_table,
    second_gain,
    gate_weight,
    up_weight,
    down_weight,
    cotangent,
):
    segment = jnp.cumsum(lax.all_gather(starts, "seq", axis=1, tiled=True)[0], dtype=jnp.int32)
    inputs = tokens[0].astype(jnp.float32)
    grad_out = cotangent[0]
    head_count = H // lax.axis_size("seq")
    head_first = lax.axis_index("seq") * head_count
    query_low = query_weight.astype(jnp.bfloat16)
    key_low = key_weight.astype(jnp.bfloat16)
    value_low = value_weight.astype(jnp.bfloat16)
    output_low = output_weight.astype(jnp.bfloat16)
    gate_low = gate_weight.astype(jnp.bfloat16)
    up_low = up_weight.astype(jnp.bfloat16)
    down_low = down_weight.astype(jnp.bfloat16)
    first_low = first_gain.astype(jnp.bfloat16)
    second_low = second_gain.astype(jnp.bfloat16)
    table_low = bias_table.astype(jnp.bfloat16)
    query_part, key_part, value_part, output_part, gate_part, up_rows, down_part = (
        lax.all_gather(query_low, "fsdp", axis=0, tiled=True),
        lax.all_gather(key_low, "fsdp", axis=0, tiled=True),
        lax.all_gather(value_low, "fsdp", axis=0, tiled=True),
        lax.all_gather(output_low, "fsdp", axis=0, tiled=True),
        lax.all_gather(gate_low, "fsdp", axis=0, tiled=True),
        lax.all_gather(up_low, "fsdp", axis=0, tiled=True),
        lax.all_gather(down_low, "fsdp", axis=0, tiled=True),
    )
    gain_one, gain_two, table_full = (
        lax.all_gather(first_low, ("seq", "fsdp"), axis=0, tiled=True),
        lax.all_gather(second_low, ("seq", "fsdp"), axis=0, tiled=True),
        lax.all_gather(table_low, ("seq", "fsdp"), axis=0, tiled=True),
    )
    gain_first = gain_one.astype(jnp.float32)
    gain_second = gain_two.astype(jnp.float32)
    bias_rows = lax.dynamic_slice_in_dim(
        table_full.astype(jnp.float32).reshape(H, BUCKETS), head_first, head_count, 0
    )
    hidden_one = rms_norm(inputs, gain_first).astype(jnp.bfloat16)
    hidden_all = gather_rows(hidden_one)
    query_head = (
        low(nt(hidden_all, query_part))
    )
    key_head = (
        low(nt(hidden_all, key_part))
    )
    value_head = (
        low(nt(hidden_all, value_part))
    )
    pairs = head_count // 2
    pair = [slice(index * PAIR, (index + 1) * PAIR) for index in range(pairs)]
    bands = [bias_bands(bias_rows[2 * index : 2 * index + 2]) for index in range(pairs)]
    qkv = [
        jnp.concatenate([query_head[:, at], key_head[:, at], value_head[:, at]], axis=1)
        for at in pair
    ]
    forward = [attention_forward(qkv[i], segment, bands[i][0]) for i in range(pairs)]
    mixed = jnp.concatenate([out for out, _ in forward], axis=1)
    resid_one = inputs + scatter_rows(nn(mixed, output_part))
    hidden_two = rms_norm(resid_one, gain_second).astype(jnp.bfloat16)
    hidden_two_all = gather_rows(hidden_two)
    gate = nt(hidden_two_all, gate_part)
    up_part = nt(hidden_two_all, up_rows)
    inner = gated_gelu(gate, up_part).astype(jnp.bfloat16)
    layer_out = (resid_one + scatter_rows(nn(inner, down_part))).astype(jnp.bfloat16)
    grad_out_all = gather_rows(grad_out)
    grad_inner = nt(grad_out_all, down_part)
    grad_down = tn(inner, grad_out_all)
    grad_gate, grad_up = jax.vjp(gated_gelu, gate, up_part)[1](grad_inner)
    grad_gate = grad_gate.astype(jnp.bfloat16)
    grad_up = grad_up.astype(jnp.bfloat16)
    grad_gate_w = tn(grad_gate, hidden_two_all)
    grad_up_w = tn(grad_up, hidden_two_all)
    grad_hidden_two = scatter_rows(nn(grad_gate, gate_part) + nn(grad_up, up_rows))
    grad_norm_two, grad_gain_two = jax.vjp(rms_norm, resid_one, gain_second)[1](grad_hidden_two)
    grad_resid = grad_out.astype(jnp.float32) + grad_norm_two
    grad_branch = grad_resid.astype(jnp.bfloat16)
    branch_all = gather_rows(grad_branch)
    grad_output_w = tn(mixed, branch_all)
    grad_heads = (
        low(nt(branch_all, output_part))
    )
    back = [
        attention_backward(
            qkv[i], grad_heads[:, pair[i]], forward[i][0], forward[i][1], segment, bands[i][1]
        )
        for i in range(pairs)
    ]
    grad_query_seq, grad_key_seq, grad_value_seq = (
        jnp.concatenate([values[part] for values in back], axis=1) for part in range(3)
    )
    grad_bias = jnp.concatenate([bucket_sums(values[3]) for values in back], axis=0)
    grad_query_w = tn(grad_query_seq, hidden_all)
    grad_key_w = tn(grad_key_seq, hidden_all)
    grad_value_w = tn(grad_value_seq, hidden_all)
    grad_hidden_one = scatter_rows(
        nn(grad_query_seq, query_part)
        + nn(grad_key_seq, key_part)
        + nn(grad_value_seq, value_part)
    )
    grad_norm_one, grad_gain_one = jax.vjp(rms_norm, inputs, gain_first)[1](grad_hidden_one)
    grad_tokens = (grad_resid + grad_norm_one).astype(jnp.bfloat16)
    grad_table = lax.dynamic_update_slice_in_dim(
        jnp.zeros((H, BUCKETS), jnp.float32), grad_bias, head_first, 0
    ).reshape(-1)
    weight_grads = (
        lax.psum_scatter(
            grad_query_w.astype(jnp.bfloat16), "fsdp", scatter_dimension=0, tiled=True
        ).astype(jnp.float32),
        lax.psum_scatter(
            grad_key_w.astype(jnp.bfloat16), "fsdp", scatter_dimension=0, tiled=True
        ).astype(jnp.float32),
        lax.psum_scatter(
            grad_value_w.astype(jnp.bfloat16), "fsdp", scatter_dimension=0, tiled=True
        ).astype(jnp.float32),
        lax.psum_scatter(
            grad_output_w.astype(jnp.bfloat16), "fsdp", scatter_dimension=0, tiled=True
        ).astype(jnp.float32),
        lax.psum_scatter(
            grad_gate_w.astype(jnp.bfloat16), "fsdp", scatter_dimension=0, tiled=True
        ).astype(jnp.float32),
        lax.psum_scatter(
            grad_up_w.astype(jnp.bfloat16), "fsdp", scatter_dimension=0, tiled=True
        ).astype(jnp.float32),
        lax.psum_scatter(
            grad_down.astype(jnp.bfloat16), "fsdp", scatter_dimension=0, tiled=True
        ).astype(jnp.float32),
    )
    small_grads = (
        lax.psum_scatter(grad_gain_one, ("seq", "fsdp"), scatter_dimension=0, tiled=True),
        lax.psum_scatter(grad_gain_two, ("seq", "fsdp"), scatter_dimension=0, tiled=True),
        lax.psum_scatter(grad_table, ("seq", "fsdp"), scatter_dimension=0, tiled=True),
    )
    return (
        layer_out[None],
        grad_tokens[None],
        small_grads[0],
        weight_grads[0],
        weight_grads[1],
        weight_grads[2],
        weight_grads[3],
        small_grads[2],
        small_grads[1],
        weight_grads[4],
        weight_grads[5],
        weight_grads[6],
    )


def solution(mesh):
    rows = P(("seq", "fsdp"), None)
    row = P(("seq", "fsdp"))
    activations = P("fsdp", "seq", None)
    in_specs = (
        activations,
        P("fsdp", "seq"),
        row,
        rows,
        rows,
        rows,
        rows,
        row,
        row,
        rows,
        rows,
        rows,
        activations,
    )
    out_specs = (
        activations,
        activations,
        row,
        rows,
        rows,
        rows,
        rows,
        row,
        row,
        rows,
        rows,
        rows,
    )
    seq, fsdp = mesh.shape["seq"], mesh.shape["fsdp"]
    plan = per_device if seq == 2 * CHIPS and H == seq * fsdp else per_device_general
    return jax.shard_map(
        plan,
        mesh=mesh,
        in_specs=in_specs,
        out_specs=out_specs,
        check_vma=False,
    )
```
